32 devices in a mesh: groups: 2 (over x), dom: 2 (over core), seq: 8 (over z, y).
Axes of the slice: x: 2, y: 2, z: 4, core: 2. Of those that a mesh axis runs over, the one named last changes fastest.
Arguments:
- latents: bfloat16 [16, 512, 1536], P(('groups', 'dom'), 'seq'), parts along dimension 0, may hold values from -6 to 6
- queries: bfloat16 [16, 512, 1536], P(('groups', 'dom'), 'seq'), parts along dimension 0, may hold values from -64 to 64
- keys: bfloat16 [16, 512, 1536], P(('groups', 'dom'), 'seq'), parts along dimension 0, may hold values from -64 to 64
- values: bfloat16 [16, 512, 1536], P(('groups', 'dom'), 'seq'), parts along dimension 0, may hold values from -6 to 6
- out_weight: bfloat16 [1536, 1536], replicated, may hold values from -0.15625 to 0.15625
- step_index: int32 [2], P('groups'), parts along dimension 0, may hold values from 1 to 27
- embed_weight: bfloat16 [1536, 1024], P('seq'), may hold values from -0.15625 to 0.15625
- norm_gain: float32 [1024], replicated, may hold values from 0.1 to 1.9
- up_weight: bfloat16 [1024, 4096], P(None, 'seq'), may hold values from -0.1875 to 0.1875
- head_weight: float32 [4096], replicated, may hold values from -0.09375 to 0.09375
- prev_logw: float32 [16], P(('groups', 'dom')), parts along dimension 0, may hold values from -20 to 320
- ancestors: int32 [16], P(('groups', 'dom')), parts along dimension 0, may hold values from 0 to 7
Outputs:
- resampled: bfloat16 [16, 512, 1536], P(('groups', 'dom'), 'seq'), parts along dimension 0
- log_weights: float32 [16], P(('groups', 'dom')), parts along dimension 0
The draws below stay inside these ranges and needn't reach their ends.
There are 2 independent parts, one for each index of `groups`. The reference program is written for one: setup_inputs(seed, part) draws one part's arguments, and reference() takes and returns one part's arrays. A program takes and returns all parts, laid end to end along the dimension named above; an argument that names none is the same for every part. Nothing has to cross between parts.
Inputs may be any that keep to these rules, and one draw needn't show every extreme that they name: `ancestors`: index of a particle of the same group.
All inputs are finite; a program needn't handle non-finite values.
Results may differ from the reference program's by a relative error of at most 0.0014.
Values may be sent and summed in bfloat16 or wider, within the bound.
No kernel may reach another device: no remote copies, remote signals or barrier semaphores. Data moves between devices by JAX's collectives and lax.ppermute only.
A program may use at most 128 MiB of HBM per device.

```python
import math
import jax
import jax.numpy as jnp
from jax import lax

D = 1536
HEADS = 24
RW = 1024
RH = 4096
STEPS = 28
P_SIZE = 8
TOKENS = 512


def query_key_pair(key):
    base = jax.random.fold_in(key, 11)
    first_key, second_key = jax.random.split(base)
    key_rows = jnp.clip(jax.random.normal(first_key, (P_SIZE, TOKENS, D), jnp.float32), -6.0, 6.0)
    query_rows = jnp.clip(jax.random.normal(second_key, (P_SIZE, TOKENS, D), jnp.float32), -6.0, 6.0)
    return (query_rows, key_rows)


def draw_queries(key, part):
    return query_key_pair(key)[0].astype(jnp.bfloat16)


def draw_keys(key, part):
    return query_key_pair(key)[1].astype(jnp.bfloat16)


def draw_prev_logw(key, part):
    base = jax.random.fold_in(key, 23)
    drawn = jnp.clip(2.0 * jax.random.normal(base, (P_SIZE,), jnp.float32), -20.0, 20.0)
    return drawn


def set_ends(result, own_key, least, high):
    place = [jax.random.randint(jax.random.fold_in(own_key, axis), (), 0, length) for axis, length in enumerate(result.shape)]
    main_axis = result.shape.index(max(result.shape))
    next_to = place[:main_axis] + [(place[main_axis] + 1) % result.shape[main_axis]] + place[main_axis + 1:]
    return result.at[tuple(place)].set(least).at[tuple(next_to)].set(high)


def shard_levels(own_key, extent, cuts, low, top_value):
    def one(axis_at, parts):
        draws = jax.random.uniform(jax.random.fold_in(jax.random.fold_in(own_key, 6), axis_at), (parts,), jnp.float32, low / len(cuts), top_value / len(cuts))
        return jnp.repeat(jnp.exp(draws), extent[axis_at] // parts).reshape((-1,) + (1,) * (len(extent) - axis_at - 1))

    factor_of = one(*cuts[0])
    for cut in cuts[1:]:
        factor_of = factor_of * one(*cut)
    return factor_of


def centred(stream_key, extent, deviation, limit, shards=(), kind=jnp.bfloat16):
    result = jax.random.normal(stream_key, extent, jnp.float32) * deviation
    if len(shards) > 0:
        result = shard_levels(stream_key, extent, shards, -0.22, 0.18) * result
    return jnp.clip(result, min=-limit, max=limit).astype(kind)


def setup_inputs(seed: int = 0, part: int = 0) -> dict:
    arg_keys = jax.random.split(jax.random.key(seed), 13)
    part_keys = jax.random.split(jax.random.fold_in(arg_keys[12], part), 13)
    return {
        "latents": centred(part_keys[0], (P_SIZE, TOKENS, D), 1.0, 6.0, ((0, 2), (1, 8))),
        "queries": draw_queries(jax.random.fold_in(jax.random.fold_in(arg_keys[12], part), 71), part),
        "keys": draw_keys(jax.random.fold_in(jax.random.fold_in(arg_keys[12], part), 71), part),
        "values": centred(part_keys[3], (P_SIZE, TOKENS, D), 1.0, 6.0, ((0, 2), (1, 8))),
        "out_weight": centred(arg_keys[4], (D, D), D ** -0.5, 0.15625),
        "step_index": jax.random.randint(part_keys[5], (1,), 1, STEPS).astype(jnp.int32),
        "embed_weight": centred(arg_keys[6], (D, RW), D ** -0.5, 0.15625, ((0, 8),)),
        "norm_gain": jnp.clip(1.0 + 0.18 * jax.random.normal(arg_keys[7], (RW,), jnp.float32), 0.1, 1.9),
        "up_weight": centred(arg_keys[8], (RW, RH), RW ** -0.5, 0.1875, ((1, 8),)),
        "head_weight": centred(arg_keys[9], (RH,), RH ** -0.5, 0.09375, (), jnp.float32),
        "prev_logw": draw_prev_logw(jax.random.fold_in(jax.random.fold_in(arg_keys[12], part), 71), part),
        "ancestors": set_ends(jax.random.randint(part_keys[11], (P_SIZE,), 0, P_SIZE), jax.random.fold_in(part_keys[11], 1), 0, P_SIZE - 1).astype(jnp.int32),
    }


potential_scale = 4.0
norm_eps = 1e-05

def particle_attention(triple):
    query_rows, key_rows, value_rows = triple
    head_width = D // HEADS
    query_heads = query_rows.reshape(TOKENS, HEADS, head_width).astype(jnp.float32)
    key_heads = key_rows.reshape(TOKENS, HEADS, head_width).astype(jnp.float32)
    value_heads = value_rows.reshape(TOKENS, HEADS, head_width).astype(jnp.float32)
    scores = jnp.einsum('qhd,khd->hqk', query_heads, key_heads) * (1.0 / math.sqrt(head_width))
    highest = lax.optimization_barrier(jnp.max(scores, axis=-1, keepdims=True))
    expanded = jnp.exp(scores - highest)
    soft_weights = (expanded / lax.optimization_barrier(jnp.sum(expanded, axis=-1, keepdims=True))).astype(jnp.bfloat16)
    soft_weights = lax.optimization_barrier(soft_weights).astype(jnp.float32)
    attended = jnp.einsum('hqk,khd->qhd', soft_weights, value_heads)
    return attended.reshape(TOKENS, D).astype(jnp.bfloat16)

def reference(latents, queries, keys, values, out_weight, step_index, embed_weight, norm_gain, up_weight, head_weight, prev_logw, ancestors):
    attended = lax.map(particle_attention, (queries, keys, values))
    flat = latents.reshape(P_SIZE * TOKENS, D).astype(jnp.float32)
    velocity = flat + jnp.dot(attended.reshape(P_SIZE * TOKENS, D), out_weight, preferred_element_type=jnp.float32)
    sigma = step_index[0].astype(jnp.float32) / STEPS
    clean = (flat - sigma * velocity).astype(jnp.bfloat16)
    stepped = (flat - velocity / STEPS).astype(jnp.bfloat16)
    embedded = jnp.dot(clean, embed_weight, preferred_element_type=jnp.float32)
    centre = lax.optimization_barrier(jnp.mean(embedded, axis=1, keepdims=True))
    centered = embedded - centre
    variance = lax.optimization_barrier(jnp.mean(centered * centered, axis=1, keepdims=True))
    features = jax.nn.gelu(centered * lax.rsqrt(variance + norm_eps) * norm_gain[None, :]).astype(jnp.bfloat16)
    hidden = jax.nn.gelu(jnp.dot(features, up_weight, preferred_element_type=jnp.float32))
    token_score = lax.optimization_barrier(jnp.sum(hidden * head_weight[None, :], axis=1))
    reward = lax.optimization_barrier(jnp.sum(token_score.reshape(P_SIZE, TOKENS), axis=1)) / math.sqrt(TOKENS)
    logits = prev_logw + potential_scale * reward
    highest = jnp.max(logits)
    log_weights = logits - (highest + jnp.log(jnp.sum(jnp.exp(logits - highest))))
    resampled = jnp.take(stepped.reshape(P_SIZE, TOKENS, D), ancestors, axis=0)
    return (resampled, log_weights)
```

```python
import functools
import math

import jax
import jax.numpy as jnp
from jax import lax
from jax.experimental import pallas as pl
from jax.experimental.pallas import tpu as pltpu
from jax.sharding import PartitionSpec as P

HEADS = 24
STEPS = 28
LANES = 128

potential_scale = 4.0
norm_eps = 1e-05
MIB = 1024 * 1024


def pack_kernel(chunks, width, q_ref, k_ref, v_ref, *out_refs):
    blocks = q_ref.shape[2] // width
    part = width // chunks
    for index, ref in enumerate((q_ref, k_ref, v_ref)):
        for block in range(blocks):
            for chunk in range(chunks):
                start = block * width + chunk * part
                out_refs[chunk][block, index] = ref[0, :, start : start + part]


def pack(queries, keys, values, chunks, width):
    particles, tokens, model_width = queries.shape
    blocks = model_width // width
    part = width // chunks
    in_spec = pl.BlockSpec((1, tokens, model_width), lambda i: (i, 0, 0))
    out_spec = pl.BlockSpec((blocks, 3, tokens, part), lambda i: (i, 0, 0, 0))
    out_shape = jax.ShapeDtypeStruct((particles * blocks, 3, tokens, part), queries.dtype)
    return pl.pallas_call(
        functools.partial(pack_kernel, chunks, width),
        grid=(particles,),
        in_specs=[in_spec] * 3,
        out_specs=[out_spec] * chunks,
        out_shape=[out_shape] * chunks,
        name="pack_heads",
    )(queries, keys, values)


def attention_kernel(head_width, block_sources, qkv_ref, out_ref):
    sources, _, tokens, columns = qkv_ref.shape
    total = sources * tokens
    rows = block_sources * tokens
    factor = 1.0 / math.sqrt(head_width) / math.log(2.0)

    def one_block(block, carry):
        span = pl.ds(block * block_sources, block_sources)
        q_all = qkv_ref[span, 0].reshape(rows, columns)
        pieces = []
        for head in range(columns // head_width):
            cols = slice(head * head_width, (head + 1) * head_width)
            k_head = qkv_ref[:, 1, :, cols].reshape(total, head_width)
            v_head = qkv_ref[:, 2, :, cols].reshape(total, head_width)
            scores = lax.dot_general(
                q_all[:, cols], k_head, (((1,), (1,)), ((), ())), preferred_element_type=jnp.float32
            )
            highest = jnp.max(scores, axis=1, keepdims=True)
            expanded = jnp.exp2((scores - highest) * factor)
            norm = 1.0 / jnp.sum(expanded, axis=1, keepdims=True)
            weights = (expanded * norm).astype(jnp.bfloat16)
            pieces.append(jnp.dot(weights, v_head, preferred_element_type=jnp.float32))
        joined = jnp.concatenate(pieces, axis=1).astype(jnp.bfloat16)
        out_ref[span] = joined.reshape(block_sources, tokens, columns)
        return carry

    lax.fori_loop(0, sources // block_sources, one_block, 0)


def attention(qkv, head_width):
    sources, _, tokens, columns = qkv.shape
    total = sources * tokens
    block_sources = max(1, min(sources, 512 // tokens))
    while sources % block_sources:
        block_sources -= 1
    heads = columns // head_width
    return pl.pallas_call(
        functools.partial(attention_kernel, head_width, block_sources),
        in_specs=[pl.BlockSpec(memory_space=pltpu.VMEM)],
        out_specs=pl.BlockSpec(memory_space=pltpu.VMEM),
        out_shape=jax.ShapeDtypeStruct((sources, tokens, columns), jnp.bfloat16),
        compiler_params=pltpu.CompilerParams(vmem_limit_bytes=32 * MIB),
        cost_estimate=pl.CostEstimate(
            flops=4 * total * total * columns,
            bytes_accessed=8 * total * columns,
            transcendentals=heads * total * total,
        ),
        name="attention",
    )(qkv)


def project_kernel(chunks, width, sigma_ref, latents_ref, weight_ref, *refs):
    attended_refs, (clean_ref, stepped_ref) = refs[:chunks], refs[chunks:]
    particles, tokens, columns = latents_ref.shape
    rows = particles * tokens
    depth = weight_ref.shape[0]
    part = width // chunks
    total = jnp.zeros((rows, columns), jnp.float32)
    for block in range(depth // width):
        for chunk in range(chunks):
            start = block * width + chunk * part
            piece = attended_refs[chunk][:, block].reshape(rows, part)
            total += jnp.dot(
                piece, weight_ref[start : start + part, :], preferred_element_type=jnp.float32
            )
    flat = latents_ref[...].reshape(rows, columns).astype(jnp.float32)
    velocity = flat + total
    clean_ref[...] = (flat - sigma_ref[0] * velocity).astype(jnp.bfloat16)
    stepped_ref[...] = (
        (flat - velocity * (1.0 / STEPS)).astype(jnp.bfloat16).reshape(particles, tokens, columns)
    )


def project(sigma, latents, out_weight, attended, width):
    particles, tokens, model_width = latents.shape
    rows = particles * tokens
    blocks = model_width // width
    chunks = len(attended)
    part = width // chunks
    columns = 512 if model_width % 512 == 0 else model_width
    attended = [piece.reshape(particles, blocks, tokens, part) for piece in attended]
    return pl.pallas_call(
        functools.partial(project_kernel, chunks, width),
        grid=(model_width // columns,),
        in_specs=[
            pl.BlockSpec(memory_space=pltpu.SMEM),
            pl.BlockSpec((particles, tokens, columns), lambda i: (0, 0, i)),
            pl.BlockSpec((model_width, columns), lambda i: (0, i)),
        ]
        + [pl.BlockSpec((particles, blocks, tokens, part), lambda i: (0, 0, 0, 0))] * chunks,
        out_specs=[
            pl.BlockSpec((rows, columns), lambda i: (0, i)),
            pl.BlockSpec((particles, tokens, columns), lambda i: (0, 0, i)),
        ],
        out_shape=[
            jax.ShapeDtypeStruct((rows, model_width), jnp.bfloat16),
            jax.ShapeDtypeStruct((particles, tokens, model_width), jnp.bfloat16),
        ],
        compiler_params=pltpu.CompilerParams(vmem_limit_bytes=32 * MIB),
        cost_estimate=pl.CostEstimate(
            flops=2 * rows * model_width * model_width,
            bytes_accessed=2 * model_width * model_width + 8 * rows * model_width,
            transcendentals=0,
        ),
        name="project",
    )(sigma, latents, out_weight, *attended)


def embed_kernel(clean_ref, weight_ref, gain_ref, features_ref, embedded_ref):
    step = pl.program_id(0)
    parts, rows, columns = embedded_ref.shape
    embedded_ref[step] = jnp.dot(
        clean_ref[...], weight_ref[0], preferred_element_type=jnp.float32
    )

    @pl.when(step == parts - 1)
    def _():
        blocks = [embedded_ref[index] for index in range(parts)]
        count = parts * columns
        centre = sum(jnp.sum(block, axis=1, keepdims=True) for block in blocks) * (1.0 / count)
        blocks = [block - centre for block in blocks]
        variance = sum(jnp.sum(block * block, axis=1, keepdims=True) for block in blocks) * (
            1.0 / count
        )
        inverse = lax.rsqrt(variance + norm_eps)
        for index, block in enumerate(blocks):
            cols = slice(index * columns, (index + 1) * columns)
            features_ref[:, cols] = jax.nn.gelu(block * inverse * gain_ref[:, cols]).astype(
                jnp.bfloat16
            )


def embed(clean, weight, gain):
    parts, depth, columns = weight.shape
    rows = clean.shape[0]
    count = parts * columns
    return pl.pallas_call(
        embed_kernel,
        grid=(parts,),
        in_specs=[
            pl.BlockSpec((rows, depth), lambda i: (0, 0)),
            pl.BlockSpec((1, depth, columns), lambda i: (i, 0, 0)),
            pl.BlockSpec((1, count), lambda i: (0, 0)),
        ],
        out_specs=pl.BlockSpec((rows, count), lambda i: (0, 0)),
        out_shape=jax.ShapeDtypeStruct((rows, count), jnp.bfloat16),
        scratch_shapes=[pltpu.VMEM((parts, rows, columns), jnp.float32)],
        compiler_params=pltpu.CompilerParams(vmem_limit_bytes=32 * MIB),
        cost_estimate=pl.CostEstimate(
            flops=2 * rows * depth * count,
            bytes_accessed=2 * depth * count + 2 * rows * (depth + count),
            transcendentals=rows * count,
        ),
        name="embed_norm",
    )(clean, weight, gain.reshape(1, count))


def reward_kernel(particles, features_ref, weight_ref, head_ref, out_ref, total_ref):
    step = pl.program_id(0)
    parts, _, depth, columns = weight_ref.shape
    rows = features_ref.shape[0]
    weight = weight_ref[...].reshape(parts * depth, columns)
    hidden = jnp.dot(features_ref[...], weight, preferred_element_type=jnp.float32)
    scored = jax.nn.gelu(hidden) * head_ref[0]

    @pl.when(step == 0)
    def _():
        total_ref[...] = jnp.zeros_like(total_ref)

    total_ref[...] += jnp.sum(scored.reshape(particles, rows // particles, columns), axis=1)

    @pl.when(step == pl.num_programs(0) - 1)
    def _():
        out_ref[...] = jnp.broadcast_to(
            jnp.sum(total_ref[...], axis=1, keepdims=True), out_ref.shape
        )


def reward(features, weight, head, particles):
    parts, blocks, depth, columns = weight.shape
    rows = features.shape[0]
    return pl.pallas_call(
        functools.partial(reward_kernel, particles),
        grid=(blocks,),
        in_specs=[
            pl.BlockSpec((rows, parts * depth), lambda i: (0, 0)),
            pl.BlockSpec((parts, 1, depth, columns), lambda i: (0, i, 0, 0)),
            pl.BlockSpec((1, 1, columns), lambda i: (i, 0, 0)),
        ],
        out_specs=pl.BlockSpec((particles, LANES), lambda i: (0, 0)),
        out_shape=jax.ShapeDtypeStruct((particles, LANES), jnp.float32),
        scratch_shapes=[pltpu.VMEM((particles, columns), jnp.float32)],
        compiler_params=pltpu.CompilerParams(vmem_limit_bytes=32 * MIB),
        cost_estimate=pl.CostEstimate(
            flops=2 * rows * parts * depth * blocks * columns,
            bytes_accessed=2 * parts * depth * blocks * columns,
            transcendentals=rows * blocks * columns,
        ),
        name="reward",
    )(features, weight, head.reshape(blocks, 1, columns))


def on_device(
    latents,
    queries,
    keys,
    values,
    out_weight,
    step_index,
    embed_weight,
    norm_gain,
    up_weight,
    head_weight,
    prev_logw,
    ancestors,
):
    seq_count = lax.axis_size("seq")
    group_count = lax.axis_size("groups")
    dom_count = lax.axis_size("dom")
    holders = group_count * dom_count
    dom_index = lax.axis_index("dom")
    holder = dom_index * group_count + lax.axis_index("groups")
    particles, tokens, model_width = latents.shape
    head_width = model_width // HEADS
    width = particles * model_width // seq_count
    chunks = 2 if width % (2 * LANES) == 0 else 1

    embed_columns = embed_weight.shape[1] // holders
    embed_share = lax.dynamic_slice_in_dim(embed_weight, holder * embed_columns, embed_columns, 1)
    embed_share = lax.all_gather(embed_share, "seq", axis=0, tiled=True)
    up_depth = up_weight.shape[0] // holders
    up_share = lax.dynamic_slice_in_dim(up_weight, holder * up_depth, up_depth, 0)
    up_share = lax.all_gather(up_share, "seq", axis=0)
    embed_parts = lax.all_gather(
        lax.all_gather(embed_share, "groups", axis=0), "dom", axis=0, tiled=True
    )
    up_parts = lax.all_gather(
        lax.all_gather(up_share, "groups", axis=0), "dom", axis=0, tiled=True
    )

    packed = pack(queries, keys, values, chunks, width)
    arrived = [lax.all_to_all(piece, "seq", 0, 0, tiled=True) for piece in packed]
    attended = [attention(piece, head_width) for piece in arrived]
    returned = [lax.all_to_all(piece, "seq", 0, 0, tiled=True) for piece in attended]

    sigma = step_index.astype(jnp.float32) / STEPS
    clean, stepped = project(sigma, latents, out_weight, returned, width)
    candidates = lax.all_gather(stepped, "dom", axis=0, tiled=True)
    features = embed(clean, embed_parts, norm_gain)
    partial_value = reward(features, up_parts, head_weight, particles)[:, 0]

    first = (lax.axis_index("seq") == 0).astype(jnp.float32)
    total_tokens = tokens * seq_count
    partial_logits = partial_value * (potential_scale / math.sqrt(total_tokens)) + prev_logw * first
    spread = (jnp.arange(dom_count) == dom_index).astype(jnp.float32)
    logits = lax.psum(spread[:, None] * partial_logits[None, :], ("dom", "seq"))
    highest = jnp.max(logits)
    log_total = highest + jnp.log(jnp.sum(jnp.exp(logits - highest)))
    log_weights = lax.dynamic_index_in_dim(logits, dom_index, 0, keepdims=False) - log_total
    resampled = jnp.take(candidates, ancestors, axis=0, mode="clip")
    return (resampled, log_weights)


def solution(mesh):
    in_specs = (
        P(("groups", "dom"), "seq", None),
        P(("groups", "dom"), "seq", None),
        P(("groups", "dom"), "seq", None),
        P(("groups", "dom"), "seq", None),
        P(),
        P("groups"),
        P("seq", None),
        P(),
        P(None, "seq"),
        P(),
        P(("groups", "dom")),
        P(("groups", "dom")),
    )
    out_specs = (P(("groups", "dom"), "seq", None), P(("groups", "dom")))
    return jax.shard_map(
        on_device, mesh=mesh, in_specs=in_specs, out_specs=out_specs, check_vma=False
    )
```

```python
import functools
import math

import jax
import jax.numpy as jnp
from jax import lax
from jax.experimental import pallas as pl
from jax.experimental.pallas import tpu as pltpu
from jax.sharding import PartitionSpec as P

HEADS = 24
STEPS = 28
LANES = 128

potential_scale = 4.0
norm_eps = 1e-05
MIB = 1024 * 1024


def pack_kernel(chunks, width, chunk, q_ref, k_ref, v_ref, out_ref):
    blocks = q_ref.shape[2] // width
    part = width // chunks
    for index, ref in enumerate((q_ref, k_ref, v_ref)):
        for block in range(blocks):
            start = block * width + chunk * part
            out_ref[block, index] = ref[0, :, start : start + part]


def pack(queries, keys, values, chunks, width, chunk):
    particles, tokens, model_width = queries.shape
    blocks = model_width // width
    part = width // chunks
    in_spec = pl.BlockSpec((1, tokens, model_width), lambda i: (i, 0, 0))
    return pl.pallas_call(
        functools.partial(pack_kernel, chunks, width, chunk),
        grid=(particles,),
        in_specs=[in_spec] * 3,
        out_specs=pl.BlockSpec((blocks, 3, tokens, part), lambda i: (i, 0, 0, 0)),
        out_shape=jax.ShapeDtypeStruct((particles * blocks, 3, tokens, part), queries.dtype),
        name="pack_heads",
    )(queries, keys, values)


def gate_kernel(*refs):
    pass


def gate(array, after):
    anywhere = pl.BlockSpec(memory_space=pl.ANY)
    return pl.pallas_call(
        gate_kernel,
        in_specs=[anywhere, anywhere],
        out_specs=anywhere,
        out_shape=jax.ShapeDtypeStruct(array.shape, array.dtype),
        input_output_aliases={0: 0},
        name="gate",
    )(array, after)


def attention_kernel(head_width, block_sources, qkv_ref, out_ref):
    sources, _, tokens, columns = qkv_ref.shape
    total = sources * tokens
    rows = block_sources * tokens
    factor = 1.0 / math.sqrt(head_width) / math.log(2.0)

    def one_block(block, carry):
        span = pl.ds(block * block_sources, block_sources)
        q_all = qkv_ref[span, 0].reshape(rows, columns)
        pieces = []
        for head in range(columns // head_width):
            cols = slice(head * head_width, (head + 1) * head_width)
            k_head = qkv_ref[:, 1, :, cols].reshape(total, head_width)
            v_head = qkv_ref[:, 2, :, cols].reshape(total, head_width)
            scores = lax.dot_general(
                q_all[:, cols], k_head, (((1,), (1,)), ((), ())), preferred_element_type=jnp.float32
            )
            highest = jnp.max(scores, axis=1, keepdims=True)
            expanded = jnp.exp2((scores - highest) * factor)
            norm = 1.0 / jnp.sum(expanded, axis=1, keepdims=True)
            weights = (expanded * norm).astype(jnp.bfloat16)
            pieces.append(jnp.dot(weights, v_head, preferred_element_type=jnp.float32))
        joined = jnp.concatenate(pieces, axis=1).astype(jnp.bfloat16)
        out_ref[span] = joined.reshape(block_sources, tokens, columns)
        return carry

    lax.fori_loop(0, sources // block_sources, one_block, 0)


def attention(qkv, head_width):
    sources, _, tokens, columns = qkv.shape
    total = sources * tokens
    block_sources = max(1, min(sources, 512 // tokens))
    while sources % block_sources:
        block_sources -= 1
    heads = columns // head_width
    return pl.pallas_call(
        functools.partial(attention_kernel, head_width, block_sources),
        in_specs=[pl.BlockSpec(memory_space=pltpu.VMEM)],
        out_specs=pl.BlockSpec(memory_space=pltpu.VMEM),
        out_shape=jax.ShapeDtypeStruct((sources, tokens, columns), jnp.bfloat16),
        compiler_params=pltpu.CompilerParams(vmem_limit_bytes=32 * MIB),
        cost_estimate=pl.CostEstimate(
            flops=4 * total * total * columns,
            bytes_accessed=8 * total * columns,
            transcendentals=heads * total * total,
        ),
        name="attention",
    )(qkv)


def project_kernel(chunks, width, sigma_ref, latents_ref, weight_ref, *refs):
    attended_refs, (clean_ref, stepped_ref) = refs[:chunks], refs[chunks:]
    particles, tokens, columns = latents_ref.shape
    rows = particles * tokens
    depth = weight_ref.shape[0]
    part = width // chunks
    total = jnp.zeros((rows, columns), jnp.float32)
    for block in range(depth // width):
        for chunk in range(chunks):
            start = block * width + chunk * part
            piece = attended_refs[chunk][:, block].reshape(rows, part)
            total += jnp.dot(
                piece, weight_ref[start : start + part, :], preferred_element_type=jnp.float32
            )
    flat = latents_ref[...].reshape(rows, columns).astype(jnp.float32)
    velocity = flat + total
    clean_ref[...] = (flat - sigma_ref[0] * velocity).astype(jnp.bfloat16)
    stepped_ref[...] = (
        (flat - velocity * (1.0 / STEPS)).astype(jnp.bfloat16).reshape(particles, tokens, columns)
    )


def project(sigma, latents, out_weight, attended, width):
    particles, tokens, model_width = latents.shape
    rows = particles * tokens
    blocks = model_width // width
    chunks = len(attended)
    part = width // chunks
    columns = 512 if model_width % 512 == 0 else model_width
    attended = [piece.reshape(particles, blocks, tokens, part) for piece in attended]
    return pl.pallas_call(
        functools.partial(project_kernel, chunks, width),
        grid=(model_width // columns,),
        in_specs=[
            pl.BlockSpec(memory_space=pltpu.SMEM),
            pl.BlockSpec((particles, tokens, columns), lambda i: (0, 0, i)),
            pl.BlockSpec((model_width, columns), lambda i: (0, i)),
        ]
        + [pl.BlockSpec((particles, blocks, tokens, part), lambda i: (0, 0, 0, 0))] * chunks,
        out_specs=[
            pl.BlockSpec((rows, columns), lambda i: (0, i)),
            pl.BlockSpec((particles, tokens, columns), lambda i: (0, 0, i)),
        ],
        out_shape=[
            jax.ShapeDtypeStruct((rows, model_width), jnp.bfloat16),
            jax.ShapeDtypeStruct((particles, tokens, model_width), jnp.bfloat16),
        ],
        compiler_params=pltpu.CompilerParams(vmem_limit_bytes=32 * MIB),
        cost_estimate=pl.CostEstimate(
            flops=2 * rows * model_width * model_width,
            bytes_accessed=2 * model_width * model_width + 8 * rows * model_width,
            transcendentals=0,
        ),
        name="project",
    )(sigma, latents, out_weight, *attended)


def embed_kernel(order_ref, clean_ref, gain_ref, *refs):
    parts = order_ref.shape[0]
    weight_refs, (features_ref, weight_vmem, embedded_ref, sems) = refs[:parts], refs[parts:]
    copies = [
        pltpu.make_async_copy(weight_refs[index], weight_vmem.at[index], sems.at[index])
        for index in range(parts)
    ]
    for copy in copies:
        copy.start()
    for index, copy in enumerate(copies):
        copy.wait()
        embedded_ref[order_ref[index]] = jnp.dot(
            clean_ref[...], weight_vmem[index], preferred_element_type=jnp.float32
        )
    columns = embedded_ref.shape[2]
    count = parts * columns
    blocks = [embedded_ref[index] for index in range(parts)]
    centre = sum(jnp.sum(block, axis=1, keepdims=True) for block in blocks) * (1.0 / count)
    blocks = [block - centre for block in blocks]
    variance = sum(jnp.sum(block * block, axis=1, keepdims=True) for block in blocks) * (
        1.0 / count
    )
    inverse = lax.rsqrt(variance + norm_eps)
    share = features_ref.shape[2]
    for index, block in enumerate(blocks):
        cols = slice(index * columns, (index + 1) * columns)
        piece = jax.nn.gelu(block * inverse * gain_ref[:, cols]).astype(jnp.bfloat16)
        start = index * columns % share
        features_ref[index * columns // share, :, start : start + columns] = piece


def embed(order, clean, weights, gain, depth_parts):
    parts = len(weights)
    depth, columns = weights[0].shape
    rows = clean.shape[0]
    count = parts * columns
    vmem = pl.BlockSpec(memory_space=pltpu.VMEM)
    return pl.pallas_call(
        embed_kernel,
        in_specs=[pl.BlockSpec(memory_space=pltpu.SMEM), vmem, vmem]
        + [pl.BlockSpec(memory_space=pl.ANY)] * parts,
        out_specs=vmem,
        out_shape=jax.ShapeDtypeStruct((depth_parts, rows, count // depth_parts), jnp.bfloat16),
        scratch_shapes=[
            pltpu.VMEM((parts, depth, columns), jnp.bfloat16),
            pltpu.VMEM((parts, rows, columns), jnp.float32),
            pltpu.SemaphoreType.DMA((parts,)),
        ],
        compiler_params=pltpu.CompilerParams(vmem_limit_bytes=56 * MIB),
        cost_estimate=pl.CostEstimate(
            flops=2 * rows * depth * count,
            bytes_accessed=2 * depth * count + 2 * rows * (depth + count),
            transcendentals=rows * count,
        ),
        name="embed_norm",
    )(order, clean, gain.reshape(1, count), *weights)


def reward_kernel(particles, scale, order_ref, features_ref, head_ref, before_ref, *refs):
    parts = order_ref.shape[0]
    weight_refs, (out_ref, total_ref) = refs[:parts], refs[parts:]
    step = pl.program_id(0)
    rows = features_ref.shape[1]
    blocks, _, columns = weight_refs[0].shape

    @pl.when(step == 0)
    def _():
        total_ref[...] = jnp.zeros_like(total_ref)

    for block in range(blocks):
        hidden = sum(
            jnp.dot(
                features_ref[order_ref[index]],
                weight_refs[index][block],
                preferred_element_type=jnp.float32,
            )
            for index in range(parts)
        )
        scored = jax.nn.gelu(hidden) * head_ref[block]
        total_ref[...] += jnp.sum(scored.reshape(particles, rows // particles, columns), axis=1)

    @pl.when(step == pl.num_programs(0) - 1)
    def _():
        sums = jnp.sum(total_ref[...], axis=1, keepdims=True) * scale
        lanes = lax.broadcasted_iota(jnp.int32, out_ref.shape[1:], 1)
        row = jnp.zeros(out_ref.shape[1:], jnp.float32)
        for particle in range(particles):
            row = jnp.where(lanes == particle, sums[particle : particle + 1], row)
        earlier = before_ref.shape[0] - 1
        if earlier:
            out_ref[:earlier] = before_ref[:earlier]
        out_ref[earlier] = row + before_ref[earlier]


def reward(order, features, weights, head, before, particles, scale):
    parts = len(weights)
    blocks, depth, columns = weights[0].shape
    rows = features.shape[1]
    group = 2 if blocks % 2 == 0 else 1
    return pl.pallas_call(
        functools.partial(reward_kernel, particles, scale),
        grid=(blocks // group,),
        in_specs=[
            pl.BlockSpec(memory_space=pltpu.SMEM),
            pl.BlockSpec(features.shape, lambda i: (0, 0, 0)),
            pl.BlockSpec((group, 1, columns), lambda i: (i, 0, 0)),
            pl.BlockSpec(before.shape, lambda i: (0, 0, 0)),
        ]
        + [pl.BlockSpec((group, depth, columns), lambda i: (i, 0, 0))] * parts,
        out_specs=pl.BlockSpec(before.shape, lambda i: (0, 0, 0)),
        out_shape=jax.ShapeDtypeStruct(before.shape, jnp.float32),
        scratch_shapes=[pltpu.VMEM((particles, columns), jnp.float32)],
        compiler_params=pltpu.CompilerParams(vmem_limit_bytes=56 * MIB),
        cost_estimate=pl.CostEstimate(
            flops=2 * rows * parts * depth * blocks * columns,
            bytes_accessed=2 * parts * depth * blocks * columns,
            transcendentals=rows * blocks * columns,
        ),
        name="reward",
    )(order, features, head, before, *weights)


def add_kernel(*refs):
    refs[-1][...] = functools.reduce(lambda total, ref: total + ref[...], refs[1:-1], refs[0][...])


def add_all(arrays):
    return pl.pallas_call(
        add_kernel,
        out_shape=jax.ShapeDtypeStruct(arrays[0].shape, arrays[0].dtype),
        name="add_partials",
    )(*arrays)


def finish_kernel(particles, mine_ref, theirs_ref, out_ref):
    own = mine_ref[0] + theirs_ref[1]
    other = mine_ref[1] + theirs_ref[0]
    lanes = lax.broadcasted_iota(jnp.int32, own.shape, 1)
    both = jnp.maximum(own, other)
    highest = jnp.max(jnp.where(lanes < particles, both, -jnp.inf), axis=1, keepdims=True)
    terms = jnp.where(lanes < particles, jnp.exp(own - highest) + jnp.exp(other - highest), 0.0)
    log_total = highest + jnp.log(jnp.sum(terms, axis=1, keepdims=True))
    out_ref[...] = (own - log_total)[:, :particles]


def finish(mine, theirs, particles):
    return pl.pallas_call(
        functools.partial(finish_kernel, particles),
        out_shape=jax.ShapeDtypeStruct((1, particles), jnp.float32),
        name="log_weights",
    )(mine, theirs).reshape(particles)


def resample_kernel(place_ref, own_ref, other_ref, out_ref, sems):
    particles = out_ref.shape[0]
    for index in range(particles):
        for candidate, ref in enumerate((own_ref, other_ref)):

            @pl.when(place_ref[0, index] == candidate)
            def _():
                pltpu.make_async_copy(
                    ref.at[place_ref[1, index]], out_ref.at[index], sems.at[index]
                ).start()

    for index in range(particles):
        pltpu.make_async_copy(own_ref.at[0], out_ref.at[index], sems.at[index]).wait()


def resample(place, own, other):
    anywhere = pl.BlockSpec(memory_space=pl.ANY)
    return pl.pallas_call(
        resample_kernel,
        in_specs=[pl.BlockSpec(memory_space=pltpu.SMEM), anywhere, anywhere],
        out_specs=anywhere,
        out_shape=jax.ShapeDtypeStruct(own.shape, own.dtype),
        scratch_shapes=[pltpu.SemaphoreType.DMA((own.shape[0],))],
        name="resample",
    )(place, own, other)


def shifted(array, axis, step):
    count = lax.axis_size(axis)
    return lax.ppermute(array, axis, [(i, (i + step) % count) for i in range(count)])


def on_device(
    latents,
    queries,
    keys,
    values,
    out_weight,
    step_index,
    embed_weight,
    norm_gain,
    up_weight,
    head_weight,
    prev_logw,
    ancestors,
):
    seq_count = lax.axis_size("seq")
    group_count = lax.axis_size("groups")
    dom_count = lax.axis_size("dom")
    holders = group_count * dom_count
    dom = lax.axis_index("dom")
    group = lax.axis_index("groups")
    particles, tokens, model_width = latents.shape
    head_width = model_width // HEADS
    width = particles * model_width // seq_count
    chunks = 2 if width % (2 * LANES) == 0 else 1

    embed_columns = embed_weight.shape[1] // holders
    embed_share = lax.dynamic_slice_in_dim(
        embed_weight, (dom * group_count + group) * embed_columns, embed_columns, 1
    )
    embed_share = lax.all_gather(embed_share, "seq", axis=0, tiled=True)
    up_depth = up_weight.shape[0] // group_count
    up_columns = up_weight.shape[1] // dom_count
    up_share = lax.dynamic_slice(
        up_weight, (group * up_depth, dom * up_columns), (up_depth, up_columns)
    )
    up_share = lax.all_gather(up_share, "seq", axis=0)

    packed = [pack(queries, keys, values, chunks, width, chunk) for chunk in range(chunks)]
    arrived = [lax.all_to_all(piece, "seq", 0, 0, tiled=True) for piece in packed]
    embed_share = gate(embed_share, packed[0])
    up_share = gate(up_share, packed[-1])
    embed_near = [embed_share] + [shifted(embed_share, "groups", k) for k in range(1, group_count)]
    up_parts = [up_share] + [shifted(up_share, "groups", k) for k in range(1, group_count)]
    attended = [attention(piece, head_width) for piece in arrived]
    returned = [lax.all_to_all(piece, "seq", 0, 0, tiled=True) for piece in attended]
    embed_near = [gate(piece, attended[0]) for piece in embed_near]
    embed_parts = embed_near + [
        shifted(piece, "dom", k) for k in range(1, dom_count) for piece in embed_near
    ]
    group_order = (group - jnp.arange(group_count)) % group_count
    dom_order = (dom - jnp.arange(dom_count)) % dom_count
    embed_order = (dom_order[:, None] * group_count + group_order[None, :]).reshape(holders)

    sigma = step_index.astype(jnp.float32) / STEPS
    clean, stepped = project(sigma, latents, out_weight, returned, width)
    stepped_other = shifted(stepped, "dom", 1)
    features = embed(embed_order, clean, embed_parts, norm_gain, group_count)
    features_other = shifted(features, "dom", 1)

    scale = potential_scale / math.sqrt(tokens * seq_count)
    head = lax.dynamic_index_in_dim(
        head_weight.reshape(seq_count, dom_count, up_columns), dom, 1, keepdims=True
    )
    first = (lax.axis_index("seq") == 0).astype(jnp.float32)
    start = jnp.pad((prev_logw * first).reshape(1, 1, particles), ((0, 0), (0, 0), (0, LANES - particles)))
    partial_own = reward(group_order, features, up_parts, head, start, particles, scale)
    partial_both = reward(
        group_order,
        features_other,
        up_parts,
        head,
        jnp.concatenate([partial_own, jnp.zeros_like(partial_own)]),
        particles,
        scale,
    )
    mine = add_all([partial_both] + [shifted(partial_both, "seq", k) for k in range(1, seq_count)])
    log_weights = finish(mine, shifted(mine, "dom", 1), particles)

    ancestors = ancestors.astype(jnp.int32)
    place = jnp.stack([(ancestors // particles != dom).astype(jnp.int32), ancestors % particles])
    resampled = resample(place, stepped, stepped_other)
    return (resampled, log_weights)


def solution(mesh):
    in_specs = (
        P(("groups", "dom"), "seq", None),
        P(("groups", "dom"), "seq", None),
        P(("groups", "dom"), "seq", None),
        P(("groups", "dom"), "seq", None),
        P(),
        P("groups"),
        P("seq", None),
        P(),
        P(None, "seq"),
        P(),
        P(("groups", "dom")),
        P(("groups", "dom")),
    )
    out_specs = (P(("groups", "dom"), "seq", None), P(("groups", "dom")))
    return jax.shard_map(
        on_device, mesh=mesh, in_specs=in_specs, out_specs=out_specs, check_vma=False
    )
```

```python
import functools
import math

import jax
import jax.numpy as jnp
from jax import lax
from jax.experimental import pallas as pl
from jax.experimental.pallas import tpu as pltpu
from jax.sharding import PartitionSpec as P

HEADS = 24
STEPS = 28
LANES = 128

potential_scale = 4.0
norm_eps = 1e-05
MIB = 1024 * 1024


def pack_kernel(q_ref, k_ref, v_ref, out_ref):
    for index, ref in enumerate((q_ref, k_ref, v_ref)):
        out_ref[:, 0, index] = ref[...]


def pack_whole_kernel(width, q_ref, k_ref, v_ref, out_ref):
    for index, ref in enumerate((q_ref, k_ref, v_ref)):
        for block in range(out_ref.shape[1]):
            out_ref[:, block, index] = ref[:, :, block * width : (block + 1) * width]


def pack(queries, keys, values, chunks, width, chunk):
    particles, tokens, model_width = queries.shape
    blocks = model_width // width
    part = width // chunks
    out_shape = jax.ShapeDtypeStruct((particles, blocks, 3, tokens, part), queries.dtype)
    params = pltpu.CompilerParams(vmem_limit_bytes=60 * MIB)
    if part % LANES == 0:
        in_spec = pl.BlockSpec((particles, tokens, part), lambda i: (0, 0, i * chunks + chunk))
        packed = pl.pallas_call(
            pack_kernel,
            grid=(blocks,),
            in_specs=[in_spec] * 3,
            out_specs=pl.BlockSpec((particles, 1, 3, tokens, part), lambda i: (0, i, 0, 0, 0)),
            out_shape=out_shape,
            compiler_params=params,
            name="pack_heads",
        )(queries, keys, values)
    else:
        packed = pl.pallas_call(
            functools.partial(pack_whole_kernel, width),
            out_shape=out_shape,
            compiler_params=params,
            name="pack_heads",
        )(queries, keys, values)
    return packed.reshape(particles * blocks, 3, tokens, part)


def gate_kernel(*refs):
    pass


def gate(arrays, after):
    anywhere = pl.BlockSpec(memory_space=pl.ANY)
    return list(
        pl.pallas_call(
        gate_kernel,
        in_specs=[anywhere] * (len(arrays) + 1),
        out_specs=[anywhere] * len(arrays),
        out_shape=[jax.ShapeDtypeStruct(array.shape, array.dtype) for array in arrays],
        input_output_aliases={index: index for index in range(len(arrays))},
        name="gate",
    )(*arrays, after)
    )


def attention_kernel(head_width, block_sources, qkv_ref, out_ref):
    sources, _, tokens, columns = qkv_ref.shape
    total = sources * tokens
    rows = block_sources * tokens
    factor = 1.0 / math.sqrt(head_width) / math.log(2.0)

    def one_block(block, carry):
        span = pl.ds(block * block_sources, block_sources)
        q_all = qkv_ref[span, 0].reshape(rows, columns)
        pieces = []
        for head in range(columns // head_width):
            cols = slice(head * head_width, (head + 1) * head_width)
            k_head = qkv_ref[:, 1, :, cols].reshape(total, head_width)
            v_head = qkv_ref[:, 2, :, cols].reshape(total, head_width)
            scores = lax.dot_general(
                q_all[:, cols], k_head, (((1,), (1,)), ((), ())), preferred_element_type=jnp.float32
            )
            highest = jnp.max(scores, axis=1, keepdims=True)
            expanded = jnp.exp2((scores - highest) * factor)
            norm = 1.0 / jnp.sum(expanded, axis=1, keepdims=True)
            weights = (expanded * norm).astype(jnp.bfloat16)
            pieces.append(jnp.dot(weights, v_head, preferred_element_type=jnp.float32))
        joined = jnp.concatenate(pieces, axis=1).astype(jnp.bfloat16)
        out_ref[span] = joined.reshape(block_sources, tokens, columns)
        return carry

    lax.fori_loop(0, sources // block_sources, one_block, 0)


def attention(qkv, head_width):
    sources, _, tokens, columns = qkv.shape
    total = sources * tokens
    block_sources = max(1, min(sources, 512 // tokens))
    while sources % block_sources:
        block_sources -= 1
    heads = columns // head_width
    step = LANES if columns % LANES == 0 and LANES % head_width == 0 else columns
    return pl.pallas_call(
        functools.partial(attention_kernel, head_width, block_sources),
        grid=(columns // step,),
        in_specs=[pl.BlockSpec((sources, 3, tokens, step), lambda i: (0, 0, 0, i))],
        out_specs=pl.BlockSpec((sources, tokens, step), lambda i: (0, 0, i)),
        out_shape=jax.ShapeDtypeStruct((sources, tokens, columns), jnp.bfloat16),
        compiler_params=pltpu.CompilerParams(vmem_limit_bytes=60 * MIB),
        cost_estimate=pl.CostEstimate(
            flops=4 * total * total * columns,
            bytes_accessed=8 * total * columns,
            transcendentals=heads * total * total,
        ),
        name="attention",
    )(qkv)


def project_kernel(chunks, width, sigma_ref, latents_ref, weight_ref, *refs):
    attended_refs, (clean_ref, stepped_ref) = refs[:chunks], refs[chunks:]
    particles, tokens, columns = latents_ref.shape
    rows = particles * tokens
    depth = weight_ref.shape[0]
    part = width // chunks
    total = jnp.zeros((rows, columns), jnp.float32)
    for block in range(depth // width):
        for chunk in range(chunks):
            start = block * width + chunk * part
            piece = attended_refs[chunk][:, block].reshape(rows, part)
            total += jnp.dot(
                piece, weight_ref[start : start + part, :], preferred_element_type=jnp.float32
            )
    flat = latents_ref[...].reshape(rows, columns).astype(jnp.float32)
    velocity = flat + total
    clean_ref[...] = (flat - sigma_ref[0] * velocity).astype(jnp.bfloat16)
    stepped_ref[...] = (
        (flat - velocity * (1.0 / STEPS)).astype(jnp.bfloat16).reshape(particles, tokens, columns)
    )


def project(sigma, latents, out_weight, attended, width):
    particles, tokens, model_width = latents.shape
    rows = particles * tokens
    blocks = model_width // width
    chunks = len(attended)
    part = width // chunks
    columns = 512 if model_width % 512 == 0 else model_width
    attended = [piece.reshape(particles, blocks, tokens, part) for piece in attended]
    return pl.pallas_call(
        functools.partial(project_kernel, chunks, width),
        grid=(model_width // columns,),
        in_specs=[
            pl.BlockSpec(memory_space=pltpu.SMEM),
            pl.BlockSpec((particles, tokens, columns), lambda i: (0, 0, i)),
            pl.BlockSpec((model_width, columns), lambda i: (0, i)),
        ]
        + [pl.BlockSpec((particles, blocks, tokens, part), lambda i: (0, 0, 0, 0))] * chunks,
        out_specs=[
            pl.BlockSpec((rows, columns), lambda i: (0, i)),
            pl.BlockSpec((particles, tokens, columns), lambda i: (0, 0, i)),
        ],
        out_shape=[
            jax.ShapeDtypeStruct((rows, model_width), jnp.bfloat16),
            jax.ShapeDtypeStruct((particles, tokens, model_width), jnp.bfloat16),
        ],
        compiler_params=pltpu.CompilerParams(vmem_limit_bytes=60 * MIB),
        cost_estimate=pl.CostEstimate(
            flops=2 * rows * model_width * model_width,
            bytes_accessed=2 * model_width * model_width + 8 * rows * model_width,
            transcendentals=0,
        ),
        name="project",
    )(sigma, latents, out_weight, *attended)


def embed_kernel(order_ref, place_ref, clean_ref, gain_ref, *refs):
    parts = order_ref.shape[0]
    weight_refs, (features_ref, weight_vmem, embedded_ref, sems) = refs[:parts], refs[parts:]
    shards, depth, columns = weight_refs[0].shape
    copies = []
    for index in range(parts):
        for shard in range(shards):
            start = pl.multiple_of(place_ref[shard] * depth, depth)
            copy = pltpu.make_async_copy(
                weight_refs[index].at[shard],
                weight_vmem.at[index, pl.ds(start, depth)],
                sems.at[index],
            )
            copy.start()
            copies.append(copy)
    for index in range(parts):
        for copy in copies[index * shards : (index + 1) * shards]:
            copy.wait()
        embedded_ref[order_ref[index]] = jnp.dot(
            clean_ref[...], weight_vmem[index], preferred_element_type=jnp.float32
        )
    count = parts * columns
    blocks = [embedded_ref[index] for index in range(parts)]
    centre = sum(jnp.sum(block, axis=1, keepdims=True) for block in blocks) * (1.0 / count)
    blocks = [block - centre for block in blocks]
    variance = sum(jnp.sum(block * block, axis=1, keepdims=True) for block in blocks) * (
        1.0 / count
    )
    inverse = lax.rsqrt(variance + norm_eps)
    share = features_ref.shape[2]
    for index, block in enumerate(blocks):
        cols = slice(index * columns, (index + 1) * columns)
        piece = jax.nn.gelu(block * inverse * gain_ref[:, cols]).astype(jnp.bfloat16)
        start = index * columns % share
        features_ref[index * columns // share, :, start : start + columns] = piece


def embed(order, place, clean, weights, gain, depth_parts):
    parts = len(weights)
    shards, shard_depth, columns = weights[0].shape
    depth = shards * shard_depth
    rows = clean.shape[0]
    count = parts * columns
    vmem = pl.BlockSpec(memory_space=pltpu.VMEM)
    smem = pl.BlockSpec(memory_space=pltpu.SMEM)
    return pl.pallas_call(
        embed_kernel,
        in_specs=[smem, smem, vmem, vmem] + [pl.BlockSpec(memory_space=pl.ANY)] * parts,
        out_specs=vmem,
        out_shape=jax.ShapeDtypeStruct((depth_parts, rows, count // depth_parts), jnp.bfloat16),
        scratch_shapes=[
            pltpu.VMEM((parts, depth, columns), jnp.bfloat16),
            pltpu.VMEM((parts, rows, columns), jnp.float32),
            pltpu.SemaphoreType.DMA((parts,)),
        ],
        compiler_params=pltpu.CompilerParams(vmem_limit_bytes=60 * MIB),
        cost_estimate=pl.CostEstimate(
            flops=2 * rows * depth * count,
            bytes_accessed=2 * depth * count + 2 * rows * (depth + count),
            transcendentals=rows * count,
        ),
        name="embed_norm",
    )(order, place, clean, gain.reshape(1, count), *weights)


def reward_kernel(particles, scale, parts, offset, *refs):
    order_ref, place_ref, features_ref, head_ref, before_ref = refs[:5]
    weight_refs, (out_ref, total_ref) = refs[5:-2], refs[-2:]
    step = pl.program_id(0)
    rows = features_ref.shape[1]
    columns = weight_refs[0].shape[2]

    @pl.when(step == 0)
    def _():
        total_ref[...] = jnp.zeros_like(total_ref)

    for group in range(len(weight_refs) // parts):
        hidden = sum(
            jnp.dot(
                features_ref[order_ref[index]],
                weight_refs[group * parts + index][0],
                preferred_element_type=jnp.float32,
            )
            for index in range(parts)
        )
        shard = place_ref[group * pl.num_programs(0) + step]
        scored = jax.nn.gelu(hidden) * head_ref[shard]
        total_ref[...] += jnp.sum(scored.reshape(particles, rows // particles, columns), axis=1)

    @pl.when(step == pl.num_programs(0) - 1)
    def _():
        sums = jnp.sum(total_ref[...], axis=1, keepdims=True) * scale
        out_rows = lax.broadcasted_iota(jnp.int32, before_ref.shape, 0)
        lanes = lax.broadcasted_iota(jnp.int32, before_ref.shape, 1)
        row = order_ref[parts] if offset == 0 else order_ref[parts + 1]
        logits = before_ref[...]
        for particle in range(particles):
            here = jnp.logical_and(out_rows == row, lanes == particle)
            logits += jnp.where(here, sums[particle : particle + 1], 0.0)
        out_ref[...] = jnp.broadcast_to(logits[None], out_ref.shape)


def reward(order, place, features, weights, parts, head, before, particles, scale, offset, copies):
    shards, depth, columns = weights[0].shape
    rows = features.shape[1]
    count = shards * len(weights) // parts
    smem = pl.BlockSpec(memory_space=pltpu.SMEM)
    return pl.pallas_call(
        functools.partial(reward_kernel, particles, scale, parts, offset),
        grid=(shards,),
        in_specs=[
            smem,
            smem,
            pl.BlockSpec(features.shape, lambda i: (0, 0, 0)),
            pl.BlockSpec(head.shape, lambda i: (0, 0, 0)),
            pl.BlockSpec(before.shape, lambda i: (0, 0)),
        ]
        + [pl.BlockSpec((1, depth, columns), lambda i: (i, 0, 0))] * len(weights),
        out_specs=pl.BlockSpec((copies, *before.shape), lambda i: (0, 0, 0)),
        out_shape=jax.ShapeDtypeStruct((copies, *before.shape), jnp.float32),
        scratch_shapes=[pltpu.VMEM((particles, columns), jnp.float32)],
        compiler_params=pltpu.CompilerParams(vmem_limit_bytes=60 * MIB),
        cost_estimate=pl.CostEstimate(
            flops=2 * rows * parts * depth * count * columns,
            bytes_accessed=2 * parts * depth * count * columns,
            transcendentals=rows * count * columns,
        ),
        name="reward",
    )(order, place, features, head, before, *weights)


def finish_kernel(particles, doms, row_ref, parts_ref, out_ref):
    logits = jnp.sum(parts_ref[...], axis=0)
    rows = lax.broadcasted_iota(jnp.int32, logits.shape, 0)
    lanes = lax.broadcasted_iota(jnp.int32, logits.shape, 1)
    valid = jnp.logical_and(rows < doms, lanes < particles)
    highest = jnp.max(jnp.where(valid, logits, -jnp.inf))
    total = jnp.sum(jnp.where(valid, jnp.exp(logits - highest), 0.0), axis=1, keepdims=True)
    log_total = highest + jnp.log(jnp.sum(total, axis=0, keepdims=True))
    own = jnp.sum(jnp.where(rows == row_ref[0], logits, 0.0), axis=0, keepdims=True)
    out_ref[...] = (own - log_total)[:, :particles]


def finish(row, parts, particles, doms):
    vmem = pl.BlockSpec(memory_space=pltpu.VMEM)
    return pl.pallas_call(
        functools.partial(finish_kernel, particles, doms),
        in_specs=[pl.BlockSpec(memory_space=pltpu.SMEM), vmem],
        out_specs=vmem,
        out_shape=jax.ShapeDtypeStruct((1, particles), jnp.float32),
        name="log_weights",
    )(row, parts).reshape(particles)


def resample_kernel(place_ref, own_ref, other_ref, out_ref):
    index = pl.program_id(0)

    @pl.when(place_ref[0, index] == 0)
    def _():
        out_ref[...] = own_ref[...]

    @pl.when(place_ref[0, index] != 0)
    def _():
        out_ref[...] = other_ref[...]


def resample(place, own, other):
    particles, tokens, columns = own.shape
    block = (1, tokens, columns)
    return pl.pallas_call(
        resample_kernel,
        grid_spec=pltpu.PrefetchScalarGridSpec(
            num_scalar_prefetch=1,
            grid=(particles,),
            in_specs=[
                pl.BlockSpec(block, lambda i, place: (place[1, i], 0, 0)),
                pl.BlockSpec(block, lambda i, place: (place[2, i], 0, 0)),
            ],
            out_specs=pl.BlockSpec(block, lambda i, place: (i, 0, 0)),
        ),
        out_shape=jax.ShapeDtypeStruct(own.shape, own.dtype),
        compiler_params=pltpu.CompilerParams(vmem_limit_bytes=60 * MIB),
        name="resample",
    )(place, own, other)


def shifted(array, axis, step):
    count = lax.axis_size(axis)
    return lax.ppermute(array, axis, [(i, (i + step) % count) for i in range(count)])


def swapped(array, axis, bit):
    return lax.ppermute(array, axis, [(i, i ^ bit) for i in range(lax.axis_size(axis))])


def on_device(
    latents,
    queries,
    keys,
    values,
    out_weight,
    step_index,
    embed_weight,
    norm_gain,
    up_weight,
    head_weight,
    prev_logw,
    ancestors,
):
    seq_count = lax.axis_size("seq")
    group_count = lax.axis_size("groups")
    dom_count = lax.axis_size("dom")
    holders = group_count * dom_count
    dom = lax.axis_index("dom")
    group = lax.axis_index("groups")
    seq = lax.axis_index("seq")
    particles, tokens, model_width = latents.shape
    head_width = model_width // HEADS
    width = particles * model_width // seq_count
    chunks = 2 if width % (2 * LANES) == 0 else 1

    embed_columns = embed_weight.shape[1] // holders
    embed_share = lax.dynamic_slice_in_dim(
        embed_weight, (dom * group_count + group) * embed_columns, embed_columns, 1
    )[None]
    up_depth = up_weight.shape[0] // group_count
    up_columns = up_weight.shape[1] // dom_count
    up_share = lax.dynamic_slice(
        up_weight, (group * up_depth, dom * up_columns), (up_depth, up_columns)
    )[None]
    bits = [1 << place for place in reversed(range(1, seq_count.bit_length() - 1))]
    offsets = [0]
    for bit in bits[:-1]:
        embed_share = jnp.concatenate([embed_share, swapped(embed_share, "seq", bit)])
        up_share = jnp.concatenate([up_share, swapped(up_share, "seq", bit)])
        offsets = offsets + [offset ^ bit for offset in offsets]

    packed = [pack(queries, keys, values, chunks, width, chunk) for chunk in range(chunks)]
    arrived = [lax.all_to_all(piece, "seq", 0, 0, tiled=True) for piece in packed]
    attended = [attention(piece, head_width) for piece in arrived]
    returned = [lax.all_to_all(piece, "seq", 0, 0, tiled=True) for piece in attended]

    embed_share, up_near = gate([embed_share, up_share], packed[-1])
    embed_share = jnp.concatenate([embed_share, swapped(embed_share, "seq", bits[-1])])
    up_far = swapped(up_near, "seq", bits[-1])
    near, far = offsets, [offset ^ bits[-1] for offset in offsets]
    embed_share, up_near, up_far = gate([embed_share, up_near, up_far], arrived[0])

    embed_share = jnp.concatenate([embed_share, swapped(embed_share, "seq", 1)])
    near_pair = swapped(up_near, "seq", 1)
    far_groups = [shifted(up_far, "groups", k) for k in range(1, group_count)]
    embed_share, near_pair, *far_groups = gate([embed_share, near_pair, *far_groups], attended[0])
    embed_near = [embed_share] + [shifted(embed_share, "groups", k) for k in range(1, group_count)]
    near_groups = [up_near] + [shifted(up_near, "groups", k) for k in range(1, group_count)]
    pair_groups = [near_pair] + [shifted(near_pair, "groups", k) for k in range(1, group_count)]
    far_groups = [up_far] + far_groups
    far_pairs = [swapped(piece, "seq", 1) for piece in far_groups]
    up_parts = near_groups + pair_groups + far_groups + far_pairs
    embed_near = gate(embed_near, attended[-1])
    embed_parts = embed_near + [
        shifted(piece, "dom", k) for k in range(1, dom_count) for piece in embed_near
    ]
    group_order = (group - jnp.arange(group_count)) % group_count
    dom_order = (dom - jnp.arange(dom_count)) % dom_count
    embed_order = (dom_order[:, None] * group_count + group_order[None, :]).reshape(holders)
    both = near + far
    embed_place = seq ^ jnp.array(both + [offset ^ 1 for offset in both], jnp.int32)
    up_place = seq ^ jnp.array(
        near + [offset ^ 1 for offset in near] + far + [offset ^ 1 for offset in far], jnp.int32
    )

    sigma = step_index.astype(jnp.float32) / STEPS
    clean, stepped = project(sigma, latents, out_weight, returned, width)
    stepped_other = shifted(stepped, "dom", 1)
    features = embed(embed_order, embed_place, clean, embed_parts, norm_gain, group_count)
    features_other = shifted(features, "dom", 1)

    scale = potential_scale / math.sqrt(tokens * seq_count)
    head = lax.dynamic_index_in_dim(
        head_weight.reshape(seq_count, dom_count, up_columns), dom, 1, keepdims=True
    )
    rows = 8
    start = jnp.where(
        jnp.logical_and(jnp.arange(rows)[:, None] == dom, seq == 0),
        jnp.pad(prev_logw, (0, LANES - particles))[None, :],
        0.0,
    )
    reward_order = jnp.concatenate([group_order, jnp.stack([dom, (dom + 1) % dom_count])])
    score = functools.partial(reward, reward_order, up_place)
    partial_own = score(
        features, up_parts, group_count, head, start, particles, scale, 0, 1
    )[0]
    partial_both = score(
        features_other, up_parts, group_count, head, partial_own, particles, scale, 1,
        dom_count * seq_count,
    )
    logits = lax.all_to_all(partial_both, ("dom", "seq"), 0, 0, tiled=True)
    log_weights = finish(dom.reshape(1), logits, particles, dom_count)

    ancestors = ancestors.astype(jnp.int32)
    elsewhere = (ancestors // particles != dom).astype(jnp.int32)
    place = jnp.stack([elsewhere, ancestors % particles, ancestors % particles])
    resampled = resample(place, stepped, stepped_other)
    return (resampled, log_weights)


def solution(mesh):
    in_specs = (
        P(("groups", "dom"), "seq", None),
        P(("groups", "dom"), "seq", None),
        P(("groups", "dom"), "seq", None),
        P(("groups", "dom"), "seq", None),
        P(),
        P("groups"),
        P("seq", None),
        P(),
        P(None, "seq"),
        P(),
        P(("groups", "dom")),
        P(("groups", "dom")),
    )
    out_specs = (P(("groups", "dom"), "seq", None), P(("groups", "dom")))
    return jax.shard_map(
        on_device, mesh=mesh, in_specs=in_specs, out_specs=out_specs, check_vma=False
    )
```

```python
import functools
import math

import jax
import jax.numpy as jnp
from jax import lax
from jax.experimental import pallas as pl
from jax.experimental.pallas import tpu as pltpu
from jax.sharding import PartitionSpec as P

HEADS = 24
STEPS = 28
LANES = 128

potential_scale = 4.0
norm_eps = 1e-05
MIB = 1024 * 1024


def pack_kernel(q_ref, k_ref, v_ref, out_ref):
    for index, ref in enumerate((q_ref, k_ref, v_ref)):
        out_ref[:, 0, index] = ref[...]


def pack_whole_kernel(width, q_ref, k_ref, v_ref, out_ref):
    for index, ref in enumerate((q_ref, k_ref, v_ref)):
        for block in range(out_ref.shape[1]):
            out_ref[:, block, index] = ref[:, :, block * width : (block + 1) * width]


def pack(queries, keys, values, chunks, width, chunk):
    particles, tokens, model_width = queries.shape
    blocks = model_width // width
    part = width // chunks
    out_shape = jax.ShapeDtypeStruct((particles, blocks, 3, tokens, part), queries.dtype)
    params = pltpu.CompilerParams(vmem_limit_bytes=60 * MIB)
    if part % LANES == 0:
        in_spec = pl.BlockSpec((particles, tokens, part), lambda i: (0, 0, i * chunks + chunk))
        packed = pl.pallas_call(
            pack_kernel,
            grid=(blocks,),
            in_specs=[in_spec] * 3,
            out_specs=pl.BlockSpec((particles, 1, 3, tokens, part), lambda i: (0, i, 0, 0, 0)),
            out_shape=out_shape,
            compiler_params=params,
            name="pack_heads",
        )(queries, keys, values)
    else:
        packed = pl.pallas_call(
            functools.partial(pack_whole_kernel, width),
            out_shape=out_shape,
            compiler_params=params,
            name="pack_heads",
        )(queries, keys, values)
    return packed.reshape(particles * blocks, 3, tokens, part)


def gate_kernel(*refs):
    pass


def gate(arrays):
    anywhere = pl.BlockSpec(memory_space=pl.ANY)
    count = len(arrays)
    gated = pl.pallas_call(
        gate_kernel,
        in_specs=[anywhere] * count,
        out_specs=[anywhere] * count,
        out_shape=[jax.ShapeDtypeStruct(array.shape, array.dtype) for array in arrays],
        input_output_aliases={index: index for index in range(count)},
        name="gate",
    )(*arrays)
    return list(gated)


def attention_kernel(head_width, block_sources, qkv_ref, out_ref):
    sources, _, tokens, columns = qkv_ref.shape
    total = sources * tokens
    rows = block_sources * tokens
    factor = 1.0 / math.sqrt(head_width) / math.log(2.0)

    def one_block(block, carry):
        span = pl.ds(block * block_sources, block_sources)
        q_all = qkv_ref[span, 0].reshape(rows, columns)
        pieces = []
        for head in range(columns // head_width):
            cols = slice(head * head_width, (head + 1) * head_width)
            k_head = qkv_ref[:, 1, :, cols].reshape(total, head_width)
            v_head = qkv_ref[:, 2, :, cols].reshape(total, head_width)
            scores = lax.dot_general(
                q_all[:, cols], k_head, (((1,), (1,)), ((), ())), preferred_element_type=jnp.float32
            )
            highest = jnp.max(scores, axis=1, keepdims=True)
            expanded = jnp.exp2((scores - highest) * factor)
            norm = 1.0 / jnp.sum(expanded, axis=1, keepdims=True)
            weights = (expanded * norm).astype(jnp.bfloat16)
            pieces.append(jnp.dot(weights, v_head, preferred_element_type=jnp.float32))
        joined = jnp.concatenate(pieces, axis=1).astype(jnp.bfloat16)
        out_ref[span] = joined.reshape(block_sources, tokens, columns)
        return carry

    lax.fori_loop(0, sources // block_sources, one_block, 0)


def attention(qkv, head_width):
    sources, _, tokens, columns = qkv.shape
    total = sources * tokens
    block_sources = max(1, min(sources, 512 // tokens))
    while sources % block_sources:
        block_sources -= 1
    heads = columns // head_width
    step = LANES if columns % LANES == 0 and LANES % head_width == 0 else columns
    return pl.pallas_call(
        functools.partial(attention_kernel, head_width, block_sources),
        grid=(columns // step,),
        in_specs=[pl.BlockSpec((sources, 3, tokens, step), lambda i: (0, 0, 0, i))],
        out_specs=pl.BlockSpec((sources, tokens, step), lambda i: (0, 0, i)),
        out_shape=jax.ShapeDtypeStruct((sources, tokens, columns), jnp.bfloat16),
        compiler_params=pltpu.CompilerParams(vmem_limit_bytes=60 * MIB),
        cost_estimate=pl.CostEstimate(
            flops=4 * total * total * columns,
            bytes_accessed=8 * total * columns,
            transcendentals=heads * total * total,
        ),
        name="attention",
    )(qkv)


def project_kernel(chunks, parts, block, refs_in, refs_out):
    order_ref, place_ref, sigma_ref, latents_ref, gain_ref, out_weight_ref = refs_in[:6]
    attended_refs, weight_refs = refs_in[6 : 6 + chunks], refs_in[6 + chunks :]
    stepped_ref, features_ref = refs_out[:2]
    out_vmem, weight_vmem, attended_ref, clean_ref, embedded_ref, out_sems, sems = refs_out[2:]
    particles, tokens, model_width = latents_ref.shape
    rows = particles * tokens
    shards, depth, columns = weight_refs[0].shape

    out_copies = []
    for index in range(model_width // block):
        cols = slice(index * block, (index + 1) * block)
        copy = pltpu.make_async_copy(
            out_weight_ref.at[:, cols], out_vmem.at[:, cols], out_sems.at[index]
        )
        copy.start()
        out_copies.append(copy)
    copies = []
    for index in range(parts):
        for shard in range(shards):
            start = pl.multiple_of(place_ref[shard] * depth, depth)
            copy = pltpu.make_async_copy(
                weight_refs[index].at[shard],
                weight_vmem.at[index, pl.ds(start, depth)],
                sems.at[index],
            )
            copy.start()
            copies.append(copy)

    part = attended_refs[0].shape[3]
    width = chunks * part
    for place in range(model_width // width):
        for chunk in range(chunks):
            start = place * width + chunk * part
            attended_ref[:, start : start + part] = attended_refs[chunk][:, place].reshape(
                rows, part
            )
    for index in range(model_width // block):
        cols = slice(index * block, (index + 1) * block)
        out_copies[index].wait()
        flat = latents_ref[:, :, cols].reshape(rows, block).astype(jnp.float32)
        velocity = flat + jnp.dot(
            attended_ref[...], out_vmem[:, cols], preferred_element_type=jnp.float32
        )
        clean_ref[:, cols] = (flat - sigma_ref[0] * velocity).astype(jnp.bfloat16)
        stepped_ref[:, :, cols] = (
            (flat - velocity * (1.0 / STEPS)).astype(jnp.bfloat16).reshape(particles, tokens, block)
        )

    for index in range(parts):
        for copy in copies[index * shards : (index + 1) * shards]:
            copy.wait()
        embedded_ref[order_ref[index]] = jnp.dot(
            clean_ref[...], weight_vmem[index], preferred_element_type=jnp.float32
        )
    count = parts * columns
    blocks = [embedded_ref[index] for index in range(parts)]
    centre = sum(jnp.sum(piece, axis=1, keepdims=True) for piece in blocks) * (1.0 / count)
    blocks = [piece - centre for piece in blocks]
    variance = sum(jnp.sum(piece * piece, axis=1, keepdims=True) for piece in blocks) * (
        1.0 / count
    )
    inverse = lax.rsqrt(variance + norm_eps)
    share = features_ref.shape[2]
    for index, piece in enumerate(blocks):
        cols = slice(index * columns, (index + 1) * columns)
        feature = jax.nn.gelu(piece * inverse * gain_ref[:, cols]).astype(jnp.bfloat16)
        start = index * columns % share
        features_ref[index * columns // share, :, start : start + columns] = feature


def project_embed(order, place, sigma, latents, attended, width, out_weight, weights, gain, depth_parts):
    particles, tokens, model_width = latents.shape
    rows = particles * tokens
    chunks, parts = len(attended), len(weights)
    columns = weights[0].shape[2]
    count = parts * columns
    block = 256 if model_width % 256 == 0 else model_width
    attended = [
        piece.reshape(particles, model_width // width, tokens, width // chunks)
        for piece in attended
    ]
    vmem = pl.BlockSpec(memory_space=pltpu.VMEM)
    smem = pl.BlockSpec(memory_space=pltpu.SMEM)
    anywhere = pl.BlockSpec(memory_space=pl.ANY)
    inputs = 6 + chunks + parts

    def kernel(*refs):
        project_kernel(chunks, parts, block, refs[:inputs], refs[inputs:])

    return pl.pallas_call(
        kernel,
        in_specs=[smem, smem, smem, vmem, vmem, anywhere] + [vmem] * chunks + [anywhere] * parts,
        out_specs=[vmem, vmem],
        out_shape=[
            jax.ShapeDtypeStruct(latents.shape, jnp.bfloat16),
            jax.ShapeDtypeStruct((depth_parts, rows, count // depth_parts), jnp.bfloat16),
        ],
        scratch_shapes=[
            pltpu.VMEM((model_width, model_width), jnp.bfloat16),
            pltpu.VMEM((parts, model_width, columns), jnp.bfloat16),
            pltpu.VMEM((rows, model_width), jnp.bfloat16),
            pltpu.VMEM((rows, model_width), jnp.bfloat16),
            pltpu.VMEM((parts, rows, columns), jnp.float32),
            pltpu.SemaphoreType.DMA((model_width // block,)),
            pltpu.SemaphoreType.DMA((parts,)),
        ],
        compiler_params=pltpu.CompilerParams(vmem_limit_bytes=60 * MIB),
        cost_estimate=pl.CostEstimate(
            flops=2 * rows * model_width * (model_width + count),
            bytes_accessed=2 * model_width * (model_width + count) + 8 * rows * model_width,
            transcendentals=rows * count,
        ),
        name="project_embed",
    )(order, place, sigma, latents, gain.reshape(1, count), out_weight, *attended, *weights)


def reward_kernel(particles, scale, parts, offset, *refs):
    order_ref, place_ref, features_ref, head_ref, before_ref = refs[:5]
    weight_refs, (out_ref, weight_vmem, sems) = refs[5:-3], refs[-3:]
    shards, depth, columns = weight_refs[0].shape
    rows = features_ref.shape[1]
    count = shards * len(weight_refs) // parts

    copies = []
    for place in range(count):
        group, shard = divmod(place, shards)
        for index in range(parts):
            copy = pltpu.make_async_copy(
                weight_refs[group * parts + index].at[shard],
                weight_vmem.at[place, index],
                sems.at[place, index],
            )
            copy.start()
            copies.append(copy)
    pieces = [features_ref[order_ref[index]] for index in range(parts)]
    total = jnp.zeros((rows, columns), jnp.float32)
    for place in range(count):
        for copy in copies[place * parts : (place + 1) * parts]:
            copy.wait()
        hidden = sum(
            jnp.dot(pieces[index], weight_vmem[place, index], preferred_element_type=jnp.float32)
            for index in range(parts)
        )
        total += jax.nn.gelu(hidden) * head_ref[place_ref[place]]

    totals = jnp.sum(total.reshape(particles, rows // particles, columns), axis=1)
    sums = jnp.sum(totals, axis=1, keepdims=True) * scale
    out_rows = lax.broadcasted_iota(jnp.int32, before_ref.shape, 0)
    lanes = lax.broadcasted_iota(jnp.int32, before_ref.shape, 1)
    row = order_ref[parts + offset]
    logits = before_ref[...]
    for particle in range(particles):
        here = jnp.logical_and(out_rows == row, lanes == particle)
        logits += jnp.where(here, sums[particle : particle + 1], 0.0)
    out_ref[...] = jnp.broadcast_to(logits[None], out_ref.shape)


def reward(order, place, features, weights, parts, head, before, particles, scale, offset, copies):
    shards, depth, columns = weights[0].shape
    rows = features.shape[1]
    count = shards * len(weights) // parts
    smem = pl.BlockSpec(memory_space=pltpu.SMEM)
    vmem = pl.BlockSpec(memory_space=pltpu.VMEM)
    return pl.pallas_call(
        functools.partial(reward_kernel, particles, scale, parts, offset),
        in_specs=[smem, smem, vmem, vmem, vmem]
        + [pl.BlockSpec(memory_space=pl.ANY)] * len(weights),
        out_specs=vmem,
        out_shape=jax.ShapeDtypeStruct((copies, *before.shape), jnp.float32),
        scratch_shapes=[
            pltpu.VMEM((count, parts, depth, columns), jnp.bfloat16),
            pltpu.SemaphoreType.DMA((count, parts)),
        ],
        compiler_params=pltpu.CompilerParams(vmem_limit_bytes=60 * MIB),
        cost_estimate=pl.CostEstimate(
            flops=2 * rows * parts * depth * count * columns,
            bytes_accessed=2 * parts * depth * count * columns,
            transcendentals=rows * count * columns,
        ),
        name="reward",
    )(order, place, features, head, before, *weights)


def finish_kernel(particles, doms, row_ref, parts_ref, out_ref):
    logits = jnp.sum(parts_ref[...], axis=0)
    rows = lax.broadcasted_iota(jnp.int32, logits.shape, 0)
    lanes = lax.broadcasted_iota(jnp.int32, logits.shape, 1)
    valid = jnp.logical_and(rows < doms, lanes < particles)
    highest = jnp.max(jnp.where(valid, logits, -jnp.inf))
    total = jnp.sum(jnp.where(valid, jnp.exp(logits - highest), 0.0), axis=1, keepdims=True)
    log_total = highest + jnp.log(jnp.sum(total, axis=0, keepdims=True))
    own = jnp.sum(jnp.where(rows == row_ref[0], logits, 0.0), axis=0, keepdims=True)
    out_ref[...] = (own - log_total)[:, :particles]


def finish(row, parts, particles, doms):
    vmem = pl.BlockSpec(memory_space=pltpu.VMEM)
    return pl.pallas_call(
        functools.partial(finish_kernel, particles, doms),
        in_specs=[pl.BlockSpec(memory_space=pltpu.SMEM), vmem],
        out_specs=vmem,
        out_shape=jax.ShapeDtypeStruct((1, particles), jnp.float32),
        name="log_weights",
    )(row, parts).reshape(particles)


def resample_kernel(place_ref, own_ref, other_ref, out_ref):
    index = pl.program_id(0)

    @pl.when(place_ref[0, index] == 0)
    def _():
        out_ref[...] = own_ref[...]

    @pl.when(place_ref[0, index] != 0)
    def _():
        out_ref[...] = other_ref[...]


def resample(place, own, other):
    particles, tokens, columns = own.shape
    block = (1, tokens, columns)
    return pl.pallas_call(
        resample_kernel,
        grid_spec=pltpu.PrefetchScalarGridSpec(
            num_scalar_prefetch=1,
            grid=(particles,),
            in_specs=[
                pl.BlockSpec(block, lambda i, place: (place[1, i], 0, 0)),
                pl.BlockSpec(block, lambda i, place: (place[2, i], 0, 0)),
            ],
            out_specs=pl.BlockSpec(block, lambda i, place: (i, 0, 0)),
        ),
        out_shape=jax.ShapeDtypeStruct(own.shape, own.dtype),
        compiler_params=pltpu.CompilerParams(vmem_limit_bytes=60 * MIB),
        name="resample",
    )(place, own, other)


def shifted(array, axis, step):
    count = lax.axis_size(axis)
    return lax.ppermute(array, axis, [(i, (i + step) % count) for i in range(count)])


def swapped(array, axis, bit):
    return lax.ppermute(array, axis, [(i, i ^ bit) for i in range(lax.axis_size(axis))])


def on_device(
    latents,
    queries,
    keys,
    values,
    out_weight,
    step_index,
    embed_weight,
    norm_gain,
    up_weight,
    head_weight,
    prev_logw,
    ancestors,
):
    seq_count = lax.axis_size("seq")
    group_count = lax.axis_size("groups")
    dom_count = lax.axis_size("dom")
    holders = group_count * dom_count
    dom = lax.axis_index("dom")
    group = lax.axis_index("groups")
    seq = lax.axis_index("seq")
    particles, tokens, model_width = latents.shape
    head_width = model_width // HEADS
    width = particles * model_width // seq_count
    chunks = 2 if width % (2 * LANES) == 0 else 1

    embed_columns = embed_weight.shape[1] // holders
    embed_share = lax.dynamic_slice_in_dim(
        embed_weight, (dom * group_count + group) * embed_columns, embed_columns, 1
    )[None]
    up_depth = up_weight.shape[0] // group_count
    up_columns = up_weight.shape[1] // dom_count
    up_share = lax.dynamic_slice(
        up_weight, (group * up_depth, dom * up_columns), (up_depth, up_columns)
    )[None]
    bits = [1 << place for place in reversed(range(1, seq_count.bit_length() - 1))]
    offsets = [0]
    for bit in bits[:-1]:
        embed_share = jnp.concatenate([embed_share, swapped(embed_share, "seq", bit)])
        up_share = jnp.concatenate([up_share, swapped(up_share, "seq", bit)])
        offsets = offsets + [offset ^ bit for offset in offsets]

    packed = [pack(queries, keys, values, chunks, width, chunk) for chunk in range(chunks)]
    arrived = [lax.all_to_all(piece, "seq", 0, 0, tiled=True) for piece in packed]

    embed_share = jnp.concatenate([embed_share, swapped(embed_share, "seq", bits[-1])])
    up_near, up_far = up_share, swapped(up_share, "seq", bits[-1])
    near, far = offsets, [offset ^ bits[-1] for offset in offsets]
    embed_share, up_near, up_far, arrived[0] = gate([embed_share, up_near, up_far, arrived[0]])

    embed_share = jnp.concatenate([embed_share, swapped(embed_share, "seq", 1)])
    near_pair = swapped(up_near, "seq", 1)
    far_groups = [shifted(up_far, "groups", k) for k in range(1, group_count)]
    attended = [attention(arrived[0], head_width)]
    if chunks > 1:
        embed_share, near_pair, arrived[1], *far_groups = gate(
            [embed_share, near_pair, arrived[1], *far_groups]
        )
        attended.append(attention(arrived[1], head_width))
    returned = [lax.all_to_all(piece, "seq", 0, 0, tiled=True) for piece in attended]
    embed_near = [embed_share] + [shifted(embed_share, "groups", k) for k in range(1, group_count)]
    near_groups = [up_near] + [shifted(up_near, "groups", k) for k in range(1, group_count)]
    pair_groups = [near_pair] + [shifted(near_pair, "groups", k) for k in range(1, group_count)]
    far_groups = [up_far] + far_groups
    far_pairs = [swapped(piece, "seq", 1) for piece in far_groups]
    up_parts = near_groups + pair_groups + far_groups + far_pairs
    if chunks > 1:
        *embed_near, returned[0] = gate([*embed_near, returned[0]])
    embed_parts = embed_near + [
        shifted(piece, "dom", k) for k in range(1, dom_count) for piece in embed_near
    ]
    group_order = (group - jnp.arange(group_count)) % group_count
    dom_order = (dom - jnp.arange(dom_count)) % dom_count
    embed_order = (dom_order[:, None] * group_count + group_order[None, :]).reshape(holders)
    both = near + far
    embed_place = seq ^ jnp.array(both + [offset ^ 1 for offset in both], jnp.int32)
    up_place = seq ^ jnp.array(
        near + [offset ^ 1 for offset in near] + far + [offset ^ 1 for offset in far], jnp.int32
    )

    sigma = step_index.astype(jnp.float32) / STEPS
    stepped, features = project_embed(
        embed_order,
        embed_place,
        sigma,
        latents,
        returned,
        width,
        out_weight,
        embed_parts,
        norm_gain,
        group_count,
    )
    stepped_other = shifted(stepped, "dom", 1)
    features_other = shifted(features, "dom", 1)

    scale = potential_scale / math.sqrt(tokens * seq_count)
    head = lax.dynamic_index_in_dim(
        head_weight.reshape(seq_count, dom_count, up_columns), dom, 1, keepdims=True
    )
    rows = 8
    start = jnp.where(
        jnp.logical_and(jnp.arange(rows)[:, None] == dom, seq == 0),
        jnp.pad(prev_logw, (0, LANES - particles))[None, :],
        0.0,
    )
    reward_order = jnp.concatenate([group_order, jnp.stack([dom, (dom + 1) % dom_count])])
    score = functools.partial(reward, reward_order, up_place)
    partial_own = score(
        features, up_parts, group_count, head, start, particles, scale, 0, 1
    )[0]
    partial_both = score(
        features_other, up_parts, group_count, head, partial_own, particles, scale, 1,
        dom_count * seq_count,
    )
    logits = lax.all_to_all(partial_both, ("dom", "seq"), 0, 0, tiled=True)
    log_weights = finish(dom.reshape(1), logits, particles, dom_count)

    ancestors = ancestors.astype(jnp.int32)
    elsewhere = (ancestors // particles != dom).astype(jnp.int32)
    place = jnp.stack([elsewhere, ancestors % particles, ancestors % particles])
    resampled = resample(place, stepped, stepped_other)
    return (resampled, log_weights)


def solution(mesh):
    in_specs = (
        P(("groups", "dom"), "seq", None),
        P(("groups", "dom"), "seq", None),
        P(("groups", "dom"), "seq", None),
        P(("groups", "dom"), "seq", None),
        P(),
        P("groups"),
        P("seq", None),
        P(),
        P(None, "seq"),
        P(),
        P(("groups", "dom")),
        P(("groups", "dom")),
    )
    out_specs = (P(("groups", "dom"), "seq", None), P(("groups", "dom")))
    return jax.shard_map(
        on_device, mesh=mesh, in_specs=in_specs, out_specs=out_specs, check_vma=False
    )
```

```python
import functools
import math

import jax
import jax.numpy as jnp
from jax import lax
from jax.experimental import pallas as pl
from jax.experimental.pallas import tpu as pltpu
from jax.sharding import PartitionSpec as P

HEADS = 24
STEPS = 28
LANES = 128

potential_scale = 4.0
norm_eps = 1e-05
MIB = 1024 * 1024


def pack_kernel(chunks, width, ids_ref, q_ref, k_ref, v_ref, *refs):
    out_refs, packed_ref = refs[:-1], refs[-1]
    particles, tokens, model_width = q_ref.shape
    blocks = model_width // width
    part = width // chunks
    count = particles * blocks
    for index, ref in enumerate((q_ref, k_ref, v_ref)):
        for particle in range(particles):
            for block in range(blocks):
                for chunk in range(chunks):
                    start = block * width + chunk * part
                    packed_ref[chunk, particle * blocks + block, index] = ref[
                        particle, :, start : start + part
                    ]
    for chunk in range(chunks):
        for place in range(count):
            out_refs[chunk * count + place][...] = packed_ref[chunk, ids_ref[2] ^ place]


def pack(ids, queries, keys, values, chunks, width):
    particles, tokens, model_width = queries.shape
    count = particles * model_width // width
    part = width // chunks
    vmem = pl.BlockSpec(memory_space=pltpu.VMEM)
    shape = jax.ShapeDtypeStruct((3, tokens, part), queries.dtype)
    packed = pl.pallas_call(
        functools.partial(pack_kernel, chunks, width),
        in_specs=[pl.BlockSpec(memory_space=pltpu.SMEM)] + [vmem] * 3,
        out_specs=[vmem] * (chunks * count),
        out_shape=[shape] * (chunks * count),
        scratch_shapes=[pltpu.VMEM((chunks, count, 3, tokens, part), queries.dtype)],
        compiler_params=pltpu.CompilerParams(vmem_limit_bytes=16 * MIB),
        name="pack_heads",
    )(ids, queries, keys, values)
    return [list(packed[chunk * count : (chunk + 1) * count]) for chunk in range(chunks)]


def gate_kernel(*refs):
    pass


def gate(*groups):
    arrays = [array for group in groups for array in group]
    anywhere = pl.BlockSpec(memory_space=pl.ANY)
    count = len(arrays)
    gated = list(
        pl.pallas_call(
            gate_kernel,
            in_specs=[anywhere] * count,
            out_specs=[anywhere] * count,
            out_shape=[jax.ShapeDtypeStruct(array.shape, array.dtype) for array in arrays],
            input_output_aliases={index: index for index in range(count)},
            compiler_params=pltpu.CompilerParams(vmem_limit_bytes=MIB),
            name="gate",
        )(*arrays)
    )
    return [[gated.pop(0) for _ in group] for group in groups]


def attention_kernel(head_width, block_sources, *refs):
    sources = len(refs) // 2
    qkv_refs, out_refs = refs[:sources], refs[sources:]
    _, tokens, columns = qkv_refs[0].shape
    factor = 1.0 / math.sqrt(head_width) / math.log(2.0)
    k_all = jnp.concatenate([ref[1] for ref in qkv_refs], axis=0)
    v_all = jnp.concatenate([ref[2] for ref in qkv_refs], axis=0)
    for block in range(0, sources, block_sources):
        span = slice(block, block + block_sources)
        q_all = jnp.concatenate([ref[0] for ref in qkv_refs[span]], axis=0)
        pieces = []
        for head in range(columns // head_width):
            cols = slice(head * head_width, (head + 1) * head_width)
            scores = lax.dot_general(
                q_all[:, cols],
                k_all[:, cols],
                (((1,), (1,)), ((), ())),
                preferred_element_type=jnp.float32,
            )
            highest = jnp.max(scores, axis=1, keepdims=True)
            expanded = jnp.exp2((scores - highest) * factor)
            norm = 1.0 / jnp.sum(expanded, axis=1, keepdims=True)
            weights = (expanded * norm).astype(jnp.bfloat16)
            pieces.append(
                jnp.dot(weights, v_all[:, cols], preferred_element_type=jnp.float32)
            )
        joined = jnp.concatenate(pieces, axis=1).astype(jnp.bfloat16)
        for index, ref in enumerate(out_refs[span]):
            ref[...] = joined[index * tokens : (index + 1) * tokens]


def attention(arrived, head_width):
    sources = len(arrived)
    _, tokens, columns = arrived[0].shape
    total = sources * tokens
    block_sources = max(1, min(sources, 512 // tokens))
    while sources % block_sources:
        block_sources -= 1
    heads = columns // head_width
    step = LANES if columns % LANES == 0 and LANES % head_width == 0 else columns
    scores_bytes = 4 * block_sources * tokens * total
    return list(
        pl.pallas_call(
            functools.partial(attention_kernel, head_width, block_sources),
            grid=(columns // step,),
            in_specs=[pl.BlockSpec((3, tokens, step), lambda i: (0, 0, i))] * sources,
            out_specs=[pl.BlockSpec((tokens, step), lambda i: (0, i))] * sources,
            out_shape=[jax.ShapeDtypeStruct((tokens, columns), jnp.bfloat16)] * sources,
            compiler_params=pltpu.CompilerParams(
                vmem_limit_bytes=8 * MIB + 6 * scores_bytes
            ),
            cost_estimate=pl.CostEstimate(
                flops=4 * total * total * columns,
                bytes_accessed=8 * total * columns,
                transcendentals=heads * total * total,
            ),
            name="attention",
        )(*arrived)
    )


def project_kernel(chunks, parts, block, offsets, depth_parts, refs_in, refs_out):
    ids_ref, latents_ref, gain_ref, out_weight_ref = refs_in[:4]
    attended_refs, weight_refs = refs_in[4:-parts], refs_in[-parts:]
    dom, group, seq = ids_ref[0], ids_ref[1], ids_ref[2]
    sigma = ids_ref[3].astype(jnp.float32) * (1.0 / STEPS)
    stepped_ref, features_ref = refs_out[:2]
    out_vmem, weight_vmem, attended_ref, clean_ref, embedded_ref, out_sems, sems = refs_out[2:]
    particles, tokens, model_width = latents_ref.shape
    rows = particles * tokens
    shards, depth, columns = weight_refs[0].shape

    out_copies = []
    for index in range(model_width // block):
        cols = slice(index * block, (index + 1) * block)
        copy = pltpu.make_async_copy(
            out_weight_ref.at[:, cols], out_vmem.at[:, cols], out_sems.at[index]
        )
        copy.start()
        out_copies.append(copy)
    copies = []
    for index in range(parts):
        for shard in range(shards):
            start = pl.multiple_of((seq ^ offsets[shard]) * depth, depth)
            copy = pltpu.make_async_copy(
                weight_refs[index].at[shard],
                weight_vmem.at[index, pl.ds(start, depth)],
                sems.at[index],
            )
            copy.start()
            copies.append(copy)

    blocks, _, width = attended_ref.shape
    part = width // chunks
    count = particles * blocks
    for chunk in range(chunks):
        for index in range(count):
            place = seq ^ index
            rows_of = pl.ds(pl.multiple_of(place // blocks * tokens, tokens), tokens)
            attended_ref[place % blocks, rows_of, chunk * part : (chunk + 1) * part] = (
                attended_refs[chunk * count + index][...]
            )
    for index in range(model_width // block):
        cols = slice(index * block, (index + 1) * block)
        out_copies[index].wait()
        flat = latents_ref[:, :, cols].reshape(rows, block).astype(jnp.float32)
        velocity = flat + sum(
            jnp.dot(
                attended_ref[place],
                out_vmem[place * width : (place + 1) * width, cols],
                preferred_element_type=jnp.float32,
            )
            for place in range(blocks)
        )
        clean_ref[:, cols] = (flat - sigma * velocity).astype(jnp.bfloat16)
        stepped_ref[:, :, cols] = (
            (flat - velocity * (1.0 / STEPS)).astype(jnp.bfloat16).reshape(particles, tokens, block)
        )

    for index in range(parts):
        for copy in copies[index * shards : (index + 1) * shards]:
            copy.wait()
        doms = parts // depth_parts
        dom_of = (dom + doms - index // depth_parts) % doms
        group_of = (group + depth_parts - index % depth_parts) % depth_parts
        embedded_ref[dom_of * depth_parts + group_of] = jnp.dot(
            clean_ref[...], weight_vmem[index], preferred_element_type=jnp.float32
        )
    count = parts * columns
    blocks = [embedded_ref[index] for index in range(parts)]
    centre = sum(jnp.sum(piece, axis=1, keepdims=True) for piece in blocks) * (1.0 / count)
    blocks = [piece - centre for piece in blocks]
    variance = sum(jnp.sum(piece * piece, axis=1, keepdims=True) for piece in blocks) * (
        1.0 / count
    )
    inverse = lax.rsqrt(variance + norm_eps)
    share = features_ref.shape[2]
    for index, piece in enumerate(blocks):
        cols = slice(index * columns, (index + 1) * columns)
        feature = jax.nn.gelu(piece * inverse * gain_ref[:, cols]).astype(jnp.bfloat16)
        start = index * columns % share
        features_ref[index * columns // share, :, start : start + columns] = feature


def project_embed(ids, offsets, latents, attended, width, out_weight, weights, gain, depth_parts):
    particles, tokens, model_width = latents.shape
    rows = particles * tokens
    chunks, parts = len(attended), len(weights)
    columns = weights[0].shape[2]
    count = parts * columns
    block = 256 if model_width % 256 == 0 else model_width
    pieces = [piece for chunk in attended for piece in chunk]
    vmem = pl.BlockSpec(memory_space=pltpu.VMEM)
    smem = pl.BlockSpec(memory_space=pltpu.SMEM)
    anywhere = pl.BlockSpec(memory_space=pl.ANY)
    inputs = 4 + len(pieces) + parts

    def kernel(*refs):
        project_kernel(
            chunks, parts, block, offsets, depth_parts, refs[:inputs], refs[inputs:]
        )

    return pl.pallas_call(
        kernel,
        in_specs=[smem, vmem, vmem, anywhere] + [vmem] * len(pieces) + [anywhere] * parts,
        out_specs=[vmem, vmem],
        out_shape=[
            jax.ShapeDtypeStruct(latents.shape, jnp.bfloat16),
            jax.ShapeDtypeStruct((depth_parts, rows, count // depth_parts), jnp.bfloat16),
        ],
        scratch_shapes=[
            pltpu.VMEM((model_width, model_width), jnp.bfloat16),
            pltpu.VMEM((parts, model_width, columns), jnp.bfloat16),
            pltpu.VMEM((model_width // width, rows, width), jnp.bfloat16),
            pltpu.VMEM((rows, model_width), jnp.bfloat16),
            pltpu.VMEM((parts, rows, columns), jnp.float32),
            pltpu.SemaphoreType.DMA((model_width // block,)),
            pltpu.SemaphoreType.DMA((parts,)),
        ],
        compiler_params=pltpu.CompilerParams(vmem_limit_bytes=28 * MIB),
        cost_estimate=pl.CostEstimate(
            flops=2 * rows * model_width * (model_width + count),
            bytes_accessed=2 * model_width * (model_width + count) + 8 * rows * model_width,
            transcendentals=rows * count,
        ),
        name="project_embed",
    )(ids, latents, gain.reshape(1, count), out_weight, *pieces, *weights)


def reward_kernel(particles, scale, parts, doms, offsets, *refs):
    ids_ref, features_ref, head_ref, before_ref = refs[:4]
    weight_refs, (out_ref, weight_vmem, sems) = refs[4:-3], refs[-3:]
    dom, group, seq = ids_ref[0], ids_ref[1], ids_ref[2]
    shards, depth, columns = weight_refs[0].shape
    rows = features_ref.shape[1]
    count = shards * len(weight_refs) // parts

    copies = []
    for place in range(count):
        pair, shard = divmod(place, shards)
        for index in range(parts):
            copy = pltpu.make_async_copy(
                weight_refs[pair * parts + index].at[shard],
                weight_vmem.at[place, index],
                sems.at[place, index],
            )
            copy.start()
            copies.append(copy)
    pieces = [features_ref[(group + parts - index) % parts] for index in range(parts)]
    total = jnp.zeros((rows, columns), jnp.float32)
    for place in range(count):
        for copy in copies[place * parts : (place + 1) * parts]:
            copy.wait()
        hidden = sum(
            jnp.dot(pieces[index], weight_vmem[place, index], preferred_element_type=jnp.float32)
            for index in range(parts)
        )
        total += jax.nn.gelu(hidden) * head_ref[(seq ^ offsets[place]) * doms + dom]

    totals = jnp.sum(total.reshape(particles, rows // particles, columns), axis=1)
    sums = jnp.sum(totals, axis=1, keepdims=True) * scale
    first = len(before_ref.shape) == 1
    shape = out_ref.shape[1:]
    out_rows = lax.broadcasted_iota(jnp.int32, shape, 0)
    lanes = lax.broadcasted_iota(jnp.int32, shape, 1)
    logits = jnp.zeros(shape, jnp.float32) if first else before_ref[...]
    row = dom if first else (dom + 1) % doms
    for particle in range(particles):
        here = jnp.logical_and(out_rows == row, lanes == particle)
        value = sums[particle : particle + 1]
        if first:
            value = value + jnp.where(seq == 0, before_ref[particle], 0.0)
        logits += jnp.where(here, value, 0.0)
    out_ref[...] = jnp.broadcast_to(logits[None], out_ref.shape)


def reward(ids, features, weights, parts, doms, offsets, head, before, particles, scale, copies):
    shards, depth, columns = weights[0].shape
    rows = features.shape[1]
    count = shards * len(weights) // parts
    smem = pl.BlockSpec(memory_space=pltpu.SMEM)
    vmem = pl.BlockSpec(memory_space=pltpu.VMEM)
    return pl.pallas_call(
        functools.partial(reward_kernel, particles, scale, parts, doms, offsets),
        in_specs=[smem, vmem, vmem, smem if before.ndim == 1 else vmem]
        + [pl.BlockSpec(memory_space=pl.ANY)] * len(weights),
        out_specs=vmem,
        out_shape=jax.ShapeDtypeStruct((copies, 8, LANES), jnp.float32),
        scratch_shapes=[
            pltpu.VMEM((count, parts, depth, columns), jnp.bfloat16),
            pltpu.SemaphoreType.DMA((count, parts)),
        ],
        compiler_params=pltpu.CompilerParams(vmem_limit_bytes=20 * MIB),
        cost_estimate=pl.CostEstimate(
            flops=2 * rows * parts * depth * count * columns,
            bytes_accessed=2 * parts * depth * count * columns,
            transcendentals=rows * count * columns,
        ),
        name="reward",
    )(ids, features, head, before, *weights)


def finish_kernel(particles, doms, ids_ref, parts_ref, resampled_ref, out_ref, same_ref):
    logits = jnp.sum(parts_ref[...], axis=0)
    rows = lax.broadcasted_iota(jnp.int32, logits.shape, 0)
    lanes = lax.broadcasted_iota(jnp.int32, logits.shape, 1)
    valid = jnp.logical_and(rows < doms, lanes < particles)
    highest = jnp.max(jnp.where(valid, logits, -jnp.inf))
    total = jnp.sum(jnp.where(valid, jnp.exp(logits - highest), 0.0), axis=1, keepdims=True)
    log_total = highest + jnp.log(jnp.sum(total, axis=0, keepdims=True))
    own = jnp.sum(jnp.where(rows == ids_ref[0], logits, 0.0), axis=0, keepdims=True)
    out_ref[...] = (own - log_total)[:, :particles]


def finish(ids, parts, resampled, particles, doms):
    vmem = pl.BlockSpec(memory_space=pltpu.VMEM)
    anywhere = pl.BlockSpec(memory_space=pl.ANY)
    log_weights, resampled = pl.pallas_call(
        functools.partial(finish_kernel, particles, doms),
        in_specs=[pl.BlockSpec(memory_space=pltpu.SMEM), vmem, anywhere],
        out_specs=[vmem, anywhere],
        out_shape=[
            jax.ShapeDtypeStruct((1, particles), jnp.float32),
            jax.ShapeDtypeStruct(resampled.shape, resampled.dtype),
        ],
        input_output_aliases={2: 1},
        compiler_params=pltpu.CompilerParams(vmem_limit_bytes=2 * MIB),
        name="log_weights",
    )(ids, parts, resampled)
    return resampled, log_weights.reshape(particles)


def resample_kernel(ids_ref, ancestors_ref, own_ref, other_ref, out_ref):
    index = pl.program_id(0)
    own = ancestors_ref[index] // pl.num_programs(0) == ids_ref[0]

    @pl.when(own)
    def _():
        out_ref[...] = own_ref[...]

    @pl.when(jnp.logical_not(own))
    def _():
        out_ref[...] = other_ref[...]


def resample(ids, ancestors, own, other):
    particles, tokens, columns = own.shape
    block = (1, tokens, columns)
    parent = pl.BlockSpec(block, lambda i, ids, ancestors: (ancestors[i] % particles, 0, 0))
    return pl.pallas_call(
        resample_kernel,
        grid_spec=pltpu.PrefetchScalarGridSpec(
            num_scalar_prefetch=2,
            grid=(particles,),
            in_specs=[parent, parent],
            out_specs=pl.BlockSpec(block, lambda i, ids, ancestors: (i, 0, 0)),
        ),
        out_shape=jax.ShapeDtypeStruct(own.shape, own.dtype),
        compiler_params=pltpu.CompilerParams(vmem_limit_bytes=4 * MIB),
        name="resample",
    )(ids, ancestors, own, other)


def shifted(array, axis, step):
    count = lax.axis_size(axis)
    return lax.ppermute(array, axis, [(i, (i + step) % count) for i in range(count)])


def swapped(array, axis, bit):
    return lax.ppermute(array, axis, [(i, i ^ bit) for i in range(lax.axis_size(axis))])


def exchange(pieces):
    return pieces[:1] + [
        swapped(piece, "seq", k + 1) for k, piece in enumerate(pieces[1:])
    ]


def on_device(
    latents,
    queries,
    keys,
    values,
    out_weight,
    step_index,
    embed_weight,
    norm_gain,
    up_weight,
    head_weight,
    prev_logw,
    ancestors,
):
    seq_count = lax.axis_size("seq")
    group_count = lax.axis_size("groups")
    dom_count = lax.axis_size("dom")
    holders = group_count * dom_count
    dom = lax.axis_index("dom")
    group = lax.axis_index("groups")
    seq = lax.axis_index("seq")
    particles, tokens, model_width = latents.shape
    head_width = model_width // HEADS
    width = particles * model_width // seq_count
    chunks = 2 if width % (2 * LANES) == 0 else 1

    ids = jnp.stack([dom, group, seq, step_index[0]]).astype(jnp.int32)

    embed_columns = embed_weight.shape[1] // holders
    embed_share = lax.dynamic_slice_in_dim(
        embed_weight, (dom * group_count + group) * embed_columns, embed_columns, 1
    )[None]
    up_depth = up_weight.shape[0] // group_count
    up_columns = up_weight.shape[1] // dom_count
    up_share = lax.dynamic_slice(
        up_weight, (group * up_depth, dom * up_columns), (up_depth, up_columns)
    )[None]
    bits = [1 << place for place in reversed(range(1, seq_count.bit_length() - 1))]
    near = [0]
    for bit in bits[:-1]:
        embed_share = jnp.concatenate([embed_share, swapped(embed_share, "seq", bit)])
        up_share = jnp.concatenate([up_share, swapped(up_share, "seq", bit)])
        near = near + [offset ^ bit for offset in near]
    far = [offset ^ bits[-1] for offset in near]

    packed = pack(ids, queries, keys, values, chunks, width)
    (embed_share, up_near), packed[0] = gate([embed_share, up_share], packed[0])

    arrived = [exchange(packed[0])]
    embed_share = jnp.concatenate([embed_share, swapped(embed_share, "seq", bits[-1])])
    up_far = swapped(up_near, "seq", bits[-1])
    (embed_share, up_near, up_far), arrived[0], *packed[1:] = gate(
        [embed_share, up_near, up_far], arrived[0], *packed[1:]
    )

    arrived += [exchange(piece) for piece in packed[1:]]
    embed_share = jnp.concatenate([embed_share, swapped(embed_share, "seq", 1)])
    near_pair = swapped(up_near, "seq", 1)
    far_groups = [up_far] + [shifted(up_far, "groups", k) for k in range(1, group_count)]
    attended = [attention(arrived[0], head_width)]
    (embed_share, near_pair), far_groups, attended[0], *arrived[1:] = gate(
        [embed_share, near_pair], far_groups, attended[0], *arrived[1:]
    )

    returned = [exchange(attended[0])]
    embed_near = [embed_share] + [shifted(embed_share, "groups", k) for k in range(1, group_count)]
    far_pairs = [swapped(far_groups[0], "seq", 1)]
    attended += [attention(piece, head_width) for piece in arrived[1:]]
    (up_near, near_pair), embed_near, far_groups[1:], returned[0], *attended[1:] = gate(
        [up_near, near_pair], embed_near, far_groups[1:], returned[0], *attended[1:]
    )

    returned += [exchange(pieces) for pieces in attended[1:]]
    embed_parts = embed_near + [
        shifted(piece, "dom", k) for k in range(1, dom_count) for piece in embed_near
    ]
    near_groups = [up_near] + [shifted(up_near, "groups", k) for k in range(1, group_count)]
    pair_groups = [near_pair] + [shifted(near_pair, "groups", k) for k in range(1, group_count)]
    far_pairs += [swapped(piece, "seq", 1) for piece in far_groups[1:]]
    up_parts = near_groups + pair_groups + far_groups + far_pairs
    embed_offsets = near + far + [offset ^ 1 for offset in near + far]
    up_offsets = near + [offset ^ 1 for offset in near] + far + [offset ^ 1 for offset in far]

    stepped, features = project_embed(
        ids,
        embed_offsets,
        latents,
        returned,
        width,
        out_weight,
        embed_parts,
        norm_gain,
        group_count,
    )
    stepped_other = shifted(stepped, "dom", 1)
    features_other = shifted(features, "dom", 1)

    scale = potential_scale / math.sqrt(tokens * seq_count)
    head = head_weight.reshape(seq_count * dom_count, 1, up_columns)
    score = functools.partial(
        reward,
        ids,
        weights=up_parts,
        parts=group_count,
        doms=dom_count,
        offsets=up_offsets,
        head=head,
        particles=particles,
        scale=scale,
    )
    partial_own = score(features, before=prev_logw, copies=1)[0]
    partial_both = score(features_other, before=partial_own, copies=dom_count * seq_count)
    logits = lax.all_to_all(partial_both, ("dom", "seq"), 0, 0, tiled=True)
    resampled = resample(ids, ancestors.astype(jnp.int32), stepped, stepped_other)
    return finish(ids, logits, resampled, particles, dom_count)


def solution(mesh):
    in_specs = (
        P(("groups", "dom"), "seq", None),
        P(("groups", "dom"), "seq", None),
        P(("groups", "dom"), "seq", None),
        P(("groups", "dom"), "seq", None),
        P(),
        P("groups"),
        P("seq", None),
        P(),
        P(None, "seq"),
        P(),
        P(("groups", "dom")),
        P(("groups", "dom")),
    )
    out_specs = (P(("groups", "dom"), "seq", None), P(("groups", "dom")))
    return jax.shard_map(
        on_device, mesh=mesh, in_specs=in_specs, out_specs=out_specs, check_vma=False
    )
```

```python
import functools
import math

import jax
import jax.numpy as jnp
from jax import lax
from jax.experimental import pallas as pl
from jax.experimental.pallas import tpu as pltpu
from jax.sharding import PartitionSpec as P

HEADS = 24
STEPS = 28
LANES = 128

potential_scale = 4.0
norm_eps = 1e-05
MIB = 1024 * 1024


def pack_kernel(chunks, width, q_ref, k_ref, v_ref, *out_refs):
    particles, _, model_width = q_ref.shape
    blocks = model_width // width
    part = width // chunks
    for index, ref in enumerate((q_ref, k_ref, v_ref)):
        for particle in range(particles):
            for block in range(blocks):
                for chunk in range(chunks):
                    start = block * width + chunk * part
                    out_refs[chunk][particle * blocks + block, index] = ref[
                        particle, :, start : start + part
                    ]


def pack(queries, keys, values, chunks, width):
    particles, tokens, model_width = queries.shape
    count = particles * model_width // width
    vmem = pl.BlockSpec(memory_space=pltpu.VMEM)
    shape = jax.ShapeDtypeStruct((count, 3, tokens, width // chunks), queries.dtype)
    return list(
        pl.pallas_call(
            functools.partial(pack_kernel, chunks, width),
            in_specs=[vmem] * 3,
            out_specs=[vmem] * chunks,
            out_shape=[shape] * chunks,
            compiler_params=pltpu.CompilerParams(vmem_limit_bytes=16 * MIB),
            name="pack_heads",
        )(queries, keys, values)
    )


def gate_kernel(*refs):
    pass


def gate(*arrays):
    anywhere = pl.BlockSpec(memory_space=pl.ANY)
    count = len(arrays)
    return list(
        pl.pallas_call(
            gate_kernel,
            in_specs=[anywhere] * count,
            out_specs=[anywhere] * count,
            out_shape=[jax.ShapeDtypeStruct(array.shape, array.dtype) for array in arrays],
            input_output_aliases={index: index for index in range(count)},
            compiler_params=pltpu.CompilerParams(vmem_limit_bytes=MIB),
            name="gate",
        )(*arrays)
    )


def attention_kernel(head_width, block_sources, qkv_ref, out_ref):
    sources, _, tokens, columns = qkv_ref.shape
    total = sources * tokens
    rows = block_sources * tokens
    factor = 1.0 / math.sqrt(head_width) / math.log(2.0)
    k_all = qkv_ref[:, 1].reshape(total, columns)
    v_all = qkv_ref[:, 2].reshape(total, columns)
    for block in range(0, sources, block_sources):
        span = slice(block, block + block_sources)
        q_all = qkv_ref[span, 0].reshape(rows, columns)
        pieces = []
        for head in range(columns // head_width):
            cols = slice(head * head_width, (head + 1) * head_width)
            scores = lax.dot_general(
                q_all[:, cols],
                k_all[:, cols],
                (((1,), (1,)), ((), ())),
                preferred_element_type=jnp.float32,
            )
            highest = jnp.max(scores, axis=1, keepdims=True)
            expanded = jnp.exp2((scores - highest) * factor)
            norm = 1.0 / jnp.sum(expanded, axis=1, keepdims=True)
            weights = (expanded * norm).astype(jnp.bfloat16)
            pieces.append(jnp.dot(weights, v_all[:, cols], preferred_element_type=jnp.float32))
        joined = jnp.concatenate(pieces, axis=1).astype(jnp.bfloat16)
        out_ref[span] = joined.reshape(block_sources, tokens, columns)


def attention(qkv, head_width):
    sources, _, tokens, columns = qkv.shape
    total = sources * tokens
    block_sources = max(1, min(sources, 512 // tokens))
    while sources % block_sources:
        block_sources -= 1
    step = LANES if columns % LANES == 0 and LANES % head_width == 0 else columns
    scores_bytes = 4 * block_sources * tokens * total
    return pl.pallas_call(
        functools.partial(attention_kernel, head_width, block_sources),
        grid=(columns // step,),
        in_specs=[pl.BlockSpec((sources, 3, tokens, step), lambda i: (0, 0, 0, i))],
        out_specs=pl.BlockSpec((sources, tokens, step), lambda i: (0, 0, i)),
        out_shape=jax.ShapeDtypeStruct((sources, tokens, columns), jnp.bfloat16),
        compiler_params=pltpu.CompilerParams(vmem_limit_bytes=8 * MIB + 6 * scores_bytes),
        cost_estimate=pl.CostEstimate(
            flops=4 * total * total * columns,
            bytes_accessed=8 * total * columns,
            transcendentals=columns // head_width * total * total,
        ),
        name="attention",
    )(qkv)


class ProjectionWeights:
    def __init__(self, weight_ref, vmem_ref, sems, chunks, wanted, width):
        depth, model_width = weight_ref.shape
        part = width // chunks
        blocks = depth // width
        self.block = 512 if model_width % 512 == 0 else model_width
        self.copies = []
        for group in range(model_width // self.block):
            cols = slice(group * self.block, (group + 1) * self.block)
            for index in range(blocks * len(wanted)):
                start = index // len(wanted) * width + wanted[index % len(wanted)] * part
                self.copies.append(
                    pltpu.make_async_copy(
                        weight_ref.at[start : start + part, cols],
                        vmem_ref.at[index * part : (index + 1) * part, cols],
                        sems.at[group, index],
                    )
                )
        self.per_group = blocks * len(wanted)
        for copy in self.copies:
            copy.start()

    def wait(self, group):
        for copy in self.copies[group * self.per_group : (group + 1) * self.per_group]:
            copy.wait()
        return slice(group * self.block, (group + 1) * self.block)


def gather_rows(piece_refs, rows_ref, particles):
    count, tokens, part = piece_refs[0].shape
    blocks = count // particles
    for index in range(blocks * len(piece_refs)):
        ref = piece_refs[index % len(piece_refs)]
        place = index // len(piece_refs)
        for particle in range(particles):
            rows_ref[
                particle * tokens : (particle + 1) * tokens, index * part : (index + 1) * part
            ] = ref[particle * blocks + place]


def first_project_kernel(chunks, width, latents_ref, weight_ref, piece_ref, out_ref, *scratch):
    weight_vmem, rows_ref, sems = scratch
    particles, tokens, model_width = latents_ref.shape
    weights = ProjectionWeights(weight_ref, weight_vmem, sems, chunks, [0], width)
    gather_rows([piece_ref], rows_ref, particles)
    for group in range(model_width // weights.block):
        cols = weights.wait(group)
        flat = latents_ref[:, :, cols].reshape(particles * tokens, weights.block)
        out_ref[:, cols] = flat.astype(jnp.float32) + jnp.dot(
            rows_ref[...], weight_vmem[:, cols], preferred_element_type=jnp.float32
        )


def first_project(latents, out_weight, piece, chunks, width):
    particles, tokens, model_width = latents.shape
    rows, depth = particles * tokens, model_width // chunks
    vmem = pl.BlockSpec(memory_space=pltpu.VMEM)
    return pl.pallas_call(
        functools.partial(first_project_kernel, chunks, width),
        in_specs=[vmem, pl.BlockSpec(memory_space=pl.ANY), vmem],
        out_specs=vmem,
        out_shape=jax.ShapeDtypeStruct((rows, model_width), jnp.float32),
        scratch_shapes=[
            pltpu.VMEM((depth, model_width), jnp.bfloat16),
            pltpu.VMEM((rows, depth), jnp.bfloat16),
            pltpu.SemaphoreType.DMA((max(1, model_width // 512), model_width // width)),
        ],
        compiler_params=pltpu.CompilerParams(vmem_limit_bytes=16 * MIB),
        cost_estimate=pl.CostEstimate(
            flops=2 * rows * depth * model_width,
            bytes_accessed=2 * depth * model_width + 8 * rows * model_width,
            transcendentals=0,
        ),
        name="first_project",
    )(latents, out_weight, piece)


def project_kernel(chunks, width, parts, offsets, depth_parts, refs_in, refs_out):
    ids_ref, latents_ref, gain_ref, out_weight_ref = refs_in[:4]
    rest, weight_refs = list(refs_in[4:-parts]), refs_in[-parts:]
    begun_ref = rest.pop(0) if chunks > 1 else latents_ref
    stepped_ref, features_ref = refs_out[:2]
    out_vmem, weight_vmem, rows_ref, clean_ref, embedded_ref, out_sems, sems = refs_out[2:]
    dom, group, seq = ids_ref[0], ids_ref[1], ids_ref[2]
    sigma = ids_ref[3].astype(jnp.float32) * (1.0 / STEPS)
    particles, tokens, model_width = latents_ref.shape
    rows = particles * tokens
    shards, depth, columns = weight_refs[0].shape

    wanted = list(range(chunks - len(rest), chunks))
    out_weights = ProjectionWeights(out_weight_ref, out_vmem, out_sems, chunks, wanted, width)
    copies = []
    for index in range(parts):
        for shard in range(shards):
            start = pl.multiple_of((seq ^ offsets[shard]) * depth, depth)
            copy = pltpu.make_async_copy(
                weight_refs[index].at[shard],
                weight_vmem.at[index, pl.ds(start, depth)],
                sems.at[index],
            )
            copy.start()
            copies.append(copy)

    gather_rows(rest, rows_ref, particles)
    for index in range(model_width // out_weights.block):
        cols = out_weights.wait(index)
        flat = latents_ref[:, :, cols].reshape(rows, out_weights.block).astype(jnp.float32)
        begun = begun_ref[:, cols] if chunks > 1 else flat
        velocity = begun + jnp.dot(
            rows_ref[...], out_vmem[:, cols], preferred_element_type=jnp.float32
        )
        clean_ref[:, cols] = (flat - sigma * velocity).astype(jnp.bfloat16)
        stepped_ref[:, :, cols] = (
            (flat - velocity * (1.0 / STEPS))
            .astype(jnp.bfloat16)
            .reshape(particles, tokens, out_weights.block)
        )

    for index in range(parts):
        for copy in copies[index * shards : (index + 1) * shards]:
            copy.wait()
        doms = parts // depth_parts
        dom_of = (dom + doms - index // depth_parts) % doms
        group_of = (group + depth_parts - index % depth_parts) % depth_parts
        embedded_ref[dom_of * depth_parts + group_of] = jnp.dot(
            clean_ref[...], weight_vmem[index], preferred_element_type=jnp.float32
        )
    count = parts * columns
    blocks = [embedded_ref[index] for index in range(parts)]
    centre = sum(jnp.sum(piece, axis=1, keepdims=True) for piece in blocks) * (1.0 / count)
    blocks = [piece - centre for piece in blocks]
    variance = sum(jnp.sum(piece * piece, axis=1, keepdims=True) for piece in blocks) * (
        1.0 / count
    )
    inverse = lax.rsqrt(variance + norm_eps)
    share = features_ref.shape[2]
    for index, piece in enumerate(blocks):
        cols = slice(index * columns, (index + 1) * columns)
        feature = jax.nn.gelu(piece * inverse * gain_ref[:, cols]).astype(jnp.bfloat16)
        start = index * columns % share
        features_ref[index * columns // share, :, start : start + columns] = feature


def project_embed(
    ids, offsets, latents, begun, attended, chunks, width, out_weight, weights, gain, depth_parts
):
    particles, tokens, model_width = latents.shape
    rows = particles * tokens
    parts = len(weights)
    columns = weights[0].shape[2]
    count = parts * columns
    out_depth = model_width * len(attended) // chunks
    pieces = ([] if begun is None else [begun]) + attended
    vmem = pl.BlockSpec(memory_space=pltpu.VMEM)
    smem = pl.BlockSpec(memory_space=pltpu.SMEM)
    anywhere = pl.BlockSpec(memory_space=pl.ANY)
    inputs = 4 + len(pieces) + parts

    def kernel(*refs):
        project_kernel(chunks, width, parts, offsets, depth_parts, refs[:inputs], refs[inputs:])

    return pl.pallas_call(
        kernel,
        in_specs=[smem, vmem, vmem, anywhere] + [vmem] * len(pieces) + [anywhere] * parts,
        out_specs=[vmem, vmem],
        out_shape=[
            jax.ShapeDtypeStruct(latents.shape, jnp.bfloat16),
            jax.ShapeDtypeStruct((depth_parts, rows, count // depth_parts), jnp.bfloat16),
        ],
        scratch_shapes=[
            pltpu.VMEM((out_depth, model_width), jnp.bfloat16),
            pltpu.VMEM((parts, model_width, columns), jnp.bfloat16),
            pltpu.VMEM((rows, out_depth), jnp.bfloat16),
            pltpu.VMEM((rows, model_width), jnp.bfloat16),
            pltpu.VMEM((parts, rows, columns), jnp.float32),
            pltpu.SemaphoreType.DMA(
                (max(1, model_width // 512), model_width // width * len(attended))
            ),
            pltpu.SemaphoreType.DMA((parts,)),
        ],
        compiler_params=pltpu.CompilerParams(vmem_limit_bytes=28 * MIB),
        cost_estimate=pl.CostEstimate(
            flops=2 * rows * model_width * (out_depth + count),
            bytes_accessed=2 * model_width * (out_depth + count) + 12 * rows * model_width,
            transcendentals=rows * count,
        ),
        name="project_embed",
    )(ids, latents, gain.reshape(1, count), out_weight, *pieces, *weights)


def reward_kernel(particles, scale, parts, doms, offsets, *refs):
    ids_ref, features_ref, head_ref, before_ref = refs[:4]
    weight_refs, (out_ref, weight_vmem, sems) = refs[4:-3], refs[-3:]
    dom, group, seq = ids_ref[0], ids_ref[1], ids_ref[2]
    shards, depth, columns = weight_refs[0].shape
    rows = features_ref.shape[1]
    count = shards * len(weight_refs) // parts

    copies = []
    for place in range(count):
        pair, shard = divmod(place, shards)
        for index in range(parts):
            copy = pltpu.make_async_copy(
                weight_refs[pair * parts + index].at[shard],
                weight_vmem.at[place, index],
                sems.at[place, index],
            )
            copy.start()
            copies.append(copy)
    pieces = [features_ref[(group + parts - index) % parts] for index in range(parts)]
    total = jnp.zeros((rows, columns), jnp.float32)
    for place in range(count):
        for copy in copies[place * parts : (place + 1) * parts]:
            copy.wait()
        hidden = sum(
            jnp.dot(pieces[index], weight_vmem[place, index], preferred_element_type=jnp.float32)
            for index in range(parts)
        )
        total += jax.nn.gelu(hidden) * head_ref[(seq ^ offsets[place]) * doms + dom]

    totals = jnp.sum(total.reshape(particles, rows // particles, columns), axis=1)
    sums = jnp.sum(totals, axis=1, keepdims=True) * scale
    first = len(before_ref.shape) == 1
    shape = out_ref.shape[1:]
    out_rows = lax.broadcasted_iota(jnp.int32, shape, 0)
    lanes = lax.broadcasted_iota(jnp.int32, shape, 1)
    logits = jnp.zeros(shape, jnp.float32) if first else before_ref[...]
    row = dom if first else (dom + 1) % doms
    for particle in range(particles):
        here = jnp.logical_and(out_rows == row, lanes == particle)
        value = sums[particle : particle + 1]
        if first:
            value = value + jnp.where(seq == 0, before_ref[particle], 0.0)
        logits += jnp.where(here, value, 0.0)
    out_ref[...] = jnp.broadcast_to(logits[None], out_ref.shape)


def reward(ids, features, weights, parts, doms, offsets, head, before, particles, scale, copies):
    shards, depth, columns = weights[0].shape
    rows = features.shape[1]
    count = shards * len(weights) // parts
    smem = pl.BlockSpec(memory_space=pltpu.SMEM)
    vmem = pl.BlockSpec(memory_space=pltpu.VMEM)
    return pl.pallas_call(
        functools.partial(reward_kernel, particles, scale, parts, doms, offsets),
        in_specs=[smem, vmem, vmem, smem if before.ndim == 1 else vmem]
        + [pl.BlockSpec(memory_space=pl.ANY)] * len(weights),
        out_specs=vmem,
        out_shape=jax.ShapeDtypeStruct((copies, 8, LANES), jnp.float32),
        scratch_shapes=[
            pltpu.VMEM((count, parts, depth, columns), jnp.bfloat16),
            pltpu.SemaphoreType.DMA((count, parts)),
        ],
        compiler_params=pltpu.CompilerParams(vmem_limit_bytes=20 * MIB),
        cost_estimate=pl.CostEstimate(
            flops=2 * rows * parts * depth * count * columns,
            bytes_accessed=2 * parts * depth * count * columns,
            transcendentals=rows * count * columns,
        ),
        name="reward",
    )(ids, features, head, before, *weights)


def add_kernel(parts_ref, out_ref):
    out_ref[...] = jnp.sum(parts_ref[...], axis=0)


def add_parts(parts):
    return pl.pallas_call(
        add_kernel,
        out_shape=jax.ShapeDtypeStruct(parts.shape[1:], parts.dtype),
        compiler_params=pltpu.CompilerParams(vmem_limit_bytes=2 * MIB),
        name="add_partials",
    )(parts)


def finish_kernel(particles, doms, ids_ref, resampled_ref, *refs):
    logit_refs, (out_ref, same_ref) = refs[:-2], refs[-2:]
    logits = sum(ref[...] for ref in logit_refs)
    rows = lax.broadcasted_iota(jnp.int32, logits.shape, 0)
    lanes = lax.broadcasted_iota(jnp.int32, logits.shape, 1)
    valid = jnp.logical_and(rows < doms, lanes < particles)
    highest = jnp.max(jnp.where(valid, logits, -jnp.inf))
    total = jnp.sum(jnp.where(valid, jnp.exp(logits - highest), 0.0), axis=1, keepdims=True)
    log_total = highest + jnp.log(jnp.sum(total, axis=0, keepdims=True))
    own = jnp.sum(jnp.where(rows == ids_ref[0], logits, 0.0), axis=0, keepdims=True)
    out_ref[...] = (own - log_total)[:, :particles]


def finish(ids, logits, resampled, particles):
    vmem = pl.BlockSpec(memory_space=pltpu.VMEM)
    anywhere = pl.BlockSpec(memory_space=pl.ANY)
    log_weights, resampled = pl.pallas_call(
        functools.partial(finish_kernel, particles, len(logits)),
        in_specs=[pl.BlockSpec(memory_space=pltpu.SMEM), anywhere] + [vmem] * len(logits),
        out_specs=[vmem, anywhere],
        out_shape=[
            jax.ShapeDtypeStruct((1, particles), jnp.float32),
            jax.ShapeDtypeStruct(resampled.shape, resampled.dtype),
        ],
        input_output_aliases={1: 1},
        compiler_params=pltpu.CompilerParams(vmem_limit_bytes=2 * MIB),
        name="log_weights",
    )(ids, resampled, *logits)
    return resampled, log_weights.reshape(particles)


def resample_kernel(ids_ref, ancestors_ref, own_ref, other_ref, out_ref):
    index = pl.program_id(0)
    own = ancestors_ref[index] // pl.num_programs(0) == ids_ref[0]

    @pl.when(own)
    def _():
        out_ref[...] = own_ref[...]

    @pl.when(jnp.logical_not(own))
    def _():
        out_ref[...] = other_ref[...]


def resample(ids, ancestors, own, other):
    particles, tokens, columns = own.shape
    block = (1, tokens, columns)
    parent = pl.BlockSpec(block, lambda i, ids, ancestors: (ancestors[i] % particles, 0, 0))
    return pl.pallas_call(
        resample_kernel,
        grid_spec=pltpu.PrefetchScalarGridSpec(
            num_scalar_prefetch=2,
            grid=(particles,),
            in_specs=[parent, parent],
            out_specs=pl.BlockSpec(block, lambda i, ids, ancestors: (i, 0, 0)),
        ),
        out_shape=jax.ShapeDtypeStruct(own.shape, own.dtype),
        compiler_params=pltpu.CompilerParams(vmem_limit_bytes=4 * MIB),
        name="resample",
    )(ids, ancestors, own, other)


def shifted(array, axis, step):
    count = lax.axis_size(axis)
    return lax.ppermute(array, axis, [(i, (i + step) % count) for i in range(count)])


def swapped(array, axis, bit):
    return lax.ppermute(array, axis, [(i, i ^ bit) for i in range(lax.axis_size(axis))])


def exchange(array):
    return lax.all_to_all(array, "seq", 0, 0, tiled=True)


def on_device(
    latents,
    queries,
    keys,
    values,
    out_weight,
    step_index,
    embed_weight,
    norm_gain,
    up_weight,
    head_weight,
    prev_logw,
    ancestors,
):
    seq_count = lax.axis_size("seq")
    group_count = lax.axis_size("groups")
    dom_count = lax.axis_size("dom")
    holders = group_count * dom_count
    dom = lax.axis_index("dom")
    group = lax.axis_index("groups")
    seq = lax.axis_index("seq")
    particles, tokens, model_width = latents.shape
    head_width = model_width // HEADS
    width = particles * model_width // seq_count
    chunks = 2 if width % (2 * LANES) == 0 else 1

    ids = jnp.stack([dom, group, seq, step_index[0]]).astype(jnp.int32)

    embed_columns = embed_weight.shape[1] // holders
    embed_share = lax.dynamic_slice_in_dim(
        embed_weight, (dom * group_count + group) * embed_columns, embed_columns, 1
    )[None]
    up_depth = up_weight.shape[0] // group_count
    up_columns = up_weight.shape[1] // dom_count
    up_share = lax.dynamic_slice(
        up_weight, (group * up_depth, dom * up_columns), (up_depth, up_columns)
    )[None]
    bits = [1 << place for place in reversed(range(1, seq_count.bit_length() - 1))]

    packed = pack(queries, keys, values, chunks, width)
    near = [0]
    for bit in bits[:-1]:
        embed_share = jnp.concatenate([embed_share, swapped(embed_share, "seq", bit)])
        near = near + [offset ^ bit for offset in near]
    far = [offset ^ bits[-1] for offset in near]
    embed_share, packed[0] = gate(embed_share, packed[0])

    arrived = [exchange(packed[0])]
    embed_share = jnp.concatenate([embed_share, swapped(embed_share, "seq", bits[-1])])
    for bit in bits[:-1]:
        up_share = jnp.concatenate([up_share, swapped(up_share, "seq", bit)])
    up_near, up_far = up_share, swapped(up_share, "seq", bits[-1])
    embed_share, up_near, up_far, arrived[0], *packed[1:] = gate(
        embed_share, up_near, up_far, arrived[0], *packed[1:]
    )

    arrived += [exchange(piece) for piece in packed[1:]]
    embed_share = jnp.concatenate([embed_share, swapped(embed_share, "seq", 1)])
    near_pair = swapped(up_near, "seq", 1)
    far_groups = [up_far] + [shifted(up_far, "groups", k) for k in range(1, group_count)]
    attended = [attention(arrived[0], head_width)]
    embed_share, near_pair, attended[0], *rest = gate(
        embed_share, near_pair, attended[0], *far_groups[1:], *arrived[1:]
    )
    far_groups[1:], arrived[1:] = rest[: group_count - 1], rest[group_count - 1 :]

    returned = [exchange(attended[0])]
    embed_near = [embed_share] + [shifted(embed_share, "groups", k) for k in range(1, group_count)]
    far_pairs = [swapped(far_groups[0], "seq", 1)]
    attended += [attention(piece, head_width) for piece in arrived[1:]]
    up_near, near_pair, returned[0], *rest = gate(
        up_near, near_pair, returned[0], *embed_near, *far_groups[1:], *attended[1:]
    )
    embed_near, rest = rest[:group_count], rest[group_count:]
    far_groups[1:], attended[1:] = rest[: group_count - 1], rest[group_count - 1 :]

    returned += [exchange(piece) for piece in attended[1:]]
    embed_parts = embed_near + [
        shifted(piece, "dom", k) for k in range(1, dom_count) for piece in embed_near
    ]
    near_groups = [up_near] + [shifted(up_near, "groups", k) for k in range(1, group_count)]
    pair_groups = [near_pair] + [shifted(near_pair, "groups", k) for k in range(1, group_count)]
    far_pairs += [swapped(piece, "seq", 1) for piece in far_groups[1:]]
    up_parts = near_groups + pair_groups + far_groups + far_pairs
    embed_offsets = near + far + [offset ^ 1 for offset in near + far]
    up_offsets = near + [offset ^ 1 for offset in near] + far + [offset ^ 1 for offset in far]

    begun = first_project(latents, out_weight, returned.pop(0), chunks, width) if chunks > 1 else None
    stepped, features = project_embed(
        ids,
        embed_offsets,
        latents,
        begun,
        returned,
        chunks,
        width,
        out_weight,
        embed_parts,
        norm_gain,
        group_count,
    )
    stepped_other = shifted(stepped, "dom", 1)
    features_other = shifted(features, "dom", 1)

    scale = potential_scale / math.sqrt(tokens * seq_count)
    head = head_weight.reshape(seq_count * dom_count, 1, up_columns)
    score = functools.partial(
        reward,
        ids,
        weights=up_parts,
        parts=group_count,
        doms=dom_count,
        offsets=up_offsets,
        head=head,
        particles=particles,
        scale=scale,
    )
    partial_own = score(features, before=prev_logw, copies=1)[0]
    partial_both = score(features_other, before=partial_own, copies=seq_count)
    logits = add_parts(exchange(partial_both))
    both_logits = [logits] + [shifted(logits, "dom", k) for k in range(1, dom_count)]
    resampled = resample(ids, ancestors.astype(jnp.int32), stepped, stepped_other)
    return finish(ids, both_logits, resampled, particles)


def solution(mesh):
    in_specs = (
        P(("groups", "dom"), "seq", None),
        P(("groups", "dom"), "seq", None),
        P(("groups", "dom"), "seq", None),
        P(("groups", "dom"), "seq", None),
        P(),
        P("groups"),
        P("seq", None),
        P(),
        P(None, "seq"),
        P(),
        P(("groups", "dom")),
        P(("groups", "dom")),
    )
    out_specs = (P(("groups", "dom"), "seq", None), P(("groups", "dom")))
    return jax.shard_map(
        on_device, mesh=mesh, in_specs=in_specs, out_specs=out_specs, check_vma=False
    )
```

```python
import functools
import math

import jax
import jax.numpy as jnp
from jax import lax
from jax.experimental import pallas as pl
from jax.experimental.pallas import tpu as pltpu
from jax.sharding import PartitionSpec as P

HEADS = 24
STEPS = 28
LANES = 128

potential_scale = 4.0
norm_eps = 1e-05
MIB = 1024 * 1024


def pack_kernel(chunks, width, q_ref, k_ref, v_ref, *out_refs):
    particles, _, model_width = q_ref.shape
    blocks = model_width // width
    part = width // chunks
    for index, ref in enumerate((q_ref, k_ref, v_ref)):
        for particle in range(particles):
            for block in range(blocks):
                for chunk in range(chunks):
                    start = block * width + chunk * part
                    out_refs[chunk][particle * blocks + block, index] = ref[
                        particle, :, start : start + part
                    ]


def pack(queries, keys, values, chunks, width):
    particles, tokens, model_width = queries.shape
    count = particles * model_width // width
    vmem = pl.BlockSpec(memory_space=pltpu.VMEM)
    shape = jax.ShapeDtypeStruct((count, 3, tokens, width // chunks), queries.dtype)
    return list(
        pl.pallas_call(
            functools.partial(pack_kernel, chunks, width),
            in_specs=[vmem] * 3,
            out_specs=[vmem] * chunks,
            out_shape=[shape] * chunks,
            compiler_params=pltpu.CompilerParams(vmem_limit_bytes=16 * MIB),
            name="pack_heads",
        )(queries, keys, values)
    )


def gate_kernel(*refs):
    pass


def gate(delayed, after):
    count = len(delayed)
    hbm = pl.BlockSpec(memory_space=pltpu.HBM)
    return list(
        pl.pallas_call(
            gate_kernel,
            in_specs=[hbm] * (count + len(after)),
            out_specs=[hbm] * count,
            out_shape=[jax.ShapeDtypeStruct(array.shape, array.dtype) for array in delayed],
            input_output_aliases={index: index for index in range(count)},
            compiler_params=pltpu.CompilerParams(vmem_limit_bytes=MIB),
            name="gate",
        )(*delayed, *after)
    )


def attention_kernel(head_width, block_sources, qkv_ref, out_ref):
    sources, _, tokens, columns = qkv_ref.shape
    total = sources * tokens
    rows = block_sources * tokens
    factor = 1.0 / math.sqrt(head_width) / math.log(2.0)
    k_all = qkv_ref[:, 1].reshape(total, columns)
    v_all = qkv_ref[:, 2].reshape(total, columns)
    for block in range(0, sources, block_sources):
        span = slice(block, block + block_sources)
        q_all = qkv_ref[span, 0].reshape(rows, columns)
        pieces = []
        for head in range(columns // head_width):
            cols = slice(head * head_width, (head + 1) * head_width)
            scores = lax.dot_general(
                q_all[:, cols],
                k_all[:, cols],
                (((1,), (1,)), ((), ())),
                preferred_element_type=jnp.float32,
            )
            highest = jnp.max(scores, axis=1, keepdims=True)
            expanded = jnp.exp2((scores - highest) * factor)
            norm = 1.0 / jnp.sum(expanded, axis=1, keepdims=True)
            weights = (expanded * norm).astype(jnp.bfloat16)
            pieces.append(jnp.dot(weights, v_all[:, cols], preferred_element_type=jnp.float32))
        joined = jnp.concatenate(pieces, axis=1).astype(jnp.bfloat16)
        out_ref[span] = joined.reshape(block_sources, tokens, columns)


def attention(qkv, head_width):
    sources, _, tokens, columns = qkv.shape
    total = sources * tokens
    block_sources = max(1, min(sources, 512 // tokens))
    while sources % block_sources:
        block_sources -= 1
    step = LANES if columns % LANES == 0 and LANES % head_width == 0 else columns
    scores_bytes = 4 * block_sources * tokens * total
    return pl.pallas_call(
        functools.partial(attention_kernel, head_width, block_sources),
        grid=(columns // step,),
        in_specs=[pl.BlockSpec((sources, 3, tokens, step), lambda i: (0, 0, 0, i))],
        out_specs=pl.BlockSpec((sources, tokens, step), lambda i: (0, 0, i)),
        out_shape=jax.ShapeDtypeStruct((sources, tokens, columns), jnp.bfloat16),
        compiler_params=pltpu.CompilerParams(vmem_limit_bytes=8 * MIB + 6 * scores_bytes),
        cost_estimate=pl.CostEstimate(
            flops=4 * total * total * columns,
            bytes_accessed=8 * total * columns,
            transcendentals=columns // head_width * total * total,
        ),
        name="attention",
    )(qkv)


class ProjectionWeights:
    def __init__(self, weight_ref, vmem_ref, sems, chunks, wanted, width):
        depth, model_width = weight_ref.shape
        part = width // chunks
        blocks = depth // width
        self.block = 512 if model_width % 512 == 0 else model_width
        self.copies = []
        for group in range(model_width // self.block):
            cols = slice(group * self.block, (group + 1) * self.block)
            for index in range(blocks * len(wanted)):
                start = index // len(wanted) * width + wanted[index % len(wanted)] * part
                self.copies.append(
                    pltpu.make_async_copy(
                        weight_ref.at[start : start + part, cols],
                        vmem_ref.at[index * part : (index + 1) * part, cols],
                        sems.at[group, index],
                    )
                )
        self.per_group = blocks * len(wanted)
        for copy in self.copies:
            copy.start()

    def wait(self, group):
        for copy in self.copies[group * self.per_group : (group + 1) * self.per_group]:
            copy.wait()
        return slice(group * self.block, (group + 1) * self.block)


def gather_rows(piece_refs, rows_ref, particles):
    count, tokens, part = piece_refs[0].shape
    blocks = count // particles
    for index in range(blocks * len(piece_refs)):
        ref = piece_refs[index % len(piece_refs)]
        place = index // len(piece_refs)
        for particle in range(particles):
            rows_ref[
                particle * tokens : (particle + 1) * tokens, index * part : (index + 1) * part
            ] = ref[particle * blocks + place]


def first_project_kernel(chunks, width, latents_ref, weight_ref, piece_ref, out_ref, *scratch):
    weight_vmem, rows_ref, sems = scratch
    particles, tokens, model_width = latents_ref.shape
    weights = ProjectionWeights(weight_ref, weight_vmem, sems, chunks, [0], width)
    gather_rows([piece_ref], rows_ref, particles)
    for group in range(model_width // weights.block):
        cols = weights.wait(group)
        flat = latents_ref[:, :, cols].reshape(particles * tokens, weights.block)
        out_ref[:, cols] = flat.astype(jnp.float32) + jnp.dot(
            rows_ref[...], weight_vmem[:, cols], preferred_element_type=jnp.float32
        )


def first_project(latents, out_weight, piece, chunks, width):
    particles, tokens, model_width = latents.shape
    rows, depth = particles * tokens, model_width // chunks
    vmem = pl.BlockSpec(memory_space=pltpu.VMEM)
    return pl.pallas_call(
        functools.partial(first_project_kernel, chunks, width),
        in_specs=[vmem, pl.BlockSpec(memory_space=pltpu.HBM), vmem],
        out_specs=vmem,
        out_shape=jax.ShapeDtypeStruct((rows, model_width), jnp.float32),
        scratch_shapes=[
            pltpu.VMEM((depth, model_width), jnp.bfloat16),
            pltpu.VMEM((rows, depth), jnp.bfloat16),
            pltpu.SemaphoreType.DMA((max(1, model_width // 512), model_width // width)),
        ],
        compiler_params=pltpu.CompilerParams(vmem_limit_bytes=16 * MIB),
        cost_estimate=pl.CostEstimate(
            flops=2 * rows * depth * model_width,
            bytes_accessed=2 * depth * model_width + 8 * rows * model_width,
            transcendentals=0,
        ),
        name="first_project",
    )(latents, out_weight, piece)


def project_kernel(chunks, width, parts, offsets, depth_parts, refs_in, refs_out):
    ids_ref, latents_ref, gain_ref, out_weight_ref = refs_in[:4]
    rest, weight_refs = list(refs_in[4:-parts]), refs_in[-parts:]
    begun_ref = rest.pop(0) if chunks > 1 else latents_ref
    stepped_ref, features_ref = refs_out[:2]
    out_vmem, weight_vmem, rows_ref, clean_ref, embedded_ref, out_sems, sems = refs_out[2:]
    dom, group, seq = ids_ref[0], ids_ref[1], ids_ref[2]
    sigma = ids_ref[3].astype(jnp.float32) * (1.0 / STEPS)
    particles, tokens, model_width = latents_ref.shape
    rows = particles * tokens
    shards, depth, columns = weight_refs[0].shape

    wanted = list(range(chunks - len(rest), chunks))
    out_weights = ProjectionWeights(out_weight_ref, out_vmem, out_sems, chunks, wanted, width)
    copies = []
    for index in range(parts):
        for shard in range(shards):
            start = pl.multiple_of((seq ^ offsets[shard]) * depth, depth)
            copy = pltpu.make_async_copy(
                weight_refs[index].at[shard],
                weight_vmem.at[index, pl.ds(start, depth)],
                sems.at[index],
            )
            copy.start()
            copies.append(copy)

    gather_rows(rest, rows_ref, particles)
    for index in range(model_width // out_weights.block):
        cols = out_weights.wait(index)
        flat = latents_ref[:, :, cols].reshape(rows, out_weights.block).astype(jnp.float32)
        begun = begun_ref[:, cols] if chunks > 1 else flat
        velocity = begun + jnp.dot(
            rows_ref[...], out_vmem[:, cols], preferred_element_type=jnp.float32
        )
        clean_ref[:, cols] = (flat - sigma * velocity).astype(jnp.bfloat16)
        stepped_ref[:, :, cols] = (
            (flat - velocity * (1.0 / STEPS))
            .astype(jnp.bfloat16)
            .reshape(particles, tokens, out_weights.block)
        )

    for index in range(parts):
        for copy in copies[index * shards : (index + 1) * shards]:
            copy.wait()
        doms = parts // depth_parts
        dom_of = (dom + doms - index // depth_parts) % doms
        group_of = (group + depth_parts - index % depth_parts) % depth_parts
        embedded_ref[dom_of * depth_parts + group_of] = jnp.dot(
            clean_ref[...], weight_vmem[index], preferred_element_type=jnp.float32
        )
    count = parts * columns
    blocks = [embedded_ref[index] for index in range(parts)]
    centre = sum(jnp.sum(piece, axis=1, keepdims=True) for piece in blocks) * (1.0 / count)
    blocks = [piece - centre for piece in blocks]
    variance = sum(jnp.sum(piece * piece, axis=1, keepdims=True) for piece in blocks) * (
        1.0 / count
    )
    inverse = lax.rsqrt(variance + norm_eps)
    share = features_ref.shape[2]
    for index, piece in enumerate(blocks):
        cols = slice(index * columns, (index + 1) * columns)
        feature = jax.nn.gelu(piece * inverse * gain_ref[:, cols]).astype(jnp.bfloat16)
        start = index * columns % share
        features_ref[index * columns // share, :, start : start + columns] = feature


def project_embed(
    ids, offsets, latents, begun, attended, chunks, width, out_weight, weights, gain, depth_parts
):
    particles, tokens, model_width = latents.shape
    rows = particles * tokens
    parts = len(weights)
    columns = weights[0].shape[2]
    count = parts * columns
    out_depth = model_width * len(attended) // chunks
    pieces = ([] if begun is None else [begun]) + attended
    vmem = pl.BlockSpec(memory_space=pltpu.VMEM)
    smem = pl.BlockSpec(memory_space=pltpu.SMEM)
    hbm = pl.BlockSpec(memory_space=pltpu.HBM)
    inputs = 4 + len(pieces) + parts

    def kernel(*refs):
        project_kernel(chunks, width, parts, offsets, depth_parts, refs[:inputs], refs[inputs:])

    return pl.pallas_call(
        kernel,
        in_specs=[smem, vmem, vmem, hbm] + [vmem] * len(pieces) + [hbm] * parts,
        out_specs=[vmem, vmem],
        out_shape=[
            jax.ShapeDtypeStruct(latents.shape, jnp.bfloat16),
            jax.ShapeDtypeStruct((depth_parts, rows, count // depth_parts), jnp.bfloat16),
        ],
        scratch_shapes=[
            pltpu.VMEM((out_depth, model_width), jnp.bfloat16),
            pltpu.VMEM((parts, model_width, columns), jnp.bfloat16),
            pltpu.VMEM((rows, out_depth), jnp.bfloat16),
            pltpu.VMEM((rows, model_width), jnp.bfloat16),
            pltpu.VMEM((parts, rows, columns), jnp.float32),
            pltpu.SemaphoreType.DMA(
                (max(1, model_width // 512), model_width // width * len(attended))
            ),
            pltpu.SemaphoreType.DMA((parts,)),
        ],
        compiler_params=pltpu.CompilerParams(vmem_limit_bytes=28 * MIB),
        cost_estimate=pl.CostEstimate(
            flops=2 * rows * model_width * (out_depth + count),
            bytes_accessed=2 * model_width * (out_depth + count) + 12 * rows * model_width,
            transcendentals=rows * count,
        ),
        name="project_embed",
    )(ids, latents, gain.reshape(1, count), out_weight, *pieces, *weights)


def reward_kernel(particles, scale, parts, doms, offsets, *refs):
    ids_ref, features_ref, head_ref, before_ref = refs[:4]
    weight_refs, (out_ref, weight_vmem, sems) = refs[4:-3], refs[-3:]
    dom, group, seq = ids_ref[0], ids_ref[1], ids_ref[2]
    shards, depth, columns = weight_refs[0].shape
    rows = features_ref.shape[1]
    count = shards * len(weight_refs) // parts

    copies = []
    for place in range(count):
        pair, shard = divmod(place, shards)
        for index in range(parts):
            copy = pltpu.make_async_copy(
                weight_refs[pair * parts + index].at[shard],
                weight_vmem.at[place, index],
                sems.at[place, index],
            )
            copy.start()
            copies.append(copy)
    pieces = [features_ref[(group + parts - index) % parts] for index in range(parts)]
    total = jnp.zeros((rows, columns), jnp.float32)
    for place in range(count):
        for copy in copies[place * parts : (place + 1) * parts]:
            copy.wait()
        hidden = sum(
            jnp.dot(pieces[index], weight_vmem[place, index], preferred_element_type=jnp.float32)
            for index in range(parts)
        )
        total += jax.nn.gelu(hidden) * head_ref[(seq ^ offsets[place]) * doms + dom]

    totals = jnp.sum(total.reshape(particles, rows // particles, columns), axis=1)
    sums = jnp.sum(totals, axis=1, keepdims=True) * scale
    first = len(before_ref.shape) == 1
    shape = out_ref.shape
    out_rows = lax.broadcasted_iota(jnp.int32, shape, 0)
    lanes = lax.broadcasted_iota(jnp.int32, shape, 1)
    logits = jnp.zeros(shape, jnp.float32) if first else before_ref[...]
    row = dom if first else (dom + 1) % doms
    for particle in range(particles):
        here = jnp.logical_and(out_rows == row, lanes == particle)
        value = sums[particle : particle + 1]
        if first:
            value = value + jnp.where(seq == 0, before_ref[particle], 0.0)
        logits += jnp.where(here, value, 0.0)
    out_ref[...] = logits


def reward(ids, features, weights, parts, doms, offsets, head, before, particles, scale):
    shards, depth, columns = weights[0].shape
    rows = features.shape[1]
    count = shards * len(weights) // parts
    smem = pl.BlockSpec(memory_space=pltpu.SMEM)
    vmem = pl.BlockSpec(memory_space=pltpu.VMEM)
    return pl.pallas_call(
        functools.partial(reward_kernel, particles, scale, parts, doms, offsets),
        in_specs=[smem, vmem, vmem, smem if before.ndim == 1 else vmem]
        + [pl.BlockSpec(memory_space=pltpu.HBM)] * len(weights),
        out_specs=vmem,
        out_shape=jax.ShapeDtypeStruct((8, LANES), jnp.float32),
        scratch_shapes=[
            pltpu.VMEM((count, parts, depth, columns), jnp.bfloat16),
            pltpu.SemaphoreType.DMA((count, parts)),
        ],
        compiler_params=pltpu.CompilerParams(vmem_limit_bytes=20 * MIB),
        cost_estimate=pl.CostEstimate(
            flops=2 * rows * parts * depth * count * columns,
            bytes_accessed=2 * parts * depth * count * columns,
            transcendentals=rows * count * columns,
        ),
        name="reward",
    )(ids, features, head, before, *weights)


def add_kernel(*refs):
    refs[-1][...] = sum(ref[...] for ref in refs[:-1])


def add_parts(parts):
    return pl.pallas_call(
        add_kernel,
        out_shape=jax.ShapeDtypeStruct(parts[0].shape, parts[0].dtype),
        compiler_params=pltpu.CompilerParams(vmem_limit_bytes=2 * MIB),
        name="add_partials",
    )(*parts)


def finish_kernel(particles, doms, ids_ref, resampled_ref, *refs):
    logit_refs, (out_ref, same_ref) = refs[:-2], refs[-2:]
    logits = sum(ref[...] for ref in logit_refs)
    rows = lax.broadcasted_iota(jnp.int32, logits.shape, 0)
    lanes = lax.broadcasted_iota(jnp.int32, logits.shape, 1)
    valid = jnp.logical_and(rows < doms, lanes < particles)
    highest = jnp.max(jnp.where(valid, logits, -jnp.inf))
    total = jnp.sum(jnp.where(valid, jnp.exp(logits - highest), 0.0), axis=1, keepdims=True)
    log_total = highest + jnp.log(jnp.sum(total, axis=0, keepdims=True))
    own = jnp.sum(jnp.where(rows == ids_ref[0], logits, 0.0), axis=0, keepdims=True)
    out_ref[...] = (own - log_total)[:, :particles]


def finish(ids, logits, resampled, particles, doms):
    vmem = pl.BlockSpec(memory_space=pltpu.VMEM)
    anywhere = pl.BlockSpec(memory_space=pl.ANY)
    log_weights, resampled = pl.pallas_call(
        functools.partial(finish_kernel, particles, doms),
        in_specs=[pl.BlockSpec(memory_space=pltpu.SMEM), anywhere] + [vmem] * len(logits),
        out_specs=[vmem, anywhere],
        out_shape=[
            jax.ShapeDtypeStruct((1, particles), jnp.float32),
            jax.ShapeDtypeStruct(resampled.shape, resampled.dtype),
        ],
        input_output_aliases={1: 1},
        compiler_params=pltpu.CompilerParams(vmem_limit_bytes=2 * MIB),
        name="log_weights",
    )(ids, resampled, *logits)
    return resampled, log_weights.reshape(particles)


def resample_kernel(ids_ref, ancestors_ref, own_ref, other_ref, out_ref):
    index = pl.program_id(0)
    own = ancestors_ref[index] // pl.num_programs(0) == ids_ref[0]

    @pl.when(own)
    def _():
        out_ref[...] = own_ref[...]

    @pl.when(jnp.logical_not(own))
    def _():
        out_ref[...] = other_ref[...]


def resample(ids, ancestors, own, other):
    particles, tokens, columns = own.shape
    block = (1, tokens, columns)
    parent = pl.BlockSpec(block, lambda i, ids, ancestors: (ancestors[i] % particles, 0, 0))
    return pl.pallas_call(
        resample_kernel,
        grid_spec=pltpu.PrefetchScalarGridSpec(
            num_scalar_prefetch=2,
            grid=(particles,),
            in_specs=[parent, parent],
            out_specs=pl.BlockSpec(block, lambda i, ids, ancestors: (i, 0, 0)),
        ),
        out_shape=jax.ShapeDtypeStruct(own.shape, own.dtype),
        compiler_params=pltpu.CompilerParams(vmem_limit_bytes=4 * MIB),
        name="resample",
    )(ids, ancestors, own, other)


def shifted(array, axis, step):
    count = lax.axis_size(axis)
    return lax.ppermute(array, axis, [(i, (i + step) % count) for i in range(count)])


def swapped(array, axis, bit):
    return lax.ppermute(array, axis, [(i, i ^ bit) for i in range(lax.axis_size(axis))])


def exchange(array):
    return lax.all_to_all(array, "seq", 0, 0, tiled=True)


def on_device(
    latents,
    queries,
    keys,
    values,
    out_weight,
    step_index,
    embed_weight,
    norm_gain,
    up_weight,
    head_weight,
    prev_logw,
    ancestors,
):
    seq_count = lax.axis_size("seq")
    group_count = lax.axis_size("groups")
    dom_count = lax.axis_size("dom")
    holders = group_count * dom_count
    dom = lax.axis_index("dom")
    group = lax.axis_index("groups")
    seq = lax.axis_index("seq")
    particles, tokens, model_width = latents.shape
    head_width = model_width // HEADS
    width = particles * model_width // seq_count
    chunks = 2 if width % (2 * LANES) == 0 else 1

    ids = jnp.stack([dom, group, seq, step_index[0]]).astype(jnp.int32)

    embed_columns = embed_weight.shape[1] // holders
    embed_share = lax.dynamic_slice_in_dim(
        embed_weight, (dom * group_count + group) * embed_columns, embed_columns, 1
    )[None]
    up_depth = up_weight.shape[0] // group_count
    up_columns = up_weight.shape[1] // dom_count
    up_share = lax.dynamic_slice(
        up_weight, (group * up_depth, dom * up_columns), (up_depth, up_columns)
    )[None]
    bits = [1 << place for place in reversed(range(1, seq_count.bit_length() - 1))]

    packed = pack(queries, keys, values, chunks, width)
    near = [0]
    for bit in bits[:-1]:
        embed_share = jnp.concatenate([embed_share, swapped(embed_share, "seq", bit)])
        near = near + [offset ^ bit for offset in near]
    far = [offset ^ bits[-1] for offset in near]
    embed_share, packed[0] = gate([embed_share, packed[0]], [])

    arrived = [exchange(packed[0])]
    for bit in bits[:-1]:
        up_share = jnp.concatenate([up_share, swapped(up_share, "seq", bit)])
    for bit in (bits[-1], 1):
        embed_share = jnp.concatenate([embed_share, swapped(embed_share, "seq", bit)])
    embed_share, up_near, *packed[1:] = gate([embed_share, up_share, *packed[1:]], arrived[:1])

    arrived += [exchange(piece) for piece in packed[1:]]
    up_far = swapped(up_near, "seq", bits[-1])
    near_pair = swapped(up_near, "seq", 1)
    near_groups = [up_near] + [shifted(up_near, "groups", k) for k in range(1, group_count)]
    embed_near = [embed_share] + [shifted(embed_share, "groups", k) for k in range(1, group_count)]
    attended = [attention(arrived[0], head_width)]
    up_far, near_pair, attended[0], *embed_near = gate(
        [up_far, near_pair, attended[0], *embed_near], arrived[1:]
    )

    returned = [exchange(attended[0])]
    far_pair = swapped(up_far, "seq", 1)
    far_groups = [up_far] + [shifted(up_far, "groups", k) for k in range(1, group_count)]
    embed_parts = embed_near + [
        shifted(piece, "dom", k) for k in range(1, dom_count) for piece in embed_near
    ]
    attended += [attention(piece, head_width) for piece in arrived[1:]]
    near_pair, far_pair, *rest = gate(
        [near_pair, far_pair, *far_groups[1:], *attended[1:]], [returned[0], *embed_parts]
    )
    far_groups[1:], attended[1:] = rest[: group_count - 1], rest[group_count - 1 :]

    returned += [exchange(piece) for piece in attended[1:]]
    pair_groups = [near_pair] + [shifted(near_pair, "groups", k) for k in range(1, group_count)]
    far_pairs = [far_pair] + [swapped(piece, "seq", 1) for piece in far_groups[1:]]
    up_parts = near_groups + pair_groups + far_groups + far_pairs
    embed_offsets = near + far + [offset ^ 1 for offset in near + far]
    up_offsets = near + [offset ^ 1 for offset in near] + far + [offset ^ 1 for offset in far]

    begun = first_project(latents, out_weight, returned.pop(0), chunks, width) if chunks > 1 else None
    stepped, features = project_embed(
        ids,
        embed_offsets,
        latents,
        begun,
        returned,
        chunks,
        width,
        out_weight,
        embed_parts,
        norm_gain,
        group_count,
    )
    stepped_other = shifted(stepped, "dom", 1)
    features_other = shifted(features, "dom", 1)

    scale = potential_scale / math.sqrt(tokens * seq_count)
    head = head_weight.reshape(seq_count * dom_count, 1, up_columns)
    score = functools.partial(
        reward,
        ids,
        weights=up_parts,
        parts=group_count,
        doms=dom_count,
        offsets=up_offsets,
        head=head,
        particles=particles,
        scale=scale,
    )
    partial_own = score(features, before=prev_logw)
    partial = score(features_other, before=partial_own)
    partial = add_parts(
        [partial] + [swapped(partial, "seq", 2 * k) for k in range(1, seq_count // 2)]
    )
    pair = [
        (d * seq_count + i, (d + k) % dom_count * seq_count + (i ^ 1))
        for k in range(1, dom_count)
        for d in range(dom_count)
        for i in range(seq_count)
    ]
    logits = [partial, swapped(partial, "seq", 1), lax.ppermute(partial, ("dom", "seq"), pair)] + [
        shifted(partial, "dom", k) for k in range(1, dom_count)
    ]
    resampled = resample(ids, ancestors.astype(jnp.int32), stepped, stepped_other)
    return finish(ids, logits, resampled, particles, dom_count)


def solution(mesh):
    in_specs = (
        P(("groups", "dom"), "seq", None),
        P(("groups", "dom"), "seq", None),
        P(("groups", "dom"), "seq", None),
        P(("groups", "dom"), "seq", None),
        P(),
        P("groups"),
        P("seq", None),
        P(),
        P(None, "seq"),
        P(),
        P(("groups", "dom")),
        P(("groups", "dom")),
    )
    out_specs = (P(("groups", "dom"), "seq", None), P(("groups", "dom")))
    return jax.shard_map(
        on_device, mesh=mesh, in_specs=in_specs, out_specs=out_specs, check_vma=False
    )
```

```python
import functools
import math

import jax
import jax.numpy as jnp
from jax import lax
from jax.experimental import pallas as pl
from jax.experimental.pallas import tpu as pltpu
from jax.sharding import PartitionSpec as P

HEADS = 24
STEPS = 28
LANES = 128

potential_scale = 4.0
norm_eps = 1e-05
MIB = 1024 * 1024


def pack_kernel(chunks, width, q_ref, k_ref, v_ref, *out_refs):
    particles, _, model_width = q_ref.shape
    blocks = model_width // width
    part = width // chunks
    for index, ref in enumerate((q_ref, k_ref, v_ref)):
        for particle in range(particles):
            for block in range(blocks):
                for chunk in range(chunks):
                    start = block * width + chunk * part
                    out_refs[chunk][particle * blocks + block, index] = ref[
                        particle, :, start : start + part
                    ]


def pack(queries, keys, values, chunks, width):
    particles, tokens, model_width = queries.shape
    count = particles * model_width // width
    vmem = pl.BlockSpec(memory_space=pltpu.VMEM)
    shape = jax.ShapeDtypeStruct((count, 3, tokens, width // chunks), queries.dtype)
    return list(
        pl.pallas_call(
            functools.partial(pack_kernel, chunks, width),
            in_specs=[vmem] * 3,
            out_specs=[vmem] * chunks,
            out_shape=[shape] * chunks,
            compiler_params=pltpu.CompilerParams(vmem_limit_bytes=60 * MIB),
            name="pack_heads",
        )(queries, keys, values)
    )


def gate_kernel(*refs):
    pass


def gate(pinned, delayed, after):
    count = len(pinned) + len(delayed)
    anywhere = pl.BlockSpec(memory_space=pl.ANY)
    specs = [pl.BlockSpec(memory_space=pltpu.HBM)] * len(pinned) + [anywhere] * len(delayed)
    arrays = [*pinned, *delayed]
    return list(
        pl.pallas_call(
            gate_kernel,
            in_specs=specs + [anywhere] * len(after),
            out_specs=specs,
            out_shape=[jax.ShapeDtypeStruct(array.shape, array.dtype) for array in arrays],
            input_output_aliases={index: index for index in range(count)},
            compiler_params=pltpu.CompilerParams(vmem_limit_bytes=MIB),
            name="gate",
        )(*arrays, *after)
    )


def attention_kernel(head_width, block_sources, qkv_ref, out_ref):
    sources, _, tokens, columns = qkv_ref.shape
    total = sources * tokens
    rows = block_sources * tokens
    factor = 1.0 / math.sqrt(head_width) / math.log(2.0)
    k_all = qkv_ref[:, 1].reshape(total, columns)
    v_all = qkv_ref[:, 2].reshape(total, columns)
    for block in range(0, sources, block_sources):
        span = slice(block, block + block_sources)
        q_all = qkv_ref[span, 0].reshape(rows, columns)
        pieces = []
        for head in range(columns // head_width):
            cols = slice(head * head_width, (head + 1) * head_width)
            scores = lax.dot_general(
                q_all[:, cols],
                k_all[:, cols],
                (((1,), (1,)), ((), ())),
                preferred_element_type=jnp.float32,
            )
            highest = jnp.max(scores, axis=1, keepdims=True)
            expanded = jnp.exp2((scores - highest) * factor)
            norm = 1.0 / jnp.sum(expanded, axis=1, keepdims=True)
            weights = (expanded * norm).astype(jnp.bfloat16)
            pieces.append(jnp.dot(weights, v_all[:, cols], preferred_element_type=jnp.float32))
        joined = jnp.concatenate(pieces, axis=1).astype(jnp.bfloat16)
        out_ref[span] = joined.reshape(block_sources, tokens, columns)


def attention(qkv, head_width):
    sources, _, tokens, columns = qkv.shape
    total = sources * tokens
    block_sources = max(1, min(sources, 512 // tokens))
    while sources % block_sources:
        block_sources -= 1
    step = LANES if columns % LANES == 0 and LANES % head_width == 0 else columns
    scores_bytes = 4 * block_sources * tokens * total
    return pl.pallas_call(
        functools.partial(attention_kernel, head_width, block_sources),
        grid=(columns // step,),
        in_specs=[pl.BlockSpec((sources, 3, tokens, step), lambda i: (0, 0, 0, i))],
        out_specs=pl.BlockSpec((sources, tokens, step), lambda i: (0, 0, i)),
        out_shape=jax.ShapeDtypeStruct((sources, tokens, columns), jnp.bfloat16),
        compiler_params=pltpu.CompilerParams(vmem_limit_bytes=60 * MIB),
        cost_estimate=pl.CostEstimate(
            flops=4 * total * total * columns,
            bytes_accessed=8 * total * columns,
            transcendentals=columns // head_width * total * total,
        ),
        name="attention",
    )(qkv)


def column_block(model_width):
    return 512 if model_width % 512 == 0 else model_width


class ProjectionWeights:
    def __init__(self, weight_ref, vmem_ref, sems, chunks, wanted, width):
        depth, model_width = weight_ref.shape
        part = width // chunks
        blocks = depth // width
        self.block = column_block(model_width)
        self.copies = []
        for group in range(model_width // self.block):
            cols = slice(group * self.block, (group + 1) * self.block)
            for index in range(blocks * len(wanted)):
                start = index // len(wanted) * width + wanted[index % len(wanted)] * part
                self.copies.append(
                    pltpu.make_async_copy(
                        weight_ref.at[start : start + part, cols],
                        vmem_ref.at[index * part : (index + 1) * part, cols],
                        sems.at[group, index],
                    )
                )
        self.per_group = blocks * len(wanted)
        for copy in self.copies:
            copy.start()

    def wait(self, group):
        for copy in self.copies[group * self.per_group : (group + 1) * self.per_group]:
            copy.wait()
        return slice(group * self.block, (group + 1) * self.block)


def gather_rows(piece_refs, rows_ref, particles):
    count, tokens, part = piece_refs[0].shape
    blocks = count // particles
    for index in range(blocks * len(piece_refs)):
        ref = piece_refs[index % len(piece_refs)]
        place = index // len(piece_refs)
        for particle in range(particles):
            rows_ref[
                particle * tokens : (particle + 1) * tokens, index * part : (index + 1) * part
            ] = ref[particle * blocks + place]


def first_project_kernel(chunks, width, latents_ref, weight_ref, piece_ref, out_ref, *scratch):
    weight_vmem, rows_ref, sems = scratch
    particles, tokens, model_width = latents_ref.shape
    weights = ProjectionWeights(weight_ref, weight_vmem, sems, chunks, [0], width)
    gather_rows([piece_ref], rows_ref, particles)
    for group in range(model_width // weights.block):
        cols = weights.wait(group)
        flat = latents_ref[:, :, cols].reshape(particles * tokens, weights.block)
        out_ref[:, cols] = flat.astype(jnp.float32) + jnp.dot(
            rows_ref[...], weight_vmem[:, cols], preferred_element_type=jnp.float32
        )


def first_project(latents, out_weight, piece, chunks, width):
    particles, tokens, model_width = latents.shape
    rows, depth = particles * tokens, model_width // chunks
    vmem = pl.BlockSpec(memory_space=pltpu.VMEM)
    return pl.pallas_call(
        functools.partial(first_project_kernel, chunks, width),
        in_specs=[vmem, pl.BlockSpec(memory_space=pltpu.HBM), vmem],
        out_specs=vmem,
        out_shape=jax.ShapeDtypeStruct((rows, model_width), jnp.float32),
        scratch_shapes=[
            pltpu.VMEM((depth, model_width), jnp.bfloat16),
            pltpu.VMEM((rows, depth), jnp.bfloat16),
            pltpu.SemaphoreType.DMA(
                (model_width // column_block(model_width), model_width // width)
            ),
        ],
        compiler_params=pltpu.CompilerParams(vmem_limit_bytes=60 * MIB),
        cost_estimate=pl.CostEstimate(
            flops=2 * rows * depth * model_width,
            bytes_accessed=2 * depth * model_width + 8 * rows * model_width,
            transcendentals=0,
        ),
        name="first_project",
    )(latents, out_weight, piece)


def project_kernel(chunks, width, pieces, parts, offsets, depth_parts, refs_in, refs_out):
    ids_ref, latents_hbm, gain_ref, out_weight_ref = refs_in[:4]
    rest, weight_refs = list(refs_in[4 : 4 + pieces]), refs_in[4 + pieces : 4 + pieces + parts]
    begun_hbm = rest.pop(0) if chunks > 1 else None
    stepped_ref, features_ref = refs_out[:2]
    out_vmem, weight_vmem, rows_ref, clean_ref, embedded_ref = refs_out[2:7]
    latents_ref, begun_ref, out_sems, sems, first_sems = refs_out[7:]
    dom, group, seq = ids_ref[0], ids_ref[1], ids_ref[2]
    sigma = ids_ref[3].astype(jnp.float32) * (1.0 / STEPS)
    particles, tokens, model_width = latents_ref.shape
    rows = particles * tokens
    shards, depth, columns = weight_refs[0].shape

    wanted = list(range(chunks - len(rest), chunks))
    block = column_block(model_width)
    first_copies = []
    for index in range(model_width // block):
        cols = slice(index * block, (index + 1) * block)
        first_copies.append(
            pltpu.make_async_copy(
                latents_hbm.at[:, :, cols], latents_ref.at[:, :, cols], first_sems.at[0, index]
            )
        )
        if chunks > 1:
            first_copies.append(
                pltpu.make_async_copy(
                    begun_hbm.at[:, cols], begun_ref.at[:, cols], first_sems.at[1, index]
                )
            )
    for copy in first_copies[: len(first_copies) // (model_width // block)]:
        copy.start()
    out_weights = ProjectionWeights(out_weight_ref, out_vmem, out_sems, chunks, wanted, width)
    for copy in first_copies[len(first_copies) // (model_width // block) :]:
        copy.start()
    copies = []
    for index in range(parts):
        for shard in range(shards):
            start = pl.multiple_of((seq ^ offsets[shard]) * depth, depth)
            copy = pltpu.make_async_copy(
                weight_refs[index].at[shard],
                weight_vmem.at[index, pl.ds(start, depth)],
                sems.at[index],
            )
            copy.start()
            copies.append(copy)

    gather_rows(rest, rows_ref, particles)
    for index in range(model_width // out_weights.block):
        cols = out_weights.wait(index)
        each = len(first_copies) // (model_width // block)
        for copy in first_copies[index * each : (index + 1) * each]:
            copy.wait()
        flat = latents_ref[:, :, cols].reshape(rows, out_weights.block).astype(jnp.float32)
        begun = begun_ref[:, cols] if chunks > 1 else flat
        velocity = begun + jnp.dot(
            rows_ref[...], out_vmem[:, cols], preferred_element_type=jnp.float32
        )
        clean_ref[:, cols] = (flat - sigma * velocity).astype(jnp.bfloat16)
        stepped_ref[:, :, cols] = (
            (flat - velocity * (1.0 / STEPS))
            .astype(jnp.bfloat16)
            .reshape(particles, tokens, out_weights.block)
        )

    for index in range(parts):
        for copy in copies[index * shards : (index + 1) * shards]:
            copy.wait()
        doms = parts // depth_parts
        dom_of = (dom + doms - index // depth_parts) % doms
        group_of = (group + depth_parts - index % depth_parts) % depth_parts
        embedded_ref[dom_of * depth_parts + group_of] = jnp.dot(
            clean_ref[...], weight_vmem[index], preferred_element_type=jnp.float32
        )
    count = parts * columns
    blocks = [embedded_ref[index] for index in range(parts)]
    centre = sum(jnp.sum(piece, axis=1, keepdims=True) for piece in blocks) * (1.0 / count)
    blocks = [piece - centre for piece in blocks]
    variance = sum(jnp.sum(piece * piece, axis=1, keepdims=True) for piece in blocks) * (
        1.0 / count
    )
    inverse = lax.rsqrt(variance + norm_eps)
    share = features_ref.shape[2]
    for index, piece in enumerate(blocks):
        cols = slice(index * columns, (index + 1) * columns)
        feature = jax.nn.gelu(piece * inverse * gain_ref[:, cols]).astype(jnp.bfloat16)
        start = index * columns % share
        features_ref[index * columns // share, :, start : start + columns] = feature


def project_embed(
    ids,
    offsets,
    latents,
    begun,
    attended,
    chunks,
    width,
    out_weight,
    weights,
    gain,
    depth_parts,
    after,
):
    particles, tokens, model_width = latents.shape
    rows = particles * tokens
    parts = len(weights)
    columns = weights[0].shape[2]
    count = parts * columns
    out_depth = model_width * len(attended) // chunks
    pieces = ([] if begun is None else [begun]) + attended
    vmem = pl.BlockSpec(memory_space=pltpu.VMEM)
    smem = pl.BlockSpec(memory_space=pltpu.SMEM)
    hbm = pl.BlockSpec(memory_space=pltpu.HBM)
    inputs = 4 + len(pieces) + parts + len(after)
    groups = model_width // column_block(model_width)

    def kernel(*refs):
        project_kernel(
            chunks,
            width,
            len(pieces),
            parts,
            offsets,
            depth_parts,
            refs[:inputs],
            refs[inputs:],
        )

    return pl.pallas_call(
        kernel,
        in_specs=[smem, hbm, vmem, hbm]
        + ([] if begun is None else [hbm])
        + [vmem] * len(attended)
        + [hbm] * parts
        + [pl.BlockSpec(memory_space=pl.ANY)] * len(after),
        out_specs=[vmem, vmem],
        out_shape=[
            jax.ShapeDtypeStruct(latents.shape, jnp.bfloat16),
            jax.ShapeDtypeStruct((depth_parts, rows, count // depth_parts), jnp.bfloat16),
        ],
        scratch_shapes=[
            pltpu.VMEM((out_depth, model_width), jnp.bfloat16),
            pltpu.VMEM((parts, model_width, columns), jnp.bfloat16),
            pltpu.VMEM((rows, out_depth), jnp.bfloat16),
            pltpu.VMEM((rows, model_width), jnp.bfloat16),
            pltpu.VMEM((parts, rows, columns), jnp.float32),
            pltpu.VMEM(latents.shape, latents.dtype),
            pltpu.VMEM((rows, model_width), jnp.float32),
            pltpu.SemaphoreType.DMA((groups, model_width // width * len(attended))),
            pltpu.SemaphoreType.DMA((parts,)),
            pltpu.SemaphoreType.DMA((2, groups)),
        ],
        compiler_params=pltpu.CompilerParams(vmem_limit_bytes=60 * MIB),
        cost_estimate=pl.CostEstimate(
            flops=2 * rows * model_width * (out_depth + count),
            bytes_accessed=2 * model_width * (out_depth + count) + 12 * rows * model_width,
            transcendentals=rows * count,
        ),
        name="project_embed",
    )(ids, latents, gain.reshape(1, count), out_weight, *pieces, *weights, *after)


def reward_kernel(particles, scale, parts, doms, offsets, joined, *refs):
    ids_ref, features_ref, head_ref, before_ref = refs[:4]
    weight_refs, (out_ref, weight_vmem, rows_ref, sems) = refs[4:-4], refs[-4:]
    dom, group, seq = ids_ref[0], ids_ref[1], ids_ref[2]
    shards, depth, columns = weight_refs[0].shape
    rows = features_ref.shape[1]
    count = shards * len(weight_refs) // parts

    copies = []
    for place in range(count):
        pair, shard = divmod(place, shards)
        lane = place % joined * columns
        for index in range(parts):
            copy = pltpu.make_async_copy(
                weight_refs[pair * parts + index].at[shard],
                weight_vmem.at[
                    place // joined,
                    index * depth : (index + 1) * depth,
                    lane : lane + columns,
                ],
                sems.at[place, index],
            )
            copy.start()
            copies.append(copy)
    for index in range(parts):
        rows_ref[:, index * depth : (index + 1) * depth] = features_ref[
            (group + parts - index) % parts
        ]
    totals = jnp.zeros((particles, joined * columns), jnp.float32)
    for step in range(count // joined):
        for copy in copies[step * joined * parts : (step + 1) * joined * parts]:
            copy.wait()
        hidden = jnp.dot(rows_ref[...], weight_vmem[step], preferred_element_type=jnp.float32)
        places = range(step * joined, (step + 1) * joined)
        head = jnp.concatenate(
            [head_ref[(seq ^ offsets[place]) * doms + dom] for place in places], axis=1
        )
        scored = jax.nn.gelu(hidden) * head
        totals += jnp.sum(scored.reshape(particles, rows // particles, -1), axis=1)

    sums = jnp.sum(totals, axis=1, keepdims=True) * scale
    first = len(before_ref.shape) == 1
    shape = out_ref.shape
    out_rows = lax.broadcasted_iota(jnp.int32, shape, 0)
    lanes = lax.broadcasted_iota(jnp.int32, shape, 1)
    logits = jnp.zeros(shape, jnp.float32) if first else before_ref[...]
    row = dom if first else (dom + 1) % doms
    for particle in range(particles):
        here = jnp.logical_and(out_rows == row, lanes == particle)
        value = sums[particle : particle + 1]
        if first:
            value = value + jnp.where(seq == 0, before_ref[particle], 0.0)
        logits += jnp.where(here, value, 0.0)
    out_ref[...] = logits


def reward(ids, features, weights, parts, doms, offsets, head, before, particles, scale):
    shards, depth, columns = weights[0].shape
    rows = features.shape[1]
    count = shards * len(weights) // parts
    joined = 2 if columns % LANES == 0 and count % 2 == 0 else 1
    smem = pl.BlockSpec(memory_space=pltpu.SMEM)
    vmem = pl.BlockSpec(memory_space=pltpu.VMEM)
    return pl.pallas_call(
        functools.partial(reward_kernel, particles, scale, parts, doms, offsets, joined),
        in_specs=[smem, vmem, vmem, smem if before.ndim == 1 else vmem]
        + [pl.BlockSpec(memory_space=pltpu.HBM)] * len(weights),
        out_specs=vmem,
        out_shape=jax.ShapeDtypeStruct((8, LANES), jnp.float32),
        scratch_shapes=[
            pltpu.VMEM((count // joined, parts * depth, joined * columns), jnp.bfloat16),
            pltpu.VMEM((rows, parts * depth), jnp.bfloat16),
            pltpu.SemaphoreType.DMA((count, parts)),
        ],
        compiler_params=pltpu.CompilerParams(vmem_limit_bytes=20 * MIB),
        cost_estimate=pl.CostEstimate(
            flops=2 * rows * parts * depth * count * columns,
            bytes_accessed=2 * parts * depth * count * columns,
            transcendentals=rows * count * columns,
        ),
        name="reward",
    )(ids, features, head, before, *weights)


def add_kernel(*refs):
    refs[-1][...] = sum(ref[...] for ref in refs[:-1])


def add_parts(parts):
    return pl.pallas_call(
        add_kernel,
        out_shape=jax.ShapeDtypeStruct(parts[0].shape, parts[0].dtype),
        compiler_params=pltpu.CompilerParams(vmem_limit_bytes=2 * MIB),
        name="add_partials",
    )(*parts)


def finish_kernel(particles, doms, ids_ref, resampled_ref, *refs):
    logit_refs, (out_ref, same_ref) = refs[:-2], refs[-2:]
    logits = sum(ref[...] for ref in logit_refs)
    rows = lax.broadcasted_iota(jnp.int32, logits.shape, 0)
    lanes = lax.broadcasted_iota(jnp.int32, logits.shape, 1)
    valid = jnp.logical_and(rows < doms, lanes < particles)
    highest = jnp.max(jnp.where(valid, logits, -jnp.inf))
    total = jnp.sum(jnp.where(valid, jnp.exp(logits - highest), 0.0), axis=1, keepdims=True)
    log_total = highest + jnp.log(jnp.sum(total, axis=0, keepdims=True))
    own = jnp.sum(jnp.where(rows == ids_ref[0], logits, 0.0), axis=0, keepdims=True)
    out_ref[...] = (own - log_total)[:, :particles]


def finish(ids, logits, resampled, particles, doms):
    vmem = pl.BlockSpec(memory_space=pltpu.VMEM)
    anywhere = pl.BlockSpec(memory_space=pl.ANY)
    log_weights, resampled = pl.pallas_call(
        functools.partial(finish_kernel, particles, doms),
        in_specs=[pl.BlockSpec(memory_space=pltpu.SMEM), anywhere] + [vmem] * len(logits),
        out_specs=[vmem, anywhere],
        out_shape=[
            jax.ShapeDtypeStruct((1, particles), jnp.float32),
            jax.ShapeDtypeStruct(resampled.shape, resampled.dtype),
        ],
        input_output_aliases={1: 1},
        compiler_params=pltpu.CompilerParams(vmem_limit_bytes=2 * MIB),
        name="log_weights",
    )(ids, resampled, *logits)
    return resampled, log_weights.reshape(particles)


def resample_kernel(ids_ref, ancestors_ref, own_ref, other_ref, out_ref):
    index = pl.program_id(0)
    own = ancestors_ref[index] // pl.num_programs(0) == ids_ref[0]

    @pl.when(own)
    def _():
        out_ref[...] = own_ref[...]

    @pl.when(jnp.logical_not(own))
    def _():
        out_ref[...] = other_ref[...]


def resample(ids, ancestors, own, other):
    particles, tokens, columns = own.shape
    block = (1, tokens, columns)
    parent = pl.BlockSpec(block, lambda i, ids, ancestors: (ancestors[i] % particles, 0, 0))
    return pl.pallas_call(
        resample_kernel,
        grid_spec=pltpu.PrefetchScalarGridSpec(
            num_scalar_prefetch=2,
            grid=(particles,),
            in_specs=[parent, parent],
            out_specs=pl.BlockSpec(block, lambda i, ids, ancestors: (i, 0, 0)),
        ),
        out_shape=jax.ShapeDtypeStruct(own.shape, own.dtype),
        compiler_params=pltpu.CompilerParams(vmem_limit_bytes=4 * MIB),
        name="resample",
    )(ids, ancestors, own, other)


def shifted(array, axis, step):
    count = lax.axis_size(axis)
    return lax.ppermute(array, axis, [(i, (i + step) % count) for i in range(count)])


def swapped(array, axis, bit):
    return lax.ppermute(array, axis, [(i, i ^ bit) for i in range(lax.axis_size(axis))])


def exchange(array):
    return lax.all_to_all(array, "seq", 0, 0, tiled=True)


def on_device(
    latents,
    queries,
    keys,
    values,
    out_weight,
    step_index,
    embed_weight,
    norm_gain,
    up_weight,
    head_weight,
    prev_logw,
    ancestors,
):
    seq_count = lax.axis_size("seq")
    group_count = lax.axis_size("groups")
    dom_count = lax.axis_size("dom")
    holders = group_count * dom_count
    dom = lax.axis_index("dom")
    group = lax.axis_index("groups")
    seq = lax.axis_index("seq")
    particles, tokens, model_width = latents.shape
    head_width = model_width // HEADS
    width = particles * model_width // seq_count
    chunks = 2 if width % (2 * LANES) == 0 else 1

    ids = jnp.stack([dom, group, seq, step_index[0]]).astype(jnp.int32)

    embed_columns = embed_weight.shape[1] // holders
    embed_share = lax.dynamic_slice_in_dim(
        embed_weight, (dom * group_count + group) * embed_columns, embed_columns, 1
    )[None]
    up_depth = up_weight.shape[0] // group_count
    up_columns = up_weight.shape[1] // dom_count
    up_share = lax.dynamic_slice(
        up_weight, (group * up_depth, dom * up_columns), (up_depth, up_columns)
    )[None]
    bits = [1 << place for place in reversed(range(1, seq_count.bit_length() - 1))]

    packed = pack(queries, keys, values, chunks, width)
    near = [0]
    for bit in bits[:-1]:
        embed_share = jnp.concatenate([embed_share, swapped(embed_share, "seq", bit)])
        near = near + [offset ^ bit for offset in near]
    far = [offset ^ bits[-1] for offset in near]
    packed[0], embed_share = gate([packed[0]], [embed_share], [])

    arrived = [exchange(packed[0])]
    for bit in bits[:-1]:
        up_share = jnp.concatenate([up_share, swapped(up_share, "seq", bit)])
    for bit in (bits[-1], 1):
        embed_share = jnp.concatenate([embed_share, swapped(embed_share, "seq", bit)])
    *packed[1:], embed_share, up_near = gate(packed[1:], [embed_share, up_share], arrived[:1])

    arrived += [exchange(piece) for piece in packed[1:]]
    up_far = swapped(up_near, "seq", bits[-1])
    near_pair = swapped(up_near, "seq", 1)
    near_groups = [up_near] + [shifted(up_near, "groups", k) for k in range(1, group_count)]
    embed_near = [embed_share] + [shifted(embed_share, "groups", k) for k in range(1, group_count)]
    attended = [attention(arrived[0], head_width)]
    attended[0], up_far, near_pair, *embed_near = gate(
        attended, [up_far, near_pair, *embed_near], arrived[1:]
    )

    returned = [exchange(attended[0])]
    far_pair = swapped(up_far, "seq", 1)
    far_groups = [up_far] + [shifted(up_far, "groups", k) for k in range(1, group_count)]
    embed_parts = embed_near + [
        shifted(piece, "dom", k) for k in range(1, dom_count) for piece in embed_near
    ]
    attended += [attention(piece, head_width) for piece in arrived[1:]]
    *rest, near_pair, far_pair = gate(
        attended[1:], [*far_groups[1:], near_pair, far_pair], [returned[0], *embed_parts]
    )
    attended[1:], far_groups[1:] = rest[: chunks - 1], rest[chunks - 1 :]

    returned += [exchange(piece) for piece in attended[1:]]
    pair_groups = [near_pair] + [shifted(near_pair, "groups", k) for k in range(1, group_count)]
    far_pairs = [far_pair] + [swapped(piece, "seq", 1) for piece in far_groups[1:]]
    up_parts = near_groups + pair_groups + far_groups + far_pairs
    embed_offsets = near + far + [offset ^ 1 for offset in near + far]
    up_offsets = near + [offset ^ 1 for offset in near] + far + [offset ^ 1 for offset in far]

    begun = first_project(latents, out_weight, returned.pop(0), chunks, width) if chunks > 1 else None
    stepped, features = project_embed(
        ids,
        embed_offsets,
        latents,
        begun,
        returned,
        chunks,
        width,
        out_weight,
        embed_parts,
        norm_gain,
        group_count,
        pair_groups[1:] + far_pairs,
    )
    stepped_other = shifted(stepped, "dom", 1)
    features_other = shifted(features, "dom", 1)

    scale = potential_scale / math.sqrt(tokens * seq_count)
    head = head_weight.reshape(seq_count * dom_count, 1, up_columns)
    score = functools.partial(
        reward,
        ids,
        weights=up_parts,
        parts=group_count,
        doms=dom_count,
        offsets=up_offsets,
        head=head,
        particles=particles,
        scale=scale,
    )
    partial_own = score(features, before=prev_logw)
    partial = score(features_other, before=partial_own)
    partial = add_parts(
        [partial] + [swapped(partial, "seq", 2 * k) for k in range(1, seq_count // 2)]
    )
    pair = [
        (d * seq_count + i, (d + k) % dom_count * seq_count + (i ^ 1))
        for k in range(1, dom_count)
        for d in range(dom_count)
        for i in range(seq_count)
    ]
    logits = [partial, swapped(partial, "seq", 1), lax.ppermute(partial, ("dom", "seq"), pair)] + [
        shifted(partial, "dom", k) for k in range(1, dom_count)
    ]
    resampled = resample(ids, ancestors.astype(jnp.int32), stepped, stepped_other)
    return finish(ids, logits, resampled, particles, dom_count)


def solution(mesh):
    in_specs = (
        P(("groups", "dom"), "seq", None),
        P(("groups", "dom"), "seq", None),
        P(("groups", "dom"), "seq", None),
        P(("groups", "dom"), "seq", None),
        P(),
        P("groups"),
        P("seq", None),
        P(),
        P(None, "seq"),
        P(),
        P(("groups", "dom")),
        P(("groups", "dom")),
    )
    out_specs = (P(("groups", "dom"), "seq", None), P(("groups", "dom")))
    return jax.shard_map(
        on_device, mesh=mesh, in_specs=in_specs, out_specs=out_specs, check_vma=False
    )
```

```python
import functools
import math

import jax
import jax.numpy as jnp
from jax import lax
from jax.experimental import pallas as pl
from jax.experimental.pallas import tpu as pltpu
from jax.sharding import PartitionSpec as P

HEADS = 24
STEPS = 28
LANES = 128

potential_scale = 4.0
norm_eps = 1e-05
MIB = 1024 * 1024


def pack_kernel(q_ref, k_ref, v_ref, *refs):
    for index, ref in enumerate((q_ref, k_ref, v_ref)):
        refs[-1][:, 0, index] = ref[...]


def pack_whole_kernel(width, q_ref, k_ref, v_ref, *refs):
    out_ref = refs[-1]
    for index, ref in enumerate((q_ref, k_ref, v_ref)):
        for block in range(out_ref.shape[1]):
            out_ref[:, block, index] = ref[:, :, block * width : (block + 1) * width]


def pack(queries, keys, values, chunks, width, chunk, after):
    particles, tokens, model_width = queries.shape
    blocks = model_width // width
    part = width // chunks
    out_shape = jax.ShapeDtypeStruct((particles, blocks, 3, tokens, part), queries.dtype)
    params = pltpu.CompilerParams(vmem_limit_bytes=60 * MIB)
    unread = [pl.BlockSpec(memory_space=pl.ANY)] * len(after)
    if part % LANES == 0:
        in_spec = pl.BlockSpec((particles, tokens, part), lambda i: (0, 0, i * chunks + chunk))
        packed = pl.pallas_call(
            pack_kernel,
            grid=(blocks,),
            in_specs=[in_spec] * 3 + unread,
            out_specs=pl.BlockSpec((particles, 1, 3, tokens, part), lambda i: (0, i, 0, 0, 0)),
            out_shape=out_shape,
            compiler_params=params,
            name="pack_heads",
        )(queries, keys, values, *after)
    else:
        vmem = pl.BlockSpec(memory_space=pltpu.VMEM)
        packed = pl.pallas_call(
            functools.partial(pack_whole_kernel, width),
            in_specs=[vmem] * 3 + unread,
            out_specs=vmem,
            out_shape=out_shape,
            compiler_params=params,
            name="pack_heads",
        )(queries, keys, values, *after)
    return packed.reshape(particles * blocks, 3, tokens, part)


def gate_kernel(*refs):
    pass


def gate(delayed, after):
    count = len(delayed)
    anywhere = pl.BlockSpec(memory_space=pl.ANY)
    return list(
        pl.pallas_call(
            gate_kernel,
            in_specs=[anywhere] * (count + len(after)),
            out_specs=[anywhere] * count,
            out_shape=[jax.ShapeDtypeStruct(array.shape, array.dtype) for array in delayed],
            input_output_aliases={index: index for index in range(count)},
            compiler_params=pltpu.CompilerParams(vmem_limit_bytes=MIB),
            name="gate",
        )(*delayed, *after)
    )


def attention_kernel(head_width, block_sources, qkv_ref, *refs):
    out_ref = refs[-1]
    sources, _, tokens, columns = qkv_ref.shape
    total = sources * tokens
    rows = block_sources * tokens
    factor = 1.0 / math.sqrt(head_width) / math.log(2.0)
    k_all = qkv_ref[:, 1].reshape(total, columns)
    v_all = qkv_ref[:, 2].reshape(total, columns)
    for block in range(0, sources, block_sources):
        span = slice(block, block + block_sources)
        q_all = qkv_ref[span, 0].reshape(rows, columns)
        pieces = []
        for head in range(columns // head_width):
            cols = slice(head * head_width, (head + 1) * head_width)
            scores = lax.dot_general(
                q_all[:, cols],
                k_all[:, cols],
                (((1,), (1,)), ((), ())),
                preferred_element_type=jnp.float32,
            )
            highest = jnp.max(scores, axis=1, keepdims=True)
            expanded = jnp.exp2((scores - highest) * factor)
            norm = 1.0 / jnp.sum(expanded, axis=1, keepdims=True)
            weights = (expanded * norm).astype(jnp.bfloat16)
            pieces.append(jnp.dot(weights, v_all[:, cols], preferred_element_type=jnp.float32))
        joined = jnp.concatenate(pieces, axis=1).astype(jnp.bfloat16)
        out_ref[span] = joined.reshape(block_sources, tokens, columns)


def attention(qkv, head_width, after):
    sources, _, tokens, columns = qkv.shape
    total = sources * tokens
    block_sources = max(1, min(sources, 512 // tokens))
    while sources % block_sources:
        block_sources -= 1
    step = LANES if columns % LANES == 0 and LANES % head_width == 0 else columns
    scores_bytes = 4 * block_sources * tokens * total
    return pl.pallas_call(
        functools.partial(attention_kernel, head_width, block_sources),
        grid=(columns // step,),
        in_specs=[pl.BlockSpec((sources, 3, tokens, step), lambda i: (0, 0, 0, i))]
        + [pl.BlockSpec(memory_space=pl.ANY)] * len(after),
        out_specs=pl.BlockSpec((sources, tokens, step), lambda i: (0, 0, i)),
        out_shape=jax.ShapeDtypeStruct((sources, tokens, columns), jnp.bfloat16),
        compiler_params=pltpu.CompilerParams(vmem_limit_bytes=8 * MIB + 6 * scores_bytes),
        cost_estimate=pl.CostEstimate(
            flops=4 * total * total * columns,
            bytes_accessed=8 * total * columns,
            transcendentals=columns // head_width * total * total,
        ),
        name="attention",
    )(qkv, *after)


def column_block(model_width):
    return 512 if model_width % 512 == 0 else model_width


class ProjectionWeights:
    def __init__(self, weight_ref, vmem_ref, sems, chunks, wanted, width):
        depth, model_width = weight_ref.shape
        part = width // chunks
        blocks = depth // width
        self.block = column_block(model_width)
        self.copies = []
        for group in range(model_width // self.block):
            cols = slice(group * self.block, (group + 1) * self.block)
            for index in range(blocks * len(wanted)):
                start = index // len(wanted) * width + wanted[index % len(wanted)] * part
                self.copies.append(
                    pltpu.make_async_copy(
                        weight_ref.at[start : start + part, cols],
                        vmem_ref.at[index * part : (index + 1) * part, cols],
                        sems.at[group, index],
                    )
                )
        self.per_group = blocks * len(wanted)
        for copy in self.copies:
            copy.start()

    def wait(self, group):
        for copy in self.copies[group * self.per_group : (group + 1) * self.per_group]:
            copy.wait()
        return slice(group * self.block, (group + 1) * self.block)


def gather_rows(piece_refs, rows_ref, particles):
    count, tokens, part = piece_refs[0].shape
    blocks = count // particles
    for index in range(blocks * len(piece_refs)):
        ref = piece_refs[index % len(piece_refs)]
        place = index // len(piece_refs)
        for particle in range(particles):
            rows_ref[
                particle * tokens : (particle + 1) * tokens, index * part : (index + 1) * part
            ] = ref[particle * blocks + place]


def first_project_kernel(chunks, width, latents_ref, weight_ref, piece_ref, *refs):
    out_ref, weight_vmem, rows_ref, sems = refs[-4:]
    particles, tokens, model_width = latents_ref.shape
    weights = ProjectionWeights(weight_ref, weight_vmem, sems, chunks, [0], width)
    gather_rows([piece_ref], rows_ref, particles)
    for group in range(model_width // weights.block):
        cols = weights.wait(group)
        flat = latents_ref[:, :, cols].reshape(particles * tokens, weights.block)
        out_ref[:, cols] = flat.astype(jnp.float32) + jnp.dot(
            rows_ref[...], weight_vmem[:, cols], preferred_element_type=jnp.float32
        )


def first_project(latents, out_weight, piece, chunks, width, after):
    particles, tokens, model_width = latents.shape
    rows, depth = particles * tokens, model_width // chunks
    vmem = pl.BlockSpec(memory_space=pltpu.VMEM)
    return pl.pallas_call(
        functools.partial(first_project_kernel, chunks, width),
        in_specs=[vmem, pl.BlockSpec(memory_space=pltpu.HBM), vmem]
        + [pl.BlockSpec(memory_space=pl.ANY)] * len(after),
        out_specs=vmem,
        out_shape=jax.ShapeDtypeStruct((rows, model_width), jnp.float32),
        scratch_shapes=[
            pltpu.VMEM((depth, model_width), jnp.bfloat16),
            pltpu.VMEM((rows, depth), jnp.bfloat16),
            pltpu.SemaphoreType.DMA(
                (model_width // column_block(model_width), model_width // width)
            ),
        ],
        compiler_params=pltpu.CompilerParams(vmem_limit_bytes=60 * MIB),
        cost_estimate=pl.CostEstimate(
            flops=2 * rows * depth * model_width,
            bytes_accessed=2 * depth * model_width + 8 * rows * model_width,
            transcendentals=0,
        ),
        name="first_project",
    )(latents, out_weight, piece, *after)


def project_kernel(chunks, width, pieces, parts, offsets, depth_parts, refs_in, refs_out):
    ids_ref, latents_hbm, gain_ref, out_weight_ref = refs_in[:4]
    rest, weight_refs = list(refs_in[4 : 4 + pieces]), refs_in[4 + pieces : 4 + pieces + parts]
    begun_hbm = rest.pop(0) if chunks > 1 else None
    stepped_ref, features_ref = refs_out[:2]
    out_vmem, weight_vmem, rows_ref, clean_ref, embedded_ref = refs_out[2:7]
    latents_ref, begun_ref, out_sems, sems, first_sems = refs_out[7:]
    dom, group, seq = ids_ref[0], ids_ref[1], ids_ref[2]
    sigma = ids_ref[3].astype(jnp.float32) * (1.0 / STEPS)
    particles, tokens, model_width = latents_ref.shape
    rows = particles * tokens
    shards, depth, columns = weight_refs[0].shape

    wanted = list(range(chunks - len(rest), chunks))
    block = column_block(model_width)
    first_copies = []
    for index in range(model_width // block):
        cols = slice(index * block, (index + 1) * block)
        first_copies.append(
            pltpu.make_async_copy(
                latents_hbm.at[:, :, cols], latents_ref.at[:, :, cols], first_sems.at[0, index]
            )
        )
        if chunks > 1:
            first_copies.append(
                pltpu.make_async_copy(
                    begun_hbm.at[:, cols], begun_ref.at[:, cols], first_sems.at[1, index]
                )
            )
    for copy in first_copies[: len(first_copies) // (model_width // block)]:
        copy.start()
    out_weights = ProjectionWeights(out_weight_ref, out_vmem, out_sems, chunks, wanted, width)
    for copy in first_copies[len(first_copies) // (model_width // block) :]:
        copy.start()
    copies = []
    for index in range(parts):
        for shard in range(shards):
            start = pl.multiple_of((seq ^ offsets[shard]) * depth, depth)
            copy = pltpu.make_async_copy(
                weight_refs[index].at[shard],
                weight_vmem.at[index, pl.ds(start, depth)],
                sems.at[index],
            )
            copy.start()
            copies.append(copy)

    gather_rows(rest, rows_ref, particles)
    for index in range(model_width // out_weights.block):
        cols = out_weights.wait(index)
        each = len(first_copies) // (model_width // block)
        for copy in first_copies[index * each : (index + 1) * each]:
            copy.wait()
        flat = latents_ref[:, :, cols].reshape(rows, out_weights.block).astype(jnp.float32)
        begun = begun_ref[:, cols] if chunks > 1 else flat
        velocity = begun + jnp.dot(
            rows_ref[...], out_vmem[:, cols], preferred_element_type=jnp.float32
        )
        clean_ref[:, cols] = (flat - sigma * velocity).astype(jnp.bfloat16)
        stepped_ref[:, :, cols] = (
            (flat - velocity * (1.0 / STEPS))
            .astype(jnp.bfloat16)
            .reshape(particles, tokens, out_weights.block)
        )

    for index in range(parts):
        for copy in copies[index * shards : (index + 1) * shards]:
            copy.wait()
        doms = parts // depth_parts
        dom_of = (dom + doms - index // depth_parts) % doms
        group_of = (group + depth_parts - index % depth_parts) % depth_parts
        embedded_ref[dom_of * depth_parts + group_of] = jnp.dot(
            clean_ref[...], weight_vmem[index], preferred_element_type=jnp.float32
        )
    count = parts * columns
    blocks = [embedded_ref[index] for index in range(parts)]
    centre = sum(jnp.sum(piece, axis=1, keepdims=True) for piece in blocks) * (1.0 / count)
    blocks = [piece - centre for piece in blocks]
    variance = sum(jnp.sum(piece * piece, axis=1, keepdims=True) for piece in blocks) * (
        1.0 / count
    )
    inverse = lax.rsqrt(variance + norm_eps)
    share = features_ref.shape[2]
    for index, piece in enumerate(blocks):
        cols = slice(index * columns, (index + 1) * columns)
        feature = jax.nn.gelu(piece * inverse * gain_ref[:, cols]).astype(jnp.bfloat16)
        start = index * columns % share
        features_ref[index * columns // share, :, start : start + columns] = feature


def project_embed(
    ids,
    offsets,
    latents,
    begun,
    attended,
    chunks,
    width,
    out_weight,
    weights,
    gain,
    depth_parts,
    after,
):
    particles, tokens, model_width = latents.shape
    rows = particles * tokens
    parts = len(weights)
    columns = weights[0].shape[2]
    count = parts * columns
    out_depth = model_width * len(attended) // chunks
    pieces = ([] if begun is None else [begun]) + attended
    vmem = pl.BlockSpec(memory_space=pltpu.VMEM)
    smem = pl.BlockSpec(memory_space=pltpu.SMEM)
    hbm = pl.BlockSpec(memory_space=pltpu.HBM)
    inputs = 4 + len(pieces) + parts + len(after)
    groups = model_width // column_block(model_width)

    def kernel(*refs):
        project_kernel(
            chunks,
            width,
            len(pieces),
            parts,
            offsets,
            depth_parts,
            refs[:inputs],
            refs[inputs:],
        )

    return pl.pallas_call(
        kernel,
        in_specs=[smem, hbm, vmem, hbm]
        + ([] if begun is None else [hbm])
        + [vmem] * len(attended)
        + [hbm] * parts
        + [pl.BlockSpec(memory_space=pl.ANY)] * len(after),
        out_specs=[vmem, vmem],
        out_shape=[
            jax.ShapeDtypeStruct(latents.shape, jnp.bfloat16),
            jax.ShapeDtypeStruct((depth_parts, rows, count // depth_parts), jnp.bfloat16),
        ],
        scratch_shapes=[
            pltpu.VMEM((out_depth, model_width), jnp.bfloat16),
            pltpu.VMEM((parts, model_width, columns), jnp.bfloat16),
            pltpu.VMEM((rows, out_depth), jnp.bfloat16),
            pltpu.VMEM((rows, model_width), jnp.bfloat16),
            pltpu.VMEM((parts, rows, columns), jnp.float32),
            pltpu.VMEM(latents.shape, latents.dtype),
            pltpu.VMEM((rows, model_width), jnp.float32),
            pltpu.SemaphoreType.DMA((groups, model_width // width * len(attended))),
            pltpu.SemaphoreType.DMA((parts,)),
            pltpu.SemaphoreType.DMA((2, groups)),
        ],
        compiler_params=pltpu.CompilerParams(vmem_limit_bytes=60 * MIB),
        cost_estimate=pl.CostEstimate(
            flops=2 * rows * model_width * (out_depth + count),
            bytes_accessed=2 * model_width * (out_depth + count) + 12 * rows * model_width,
            transcendentals=rows * count,
        ),
        name="project_embed",
    )(ids, latents, gain.reshape(1, count), out_weight, *pieces, *weights, *after)


def reward_kernel(particles, scale, parts, doms, offsets, joined, *refs):
    ids_ref, features_ref, head_ref, before_ref = refs[:4]
    weight_refs, (out_ref, weight_vmem, rows_ref, sems) = refs[4:-4], refs[-4:]
    dom, group, seq = ids_ref[0], ids_ref[1], ids_ref[2]
    shards, depth, columns = weight_refs[0].shape
    rows = features_ref.shape[1]
    count = shards * len(weight_refs) // parts

    copies = []
    for place in range(count):
        pair, shard = divmod(place, shards)
        lane = place % joined * columns
        for index in range(parts):
            copy = pltpu.make_async_copy(
                weight_refs[pair * parts + index].at[shard],
                weight_vmem.at[
                    place // joined,
                    index * depth : (index + 1) * depth,
                    lane : lane + columns,
                ],
                sems.at[place, index],
            )
            copy.start()
            copies.append(copy)
    for index in range(parts):
        rows_ref[:, index * depth : (index + 1) * depth] = features_ref[
            (group + parts - index) % parts
        ]
    totals = jnp.zeros((particles, joined * columns), jnp.float32)
    for step in range(count // joined):
        for copy in copies[step * joined * parts : (step + 1) * joined * parts]:
            copy.wait()
        hidden = jnp.dot(rows_ref[...], weight_vmem[step], preferred_element_type=jnp.float32)
        places = range(step * joined, (step + 1) * joined)
        head = jnp.concatenate(
            [head_ref[(seq ^ offsets[place]) * doms + dom] for place in places], axis=1
        )
        scored = jax.nn.gelu(hidden) * head
        totals += jnp.sum(scored.reshape(particles, rows // particles, -1), axis=1)

    sums = jnp.sum(totals, axis=1, keepdims=True) * scale
    first = len(before_ref.shape) == 1
    shape = out_ref.shape
    out_rows = lax.broadcasted_iota(jnp.int32, shape, 0)
    lanes = lax.broadcasted_iota(jnp.int32, shape, 1)
    logits = jnp.zeros(shape, jnp.float32) if first else before_ref[...]
    row = dom if first else (dom + 1) % doms
    for particle in range(particles):
        here = jnp.logical_and(out_rows == row, lanes == particle)
        value = sums[particle : particle + 1]
        if first:
            value = value + jnp.where(seq == 0, before_ref[particle], 0.0)
        logits += jnp.where(here, value, 0.0)
    out_ref[...] = logits


def reward(ids, features, weights, parts, doms, offsets, head, before, particles, scale):
    shards, depth, columns = weights[0].shape
    rows = features.shape[1]
    count = shards * len(weights) // parts
    joined = 2 if columns % LANES == 0 and count % 2 == 0 else 1
    smem = pl.BlockSpec(memory_space=pltpu.SMEM)
    vmem = pl.BlockSpec(memory_space=pltpu.VMEM)
    return pl.pallas_call(
        functools.partial(reward_kernel, particles, scale, parts, doms, offsets, joined),
        in_specs=[smem, vmem, vmem, smem if before.ndim == 1 else vmem]
        + [pl.BlockSpec(memory_space=pltpu.HBM)] * len(weights),
        out_specs=vmem,
        out_shape=jax.ShapeDtypeStruct((8, LANES), jnp.float32),
        scratch_shapes=[
            pltpu.VMEM((count // joined, parts * depth, joined * columns), jnp.bfloat16),
            pltpu.VMEM((rows, parts * depth), jnp.bfloat16),
            pltpu.SemaphoreType.DMA((count, parts)),
        ],
        compiler_params=pltpu.CompilerParams(vmem_limit_bytes=60 * MIB),
        cost_estimate=pl.CostEstimate(
            flops=2 * rows * parts * depth * count * columns,
            bytes_accessed=2 * parts * depth * count * columns,
            transcendentals=rows * count * columns,
        ),
        name="reward",
    )(ids, features, head, before, *weights)


def add_kernel(*refs):
    refs[-1][...] = sum(ref[...] for ref in refs[:-1])


def add_parts(parts):
    return pl.pallas_call(
        add_kernel,
        out_shape=jax.ShapeDtypeStruct(parts[0].shape, parts[0].dtype),
        compiler_params=pltpu.CompilerParams(vmem_limit_bytes=2 * MIB),
        name="add_partials",
    )(*parts)


def finish_kernel(particles, doms, ids_ref, resampled_ref, *refs):
    logit_refs, (out_ref, same_ref) = refs[:-2], refs[-2:]
    logits = sum(ref[...] for ref in logit_refs)
    rows = lax.broadcasted_iota(jnp.int32, logits.shape, 0)
    lanes = lax.broadcasted_iota(jnp.int32, logits.shape, 1)
    valid = jnp.logical_and(rows < doms, lanes < particles)
    highest = jnp.max(jnp.where(valid, logits, -jnp.inf))
    total = jnp.sum(jnp.where(valid, jnp.exp(logits - highest), 0.0), axis=1, keepdims=True)
    log_total = highest + jnp.log(jnp.sum(total, axis=0, keepdims=True))
    own = jnp.sum(jnp.where(rows == ids_ref[0], logits, 0.0), axis=0, keepdims=True)
    out_ref[...] = (own - log_total)[:, :particles]


def finish(ids, logits, resampled, particles, doms):
    vmem = pl.BlockSpec(memory_space=pltpu.VMEM)
    anywhere = pl.BlockSpec(memory_space=pl.ANY)
    log_weights, resampled = pl.pallas_call(
        functools.partial(finish_kernel, particles, doms),
        in_specs=[pl.BlockSpec(memory_space=pltpu.SMEM), anywhere] + [vmem] * len(logits),
        out_specs=[vmem, anywhere],
        out_shape=[
            jax.ShapeDtypeStruct((1, particles), jnp.float32),
            jax.ShapeDtypeStruct(resampled.shape, resampled.dtype),
        ],
        input_output_aliases={1: 1},
        compiler_params=pltpu.CompilerParams(vmem_limit_bytes=2 * MIB),
        name="log_weights",
    )(ids, resampled, *logits)
    return resampled, log_weights.reshape(particles)


def resample_kernel(ids_ref, ancestors_ref, own_ref, other_ref, out_ref):
    index = pl.program_id(0)
    own = ancestors_ref[index] // pl.num_programs(0) == ids_ref[0]

    @pl.when(own)
    def _():
        out_ref[...] = own_ref[...]

    @pl.when(jnp.logical_not(own))
    def _():
        out_ref[...] = other_ref[...]


def resample(ids, ancestors, own, other):
    particles, tokens, columns = own.shape
    block = (1, tokens, columns)
    parent = pl.BlockSpec(block, lambda i, ids, ancestors: (ancestors[i] % particles, 0, 0))
    return pl.pallas_call(
        resample_kernel,
        grid_spec=pltpu.PrefetchScalarGridSpec(
            num_scalar_prefetch=2,
            grid=(particles,),
            in_specs=[parent, parent],
            out_specs=pl.BlockSpec(block, lambda i, ids, ancestors: (i, 0, 0)),
        ),
        out_shape=jax.ShapeDtypeStruct(own.shape, own.dtype),
        compiler_params=pltpu.CompilerParams(vmem_limit_bytes=4 * MIB),
        name="resample",
    )(ids, ancestors, own, other)


def shifted(array, axis, step):
    count = lax.axis_size(axis)
    return lax.ppermute(array, axis, [(i, (i + step) % count) for i in range(count)])


def swapped(array, axis, bit):
    return lax.ppermute(array, axis, [(i, i ^ bit) for i in range(lax.axis_size(axis))])


def exchange(array):
    return lax.all_to_all(array, "seq", 0, 0, tiled=True)


def on_device(
    latents,
    queries,
    keys,
    values,
    out_weight,
    step_index,
    embed_weight,
    norm_gain,
    up_weight,
    head_weight,
    prev_logw,
    ancestors,
):
    seq_count = lax.axis_size("seq")
    group_count = lax.axis_size("groups")
    dom_count = lax.axis_size("dom")
    holders = group_count * dom_count
    dom = lax.axis_index("dom")
    group = lax.axis_index("groups")
    seq = lax.axis_index("seq")
    particles, tokens, model_width = latents.shape
    head_width = model_width // HEADS
    width = particles * model_width // seq_count
    chunks = 2 if width % (2 * LANES) == 0 else 1

    ids = jnp.stack([dom, group, seq, step_index[0]]).astype(jnp.int32)

    embed_columns = embed_weight.shape[1] // holders
    embed_share = lax.dynamic_slice_in_dim(
        embed_weight, (dom * group_count + group) * embed_columns, embed_columns, 1
    )[None]
    up_depth = up_weight.shape[0] // group_count
    up_columns = up_weight.shape[1] // dom_count
    up_share = lax.dynamic_slice(
        up_weight, (group * up_depth, dom * up_columns), (up_depth, up_columns)
    )[None]
    bits = [1 << place for place in reversed(range(1, seq_count.bit_length() - 1))]
    near = [0]
    for bit in bits[:-2]:
        embed_share = jnp.concatenate([embed_share, swapped(embed_share, "seq", bit)])
        up_share = jnp.concatenate([up_share, swapped(up_share, "seq", bit)])
        near = near + [offset ^ bit for offset in near]
    high, low = bits[-2:]

    def over_groups(array):
        return [array] + [shifted(array, "groups", k) for k in range(1, group_count)]

    def pair_of(arrays):
        return [swapped(array, "seq", 1) for array in arrays]

    packed = [pack(queries, keys, values, chunks, width, 0, [])]
    arrived = [exchange(packed[0])]
    embed_share = jnp.concatenate([embed_share, swapped(embed_share, "seq", high)])
    up_high, up_low = swapped(up_share, "seq", high), swapped(up_share, "seq", low)
    own_groups, own_pair = over_groups(up_share), swapped(up_share, "seq", 1)
    first = [up_high, up_low, own_pair, *own_groups[1:]]
    [embed_share] = gate([embed_share], first)
    for bit in (low, 1):
        embed_share = jnp.concatenate([embed_share, swapped(embed_share, "seq", bit)])
    packed += [
        pack(queries, keys, values, chunks, width, chunk, [embed_share, *first])
        for chunk in range(1, chunks)
    ]

    arrived += [exchange(piece) for piece in packed[1:]]
    up_both = swapped(up_high, "seq", low)
    embed_near = over_groups(embed_share)
    high_groups, low_groups = over_groups(up_high), over_groups(up_low)
    high_pair, low_pair = swapped(up_high, "seq", 1), swapped(up_low, "seq", 1)
    own_pairs = [own_pair] + pair_of(own_groups[1:])
    second = [up_both, high_pair, low_pair, *own_pairs[1:], *embed_near[1:]]
    second += high_groups[1:] + low_groups[1:]
    attended = [attention(arrived[0], head_width, [])]
    attended += [attention(piece, head_width, second) for piece in arrived[1:]]

    returned = [exchange(attended[0])]
    embed_parts = embed_near + [
        shifted(piece, "dom", k) for k in range(1, dom_count) for piece in embed_near
    ]
    both_groups, both_pair = over_groups(up_both), swapped(up_both, "seq", 1)
    high_pairs = over_groups(high_pair)
    third = [both_pair, *embed_parts[group_count:], *both_groups[1:], *high_pairs[1:]]
    if chunks > 1:
        begun = first_project(latents, out_weight, returned.pop(0), chunks, width, third)
    else:
        begun = None

    returned += [exchange(piece) for piece in attended[1:]]
    both_pairs = over_groups(both_pair)
    low_pairs = [low_pair] + pair_of(low_groups[1:])
    up_parts = own_groups + own_pairs + high_groups + high_pairs
    up_parts += low_groups + low_pairs + both_groups + both_pairs
    up_offsets = [
        offset ^ bit ^ pair for bit in (0, high, low, high ^ low) for pair in (0, 1) for offset in near
    ]
    embed_offsets = near + [offset ^ high for offset in near]
    for bit in (low, 1):
        embed_offsets = embed_offsets + [offset ^ bit for offset in embed_offsets]

    stepped, features = project_embed(
        ids,
        embed_offsets,
        latents,
        begun,
        returned,
        chunks,
        width,
        out_weight,
        embed_parts,
        norm_gain,
        group_count,
        [*both_pairs[1:], *low_pairs[1:], *third],
    )
    stepped_other = shifted(stepped, "dom", 1)
    features_other = shifted(features, "dom", 1)

    scale = potential_scale / math.sqrt(tokens * seq_count)
    head = head_weight.reshape(seq_count * dom_count, 1, up_columns)
    score = functools.partial(
        reward,
        ids,
        weights=up_parts,
        parts=group_count,
        doms=dom_count,
        offsets=up_offsets,
        head=head,
        particles=particles,
        scale=scale,
    )
    partial_own = score(features, before=prev_logw)
    partial = score(features_other, before=partial_own)
    partial = add_parts(
        [partial] + [swapped(partial, "seq", 2 * k) for k in range(1, seq_count // 2)]
    )
    pair = [
        (d * seq_count + i, (d + k) % dom_count * seq_count + (i ^ 1))
        for k in range(1, dom_count)
        for d in range(dom_count)
        for i in range(seq_count)
    ]
    logits = [partial, swapped(partial, "seq", 1), lax.ppermute(partial, ("dom", "seq"), pair)] + [
        shifted(partial, "dom", k) for k in range(1, dom_count)
    ]
    resampled = resample(ids, ancestors.astype(jnp.int32), stepped, stepped_other)
    return finish(ids, logits, resampled, particles, dom_count)


def solution(mesh):
    in_specs = (
        P(("groups", "dom"), "seq", None),
        P(("groups", "dom"), "seq", None),
        P(("groups", "dom"), "seq", None),
        P(("groups", "dom"), "seq", None),
        P(),
        P("groups"),
        P("seq", None),
        P(),
        P(None, "seq"),
        P(),
        P(("groups", "dom")),
        P(("groups", "dom")),
    )
    out_specs = (P(("groups", "dom"), "seq", None), P(("groups", "dom")))
    return jax.shard_map(
        on_device, mesh=mesh, in_specs=in_specs, out_specs=out_specs, check_vma=False
    )
```

```python
import functools
import math

import jax
import jax.numpy as jnp
from jax import lax
from jax.experimental import pallas as pl
from jax.experimental.pallas import tpu as pltpu
from jax.sharding import PartitionSpec as P

HEADS = 24
STEPS = 28
LANES = 128

potential_scale = 4.0
norm_eps = 1e-05
MIB = 1024 * 1024


def pack_kernel(chunks, width, q_ref, k_ref, v_ref, *out_refs):
    particles, _, model_width = q_ref.shape
    blocks = model_width // width
    part = width // chunks
    for index, ref in enumerate((q_ref, k_ref, v_ref)):
        for particle in range(particles):
            for block in range(blocks):
                for chunk in range(chunks):
                    start = block * width + chunk * part
                    out_refs[chunk][particle * blocks + block, index] = ref[
                        particle, :, start : start + part
                    ]


def pack(queries, keys, values, chunks, width):
    particles, tokens, model_width = queries.shape
    count = particles * model_width // width
    vmem = pl.BlockSpec(memory_space=pltpu.VMEM)
    shape = jax.ShapeDtypeStruct((count, 3, tokens, width // chunks), queries.dtype)
    return list(
        pl.pallas_call(
            functools.partial(pack_kernel, chunks, width),
            in_specs=[vmem] * 3,
            out_specs=[vmem] * chunks,
            out_shape=[shape] * chunks,
            compiler_params=pltpu.CompilerParams(vmem_limit_bytes=60 * MIB),
            name="pack_heads",
        )(queries, keys, values)
    )


def gate_kernel(*refs):
    pass


def gate(array, after):
    hbm = pl.BlockSpec(memory_space=pltpu.HBM)
    return pl.pallas_call(
        gate_kernel,
        in_specs=[hbm] + [pl.BlockSpec(memory_space=pl.ANY)] * len(after),
        out_specs=hbm,
        out_shape=jax.ShapeDtypeStruct(array.shape, array.dtype),
        input_output_aliases={0: 0},
        compiler_params=pltpu.CompilerParams(vmem_limit_bytes=60 * MIB),
        name="gate",
    )(array, *after)


def attention_kernel(head_width, block_sources, qkv_ref, out_ref):
    sources, _, tokens, columns = qkv_ref.shape
    total = sources * tokens
    rows = block_sources * tokens
    factor = 1.0 / math.sqrt(head_width) / math.log(2.0)
    k_all = qkv_ref[:, 1].reshape(total, columns)
    v_all = qkv_ref[:, 2].reshape(total, columns)
    for block in range(0, sources, block_sources):
        span = slice(block, block + block_sources)
        q_all = qkv_ref[span, 0].reshape(rows, columns)
        pieces = []
        for head in range(columns // head_width):
            cols = slice(head * head_width, (head + 1) * head_width)
            scores = lax.dot_general(
                q_all[:, cols],
                k_all[:, cols],
                (((1,), (1,)), ((), ())),
                preferred_element_type=jnp.float32,
            )
            highest = jnp.max(scores, axis=1, keepdims=True)
            expanded = jnp.exp2((scores - highest) * factor)
            norm = 1.0 / jnp.sum(expanded, axis=1, keepdims=True)
            weights = (expanded * norm).astype(jnp.bfloat16)
            pieces.append(jnp.dot(weights, v_all[:, cols], preferred_element_type=jnp.float32))
        joined = jnp.concatenate(pieces, axis=1).astype(jnp.bfloat16)
        out_ref[span] = joined.reshape(block_sources, tokens, columns)


def attention(qkv, head_width):
    sources, _, tokens, columns = qkv.shape
    total = sources * tokens
    block_sources = max(1, min(sources, 512 // tokens))
    while sources % block_sources:
        block_sources -= 1
    step = LANES if columns % LANES == 0 and LANES % head_width == 0 else columns
    scores_bytes = 4 * block_sources * tokens * total
    return pl.pallas_call(
        functools.partial(attention_kernel, head_width, block_sources),
        grid=(columns // step,),
        in_specs=[pl.BlockSpec((sources, 3, tokens, step), lambda i: (0, 0, 0, i))],
        out_specs=pl.BlockSpec((sources, tokens, step), lambda i: (0, 0, i)),
        out_shape=jax.ShapeDtypeStruct((sources, tokens, columns), jnp.bfloat16),
        compiler_params=pltpu.CompilerParams(vmem_limit_bytes=60 * MIB),
        cost_estimate=pl.CostEstimate(
            flops=4 * total * total * columns,
            bytes_accessed=8 * total * columns,
            transcendentals=columns // head_width * total * total,
        ),
        name="attention",
    )(qkv)


def column_block(model_width):
    return 512 if model_width % 512 == 0 else model_width


class ProjectionWeights:
    def __init__(self, weight_ref, vmem_ref, sems, chunks, wanted, width):
        depth, model_width = weight_ref.shape
        part = width // chunks
        blocks = depth // width
        self.block = column_block(model_width)
        self.copies = []
        for group in range(model_width // self.block):
            cols = slice(group * self.block, (group + 1) * self.block)
            for index in range(blocks * len(wanted)):
                start = index // len(wanted) * width + wanted[index % len(wanted)] * part
                self.copies.append(
                    pltpu.make_async_copy(
                        weight_ref.at[start : start + part, cols],
                        vmem_ref.at[index * part : (index + 1) * part, cols],
                        sems.at[group, index],
                    )
                )
        self.per_group = blocks * len(wanted)
        for copy in self.copies:
            copy.start()

    def wait(self, group):
        for copy in self.copies[group * self.per_group : (group + 1) * self.per_group]:
            copy.wait()
        return slice(group * self.block, (group + 1) * self.block)


def gather_rows(piece_refs, rows_ref, particles):
    count, tokens, part = piece_refs[0].shape
    blocks = count // particles
    for index in range(blocks * len(piece_refs)):
        ref = piece_refs[index % len(piece_refs)]
        place = index // len(piece_refs)
        for particle in range(particles):
            rows_ref[
                particle * tokens : (particle + 1) * tokens, index * part : (index + 1) * part
            ] = ref[particle * blocks + place]


def first_project_kernel(chunks, width, latents_ref, weight_ref, piece_ref, out_ref, *scratch):
    weight_vmem, rows_ref, sems = scratch
    particles, tokens, model_width = latents_ref.shape
    weights = ProjectionWeights(weight_ref, weight_vmem, sems, chunks, [0], width)
    gather_rows([piece_ref], rows_ref, particles)
    for group in range(model_width // weights.block):
        cols = weights.wait(group)
        flat = latents_ref[:, :, cols].reshape(particles * tokens, weights.block)
        out_ref[:, cols] = flat.astype(jnp.float32) + jnp.dot(
            rows_ref[...], weight_vmem[:, cols], preferred_element_type=jnp.float32
        )


def first_project(latents, out_weight, piece, chunks, width):
    particles, tokens, model_width = latents.shape
    rows, depth = particles * tokens, model_width // chunks
    vmem = pl.BlockSpec(memory_space=pltpu.VMEM)
    return pl.pallas_call(
        functools.partial(first_project_kernel, chunks, width),
        in_specs=[vmem, pl.BlockSpec(memory_space=pltpu.HBM), vmem],
        out_specs=vmem,
        out_shape=jax.ShapeDtypeStruct((rows, model_width), jnp.float32),
        scratch_shapes=[
            pltpu.VMEM((depth, model_width), jnp.bfloat16),
            pltpu.VMEM((rows, depth), jnp.bfloat16),
            pltpu.SemaphoreType.DMA(
                (model_width // column_block(model_width), model_width // width)
            ),
        ],
        compiler_params=pltpu.CompilerParams(vmem_limit_bytes=60 * MIB),
        cost_estimate=pl.CostEstimate(
            flops=2 * rows * depth * model_width,
            bytes_accessed=2 * depth * model_width + 8 * rows * model_width,
            transcendentals=0,
        ),
        name="first_project",
    )(latents, out_weight, piece)


def project_kernel(chunks, width, pieces, parts, offsets, depth_parts, refs_in, refs_out):
    ids_ref, latents_hbm, gain_ref, out_weight_ref = refs_in[:4]
    rest, weight_refs = list(refs_in[4 : 4 + pieces]), refs_in[4 + pieces : 4 + pieces + parts]
    begun_hbm = rest.pop(0) if chunks > 1 else None
    stepped_ref, features_ref = refs_out[:2]
    out_vmem, weight_vmem, rows_ref, clean_ref, embedded_ref = refs_out[2:7]
    latents_ref, begun_ref, out_sems, sems, first_sems = refs_out[7:]
    dom, group, seq = ids_ref[0], ids_ref[1], ids_ref[2]
    sigma = ids_ref[3].astype(jnp.float32) * (1.0 / STEPS)
    particles, tokens, model_width = latents_ref.shape
    rows = particles * tokens
    shards, depth, columns = weight_refs[0].shape

    wanted = list(range(chunks - len(rest), chunks))
    block = column_block(model_width)
    first_copies = []
    for index in range(model_width // block):
        cols = slice(index * block, (index + 1) * block)
        first_copies.append(
            pltpu.make_async_copy(
                latents_hbm.at[:, :, cols], latents_ref.at[:, :, cols], first_sems.at[0, index]
            )
        )
        if chunks > 1:
            first_copies.append(
                pltpu.make_async_copy(
                    begun_hbm.at[:, cols], begun_ref.at[:, cols], first_sems.at[1, index]
                )
            )
    for copy in first_copies[: len(first_copies) // (model_width // block)]:
        copy.start()
    out_weights = ProjectionWeights(out_weight_ref, out_vmem, out_sems, chunks, wanted, width)
    for copy in first_copies[len(first_copies) // (model_width // block) :]:
        copy.start()
    copies = []
    for index in range(parts):
        for shard in range(shards):
            start = pl.multiple_of((seq ^ offsets[shard]) * depth, depth)
            copy = pltpu.make_async_copy(
                weight_refs[index].at[shard],
                weight_vmem.at[index, pl.ds(start, depth)],
                sems.at[index],
            )
            copy.start()
            copies.append(copy)

    gather_rows(rest, rows_ref, particles)
    for index in range(model_width // out_weights.block):
        cols = out_weights.wait(index)
        each = len(first_copies) // (model_width // block)
        for copy in first_copies[index * each : (index + 1) * each]:
            copy.wait()
        flat = latents_ref[:, :, cols].reshape(rows, out_weights.block).astype(jnp.float32)
        begun = begun_ref[:, cols] if chunks > 1 else flat
        velocity = begun + jnp.dot(
            rows_ref[...], out_vmem[:, cols], preferred_element_type=jnp.float32
        )
        clean_ref[:, cols] = (flat - sigma * velocity).astype(jnp.bfloat16)
        stepped_ref[:, :, cols] = (
            (flat - velocity * (1.0 / STEPS))
            .astype(jnp.bfloat16)
            .reshape(particles, tokens, out_weights.block)
        )

    for index in range(parts):
        for copy in copies[index * shards : (index + 1) * shards]:
            copy.wait()
        doms = parts // depth_parts
        dom_of = (dom + doms - index // depth_parts) % doms
        group_of = (group + depth_parts - index % depth_parts) % depth_parts
        embedded_ref[dom_of * depth_parts + group_of] = jnp.dot(
            clean_ref[...], weight_vmem[index], preferred_element_type=jnp.float32
        )
    count = parts * columns
    blocks = [embedded_ref[index] for index in range(parts)]
    centre = sum(jnp.sum(piece, axis=1, keepdims=True) for piece in blocks) * (1.0 / count)
    blocks = [piece - centre for piece in blocks]
    variance = sum(jnp.sum(piece * piece, axis=1, keepdims=True) for piece in blocks) * (
        1.0 / count
    )
    inverse = lax.rsqrt(variance + norm_eps)
    share = features_ref.shape[2]
    for index, piece in enumerate(blocks):
        cols = slice(index * columns, (index + 1) * columns)
        feature = jax.nn.gelu(piece * inverse * gain_ref[:, cols]).astype(jnp.bfloat16)
        start = index * columns % share
        features_ref[index * columns // share, :, start : start + columns] = feature


def project_embed(
    ids,
    offsets,
    latents,
    begun,
    attended,
    chunks,
    width,
    out_weight,
    weights,
    gain,
    depth_parts,
    after,
):
    particles, tokens, model_width = latents.shape
    rows = particles * tokens
    parts = len(weights)
    columns = weights[0].shape[2]
    count = parts * columns
    out_depth = model_width * len(attended) // chunks
    pieces = ([] if begun is None else [begun]) + attended
    vmem = pl.BlockSpec(memory_space=pltpu.VMEM)
    smem = pl.BlockSpec(memory_space=pltpu.SMEM)
    hbm = pl.BlockSpec(memory_space=pltpu.HBM)
    inputs = 4 + len(pieces) + parts + len(after)
    groups = model_width // column_block(model_width)

    def kernel(*refs):
        project_kernel(
            chunks,
            width,
            len(pieces),
            parts,
            offsets,
            depth_parts,
            refs[:inputs],
            refs[inputs:],
        )

    return pl.pallas_call(
        kernel,
        in_specs=[smem, hbm, vmem, hbm]
        + ([] if begun is None else [hbm])
        + [vmem] * len(attended)
        + [hbm] * parts
        + [pl.BlockSpec(memory_space=pl.ANY)] * len(after),
        out_specs=[vmem, vmem],
        out_shape=[
            jax.ShapeDtypeStruct(latents.shape, jnp.bfloat16),
            jax.ShapeDtypeStruct((depth_parts, rows, count // depth_parts), jnp.bfloat16),
        ],
        scratch_shapes=[
            pltpu.VMEM((out_depth, model_width), jnp.bfloat16),
            pltpu.VMEM((parts, model_width, columns), jnp.bfloat16),
            pltpu.VMEM((rows, out_depth), jnp.bfloat16),
            pltpu.VMEM((rows, model_width), jnp.bfloat16),
            pltpu.VMEM((parts, rows, columns), jnp.float32),
            pltpu.VMEM(latents.shape, latents.dtype),
            pltpu.VMEM((rows, model_width), jnp.float32),
            pltpu.SemaphoreType.DMA((groups, model_width // width * len(attended))),
            pltpu.SemaphoreType.DMA((parts,)),
            pltpu.SemaphoreType.DMA((2, groups)),
        ],
        compiler_params=pltpu.CompilerParams(vmem_limit_bytes=60 * MIB),
        cost_estimate=pl.CostEstimate(
            flops=2 * rows * model_width * (out_depth + count),
            bytes_accessed=2 * model_width * (out_depth + count) + 12 * rows * model_width,
            transcendentals=rows * count,
        ),
        name="project_embed",
    )(ids, latents, gain.reshape(1, count), out_weight, *pieces, *weights, *after)


def reward_kernel(particles, scale, parts, doms, offsets, joined, *refs):
    ids_ref, features_ref, head_ref, before_ref = refs[:4]
    weight_refs, (out_ref, weight_vmem, rows_ref, sems) = refs[4:-4], refs[-4:]
    dom, group, seq = ids_ref[0], ids_ref[1], ids_ref[2]
    _, depth, columns = weight_refs[0].shape
    rows = features_ref.shape[1]
    places = [
        (pair, shard)
        for pair in range(len(weight_refs) // parts)
        for shard in range(weight_refs[pair * parts].shape[0])
    ]
    count = len(places)

    copies = []
    for place, (pair, shard) in enumerate(places):
        lane = place % joined * columns
        for index in range(parts):
            copy = pltpu.make_async_copy(
                weight_refs[pair * parts + index].at[shard],
                weight_vmem.at[
                    place // joined,
                    index * depth : (index + 1) * depth,
                    lane : lane + columns,
                ],
                sems.at[place, index],
            )
            copy.start()
            copies.append(copy)
    for index in range(parts):
        rows_ref[:, index * depth : (index + 1) * depth] = features_ref[
            (group + parts - index) % parts
        ]
    totals = jnp.zeros((particles, joined * columns), jnp.float32)
    for step in range(count // joined):
        for copy in copies[step * joined * parts : (step + 1) * joined * parts]:
            copy.wait()
        hidden = jnp.dot(rows_ref[...], weight_vmem[step], preferred_element_type=jnp.float32)
        head = jnp.concatenate(
            [
                head_ref[(seq ^ offset) * doms + dom]
                for offset in offsets[step * joined : (step + 1) * joined]
            ],
            axis=1,
        )
        scored = jax.nn.gelu(hidden) * head
        totals += jnp.sum(scored.reshape(particles, rows // particles, -1), axis=1)

    sums = jnp.sum(totals, axis=1, keepdims=True) * scale
    first = len(before_ref.shape) == 1
    shape = out_ref.shape
    out_rows = lax.broadcasted_iota(jnp.int32, shape, 0)
    lanes = lax.broadcasted_iota(jnp.int32, shape, 1)
    logits = jnp.zeros(shape, jnp.float32) if first else before_ref[...]
    row = dom if first else (dom + 1) % doms
    for particle in range(particles):
        here = jnp.logical_and(out_rows == row, lanes == particle)
        value = sums[particle : particle + 1]
        if first:
            value = value + jnp.where(seq == 0, before_ref[particle], 0.0)
        logits += jnp.where(here, value, 0.0)
    out_ref[...] = logits


def reward(ids, features, weights, parts, doms, offsets, head, before, particles, scale):
    _, depth, columns = weights[0].shape
    rows = features.shape[1]
    count = len(offsets)
    joined = 2 if columns % LANES == 0 and count % 2 == 0 else 1
    smem = pl.BlockSpec(memory_space=pltpu.SMEM)
    vmem = pl.BlockSpec(memory_space=pltpu.VMEM)
    return pl.pallas_call(
        functools.partial(reward_kernel, particles, scale, parts, doms, offsets, joined),
        in_specs=[smem, vmem, vmem, smem if before.ndim == 1 else vmem]
        + [pl.BlockSpec(memory_space=pltpu.HBM)] * len(weights),
        out_specs=vmem,
        out_shape=jax.ShapeDtypeStruct((8, LANES), jnp.float32),
        scratch_shapes=[
            pltpu.VMEM((count // joined, parts * depth, joined * columns), jnp.bfloat16),
            pltpu.VMEM((rows, parts * depth), jnp.bfloat16),
            pltpu.SemaphoreType.DMA((count, parts)),
        ],
        compiler_params=pltpu.CompilerParams(vmem_limit_bytes=20 * MIB),
        cost_estimate=pl.CostEstimate(
            flops=2 * rows * parts * depth * count * columns,
            bytes_accessed=2 * parts * depth * count * columns,
            transcendentals=rows * count * columns,
        ),
        name="reward",
    )(ids, features, head, before, *weights)


def add_kernel(*refs):
    refs[-1][...] = sum(ref[...] for ref in refs[:-1])


def add_parts(parts):
    return pl.pallas_call(
        add_kernel,
        out_shape=jax.ShapeDtypeStruct(parts[0].shape, parts[0].dtype),
        compiler_params=pltpu.CompilerParams(vmem_limit_bytes=2 * MIB),
        name="add_partials",
    )(*parts)


def finish_kernel(particles, doms, ids_ref, resampled_ref, *refs):
    logit_refs, (out_ref, same_ref) = refs[:-2], refs[-2:]
    logits = sum(ref[...] for ref in logit_refs)
    rows = lax.broadcasted_iota(jnp.int32, logits.shape, 0)
    lanes = lax.broadcasted_iota(jnp.int32, logits.shape, 1)
    valid = jnp.logical_and(rows < doms, lanes < particles)
    highest = jnp.max(jnp.where(valid, logits, -jnp.inf))
    total = jnp.sum(jnp.where(valid, jnp.exp(logits - highest), 0.0), axis=1, keepdims=True)
    log_total = highest + jnp.log(jnp.sum(total, axis=0, keepdims=True))
    own = jnp.sum(jnp.where(rows == ids_ref[0], logits, 0.0), axis=0, keepdims=True)
    out_ref[...] = (own - log_total)[:, :particles]


def finish(ids, logits, resampled, particles, doms):
    vmem = pl.BlockSpec(memory_space=pltpu.VMEM)
    anywhere = pl.BlockSpec(memory_space=pl.ANY)
    log_weights, resampled = pl.pallas_call(
        functools.partial(finish_kernel, particles, doms),
        in_specs=[pl.BlockSpec(memory_space=pltpu.SMEM), anywhere] + [vmem] * len(logits),
        out_specs=[vmem, anywhere],
        out_shape=[
            jax.ShapeDtypeStruct((1, particles), jnp.float32),
            jax.ShapeDtypeStruct(resampled.shape, resampled.dtype),
        ],
        input_output_aliases={1: 1},
        compiler_params=pltpu.CompilerParams(vmem_limit_bytes=2 * MIB),
        name="log_weights",
    )(ids, resampled, *logits)
    return resampled, log_weights.reshape(particles)


def resample_kernel(ids_ref, ancestors_ref, own_ref, other_ref, out_ref):
    index = pl.program_id(0)
    own = ancestors_ref[index] // pl.num_programs(0) == ids_ref[0]

    @pl.when(own)
    def _():
        out_ref[...] = own_ref[...]

    @pl.when(jnp.logical_not(own))
    def _():
        out_ref[...] = other_ref[...]


def resample(ids, ancestors, own, other):
    particles, tokens, columns = own.shape
    block = (1, tokens, columns)
    parent = pl.BlockSpec(block, lambda i, ids, ancestors: (ancestors[i] % particles, 0, 0))
    return pl.pallas_call(
        resample_kernel,
        grid_spec=pltpu.PrefetchScalarGridSpec(
            num_scalar_prefetch=2,
            grid=(particles,),
            in_specs=[parent, parent],
            out_specs=pl.BlockSpec(block, lambda i, ids, ancestors: (i, 0, 0)),
        ),
        out_shape=jax.ShapeDtypeStruct(own.shape, own.dtype),
        compiler_params=pltpu.CompilerParams(vmem_limit_bytes=4 * MIB),
        name="resample",
    )(ids, ancestors, own, other)


def shifted(array, axis, step):
    count = lax.axis_size(axis)
    return lax.ppermute(array, axis, [(i, (i + step) % count) for i in range(count)])


def swapped(array, axis, bit):
    return lax.ppermute(array, axis, [(i, i ^ bit) for i in range(lax.axis_size(axis))])


def exchange(array):
    return lax.all_to_all(array, "seq", 0, 0, tiled=True)


def on_device(
    latents,
    queries,
    keys,
    values,
    out_weight,
    step_index,
    embed_weight,
    norm_gain,
    up_weight,
    head_weight,
    prev_logw,
    ancestors,
):
    seq_count = lax.axis_size("seq")
    group_count = lax.axis_size("groups")
    dom_count = lax.axis_size("dom")
    holders = group_count * dom_count
    dom = lax.axis_index("dom")
    group = lax.axis_index("groups")
    seq = lax.axis_index("seq")
    particles, tokens, model_width = latents.shape
    head_width = model_width // HEADS
    width = particles * model_width // seq_count
    chunks = 2 if width % (2 * LANES) == 0 else 1

    ids = jnp.stack([dom, group, seq, step_index[0]]).astype(jnp.int32)

    embed_columns = embed_weight.shape[1] // holders
    embed_share = lax.dynamic_slice_in_dim(
        embed_weight, (dom * group_count + group) * embed_columns, embed_columns, 1
    )[None]
    up_depth = up_weight.shape[0] // group_count
    up_columns = up_weight.shape[1] // dom_count
    up_share = lax.dynamic_slice(
        up_weight, (group * up_depth, dom * up_columns), (up_depth, up_columns)
    )[None]
    bits = [1 << place for place in reversed(range(1, seq_count.bit_length() - 1))]
    near = [0]
    for bit in bits[:-2]:
        embed_share = jnp.concatenate([embed_share, swapped(embed_share, "seq", bit)])
        up_share = jnp.concatenate([up_share, swapped(up_share, "seq", bit)])
        near = near + [offset ^ bit for offset in near]
    high, low = bits[-2:]

    def over_groups(array):
        return [array] + [shifted(array, "groups", k) for k in range(1, group_count)]

    packed = pack(queries, keys, values, chunks, width)
    embed_share = jnp.concatenate([embed_share, swapped(embed_share, "seq", high)])
    packed[0] = gate(packed[0], [embed_share])

    arrived = [exchange(packed[0])]
    up_high = swapped(up_share, "seq", high)
    own_pair, own_groups = swapped(up_share, "seq", 1), over_groups(up_share)
    for bit in (low, 1):
        embed_share = jnp.concatenate([embed_share, swapped(embed_share, "seq", bit)])
    after = [arrived[0], embed_share, up_high, own_pair, *own_groups[1:]]
    packed[1:] = [gate(piece, after) for piece in packed[1:]]

    arrived += [exchange(piece) for piece in packed[1:]]
    up_far = swapped(jnp.concatenate([up_share, up_high]), "seq", low)
    high_pair, high_groups = swapped(up_high, "seq", 1), over_groups(up_high)
    own_pairs = [own_pair] + [swapped(piece, "seq", 1) for piece in own_groups[1:]]
    embed_near = over_groups(embed_share)
    attended = [attention(arrived[0], head_width)]
    after = [up_far, high_pair, *high_groups[1:], *own_pairs[1:], *embed_near[1:]]
    attended[0] = gate(attended[0], [*after, *arrived[1:]])

    returned = [exchange(attended[0])]
    far_pair, far_groups = swapped(up_far, "seq", 1), over_groups(up_far)
    embed_parts = embed_near + [
        shifted(piece, "dom", k) for k in range(1, dom_count) for piece in embed_near
    ]
    attended += [attention(piece, head_width) for piece in arrived[1:]]
    after = [returned[0], *far_groups[1:], *embed_parts[group_count:]]
    attended[1:] = [gate(piece, after) for piece in attended[1:]]

    returned += [exchange(piece) for piece in attended[1:]]
    high_pairs = [high_pair] + [swapped(piece, "seq", 1) for piece in high_groups[1:]]
    far_pairs = over_groups(far_pair)
    up_parts = [own_groups, own_pairs, high_groups, high_pairs, far_groups, far_pairs]
    far = [offset ^ low for offset in near + [offset ^ high for offset in near]]
    up_offsets = [
        [offset ^ bit for offset in offsets]
        for offsets in (near, [offset ^ high for offset in near], far)
        for bit in (0, 1)
    ]
    embed_offsets = near + [offset ^ high for offset in near]
    for bit in (low, 1):
        embed_offsets = embed_offsets + [offset ^ bit for offset in embed_offsets]

    begun = first_project(latents, out_weight, returned.pop(0), chunks, width) if chunks > 1 else None
    stepped, features = project_embed(
        ids,
        embed_offsets,
        latents,
        begun,
        returned,
        chunks,
        width,
        out_weight,
        embed_parts,
        norm_gain,
        group_count,
        [*high_pairs[1:], *far_pairs],
    )
    stepped_other = shifted(stepped, "dom", 1)
    features_other = shifted(features, "dom", 1)

    scale = potential_scale / math.sqrt(tokens * seq_count)
    head = head_weight.reshape(seq_count * dom_count, 1, up_columns)
    score = functools.partial(
        reward,
        ids,
        weights=[piece for pieces in up_parts for piece in pieces],
        parts=group_count,
        doms=dom_count,
        offsets=[offset for offsets in up_offsets for offset in offsets],
        head=head,
        particles=particles,
        scale=scale,
    )
    partial_own = score(features, before=prev_logw)
    partial = score(features_other, before=partial_own)
    partial = add_parts(
        [partial] + [swapped(partial, "seq", 2 * k) for k in range(1, seq_count // 2)]
    )
    pair = [
        (d * seq_count + i, (d + k) % dom_count * seq_count + (i ^ 1))
        for k in range(1, dom_count)
        for d in range(dom_count)
        for i in range(seq_count)
    ]
    logits = [partial, swapped(partial, "seq", 1), lax.ppermute(partial, ("dom", "seq"), pair)] + [
        shifted(partial, "dom", k) for k in range(1, dom_count)
    ]
    resampled = resample(ids, ancestors.astype(jnp.int32), stepped, stepped_other)
    return finish(ids, logits, resampled, particles, dom_count)


def solution(mesh):
    in_specs = (
        P(("groups", "dom"), "seq", None),
        P(("groups", "dom"), "seq", None),
        P(("groups", "dom"), "seq", None),
        P(("groups", "dom"), "seq", None),
        P(),
        P("groups"),
        P("seq", None),
        P(),
        P(None, "seq"),
        P(),
        P(("groups", "dom")),
        P(("groups", "dom")),
    )
    out_specs = (P(("groups", "dom"), "seq", None), P(("groups", "dom")))
    return jax.shard_map(
        on_device, mesh=mesh, in_specs=in_specs, out_specs=out_specs, check_vma=False
    )
```

```python
import functools
import math

import jax
import jax.numpy as jnp
from jax import lax
from jax.experimental import pallas as pl
from jax.experimental.pallas import tpu as pltpu
from jax.sharding import PartitionSpec as P

HEADS = 24
STEPS = 28
LANES = 128

potential_scale = 4.0
norm_eps = 1e-05
MIB = 1024 * 1024


def pack_kernel(splits, width, q_ref, k_ref, v_ref, *out_refs):
    particles, _, model_width = q_ref.shape
    blocks = model_width // width
    for index, ref in enumerate((q_ref, k_ref, v_ref)):
        for particle in range(particles):
            for block in range(blocks):
                for out_ref, (start, size) in zip(out_refs, splits):
                    first = block * width + start
                    out_ref[particle * blocks + block, index] = ref[
                        particle, :, first : first + size
                    ]


def pack(queries, keys, values, splits, width):
    particles, tokens, model_width = queries.shape
    count = particles * model_width // width
    vmem = pl.BlockSpec(memory_space=pltpu.VMEM)
    return list(
        pl.pallas_call(
            functools.partial(pack_kernel, splits, width),
            in_specs=[vmem] * 3,
            out_specs=[vmem] * len(splits),
            out_shape=[
                jax.ShapeDtypeStruct((count, 3, tokens, size), queries.dtype)
                for _, size in splits
            ],
            compiler_params=pltpu.CompilerParams(vmem_limit_bytes=60 * MIB),
            name="pack_heads",
        )(queries, keys, values)
    )


def gate_kernel(*refs):
    pass


def gate(array, after):
    hbm = pl.BlockSpec(memory_space=pltpu.HBM)
    return pl.pallas_call(
        gate_kernel,
        in_specs=[hbm] + [pl.BlockSpec(memory_space=pl.ANY)] * len(after),
        out_specs=hbm,
        out_shape=jax.ShapeDtypeStruct(array.shape, array.dtype),
        input_output_aliases={0: 0},
        compiler_params=pltpu.CompilerParams(vmem_limit_bytes=60 * MIB),
        name="gate",
    )(array, *after)


def attention_kernel(head_width, block_sources, qkv_ref, *refs):
    out_ref = refs[-1]
    sources, _, tokens, columns = qkv_ref.shape
    total = sources * tokens
    rows = block_sources * tokens
    factor = 1.0 / math.sqrt(head_width) / math.log(2.0)
    k_all = qkv_ref[:, 1].reshape(total, columns)
    v_all = qkv_ref[:, 2].reshape(total, columns)
    for block in range(0, sources, block_sources):
        span = slice(block, block + block_sources)
        q_all = qkv_ref[span, 0].reshape(rows, columns)
        pieces = []
        for head in range(columns // head_width):
            cols = slice(head * head_width, (head + 1) * head_width)
            scores = lax.dot_general(
                q_all[:, cols],
                k_all[:, cols],
                (((1,), (1,)), ((), ())),
                preferred_element_type=jnp.float32,
            )
            highest = jnp.max(scores, axis=1, keepdims=True)
            expanded = jnp.exp2((scores - highest) * factor)
            norm = 1.0 / jnp.sum(expanded, axis=1, keepdims=True)
            weights = (expanded * norm).astype(jnp.bfloat16)
            pieces.append(jnp.dot(weights, v_all[:, cols], preferred_element_type=jnp.float32))
        joined = jnp.concatenate(pieces, axis=1).astype(jnp.bfloat16)
        out_ref[span] = joined.reshape(block_sources, tokens, columns)


def attention(qkv, head_width, width, start, earlier, after):
    sources, _, tokens, columns = qkv.shape
    total = sources * tokens
    block_sources = max(1, min(sources, 512 // tokens))
    while sources % block_sources:
        block_sources -= 1
    step = LANES if columns % LANES == 0 and LANES % head_width == 0 else columns
    first = start // step
    unread = earlier + after
    return pl.pallas_call(
        functools.partial(attention_kernel, head_width, block_sources),
        grid=(columns // step,),
        in_specs=[pl.BlockSpec((sources, 3, tokens, step), lambda i: (0, 0, 0, i))]
        + [pl.BlockSpec(memory_space=pl.ANY)] * len(unread),
        out_specs=pl.BlockSpec((sources, tokens, step), lambda i: (0, 0, first + i)),
        out_shape=jax.ShapeDtypeStruct((sources, tokens, width), jnp.bfloat16),
        input_output_aliases={1: 0} if earlier else {},
        compiler_params=pltpu.CompilerParams(vmem_limit_bytes=60 * MIB),
        cost_estimate=pl.CostEstimate(
            flops=4 * total * total * columns,
            bytes_accessed=8 * total * columns,
            transcendentals=columns // head_width * total * total,
        ),
        name="attention",
    )(qkv, *unread)


def column_block(model_width):
    return 512 if model_width % 512 == 0 else model_width


def project_kernel(parts, offsets, depth_parts, refs_in, refs_out):
    ids_ref, latents_hbm, gain_ref, out_weight_ref, attended_ref = refs_in[:5]
    weight_refs = refs_in[5 : 5 + parts]
    stepped_ref, features_ref = refs_out[:2]
    out_vmem, weight_vmem, rows_ref, clean_ref, embedded_ref, latents_ref = refs_out[2:8]
    out_sems, sems = refs_out[8:]
    dom, group, seq = ids_ref[0], ids_ref[1], ids_ref[2]
    sigma = ids_ref[3].astype(jnp.float32) * (1.0 / STEPS)
    particles, tokens, model_width = latents_ref.shape
    rows = particles * tokens
    shards, depth, columns = weight_refs[0].shape

    block = column_block(model_width)
    first_copies = []
    for index in range(model_width // block):
        cols = slice(index * block, (index + 1) * block)
        first_copies += [
            pltpu.make_async_copy(
                out_weight_ref.at[:, cols], out_vmem.at[:, cols], out_sems.at[0, index]
            ),
            pltpu.make_async_copy(
                latents_hbm.at[:, :, cols], latents_ref.at[:, :, cols], out_sems.at[1, index]
            ),
        ]
    copies = []
    for index in range(parts):
        for shard in range(shards):
            start = pl.multiple_of((seq ^ offsets[shard]) * depth, depth)
            copies.append(
                pltpu.make_async_copy(
                    weight_refs[index].at[shard],
                    weight_vmem.at[index, pl.ds(start, depth)],
                    sems.at[index],
                )
            )
    for copy in first_copies + copies:
        copy.start()

    count, _, width = attended_ref.shape
    blocks = count // particles
    for piece in range(count):
        particle, place = divmod(piece, blocks)
        rows_ref[
            particle * tokens : (particle + 1) * tokens, place * width : (place + 1) * width
        ] = attended_ref[piece]
    for index in range(model_width // block):
        cols = slice(index * block, (index + 1) * block)
        for copy in first_copies[2 * index : 2 * index + 2]:
            copy.wait()
        flat = latents_ref[:, :, cols].reshape(rows, block).astype(jnp.float32)
        velocity = flat + jnp.dot(
            rows_ref[...], out_vmem[:, cols], preferred_element_type=jnp.float32
        )
        clean_ref[:, cols] = (flat - sigma * velocity).astype(jnp.bfloat16)
        stepped_ref[:, :, cols] = (
            (flat - velocity * (1.0 / STEPS)).astype(jnp.bfloat16).reshape(particles, tokens, block)
        )

    for index in range(parts):
        for copy in copies[index * shards : (index + 1) * shards]:
            copy.wait()
        doms = parts // depth_parts
        dom_of = (dom + doms - index // depth_parts) % doms
        group_of = (group + depth_parts - index % depth_parts) % depth_parts
        embedded_ref[dom_of * depth_parts + group_of] = jnp.dot(
            clean_ref[...], weight_vmem[index], preferred_element_type=jnp.float32
        )
    count = parts * columns
    blocks = [embedded_ref[index] for index in range(parts)]
    centre = sum(jnp.sum(piece, axis=1, keepdims=True) for piece in blocks) * (1.0 / count)
    blocks = [piece - centre for piece in blocks]
    variance = sum(jnp.sum(piece * piece, axis=1, keepdims=True) for piece in blocks) * (
        1.0 / count
    )
    inverse = lax.rsqrt(variance + norm_eps)
    share = features_ref.shape[2]
    for index, piece in enumerate(blocks):
        cols = slice(index * columns, (index + 1) * columns)
        feature = jax.nn.gelu(piece * inverse * gain_ref[:, cols]).astype(jnp.bfloat16)
        start = index * columns % share
        features_ref[index * columns // share, :, start : start + columns] = feature


def project_embed(
    ids, offsets, latents, attended, out_weight, weights, gain, depth_parts, after
):
    particles, tokens, model_width = latents.shape
    rows = particles * tokens
    parts = len(weights)
    columns = weights[0].shape[2]
    count = parts * columns
    groups = model_width // column_block(model_width)
    vmem = pl.BlockSpec(memory_space=pltpu.VMEM)
    hbm = pl.BlockSpec(memory_space=pltpu.HBM)
    inputs = 5 + parts + len(after)

    def kernel(*refs):
        project_kernel(parts, offsets, depth_parts, refs[:inputs], refs[inputs:])

    return pl.pallas_call(
        kernel,
        in_specs=[pl.BlockSpec(memory_space=pltpu.SMEM), hbm, vmem, hbm, vmem]
        + [hbm] * parts
        + [pl.BlockSpec(memory_space=pl.ANY)] * len(after),
        out_specs=[vmem, vmem],
        out_shape=[
            jax.ShapeDtypeStruct(latents.shape, jnp.bfloat16),
            jax.ShapeDtypeStruct((depth_parts, rows, count // depth_parts), jnp.bfloat16),
        ],
        scratch_shapes=[
            pltpu.VMEM((model_width, model_width), jnp.bfloat16),
            pltpu.VMEM((parts, model_width, columns), jnp.bfloat16),
            pltpu.VMEM((rows, model_width), jnp.bfloat16),
            pltpu.VMEM((rows, model_width), jnp.bfloat16),
            pltpu.VMEM((parts, rows, columns), jnp.float32),
            pltpu.VMEM(latents.shape, latents.dtype),
            pltpu.SemaphoreType.DMA((2, groups)),
            pltpu.SemaphoreType.DMA((parts,)),
        ],
        compiler_params=pltpu.CompilerParams(vmem_limit_bytes=60 * MIB),
        cost_estimate=pl.CostEstimate(
            flops=2 * rows * model_width * (model_width + count),
            bytes_accessed=2 * model_width * (model_width + count) + 8 * rows * model_width,
            transcendentals=rows * count,
        ),
        name="project_embed",
    )(ids, latents, gain.reshape(1, count), out_weight, attended, *weights, *after)


def reward_kernel(particles, scale, parts, doms, offsets, joined, *refs):
    ids_ref, features_ref, head_ref, before_ref = refs[:4]
    weight_refs, (out_ref, weight_vmem, rows_ref, sems) = refs[4:-4], refs[-4:]
    dom, group, seq = ids_ref[0], ids_ref[1], ids_ref[2]
    _, depth, columns = weight_refs[0].shape
    rows = features_ref.shape[1]
    places = [
        (pair, shard)
        for pair in range(len(weight_refs) // parts)
        for shard in range(weight_refs[pair * parts].shape[0])
    ]
    count = len(places)

    copies = []
    for place, (pair, shard) in enumerate(places):
        lane = place % joined * columns
        for index in range(parts):
            copy = pltpu.make_async_copy(
                weight_refs[pair * parts + index].at[shard],
                weight_vmem.at[
                    place // joined,
                    index * depth : (index + 1) * depth,
                    lane : lane + columns,
                ],
                sems.at[place, index],
            )
            copy.start()
            copies.append(copy)
    for index in range(parts):
        rows_ref[:, index * depth : (index + 1) * depth] = features_ref[
            (group + parts - index) % parts
        ]
    totals = jnp.zeros((particles, joined * columns), jnp.float32)
    for step in range(count // joined):
        for copy in copies[step * joined * parts : (step + 1) * joined * parts]:
            copy.wait()
        hidden = jnp.dot(rows_ref[...], weight_vmem[step], preferred_element_type=jnp.float32)
        head = jnp.concatenate(
            [
                head_ref[(seq ^ offset) * doms + dom]
                for offset in offsets[step * joined : (step + 1) * joined]
            ],
            axis=1,
        )
        scored = jax.nn.gelu(hidden) * head
        totals += jnp.sum(scored.reshape(particles, rows // particles, -1), axis=1)

    sums = jnp.sum(totals, axis=1, keepdims=True) * scale
    first = len(before_ref.shape) == 1
    shape = out_ref.shape[-2:]
    out_rows = lax.broadcasted_iota(jnp.int32, shape, 0)
    lanes = lax.broadcasted_iota(jnp.int32, shape, 1)
    logits = jnp.zeros(shape, jnp.float32) if first else before_ref[...]
    row = dom if first else (dom + 1) % doms
    for particle in range(particles):
        here = jnp.logical_and(out_rows == row, lanes == particle)
        value = sums[particle : particle + 1]
        if first:
            value = value + jnp.where(seq == 0, before_ref[particle], 0.0)
        logits += jnp.where(here, value, 0.0)
    out_ref[...] = jnp.broadcast_to(logits, out_ref.shape)


def reward(ids, features, weights, parts, doms, offsets, head, before, particles, scale, copies):
    _, depth, columns = weights[0].shape
    rows = features.shape[1]
    count = len(offsets)
    joined = 2 if columns % LANES == 0 and count % 2 == 0 else 1
    smem = pl.BlockSpec(memory_space=pltpu.SMEM)
    vmem = pl.BlockSpec(memory_space=pltpu.VMEM)
    return pl.pallas_call(
        functools.partial(reward_kernel, particles, scale, parts, doms, offsets, joined),
        in_specs=[smem, vmem, vmem, smem if before.ndim == 1 else vmem]
        + [pl.BlockSpec(memory_space=pltpu.HBM)] * len(weights),
        out_specs=vmem,
        out_shape=jax.ShapeDtypeStruct((*copies, 8, LANES), jnp.float32),
        scratch_shapes=[
            pltpu.VMEM((count // joined, parts * depth, joined * columns), jnp.bfloat16),
            pltpu.VMEM((rows, parts * depth), jnp.bfloat16),
            pltpu.SemaphoreType.DMA((count, parts)),
        ],
        compiler_params=pltpu.CompilerParams(vmem_limit_bytes=60 * MIB),
        cost_estimate=pl.CostEstimate(
            flops=2 * rows * parts * depth * count * columns,
            bytes_accessed=2 * parts * depth * count * columns,
            transcendentals=rows * count * columns,
        ),
        name="reward",
    )(ids, features, head, before, *weights)


def finish_kernel(particles, doms, ids_ref, resampled_ref, parts_ref, out_ref, same_ref):
    logits = jnp.sum(parts_ref[...], axis=0)
    rows = lax.broadcasted_iota(jnp.int32, logits.shape, 0)
    lanes = lax.broadcasted_iota(jnp.int32, logits.shape, 1)
    valid = jnp.logical_and(rows < doms, lanes < particles)
    highest = jnp.max(jnp.where(valid, logits, -jnp.inf))
    total = jnp.sum(jnp.where(valid, jnp.exp(logits - highest), 0.0), axis=1, keepdims=True)
    log_total = highest + jnp.log(jnp.sum(total, axis=0, keepdims=True))
    own = jnp.sum(jnp.where(rows == ids_ref[0], logits, 0.0), axis=0, keepdims=True)
    out_ref[...] = (own - log_total)[:, :particles]


def finish(ids, parts, resampled, particles, doms):
    vmem = pl.BlockSpec(memory_space=pltpu.VMEM)
    anywhere = pl.BlockSpec(memory_space=pl.ANY)
    log_weights, resampled = pl.pallas_call(
        functools.partial(finish_kernel, particles, doms),
        in_specs=[pl.BlockSpec(memory_space=pltpu.SMEM), anywhere, vmem],
        out_specs=[vmem, anywhere],
        out_shape=[
            jax.ShapeDtypeStruct((1, particles), jnp.float32),
            jax.ShapeDtypeStruct(resampled.shape, resampled.dtype),
        ],
        input_output_aliases={1: 1},
        compiler_params=pltpu.CompilerParams(vmem_limit_bytes=2 * MIB),
        name="log_weights",
    )(ids, resampled, parts)
    return resampled, log_weights.reshape(particles)


def resample_kernel(ids_ref, ancestors_ref, own_ref, other_ref, out_ref):
    index = pl.program_id(0)
    own = ancestors_ref[index] // pl.num_programs(0) == ids_ref[0]

    @pl.when(own)
    def _():
        out_ref[...] = own_ref[...]

    @pl.when(jnp.logical_not(own))
    def _():
        out_ref[...] = other_ref[...]


def resample(ids, ancestors, own, other):
    particles, tokens, columns = own.shape
    block = (1, tokens, columns)
    parent = pl.BlockSpec(block, lambda i, ids, ancestors: (ancestors[i] % particles, 0, 0))
    return pl.pallas_call(
        resample_kernel,
        grid_spec=pltpu.PrefetchScalarGridSpec(
            num_scalar_prefetch=2,
            grid=(particles,),
            in_specs=[parent, parent],
            out_specs=pl.BlockSpec(block, lambda i, ids, ancestors: (i, 0, 0)),
        ),
        out_shape=jax.ShapeDtypeStruct(own.shape, own.dtype),
        compiler_params=pltpu.CompilerParams(vmem_limit_bytes=4 * MIB),
        name="resample",
    )(ids, ancestors, own, other)


def shifted(array, axis, step):
    count = lax.axis_size(axis)
    return lax.ppermute(array, axis, [(i, (i + step) % count) for i in range(count)])


def swapped(array, axis, bit):
    return lax.ppermute(array, axis, [(i, i ^ bit) for i in range(lax.axis_size(axis))])


def exchange(array):
    return lax.all_to_all(array, "seq", 0, 0, tiled=True)


def on_device(
    latents,
    queries,
    keys,
    values,
    out_weight,
    step_index,
    embed_weight,
    norm_gain,
    up_weight,
    head_weight,
    prev_logw,
    ancestors,
):
    seq_count = lax.axis_size("seq")
    group_count = lax.axis_size("groups")
    dom_count = lax.axis_size("dom")
    holders = group_count * dom_count
    dom = lax.axis_index("dom")
    group = lax.axis_index("groups")
    seq = lax.axis_index("seq")
    particles, tokens, model_width = latents.shape
    head_width = model_width // HEADS
    width = particles * model_width // seq_count
    splits = [(0, width)]
    if width % LANES == 0 and width >= 2 * LANES:
        start = -(-2 * width // (3 * LANES)) * LANES
        splits = [(0, start), (start, width - start)]

    ids = jnp.stack([dom, group, seq, step_index[0]]).astype(jnp.int32)

    embed_columns = embed_weight.shape[1] // holders
    embed_share = lax.dynamic_slice_in_dim(
        embed_weight, (dom * group_count + group) * embed_columns, embed_columns, 1
    )[None]
    up_depth = up_weight.shape[0] // group_count
    up_columns = up_weight.shape[1] // dom_count
    up_share = lax.dynamic_slice(
        up_weight, (group * up_depth, dom * up_columns), (up_depth, up_columns)
    )[None]
    bits = [1 << place for place in reversed(range(1, seq_count.bit_length() - 1))]
    near = [0]
    for bit in bits[:-2]:
        embed_share = jnp.concatenate([embed_share, swapped(embed_share, "seq", bit)])
        up_share = jnp.concatenate([up_share, swapped(up_share, "seq", bit)])
        near = near + [offset ^ bit for offset in near]
    high, low = bits[-2:]

    def over_groups(array):
        return [array] + [shifted(array, "groups", k) for k in range(1, group_count)]

    packed = pack(queries, keys, values, splits, width)
    embed_share = jnp.concatenate([embed_share, swapped(embed_share, "seq", high)])
    packed[0] = gate(packed[0], [embed_share])

    arrived = [exchange(packed[0])]
    up_high = swapped(up_share, "seq", high)
    own_pair, own_groups = swapped(up_share, "seq", 1), over_groups(up_share)
    for bit in (low, 1):
        embed_share = jnp.concatenate([embed_share, swapped(embed_share, "seq", bit)])
    after = [arrived[0], embed_share, up_high, own_pair, *own_groups[1:]]
    packed[1:] = [gate(piece, after) for piece in packed[1:]]

    arrived += [exchange(piece) for piece in packed[1:]]
    up_far = swapped(jnp.concatenate([up_share, up_high]), "seq", low)
    high_pair, high_groups = swapped(up_high, "seq", 1), over_groups(up_high)
    own_pairs = [own_pair] + [swapped(piece, "seq", 1) for piece in own_groups[1:]]
    embed_near = over_groups(embed_share)
    after = [up_far, high_pair, *high_groups[1:], *own_pairs[1:], *embed_near[1:]]
    attended = []
    for piece, (start, _) in zip(arrived, splits):
        attended = [
            attention(piece, head_width, width, start, attended, after if attended else [])
        ]

    returned = exchange(attended[0])
    far_pair, far_groups = swapped(up_far, "seq", 1), over_groups(up_far)
    embed_parts = embed_near + [
        shifted(piece, "dom", k) for k in range(1, dom_count) for piece in embed_near
    ]
    high_pairs = [high_pair] + [swapped(piece, "seq", 1) for piece in high_groups[1:]]
    far_pairs = over_groups(far_pair)
    up_parts = [own_groups, own_pairs, high_groups, high_pairs, far_groups, far_pairs]
    far = [offset ^ low for offset in near + [offset ^ high for offset in near]]
    up_offsets = [
        [offset ^ bit for offset in offsets]
        for offsets in (near, [offset ^ high for offset in near], far)
        for bit in (0, 1)
    ]
    embed_offsets = near + [offset ^ high for offset in near]
    for bit in (low, 1):
        embed_offsets = embed_offsets + [offset ^ bit for offset in embed_offsets]

    stepped, features = project_embed(
        ids,
        embed_offsets,
        latents,
        returned,
        out_weight,
        embed_parts,
        norm_gain,
        group_count,
        [*high_pairs[1:], *far_groups[1:], *far_pairs],
    )
    stepped_other = shifted(stepped, "dom", 1)
    features_other = shifted(features, "dom", 1)

    scale = potential_scale / math.sqrt(tokens * seq_count)
    head = head_weight.reshape(seq_count * dom_count, 1, up_columns)
    score = functools.partial(
        reward,
        ids,
        weights=[piece for pieces in up_parts for piece in pieces],
        parts=group_count,
        doms=dom_count,
        offsets=[offset for offsets in up_offsets for offset in offsets],
        head=head,
        particles=particles,
        scale=scale,
    )
    partial_own = score(features, before=prev_logw, copies=())
    partial = score(features_other, before=partial_own, copies=(dom_count * seq_count,))
    logits = lax.all_to_all(partial, ("dom", "seq"), 0, 0, tiled=True)
    resampled = resample(ids, ancestors.astype(jnp.int32), stepped, stepped_other)
    return finish(ids, logits, resampled, particles, dom_count)


def solution(mesh):
    in_specs = (
        P(("groups", "dom"), "seq", None),
        P(("groups", "dom"), "seq", None),
        P(("groups", "dom"), "seq", None),
        P(("groups", "dom"), "seq", None),
        P(),
        P("groups"),
        P("seq", None),
        P(),
        P(None, "seq"),
        P(),
        P(("groups", "dom")),
        P(("groups", "dom")),
    )
    out_specs = (P(("groups", "dom"), "seq", None), P(("groups", "dom")))
    return jax.shard_map(
        on_device, mesh=mesh, in_specs=in_specs, out_specs=out_specs, check_vma=False
    )
```

```python
import functools
import math

import jax
import jax.numpy as jnp
from jax import lax
from jax.experimental import pallas as pl
from jax.experimental.pallas import tpu as pltpu
from jax.sharding import PartitionSpec as P

HEADS = 24
STEPS = 28
LANES = 128

potential_scale = 4.0
norm_eps = 1e-05
MIB = 1024 * 1024


def pack_kernel(chunks, width, q_ref, k_ref, v_ref, *out_refs):
    particles, _, model_width = q_ref.shape
    blocks = model_width // width
    part = width // chunks
    for index, ref in enumerate((q_ref, k_ref, v_ref)):
        for particle in range(particles):
            for block in range(blocks):
                for chunk in range(chunks):
                    start = block * width + chunk * part
                    out_refs[chunk][particle * blocks + block, index] = ref[
                        particle, :, start : start + part
                    ]


def pack(queries, keys, values, chunks, width):
    particles, tokens, model_width = queries.shape
    count = particles * model_width // width
    vmem = pl.BlockSpec(memory_space=pltpu.VMEM)
    shape = jax.ShapeDtypeStruct((count, 3, tokens, width // chunks), queries.dtype)
    return list(
        pl.pallas_call(
            functools.partial(pack_kernel, chunks, width),
            in_specs=[vmem] * 3,
            out_specs=[vmem] * chunks,
            out_shape=[shape] * chunks,
            compiler_params=pltpu.CompilerParams(vmem_limit_bytes=60 * MIB),
            name="pack_heads",
        )(queries, keys, values)
    )


def gate_kernel(*refs):
    pass


def gate(array, after):
    hbm = pl.BlockSpec(memory_space=pltpu.HBM)
    return pl.pallas_call(
        gate_kernel,
        in_specs=[hbm] + [pl.BlockSpec(memory_space=pl.ANY)] * len(after),
        out_specs=hbm,
        out_shape=jax.ShapeDtypeStruct(array.shape, array.dtype),
        input_output_aliases={0: 0},
        compiler_params=pltpu.CompilerParams(vmem_limit_bytes=60 * MIB),
        name="gate",
    )(array, *after)


def attention_kernel(head_width, block_sources, qkv_ref, out_ref):
    sources, _, tokens, columns = qkv_ref.shape
    total = sources * tokens
    rows = block_sources * tokens
    factor = 1.0 / math.sqrt(head_width) / math.log(2.0)
    k_all = qkv_ref[:, 1].reshape(total, columns)
    v_all = qkv_ref[:, 2].reshape(total, columns)
    for block in range(0, sources, block_sources):
        span = slice(block, block + block_sources)
        q_all = qkv_ref[span, 0].reshape(rows, columns)
        pieces = []
        for head in range(columns // head_width):
            cols = slice(head * head_width, (head + 1) * head_width)
            scores = lax.dot_general(
                q_all[:, cols],
                k_all[:, cols],
                (((1,), (1,)), ((), ())),
                preferred_element_type=jnp.float32,
            )
            highest = jnp.max(scores, axis=1, keepdims=True)
            expanded = jnp.exp2((scores - highest) * factor)
            norm = 1.0 / jnp.sum(expanded, axis=1, keepdims=True)
            weighted = jnp.dot(
                expanded.astype(jnp.bfloat16), v_all[:, cols], preferred_element_type=jnp.float32
            )
            pieces.append(weighted * norm)
        joined = jnp.concatenate(pieces, axis=1).astype(jnp.bfloat16)
        out_ref[span] = joined.reshape(block_sources, tokens, columns)


def attention(qkv, head_width):
    sources, _, tokens, columns = qkv.shape
    total = sources * tokens
    block_sources = max(1, min(sources, 512 // tokens))
    while sources % block_sources:
        block_sources -= 1
    step = LANES if columns % LANES == 0 and LANES % head_width == 0 else columns
    scores_bytes = 4 * block_sources * tokens * total
    return pl.pallas_call(
        functools.partial(attention_kernel, head_width, block_sources),
        grid=(columns // step,),
        in_specs=[pl.BlockSpec((sources, 3, tokens, step), lambda i: (0, 0, 0, i))],
        out_specs=pl.BlockSpec((sources, tokens, step), lambda i: (0, 0, i)),
        out_shape=jax.ShapeDtypeStruct((sources, tokens, columns), jnp.bfloat16),
        compiler_params=pltpu.CompilerParams(vmem_limit_bytes=60 * MIB),
        cost_estimate=pl.CostEstimate(
            flops=4 * total * total * columns,
            bytes_accessed=8 * total * columns,
            transcendentals=columns // head_width * total * total,
        ),
        name="attention",
    )(qkv)


def column_block(model_width):
    return 512 if model_width % 512 == 0 else model_width


class ProjectionWeights:
    def __init__(self, weight_ref, vmem_ref, sems, chunks, wanted, width):
        depth, model_width = weight_ref.shape
        part = width // chunks
        blocks = depth // width
        self.block = column_block(model_width)
        self.copies = []
        for group in range(model_width // self.block):
            cols = slice(group * self.block, (group + 1) * self.block)
            for index in range(blocks * len(wanted)):
                start = index // len(wanted) * width + wanted[index % len(wanted)] * part
                self.copies.append(
                    pltpu.make_async_copy(
                        weight_ref.at[start : start + part, cols],
                        vmem_ref.at[index * part : (index + 1) * part, cols],
                        sems.at[group, index],
                    )
                )
        self.per_group = blocks * len(wanted)
        for copy in self.copies:
            copy.start()

    def wait(self, group):
        for copy in self.copies[group * self.per_group : (group + 1) * self.per_group]:
            copy.wait()
        return slice(group * self.block, (group + 1) * self.block)


def gather_rows(piece_refs, rows_ref, particles):
    count, tokens, part = piece_refs[0].shape
    blocks = count // particles
    for index in range(blocks * len(piece_refs)):
        ref = piece_refs[index % len(piece_refs)]
        place = index // len(piece_refs)
        for particle in range(particles):
            rows_ref[
                particle * tokens : (particle + 1) * tokens, index * part : (index + 1) * part
            ] = ref[particle * blocks + place]


def first_project_kernel(chunks, width, latents_ref, weight_ref, piece_ref, out_ref, *scratch):
    weight_vmem, rows_ref, sems = scratch
    particles, tokens, model_width = latents_ref.shape
    weights = ProjectionWeights(weight_ref, weight_vmem, sems, chunks, [0], width)
    gather_rows([piece_ref], rows_ref, particles)
    for group in range(model_width // weights.block):
        cols = weights.wait(group)
        flat = latents_ref[:, :, cols].reshape(particles * tokens, weights.block)
        out_ref[:, cols] = flat.astype(jnp.float32) + jnp.dot(
            rows_ref[...], weight_vmem[:, cols], preferred_element_type=jnp.float32
        )


def first_project(latents, out_weight, piece, chunks, width):
    particles, tokens, model_width = latents.shape
    rows, depth = particles * tokens, model_width // chunks
    vmem = pl.BlockSpec(memory_space=pltpu.VMEM)
    return pl.pallas_call(
        functools.partial(first_project_kernel, chunks, width),
        in_specs=[vmem, pl.BlockSpec(memory_space=pltpu.HBM), vmem],
        out_specs=vmem,
        out_shape=jax.ShapeDtypeStruct((rows, model_width), jnp.float32),
        scratch_shapes=[
            pltpu.VMEM((depth, model_width), jnp.bfloat16),
            pltpu.VMEM((rows, depth), jnp.bfloat16),
            pltpu.SemaphoreType.DMA(
                (model_width // column_block(model_width), model_width // width)
            ),
        ],
        compiler_params=pltpu.CompilerParams(vmem_limit_bytes=60 * MIB),
        cost_estimate=pl.CostEstimate(
            flops=2 * rows * depth * model_width,
            bytes_accessed=2 * depth * model_width + 8 * rows * model_width,
            transcendentals=0,
        ),
        name="first_project",
    )(latents, out_weight, piece)


def project_kernel(chunks, width, pieces, parts, offsets, depth_parts, refs_in, refs_out):
    ids_ref, latents_hbm, gain_ref, out_weight_ref = refs_in[:4]
    rest, weight_refs = list(refs_in[4 : 4 + pieces]), refs_in[4 + pieces : 4 + pieces + parts]
    begun_hbm = rest.pop(0) if chunks > 1 else None
    stepped_ref, features_ref = refs_out[:2]
    out_vmem, weight_vmem, rows_ref, clean_ref, embedded_ref = refs_out[2:7]
    latents_ref, begun_ref, out_sems, sems, first_sems = refs_out[7:]
    dom, group, seq = ids_ref[0], ids_ref[1], ids_ref[2]
    sigma = ids_ref[3].astype(jnp.float32) * (1.0 / STEPS)
    particles, tokens, model_width = latents_ref.shape
    rows = particles * tokens
    shards, depth, columns = weight_refs[0].shape

    wanted = list(range(chunks - len(rest), chunks))
    block = column_block(model_width)
    first_copies = []
    for index in range(model_width // block):
        cols = slice(index * block, (index + 1) * block)
        first_copies.append(
            pltpu.make_async_copy(
                latents_hbm.at[:, :, cols], latents_ref.at[:, :, cols], first_sems.at[0, index]
            )
        )
        if chunks > 1:
            first_copies.append(
                pltpu.make_async_copy(
                    begun_hbm.at[:, cols], begun_ref.at[:, cols], first_sems.at[1, index]
                )
            )
    for copy in first_copies[: len(first_copies) // (model_width // block)]:
        copy.start()
    out_weights = ProjectionWeights(out_weight_ref, out_vmem, out_sems, chunks, wanted, width)
    for copy in first_copies[len(first_copies) // (model_width // block) :]:
        copy.start()
    copies = []
    for index in range(parts):
        for shard in range(shards):
            start = pl.multiple_of((seq ^ offsets[shard]) * depth, depth)
            copy = pltpu.make_async_copy(
                weight_refs[index].at[shard],
                weight_vmem.at[index, pl.ds(start, depth)],
                sems.at[index],
            )
            copy.start()
            copies.append(copy)

    gather_rows(rest, rows_ref, particles)
    for index in range(model_width // out_weights.block):
        cols = out_weights.wait(index)
        each = len(first_copies) // (model_width // block)
        for copy in first_copies[index * each : (index + 1) * each]:
            copy.wait()
        flat = latents_ref[:, :, cols].reshape(rows, out_weights.block).astype(jnp.float32)
        begun = begun_ref[:, cols] if chunks > 1 else flat
        velocity = begun + jnp.dot(
            rows_ref[...], out_vmem[:, cols], preferred_element_type=jnp.float32
        )
        clean_ref[:, cols] = (flat - sigma * velocity).astype(jnp.bfloat16)
        stepped_ref[:, :, cols] = (
            (flat - velocity * (1.0 / STEPS))
            .astype(jnp.bfloat16)
            .reshape(particles, tokens, out_weights.block)
        )

    for index in range(parts):
        for copy in copies[index * shards : (index + 1) * shards]:
            copy.wait()
        doms = parts // depth_parts
        dom_of = (dom + doms - index // depth_parts) % doms
        group_of = (group + depth_parts - index % depth_parts) % depth_parts
        embedded_ref[dom_of * depth_parts + group_of] = jnp.dot(
            clean_ref[...], weight_vmem[index], preferred_element_type=jnp.float32
        )
    count = parts * columns
    blocks = [embedded_ref[index] for index in range(parts)]
    centre = sum(jnp.sum(piece, axis=1, keepdims=True) for piece in blocks) * (1.0 / count)
    blocks = [piece - centre for piece in blocks]
    variance = sum(jnp.sum(piece * piece, axis=1, keepdims=True) for piece in blocks) * (
        1.0 / count
    )
    inverse = lax.rsqrt(variance + norm_eps)
    share = features_ref.shape[2]
    for index, piece in enumerate(blocks):
        cols = slice(index * columns, (index + 1) * columns)
        feature = jax.nn.gelu(piece * inverse * gain_ref[:, cols]).astype(jnp.bfloat16)
        start = index * columns % share
        features_ref[index * columns // share, :, start : start + columns] = feature


def project_embed(
    ids,
    offsets,
    latents,
    begun,
    attended,
    chunks,
    width,
    out_weight,
    weights,
    gain,
    depth_parts,
    after,
):
    particles, tokens, model_width = latents.shape
    rows = particles * tokens
    parts = len(weights)
    columns = weights[0].shape[2]
    count = parts * columns
    out_depth = model_width * len(attended) // chunks
    pieces = ([] if begun is None else [begun]) + attended
    vmem = pl.BlockSpec(memory_space=pltpu.VMEM)
    smem = pl.BlockSpec(memory_space=pltpu.SMEM)
    hbm = pl.BlockSpec(memory_space=pltpu.HBM)
    inputs = 4 + len(pieces) + parts + len(after)
    groups = model_width // column_block(model_width)

    def kernel(*refs):
        project_kernel(
            chunks,
            width,
            len(pieces),
            parts,
            offsets,
            depth_parts,
            refs[:inputs],
            refs[inputs:],
        )

    return pl.pallas_call(
        kernel,
        in_specs=[smem, hbm, vmem, hbm]
        + ([] if begun is None else [hbm])
        + [vmem] * len(attended)
        + [hbm] * parts
        + [pl.BlockSpec(memory_space=pl.ANY)] * len(after),
        out_specs=[vmem, vmem],
        out_shape=[
            jax.ShapeDtypeStruct(latents.shape, jnp.bfloat16),
            jax.ShapeDtypeStruct((depth_parts, rows, count // depth_parts), jnp.bfloat16),
        ],
        scratch_shapes=[
            pltpu.VMEM((out_depth, model_width), jnp.bfloat16),
            pltpu.VMEM((parts, model_width, columns), jnp.bfloat16),
            pltpu.VMEM((rows, out_depth), jnp.bfloat16),
            pltpu.VMEM((rows, model_width), jnp.bfloat16),
            pltpu.VMEM((parts, rows, columns), jnp.float32),
            pltpu.VMEM(latents.shape, latents.dtype),
            pltpu.VMEM((rows, model_width), jnp.float32),
            pltpu.SemaphoreType.DMA((groups, model_width // width * len(attended))),
            pltpu.SemaphoreType.DMA((parts,)),
            pltpu.SemaphoreType.DMA((2, groups)),
        ],
        compiler_params=pltpu.CompilerParams(vmem_limit_bytes=60 * MIB),
        cost_estimate=pl.CostEstimate(
            flops=2 * rows * model_width * (out_depth + count),
            bytes_accessed=2 * model_width * (out_depth + count) + 12 * rows * model_width,
            transcendentals=rows * count,
        ),
        name="project_embed",
    )(ids, latents, gain.reshape(1, count), out_weight, *pieces, *weights, *after)


def reward_kernel(particles, scale, parts, doms, offsets, joined, *refs):
    ids_ref, prev_ref, head_ref = refs[:3]
    features_refs, weight_refs = refs[3 : 3 + doms], refs[3 + doms : -4]
    out_ref, weight_vmem, rows_ref, sems = refs[-4:]
    dom, group, seq = ids_ref[0], ids_ref[1], ids_ref[2]
    _, depth, columns = weight_refs[0].shape
    rows = features_refs[0].shape[1]
    places = [
        (pair, shard)
        for pair in range(len(weight_refs) // parts)
        for shard in range(weight_refs[pair * parts].shape[0])
    ]
    count = len(places)

    copies = []
    for place, (pair, shard) in enumerate(places):
        lane = place % joined * columns
        for index in range(parts):
            copy = pltpu.make_async_copy(
                weight_refs[pair * parts + index].at[shard],
                weight_vmem.at[
                    place // joined,
                    index * depth : (index + 1) * depth,
                    lane : lane + columns,
                ],
                sems.at[place, index],
            )
            copy.start()
            copies.append(copy)
    for step, features_ref in enumerate(features_refs):
        for index in range(parts):
            rows_ref[step * rows : (step + 1) * rows, index * depth : (index + 1) * depth] = (
                features_ref[(group + parts - index) % parts]
            )
    totals = jnp.zeros((doms * particles, joined * columns), jnp.float32)
    for step in range(count // joined):
        for copy in copies[step * joined * parts : (step + 1) * joined * parts]:
            copy.wait()
        hidden = jnp.dot(rows_ref[...], weight_vmem[step], preferred_element_type=jnp.float32)
        head = jnp.concatenate(
            [
                head_ref[(seq ^ offset) * doms + dom]
                for offset in offsets[step * joined : (step + 1) * joined]
            ],
            axis=1,
        )
        scored = jax.nn.gelu(hidden) * head
        totals += jnp.sum(scored.reshape(doms * particles, rows // particles, -1), axis=1)

    sums = jnp.sum(totals, axis=1, keepdims=True) * scale
    shape = out_ref.shape[1:]
    out_rows = lax.broadcasted_iota(jnp.int32, shape, 0)
    lanes = lax.broadcasted_iota(jnp.int32, shape, 1)
    logits = jnp.zeros(shape, jnp.float32)
    for index in range(doms * particles):
        step, particle = divmod(index, particles)
        value = sums[index : index + 1]
        if step == 0:
            value = value + jnp.where(seq == 0, prev_ref[particle], 0.0)
        here = jnp.logical_and(out_rows == (dom + doms - step) % doms, lanes == particle)
        logits += jnp.where(here, value, 0.0)
    out_ref[...] = jnp.broadcast_to(logits[None], out_ref.shape)


def reward(ids, prev_logw, features, weights, parts, offsets, head, particles, scale, copies):
    _, depth, columns = weights[0].shape
    rows, doms = features[0].shape[1], len(features)
    count = len(offsets)
    joined = 2 if columns % LANES == 0 and count % 2 == 0 else 1
    smem = pl.BlockSpec(memory_space=pltpu.SMEM)
    vmem = pl.BlockSpec(memory_space=pltpu.VMEM)
    return pl.pallas_call(
        functools.partial(reward_kernel, particles, scale, parts, doms, offsets, joined),
        in_specs=[smem, smem, vmem]
        + [vmem] * doms
        + [pl.BlockSpec(memory_space=pltpu.HBM)] * len(weights),
        out_specs=vmem,
        out_shape=jax.ShapeDtypeStruct((copies, 8, LANES), jnp.float32),
        scratch_shapes=[
            pltpu.VMEM((count // joined, parts * depth, joined * columns), jnp.bfloat16),
            pltpu.VMEM((doms * rows, parts * depth), jnp.bfloat16),
            pltpu.SemaphoreType.DMA((count, parts)),
        ],
        compiler_params=pltpu.CompilerParams(vmem_limit_bytes=60 * MIB),
        cost_estimate=pl.CostEstimate(
            flops=2 * doms * rows * parts * depth * count * columns,
            bytes_accessed=2 * parts * depth * count * columns,
            transcendentals=doms * rows * count * columns,
        ),
        name="reward",
    )(ids, prev_logw, head, *features, *weights)


def finish_kernel(particles, doms, ids_ref, resampled_ref, parts_ref, out_ref, same_ref):
    logits = jnp.sum(parts_ref[...], axis=0)
    rows = lax.broadcasted_iota(jnp.int32, logits.shape, 0)
    lanes = lax.broadcasted_iota(jnp.int32, logits.shape, 1)
    valid = jnp.logical_and(rows < doms, lanes < particles)
    highest = jnp.max(jnp.where(valid, logits, -jnp.inf))
    total = jnp.sum(jnp.where(valid, jnp.exp(logits - highest), 0.0), axis=1, keepdims=True)
    log_total = highest + jnp.log(jnp.sum(total, axis=0, keepdims=True))
    own = jnp.sum(jnp.where(rows == ids_ref[0], logits, 0.0), axis=0, keepdims=True)
    out_ref[...] = (own - log_total)[:, :particles]


def finish(ids, parts, resampled, particles, doms):
    vmem = pl.BlockSpec(memory_space=pltpu.VMEM)
    anywhere = pl.BlockSpec(memory_space=pl.ANY)
    log_weights, resampled = pl.pallas_call(
        functools.partial(finish_kernel, particles, doms),
        in_specs=[pl.BlockSpec(memory_space=pltpu.SMEM), anywhere, vmem],
        out_specs=[vmem, anywhere],
        out_shape=[
            jax.ShapeDtypeStruct((1, particles), jnp.float32),
            jax.ShapeDtypeStruct(resampled.shape, resampled.dtype),
        ],
        input_output_aliases={1: 1},
        compiler_params=pltpu.CompilerParams(vmem_limit_bytes=2 * MIB),
        name="log_weights",
    )(ids, resampled, parts)
    return resampled, log_weights.reshape(particles)


def resample_kernel(ids_ref, ancestors_ref, own_ref, other_ref, out_ref):
    index = pl.program_id(0)
    own = ancestors_ref[index] // pl.num_programs(0) == ids_ref[0]

    @pl.when(own)
    def _():
        out_ref[...] = own_ref[...]

    @pl.when(jnp.logical_not(own))
    def _():
        out_ref[...] = other_ref[...]


def resample(ids, ancestors, own, other):
    particles, tokens, columns = own.shape
    block = (1, tokens, columns)
    parent = pl.BlockSpec(block, lambda i, ids, ancestors: (ancestors[i] % particles, 0, 0))
    return pl.pallas_call(
        resample_kernel,
        grid_spec=pltpu.PrefetchScalarGridSpec(
            num_scalar_prefetch=2,
            grid=(particles,),
            in_specs=[parent, parent],
            out_specs=pl.BlockSpec(block, lambda i, ids, ancestors: (i, 0, 0)),
        ),
        out_shape=jax.ShapeDtypeStruct(own.shape, own.dtype),
        compiler_params=pltpu.CompilerParams(vmem_limit_bytes=4 * MIB),
        name="resample",
    )(ids, ancestors, own, other)


def shifted(array, axis, step):
    count = lax.axis_size(axis)
    return lax.ppermute(array, axis, [(i, (i + step) % count) for i in range(count)])


def swapped(array, axis, bit):
    return lax.ppermute(array, axis, [(i, i ^ bit) for i in range(lax.axis_size(axis))])


def exchange(array):
    return lax.all_to_all(array, "seq", 0, 0, tiled=True)


def on_device(
    latents,
    queries,
    keys,
    values,
    out_weight,
    step_index,
    embed_weight,
    norm_gain,
    up_weight,
    head_weight,
    prev_logw,
    ancestors,
):
    seq_count = lax.axis_size("seq")
    group_count = lax.axis_size("groups")
    dom_count = lax.axis_size("dom")
    holders = group_count * dom_count
    dom = lax.axis_index("dom")
    group = lax.axis_index("groups")
    seq = lax.axis_index("seq")
    particles, tokens, model_width = latents.shape
    head_width = model_width // HEADS
    width = particles * model_width // seq_count
    chunks = 2 if width % (2 * LANES) == 0 else 1

    ids = jnp.stack([dom, group, seq, step_index[0]]).astype(jnp.int32)

    embed_columns = embed_weight.shape[1] // holders
    embed_share = lax.dynamic_slice_in_dim(
        embed_weight, (dom * group_count + group) * embed_columns, embed_columns, 1
    )[None]
    up_depth = up_weight.shape[0] // group_count
    up_columns = up_weight.shape[1] // dom_count
    up_share = lax.dynamic_slice(
        up_weight, (group * up_depth, dom * up_columns), (up_depth, up_columns)
    )[None]
    bits = [1 << place for place in reversed(range(1, seq_count.bit_length() - 1))]
    near = [0]
    for bit in bits[:-2]:
        embed_share = jnp.concatenate([embed_share, swapped(embed_share, "seq", bit)])
        up_share = jnp.concatenate([up_share, swapped(up_share, "seq", bit)])
        near = near + [offset ^ bit for offset in near]
    high, low = bits[-2:]

    def over_groups(array):
        return [array] + [shifted(array, "groups", k) for k in range(1, group_count)]

    packed = pack(queries, keys, values, chunks, width)
    embed_share = jnp.concatenate([embed_share, swapped(embed_share, "seq", high)])
    packed[0] = gate(packed[0], [embed_share])

    arrived = [exchange(packed[0])]
    up_high, up_low = swapped(up_share, "seq", high), swapped(up_share, "seq", low)
    own_pair, own_groups = swapped(up_share, "seq", 1), over_groups(up_share)
    for bit in (low, 1):
        embed_share = jnp.concatenate([embed_share, swapped(embed_share, "seq", bit)])
    after = [arrived[0], embed_share, up_high, up_low, own_pair, *own_groups[1:]]
    packed[1:] = [gate(piece, after) for piece in packed[1:]]

    arrived += [exchange(piece) for piece in packed[1:]]
    up_both = swapped(up_high, "seq", low)
    high_pair, high_groups = swapped(up_high, "seq", 1), over_groups(up_high)
    low_pair, low_groups = swapped(up_low, "seq", 1), over_groups(up_low)
    embed_near = over_groups(embed_share)
    attended = [attention(arrived[0], head_width)]
    after = [up_both, high_pair, low_pair, *high_groups[1:], *low_groups[1:], *embed_near[1:]]
    attended[0] = gate(attended[0], [*after, *arrived[1:]])

    returned = [exchange(attended[0])]
    both_pair, both_groups = swapped(up_both, "seq", 1), over_groups(up_both)
    high_pairs = over_groups(high_pair)
    attended += [attention(piece, head_width) for piece in arrived[1:]]
    after = [returned[0], both_pair, *both_groups[1:], *high_pairs[1:]]
    attended[1:] = [gate(piece, after) for piece in attended[1:]]

    returned += [exchange(piece) for piece in attended[1:]]
    embed_parts = embed_near + [
        shifted(piece, "dom", k) for k in range(1, dom_count) for piece in embed_near
    ]
    own_pairs, both_pairs = over_groups(own_pair), over_groups(both_pair)
    low_pairs = [low_pair] + [swapped(piece, "seq", 1) for piece in low_groups[1:]]
    up_parts = own_groups + own_pairs + high_groups + high_pairs
    up_parts += low_groups + low_pairs + both_groups + both_pairs
    up_offsets = [
        offset ^ bit ^ pair for bit in (0, high, low, high ^ low) for pair in (0, 1) for offset in near
    ]
    embed_offsets = near + [offset ^ high for offset in near]
    for bit in (low, 1):
        embed_offsets = embed_offsets + [offset ^ bit for offset in embed_offsets]

    begun = first_project(latents, out_weight, returned.pop(0), chunks, width) if chunks > 1 else None
    stepped, features = project_embed(
        ids,
        embed_offsets,
        latents,
        begun,
        returned,
        chunks,
        width,
        out_weight,
        embed_parts,
        norm_gain,
        group_count,
        [*own_pairs[1:], *low_pairs[1:], *both_pairs[1:]],
    )
    stepped_other = shifted(stepped, "dom", 1)
    features_other = shifted(features, "dom", 1)

    scale = potential_scale / math.sqrt(tokens * seq_count)
    head = head_weight.reshape(seq_count * dom_count, 1, up_columns)
    partial = reward(
        ids,
        prev_logw,
        [features, features_other],
        up_parts,
        group_count,
        up_offsets,
        head,
        particles,
        scale,
        dom_count * seq_count,
    )
    logits = lax.all_to_all(partial, ("dom", "seq"), 0, 0, tiled=True)
    resampled = resample(ids, ancestors.astype(jnp.int32), stepped, stepped_other)
    return finish(ids, logits, resampled, particles, dom_count)


def solution(mesh):
    in_specs = (
        P(("groups", "dom"), "seq", None),
        P(("groups", "dom"), "seq", None),
        P(("groups", "dom"), "seq", None),
        P(("groups", "dom"), "seq", None),
        P(),
        P("groups"),
        P("seq", None),
        P(),
        P(None, "seq"),
        P(),
        P(("groups", "dom")),
        P(("groups", "dom")),
    )
    out_specs = (P(("groups", "dom"), "seq", None), P(("groups", "dom")))
    return jax.shard_map(
        on_device, mesh=mesh, in_specs=in_specs, out_specs=out_specs, check_vma=False
    )
```

```python
import functools
import math

import jax
import jax.numpy as jnp
from jax import lax
from jax.experimental import pallas as pl
from jax.experimental.pallas import tpu as pltpu
from jax.sharding import PartitionSpec as P

HEADS = 24
STEPS = 28
LANES = 128

potential_scale = 4.0
norm_eps = 1e-05
MIB = 1024 * 1024


def pack_kernel(chunks, width, q_ref, k_ref, v_ref, *out_refs):
    particles, _, model_width = q_ref.shape
    blocks = model_width // width
    part = width // chunks
    for index, ref in enumerate((q_ref, k_ref, v_ref)):
        for particle in range(particles):
            for block in range(blocks):
                for chunk in range(chunks):
                    start = block * width + chunk * part
                    out_refs[chunk][particle * blocks + block, index] = ref[
                        particle, :, start : start + part
                    ]


def pack(queries, keys, values, chunks, width):
    particles, tokens, model_width = queries.shape
    count = particles * model_width // width
    vmem = pl.BlockSpec(memory_space=pltpu.VMEM)
    shape = jax.ShapeDtypeStruct((count, 3, tokens, width // chunks), queries.dtype)
    return list(
        pl.pallas_call(
            functools.partial(pack_kernel, chunks, width),
            in_specs=[vmem] * 3,
            out_specs=[vmem] * chunks,
            out_shape=[shape] * chunks,
            compiler_params=pltpu.CompilerParams(vmem_limit_bytes=60 * MIB),
            name="pack_heads",
        )(queries, keys, values)
    )


def gate_kernel(*refs):
    pass


def gate(array, after):
    hbm = pl.BlockSpec(memory_space=pltpu.HBM)
    return pl.pallas_call(
        gate_kernel,
        in_specs=[hbm] + [pl.BlockSpec(memory_space=pl.ANY)] * len(after),
        out_specs=hbm,
        out_shape=jax.ShapeDtypeStruct(array.shape, array.dtype),
        input_output_aliases={0: 0},
        compiler_params=pltpu.CompilerParams(vmem_limit_bytes=60 * MIB),
        name="gate",
    )(array, *after)


def attention_kernel(head_width, block_sources, qkv_ref, out_ref):
    sources, _, tokens, columns = qkv_ref.shape
    total = sources * tokens
    rows = block_sources * tokens
    factor = 1.0 / math.sqrt(head_width) / math.log(2.0)
    k_all = qkv_ref[:, 1].reshape(total, columns)
    v_all = qkv_ref[:, 2].reshape(total, columns)
    for block in range(0, sources, block_sources):
        span = slice(block, block + block_sources)
        q_all = qkv_ref[span, 0].reshape(rows, columns)
        pieces = []
        for head in range(columns // head_width):
            cols = slice(head * head_width, (head + 1) * head_width)
            scores = lax.dot_general(
                q_all[:, cols],
                k_all[:, cols],
                (((1,), (1,)), ((), ())),
                preferred_element_type=jnp.float32,
            )
            highest = jnp.max(scores, axis=1, keepdims=True)
            expanded = jnp.exp2((scores - highest) * factor)
            norm = 1.0 / jnp.sum(expanded, axis=1, keepdims=True)
            weights = (expanded * norm).astype(jnp.bfloat16)
            pieces.append(jnp.dot(weights, v_all[:, cols], preferred_element_type=jnp.float32))
        joined = jnp.concatenate(pieces, axis=1).astype(jnp.bfloat16)
        out_ref[span] = joined.reshape(block_sources, tokens, columns)


def attention(qkv, head_width):
    sources, _, tokens, columns = qkv.shape
    total = sources * tokens
    block_sources = max(1, min(sources, 512 // tokens))
    while sources % block_sources:
        block_sources -= 1
    step = LANES if columns % LANES == 0 and LANES % head_width == 0 else columns
    scores_bytes = 4 * block_sources * tokens * total
    return pl.pallas_call(
        functools.partial(attention_kernel, head_width, block_sources),
        grid=(columns // step,),
        in_specs=[pl.BlockSpec((sources, 3, tokens, step), lambda i: (0, 0, 0, i))],
        out_specs=pl.BlockSpec((sources, tokens, step), lambda i: (0, 0, i)),
        out_shape=jax.ShapeDtypeStruct((sources, tokens, columns), jnp.bfloat16),
        compiler_params=pltpu.CompilerParams(vmem_limit_bytes=60 * MIB),
        cost_estimate=pl.CostEstimate(
            flops=4 * total * total * columns,
            bytes_accessed=8 * total * columns,
            transcendentals=columns // head_width * total * total,
        ),
        name="attention",
    )(qkv)


def column_block(model_width):
    return 512 if model_width % 512 == 0 else model_width


class ProjectionWeights:
    def __init__(self, weight_ref, vmem_ref, sems, chunks, wanted, width):
        depth, model_width = weight_ref.shape
        part = width // chunks
        blocks = depth // width
        self.block = column_block(model_width)
        self.copies = []
        for group in range(model_width // self.block):
            cols = slice(group * self.block, (group + 1) * self.block)
            for index in range(blocks * len(wanted)):
                start = index // len(wanted) * width + wanted[index % len(wanted)] * part
                self.copies.append(
                    pltpu.make_async_copy(
                        weight_ref.at[start : start + part, cols],
                        vmem_ref.at[index * part : (index + 1) * part, cols],
                        sems.at[group, index],
                    )
                )
        self.per_group = blocks * len(wanted)
        for copy in self.copies:
            copy.start()

    def wait(self, group):
        for copy in self.copies[group * self.per_group : (group + 1) * self.per_group]:
            copy.wait()
        return slice(group * self.block, (group + 1) * self.block)


def gather_rows(piece_refs, rows_ref, particles):
    count, tokens, part = piece_refs[0].shape
    blocks = count // particles
    for index in range(blocks * len(piece_refs)):
        ref = piece_refs[index % len(piece_refs)]
        place = index // len(piece_refs)
        for particle in range(particles):
            rows_ref[
                particle * tokens : (particle + 1) * tokens, index * part : (index + 1) * part
            ] = ref[particle * blocks + place]


def first_project_kernel(chunks, width, latents_ref, weight_ref, piece_ref, out_ref, *scratch):
    weight_vmem, rows_ref, sems = scratch
    particles, tokens, model_width = latents_ref.shape
    weights = ProjectionWeights(weight_ref, weight_vmem, sems, chunks, [0], width)
    gather_rows([piece_ref], rows_ref, particles)
    for group in range(model_width // weights.block):
        cols = weights.wait(group)
        flat = latents_ref[:, :, cols].reshape(particles * tokens, weights.block)
        out_ref[:, cols] = flat.astype(jnp.float32) + jnp.dot(
            rows_ref[...], weight_vmem[:, cols], preferred_element_type=jnp.float32
        )


def first_project(latents, out_weight, piece, chunks, width):
    particles, tokens, model_width = latents.shape
    rows, depth = particles * tokens, model_width // chunks
    vmem = pl.BlockSpec(memory_space=pltpu.VMEM)
    return pl.pallas_call(
        functools.partial(first_project_kernel, chunks, width),
        in_specs=[vmem, pl.BlockSpec(memory_space=pltpu.HBM), vmem],
        out_specs=vmem,
        out_shape=jax.ShapeDtypeStruct((rows, model_width), jnp.float32),
        scratch_shapes=[
            pltpu.VMEM((depth, model_width), jnp.bfloat16),
            pltpu.VMEM((rows, depth), jnp.bfloat16),
            pltpu.SemaphoreType.DMA(
                (model_width // column_block(model_width), model_width // width)
            ),
        ],
        compiler_params=pltpu.CompilerParams(vmem_limit_bytes=60 * MIB),
        cost_estimate=pl.CostEstimate(
            flops=2 * rows * depth * model_width,
            bytes_accessed=2 * depth * model_width + 8 * rows * model_width,
            transcendentals=0,
        ),
        name="first_project",
    )(latents, out_weight, piece)


def project_kernel(chunks, width, parts, offsets, depth_parts, refs_in, refs_out):
    ids_ref, latents_hbm, gain_ref, out_weight_ref, piece_ref = refs_in[:5]
    weight_refs = refs_in[5 : 5 + parts]
    begun_hbm = refs_in[5 + parts] if chunks > 1 else None
    stepped_hbm, features_ref = refs_out[:2]
    out_vmem, weight_vmem, rows_ref, clean_ref, embedded_ref = refs_out[2:7]
    latents_ref, begun_ref, stepped_ref, piece_vmem = refs_out[7:11]
    out_sems, sems, first_sems, rows_sem = refs_out[11:]
    dom, group, seq = ids_ref[0], ids_ref[1], ids_ref[2]
    sigma = ids_ref[3].astype(jnp.float32) * (1.0 / STEPS)
    particles, tokens, model_width = latents_ref.shape
    rows = particles * tokens
    shards, depth, columns = weight_refs[0].shape

    count, _, part = piece_ref.shape
    blocks = count // particles
    row_copies, slots = [], []
    for piece in range(count):
        particle, place = divmod(piece, blocks)
        slots.append(
            (
                slice(particle * tokens, (particle + 1) * tokens),
                slice(place * part, (place + 1) * part),
            )
        )
        to = rows_ref.at[slots[-1]] if part % LANES == 0 else piece_vmem.at[piece]
        row_copies.append(pltpu.make_async_copy(piece_ref.at[piece], to, rows_sem.at[piece]))
    block = column_block(model_width)
    groups = [slice(i * block, (i + 1) * block) for i in range(model_width // block)]
    group_copies = []
    for index, cols in enumerate(groups):
        begins = [(latents_hbm.at[:, :, cols], latents_ref.at[:, :, cols], 0)]
        if chunks > 1:
            begins.append((begun_hbm.at[:, cols], begun_ref.at[:, cols], 1))
        own = [pltpu.make_async_copy(a, b, first_sems.at[i, index]) for a, b, i in begins]
        for place in range(blocks):
            start = place * width + (chunks - 1) * part
            own.append(
                pltpu.make_async_copy(
                    out_weight_ref.at[start : start + part, cols],
                    out_vmem.at[place * part : (place + 1) * part, cols],
                    out_sems.at[index, place],
                )
            )
        group_copies.append(own)
    copies = []
    for index in range(parts):
        for shard in range(shards):
            start = pl.multiple_of((seq ^ offsets[shard]) * depth, depth)
            copies.append(
                pltpu.make_async_copy(
                    weight_refs[index].at[shard],
                    weight_vmem.at[index, pl.ds(start, depth)],
                    sems.at[index],
                )
            )
    for copy in row_copies + [copy for own in group_copies for copy in own] + copies:
        copy.start()
    stepped_copies = [
        pltpu.make_async_copy(
            stepped_ref.at[:, :, cols], stepped_hbm.at[:, :, cols], first_sems.at[2, index]
        )
        for index, cols in enumerate(groups)
    ]
    for copy in row_copies:
        copy.wait()
    if part % LANES:
        for piece, slot in enumerate(slots):
            rows_ref[slot] = piece_vmem[piece]
    for index, cols in enumerate(groups):
        for copy in group_copies[index]:
            copy.wait()
        flat = latents_ref[:, :, cols].reshape(rows, block).astype(jnp.float32)
        begun = begun_ref[:, cols] if chunks > 1 else flat
        velocity = begun + jnp.dot(
            rows_ref[...], out_vmem[:, cols], preferred_element_type=jnp.float32
        )
        clean_ref[:, cols] = (flat - sigma * velocity).astype(jnp.bfloat16)
        stepped_ref[:, :, cols] = (
            (flat - velocity * (1.0 / STEPS)).astype(jnp.bfloat16).reshape(particles, tokens, block)
        )
        stepped_copies[index].start()

    for index in range(parts):
        for copy in copies[index * shards : (index + 1) * shards]:
            copy.wait()
        doms = parts // depth_parts
        dom_of = (dom + doms - index // depth_parts) % doms
        group_of = (group + depth_parts - index % depth_parts) % depth_parts
        embedded_ref[dom_of * depth_parts + group_of] = jnp.dot(
            clean_ref[...], weight_vmem[index], preferred_element_type=jnp.float32
        )
    count = parts * columns
    blocks = [embedded_ref[index] for index in range(parts)]
    centre = sum(jnp.sum(piece, axis=1, keepdims=True) for piece in blocks) * (1.0 / count)
    blocks = [piece - centre for piece in blocks]
    variance = sum(jnp.sum(piece * piece, axis=1, keepdims=True) for piece in blocks) * (
        1.0 / count
    )
    inverse = lax.rsqrt(variance + norm_eps)
    share = features_ref.shape[2]
    for index, piece in enumerate(blocks):
        cols = slice(index * columns, (index + 1) * columns)
        feature = jax.nn.gelu(piece * inverse * gain_ref[:, cols]).astype(jnp.bfloat16)
        start = index * columns % share
        features_ref[index * columns // share, :, start : start + columns] = feature
    for copy in stepped_copies:
        copy.wait()


def project_embed(
    ids,
    offsets,
    latents,
    begun,
    piece,
    chunks,
    width,
    out_weight,
    weights,
    gain,
    depth_parts,
    after,
):
    particles, tokens, model_width = latents.shape
    rows = particles * tokens
    parts = len(weights)
    columns = weights[0].shape[2]
    count = parts * columns
    blocks = model_width // width
    out_depth = blocks * piece.shape[2]
    groups = model_width // column_block(model_width)
    vmem = pl.BlockSpec(memory_space=pltpu.VMEM)
    hbm = pl.BlockSpec(memory_space=pltpu.HBM)
    begun = [] if begun is None else [begun]
    inputs = 5 + parts + len(begun) + len(after)

    def kernel(*refs):
        project_kernel(chunks, width, parts, offsets, depth_parts, refs[:inputs], refs[inputs:])

    return pl.pallas_call(
        kernel,
        in_specs=[pl.BlockSpec(memory_space=pltpu.SMEM), hbm, vmem, hbm, hbm]
        + [hbm] * (parts + len(begun))
        + [pl.BlockSpec(memory_space=pl.ANY)] * len(after),
        out_specs=[hbm, vmem],
        out_shape=[
            jax.ShapeDtypeStruct(latents.shape, jnp.bfloat16),
            jax.ShapeDtypeStruct((depth_parts, rows, count // depth_parts), jnp.bfloat16),
        ],
        scratch_shapes=[
            pltpu.VMEM((out_depth, model_width), jnp.bfloat16),
            pltpu.VMEM((parts, model_width, columns), jnp.bfloat16),
            pltpu.VMEM((rows, out_depth), jnp.bfloat16),
            pltpu.VMEM((rows, model_width), jnp.bfloat16),
            pltpu.VMEM((parts, rows, columns), jnp.float32),
            pltpu.VMEM(latents.shape, latents.dtype),
            pltpu.VMEM((rows, model_width), jnp.float32),
            pltpu.VMEM(latents.shape, latents.dtype),
            pltpu.VMEM(piece.shape, piece.dtype),
            pltpu.SemaphoreType.DMA((groups, blocks)),
            pltpu.SemaphoreType.DMA((parts,)),
            pltpu.SemaphoreType.DMA((3, groups)),
            pltpu.SemaphoreType.DMA((piece.shape[0],)),
        ],
        compiler_params=pltpu.CompilerParams(vmem_limit_bytes=60 * MIB),
        cost_estimate=pl.CostEstimate(
            flops=2 * rows * model_width * (out_depth + count),
            bytes_accessed=2 * model_width * (out_depth + count) + 12 * rows * model_width,
            transcendentals=rows * count,
        ),
        name="project_embed",
    )(
        ids,
        latents,
        gain.reshape(1, count),
        out_weight,
        piece,
        *weights,
        *begun,
        *after,
    )


def reward_kernel(particles, scale, parts, doms, offsets, joined, *refs):
    ids_ref, prev_ref, head_ref = refs[:3]
    features_refs, weight_refs = refs[3 : 3 + doms], refs[3 + doms : -5]
    out_ref, weight_vmem, rows_ref, sems, row_sems = refs[-5:]
    dom, group, seq = ids_ref[0], ids_ref[1], ids_ref[2]
    _, depth, columns = weight_refs[0].shape
    rows = features_refs[0].shape[1]
    places = [
        (pair, shard)
        for pair in range(len(weight_refs) // parts)
        for shard in range(weight_refs[pair * parts].shape[0])
    ]
    count = len(places)

    row_copies = []
    for step, features_ref in enumerate(features_refs):
        for index in range(parts):
            copy = pltpu.make_async_copy(
                features_ref.at[(group + parts - index) % parts],
                rows_ref.at[
                    step * rows : (step + 1) * rows, index * depth : (index + 1) * depth
                ],
                row_sems.at[step, index],
            )
            copy.start()
            row_copies.append(copy)
    copies = []
    for place, (pair, shard) in enumerate(places):
        lane = place % joined * columns
        for index in range(parts):
            copy = pltpu.make_async_copy(
                weight_refs[pair * parts + index].at[shard],
                weight_vmem.at[
                    place // joined,
                    index * depth : (index + 1) * depth,
                    lane : lane + columns,
                ],
                sems.at[place, index],
            )
            copy.start()
            copies.append(copy)
    for copy in row_copies:
        copy.wait()
    totals = jnp.zeros((doms * particles, joined * columns), jnp.float32)
    for step in range(count // joined):
        for copy in copies[step * joined * parts : (step + 1) * joined * parts]:
            copy.wait()
        hidden = jnp.dot(rows_ref[...], weight_vmem[step], preferred_element_type=jnp.float32)
        head = jnp.concatenate(
            [
                head_ref[(seq ^ offset) * doms + dom]
                for offset in offsets[step * joined : (step + 1) * joined]
            ],
            axis=1,
        )
        scored = jax.nn.gelu(hidden) * head
        totals += jnp.sum(scored.reshape(doms * particles, rows // particles, -1), axis=1)

    sums = jnp.sum(totals, axis=1, keepdims=True) * scale
    shape = out_ref.shape[1:]
    out_rows = lax.broadcasted_iota(jnp.int32, shape, 0)
    lanes = lax.broadcasted_iota(jnp.int32, shape, 1)
    logits = jnp.zeros(shape, jnp.float32)
    for index in range(doms * particles):
        step, particle = divmod(index, particles)
        value = sums[index : index + 1]
        if step == 0:
            value = value + jnp.where(seq == 0, prev_ref[particle], 0.0)
        here = jnp.logical_and(out_rows == (dom + doms - step) % doms, lanes == particle)
        logits += jnp.where(here, value, 0.0)
    out_ref[...] = jnp.broadcast_to(logits[None], out_ref.shape)


def reward(ids, prev_logw, features, weights, parts, offsets, head, particles, scale, copies):
    _, depth, columns = weights[0].shape
    rows, doms = features[0].shape[1], len(features)
    count = len(offsets)
    joined = 2 if columns % LANES == 0 and count % 2 == 0 else 1
    smem = pl.BlockSpec(memory_space=pltpu.SMEM)
    vmem = pl.BlockSpec(memory_space=pltpu.VMEM)
    return pl.pallas_call(
        functools.partial(reward_kernel, particles, scale, parts, doms, offsets, joined),
        in_specs=[smem, smem, vmem]
        + [pl.BlockSpec(memory_space=pltpu.HBM)] * (doms + len(weights)),
        out_specs=vmem,
        out_shape=jax.ShapeDtypeStruct((copies, 8, LANES), jnp.float32),
        scratch_shapes=[
            pltpu.VMEM((count // joined, parts * depth, joined * columns), jnp.bfloat16),
            pltpu.VMEM((doms * rows, parts * depth), jnp.bfloat16),
            pltpu.SemaphoreType.DMA((count, parts)),
            pltpu.SemaphoreType.DMA((doms, parts)),
        ],
        compiler_params=pltpu.CompilerParams(vmem_limit_bytes=60 * MIB),
        cost_estimate=pl.CostEstimate(
            flops=2 * doms * rows * parts * depth * count * columns,
            bytes_accessed=2 * parts * depth * count * columns,
            transcendentals=doms * rows * count * columns,
        ),
        name="reward",
    )(ids, prev_logw, head, *features, *weights)


def finish_kernel(particles, doms, ids_ref, resampled_ref, parts_ref, out_ref, same_ref):
    logits = jnp.sum(parts_ref[...], axis=0)
    rows = lax.broadcasted_iota(jnp.int32, logits.shape, 0)
    lanes = lax.broadcasted_iota(jnp.int32, logits.shape, 1)
    valid = jnp.logical_and(rows < doms, lanes < particles)
    highest = jnp.max(jnp.where(valid, logits, -jnp.inf))
    total = jnp.sum(jnp.where(valid, jnp.exp(logits - highest), 0.0), axis=1, keepdims=True)
    log_total = highest + jnp.log(jnp.sum(total, axis=0, keepdims=True))
    own = jnp.sum(jnp.where(rows == ids_ref[0], logits, 0.0), axis=0, keepdims=True)
    out_ref[...] = (own - log_total)[:, :particles]


def finish(ids, parts, resampled, particles, doms):
    vmem = pl.BlockSpec(memory_space=pltpu.VMEM)
    anywhere = pl.BlockSpec(memory_space=pl.ANY)
    log_weights, resampled = pl.pallas_call(
        functools.partial(finish_kernel, particles, doms),
        in_specs=[pl.BlockSpec(memory_space=pltpu.SMEM), anywhere, vmem],
        out_specs=[vmem, anywhere],
        out_shape=[
            jax.ShapeDtypeStruct((1, particles), jnp.float32),
            jax.ShapeDtypeStruct(resampled.shape, resampled.dtype),
        ],
        input_output_aliases={1: 1},
        compiler_params=pltpu.CompilerParams(vmem_limit_bytes=2 * MIB),
        name="log_weights",
    )(ids, resampled, parts)
    return resampled, log_weights.reshape(particles)


def resample_kernel(ids_ref, ancestors_ref, own_ref, other_ref, out_ref):
    index = pl.program_id(0)
    own = ancestors_ref[index] // pl.num_programs(0) == ids_ref[0]

    @pl.when(own)
    def _():
        out_ref[...] = own_ref[...]

    @pl.when(jnp.logical_not(own))
    def _():
        out_ref[...] = other_ref[...]


def resample(ids, ancestors, own, other):
    particles, tokens, columns = own.shape
    block = (1, tokens, columns)
    parent = pl.BlockSpec(block, lambda i, ids, ancestors: (ancestors[i] % particles, 0, 0))
    return pl.pallas_call(
        resample_kernel,
        grid_spec=pltpu.PrefetchScalarGridSpec(
            num_scalar_prefetch=2,
            grid=(particles,),
            in_specs=[parent, parent],
            out_specs=pl.BlockSpec(block, lambda i, ids, ancestors: (i, 0, 0)),
        ),
        out_shape=jax.ShapeDtypeStruct(own.shape, own.dtype),
        compiler_params=pltpu.CompilerParams(vmem_limit_bytes=4 * MIB),
        name="resample",
    )(ids, ancestors, own, other)


def shifted(array, axis, step):
    count = lax.axis_size(axis)
    return lax.ppermute(array, axis, [(i, (i + step) % count) for i in range(count)])


def swapped(array, axis, bit):
    return lax.ppermute(array, axis, [(i, i ^ bit) for i in range(lax.axis_size(axis))])


def exchange(array):
    return lax.all_to_all(array, "seq", 0, 0, tiled=True)


def on_device(
    latents,
    queries,
    keys,
    values,
    out_weight,
    step_index,
    embed_weight,
    norm_gain,
    up_weight,
    head_weight,
    prev_logw,
    ancestors,
):
    seq_count = lax.axis_size("seq")
    group_count = lax.axis_size("groups")
    dom_count = lax.axis_size("dom")
    holders = group_count * dom_count
    dom = lax.axis_index("dom")
    group = lax.axis_index("groups")
    seq = lax.axis_index("seq")
    particles, tokens, model_width = latents.shape
    head_width = model_width // HEADS
    width = particles * model_width // seq_count
    chunks = 2 if width % (2 * LANES) == 0 else 1

    ids = jnp.stack([dom, group, seq, step_index[0]]).astype(jnp.int32)

    embed_columns = embed_weight.shape[1] // holders
    embed_share = lax.dynamic_slice_in_dim(
        embed_weight, (dom * group_count + group) * embed_columns, embed_columns, 1
    )[None]
    up_depth = up_weight.shape[0] // group_count
    up_columns = up_weight.shape[1] // dom_count
    up_share = lax.dynamic_slice(
        up_weight, (group * up_depth, dom * up_columns), (up_depth, up_columns)
    )[None]
    bits = [1 << place for place in reversed(range(1, seq_count.bit_length() - 1))]
    near = [0]
    for bit in bits[:-2]:
        embed_share = jnp.concatenate([embed_share, swapped(embed_share, "seq", bit)])
        up_share = jnp.concatenate([up_share, swapped(up_share, "seq", bit)])
        near = near + [offset ^ bit for offset in near]
    high, low = bits[-2:]

    def over_groups(array):
        return [array] + [shifted(array, "groups", k) for k in range(1, group_count)]

    packed = pack(queries, keys, values, chunks, width)
    embed_share = jnp.concatenate([embed_share, swapped(embed_share, "seq", high)])
    packed[0] = gate(packed[0], [embed_share])

    arrived = [exchange(packed[0])]
    up_high, up_low = swapped(up_share, "seq", high), swapped(up_share, "seq", low)
    own_pair, own_groups = swapped(up_share, "seq", 1), over_groups(up_share)
    for bit in (low, 1):
        embed_share = jnp.concatenate([embed_share, swapped(embed_share, "seq", bit)])
    after = [arrived[0], embed_share, up_high, up_low, own_pair, *own_groups[1:]]
    packed[1:] = [gate(piece, after) for piece in packed[1:]]

    arrived += [exchange(piece) for piece in packed[1:]]
    up_both = swapped(up_high, "seq", low)
    high_pair, high_groups = swapped(up_high, "seq", 1), over_groups(up_high)
    low_pair, low_groups = swapped(up_low, "seq", 1), over_groups(up_low)
    own_pairs = [own_pair] + [swapped(piece, "seq", 1) for piece in own_groups[1:]]
    embed_near = over_groups(embed_share)
    attended = [attention(arrived[0], head_width)]
    after = [up_both, high_pair, low_pair, *high_groups[1:], *low_groups[1:], *embed_near[1:]]
    attended[0] = gate(attended[0], [*after, *own_pairs[1:], *arrived[1:]])

    returned = [exchange(attended[0])]
    both_pair, both_groups = swapped(up_both, "seq", 1), over_groups(up_both)
    high_pairs = over_groups(high_pair)
    low_pairs = [low_pair] + [swapped(piece, "seq", 1) for piece in low_groups[1:]]
    attended += [attention(piece, head_width) for piece in arrived[1:]]
    after = [returned[0], both_pair, *both_groups[1:], *high_pairs[1:], *low_pairs[1:]]
    attended[1:] = [gate(piece, after) for piece in attended[1:]]

    returned += [exchange(piece) for piece in attended[1:]]
    embed_parts = embed_near + [
        shifted(piece, "dom", k) for k in range(1, dom_count) for piece in embed_near
    ]
    both_pairs = over_groups(both_pair)
    up_parts = own_groups + own_pairs + high_groups + high_pairs
    up_parts += low_groups + low_pairs + both_groups + both_pairs
    up_offsets = [
        offset ^ bit ^ pair for bit in (0, high, low, high ^ low) for pair in (0, 1) for offset in near
    ]
    embed_offsets = near + [offset ^ high for offset in near]
    for bit in (low, 1):
        embed_offsets = embed_offsets + [offset ^ bit for offset in embed_offsets]

    begun = first_project(latents, out_weight, returned.pop(0), chunks, width) if chunks > 1 else None
    stepped, features = project_embed(
        ids,
        embed_offsets,
        latents,
        begun,
        returned[0],
        chunks,
        width,
        out_weight,
        embed_parts,
        norm_gain,
        group_count,
        both_pairs[1:],
    )
    stepped_other = shifted(stepped, "dom", 1)
    features_other = shifted(features, "dom", 1)

    scale = potential_scale / math.sqrt(tokens * seq_count)
    head = head_weight.reshape(seq_count * dom_count, 1, up_columns)
    partial = reward(
        ids,
        prev_logw,
        [features, features_other],
        up_parts,
        group_count,
        up_offsets,
        head,
        particles,
        scale,
        dom_count * seq_count,
    )
    logits = lax.all_to_all(partial, ("dom", "seq"), 0, 0, tiled=True)
    resampled = resample(ids, ancestors.astype(jnp.int32), stepped, stepped_other)
    return finish(ids, logits, resampled, particles, dom_count)


def solution(mesh):
    in_specs = (
        P(("groups", "dom"), "seq", None),
        P(("groups", "dom"), "seq", None),
        P(("groups", "dom"), "seq", None),
        P(("groups", "dom"), "seq", None),
        P(),
        P("groups"),
        P("seq", None),
        P(),
        P(None, "seq"),
        P(),
        P(("groups", "dom")),
        P(("groups", "dom")),
    )
    out_specs = (P(("groups", "dom"), "seq", None), P(("groups", "dom")))
    return jax.shard_map(
        on_device, mesh=mesh, in_specs=in_specs, out_specs=out_specs, check_vma=False
    )
```

```python
import functools
import math

import jax
import jax.numpy as jnp
from jax import lax
from jax.experimental import pallas as pl
from jax.experimental.pallas import tpu as pltpu
from jax.sharding import PartitionSpec as P

HEADS = 24
STEPS = 28
LANES = 128

potential_scale = 4.0
norm_eps = 1e-05
MIB = 1024 * 1024


def pack_kernel(chunks, width, q_ref, k_ref, v_ref, *out_refs):
    particles, _, model_width = q_ref.shape
    blocks = model_width // width
    part = width // chunks
    for index, ref in enumerate((q_ref, k_ref, v_ref)):
        for particle in range(particles):
            for block in range(blocks):
                for chunk in range(chunks):
                    start = block * width + chunk * part
                    out_refs[chunk][particle * blocks + block, index] = ref[
                        particle, :, start : start + part
                    ]


def pack(queries, keys, values, chunks, width):
    particles, tokens, model_width = queries.shape
    count = particles * model_width // width
    vmem = pl.BlockSpec(memory_space=pltpu.VMEM)
    shape = jax.ShapeDtypeStruct((count, 3, tokens, width // chunks), queries.dtype)
    return list(
        pl.pallas_call(
            functools.partial(pack_kernel, chunks, width),
            in_specs=[vmem] * 3,
            out_specs=[vmem] * chunks,
            out_shape=[shape] * chunks,
            compiler_params=pltpu.CompilerParams(vmem_limit_bytes=60 * MIB),
            name="pack_heads",
        )(queries, keys, values)
    )


def gate_kernel(*refs):
    pass


def gate(array, after):
    hbm = pl.BlockSpec(memory_space=pltpu.HBM)
    return pl.pallas_call(
        gate_kernel,
        in_specs=[hbm] + [pl.BlockSpec(memory_space=pl.ANY)] * len(after),
        out_specs=hbm,
        out_shape=jax.ShapeDtypeStruct(array.shape, array.dtype),
        input_output_aliases={0: 0},
        compiler_params=pltpu.CompilerParams(vmem_limit_bytes=60 * MIB),
        name="gate",
    )(array, *after)


def attention_kernel(head_width, block_sources, qkv_ref, out_ref):
    sources, _, tokens, columns = qkv_ref.shape
    total = sources * tokens
    rows = block_sources * tokens
    factor = 1.0 / math.sqrt(head_width) / math.log(2.0)
    k_all = qkv_ref[:, 1].reshape(total, columns)
    v_all = qkv_ref[:, 2].reshape(total, columns)
    for block in range(0, sources, block_sources):
        span = slice(block, block + block_sources)
        q_all = qkv_ref[span, 0].reshape(rows, columns)
        pieces = []
        for head in range(columns // head_width):
            cols = slice(head * head_width, (head + 1) * head_width)
            scores = lax.dot_general(
                q_all[:, cols],
                k_all[:, cols],
                (((1,), (1,)), ((), ())),
                preferred_element_type=jnp.float32,
            )
            highest = jnp.max(scores, axis=1, keepdims=True)
            expanded = jnp.exp2((scores - highest) * factor)
            norm = 1.0 / jnp.sum(expanded, axis=1, keepdims=True)
            weights = (expanded * norm).astype(jnp.bfloat16)
            pieces.append(jnp.dot(weights, v_all[:, cols], preferred_element_type=jnp.float32))
        joined = jnp.concatenate(pieces, axis=1).astype(jnp.bfloat16)
        out_ref[span] = joined.reshape(block_sources, tokens, columns)


def attention(qkv, head_width):
    sources, _, tokens, columns = qkv.shape
    total = sources * tokens
    block_sources = max(1, min(sources, 512 // tokens))
    while sources % block_sources:
        block_sources -= 1
    step = LANES if columns % LANES == 0 and LANES % head_width == 0 else columns
    scores_bytes = 4 * block_sources * tokens * total
    return pl.pallas_call(
        functools.partial(attention_kernel, head_width, block_sources),
        grid=(columns // step,),
        in_specs=[pl.BlockSpec((sources, 3, tokens, step), lambda i: (0, 0, 0, i))],
        out_specs=pl.BlockSpec((sources, tokens, step), lambda i: (0, 0, i)),
        out_shape=jax.ShapeDtypeStruct((sources, tokens, columns), jnp.bfloat16),
        compiler_params=pltpu.CompilerParams(vmem_limit_bytes=8 * MIB + 6 * scores_bytes),
        cost_estimate=pl.CostEstimate(
            flops=4 * total * total * columns,
            bytes_accessed=8 * total * columns,
            transcendentals=columns // head_width * total * total,
        ),
        name="attention",
    )(qkv)


def column_block(model_width):
    return 512 if model_width % 512 == 0 else model_width


class ProjectionWeights:
    def __init__(self, weight_ref, vmem_ref, sems, chunks, wanted, width):
        depth, model_width = weight_ref.shape
        part = width // chunks
        blocks = depth // width
        self.block = column_block(model_width)
        self.copies = []
        for group in range(model_width // self.block):
            cols = slice(group * self.block, (group + 1) * self.block)
            for index in range(blocks * len(wanted)):
                start = index // len(wanted) * width + wanted[index % len(wanted)] * part
                self.copies.append(
                    pltpu.make_async_copy(
                        weight_ref.at[start : start + part, cols],
                        vmem_ref.at[index * part : (index + 1) * part, cols],
                        sems.at[group, index],
                    )
                )
        self.per_group = blocks * len(wanted)
        for copy in self.copies:
            copy.start()

    def wait(self, group):
        for copy in self.copies[group * self.per_group : (group + 1) * self.per_group]:
            copy.wait()
        return slice(group * self.block, (group + 1) * self.block)


def gather_rows(piece_refs, rows_ref, particles):
    count, tokens, part = piece_refs[0].shape
    blocks = count // particles
    for index in range(blocks * len(piece_refs)):
        ref = piece_refs[index % len(piece_refs)]
        place = index // len(piece_refs)
        for particle in range(particles):
            rows_ref[
                particle * tokens : (particle + 1) * tokens, index * part : (index + 1) * part
            ] = ref[particle * blocks + place]


def first_project_kernel(chunks, width, latents_ref, weight_ref, piece_ref, out_ref, *scratch):
    weight_vmem, rows_ref, sems = scratch
    particles, tokens, model_width = latents_ref.shape
    weights = ProjectionWeights(weight_ref, weight_vmem, sems, chunks, [0], width)
    gather_rows([piece_ref], rows_ref, particles)
    for group in range(model_width // weights.block):
        cols = weights.wait(group)
        flat = latents_ref[:, :, cols].reshape(particles * tokens, weights.block)
        out_ref[:, cols] = flat.astype(jnp.float32) + jnp.dot(
            rows_ref[...], weight_vmem[:, cols], preferred_element_type=jnp.float32
        )


def first_project(latents, out_weight, piece, chunks, width):
    particles, tokens, model_width = latents.shape
    rows, depth = particles * tokens, model_width // chunks
    vmem = pl.BlockSpec(memory_space=pltpu.VMEM)
    return pl.pallas_call(
        functools.partial(first_project_kernel, chunks, width),
        in_specs=[vmem, pl.BlockSpec(memory_space=pltpu.HBM), vmem],
        out_specs=vmem,
        out_shape=jax.ShapeDtypeStruct((rows, model_width), jnp.float32),
        scratch_shapes=[
            pltpu.VMEM((depth, model_width), jnp.bfloat16),
            pltpu.VMEM((rows, depth), jnp.bfloat16),
            pltpu.SemaphoreType.DMA(
                (model_width // column_block(model_width), model_width // width)
            ),
        ],
        compiler_params=pltpu.CompilerParams(vmem_limit_bytes=60 * MIB),
        cost_estimate=pl.CostEstimate(
            flops=2 * rows * depth * model_width,
            bytes_accessed=2 * depth * model_width + 8 * rows * model_width,
            transcendentals=0,
        ),
        name="first_project",
    )(latents, out_weight, piece)


def project_kernel(chunks, width, pieces, parts, offsets, depth_parts, refs_in, refs_out):
    ids_ref, latents_hbm, gain_ref, out_weight_ref = refs_in[:4]
    rest, weight_refs = list(refs_in[4 : 4 + pieces]), refs_in[4 + pieces : 4 + pieces + parts]
    begun_hbm = rest.pop(0) if chunks > 1 else None
    stepped_ref, features_ref = refs_out[:2]
    out_vmem, weight_vmem, rows_ref, clean_ref, embedded_ref = refs_out[2:7]
    latents_ref, begun_ref, out_sems, sems, first_sems = refs_out[7:]
    dom, group, seq = ids_ref[0], ids_ref[1], ids_ref[2]
    sigma = ids_ref[3].astype(jnp.float32) * (1.0 / STEPS)
    particles, tokens, model_width = latents_ref.shape
    rows = particles * tokens
    shards, depth, columns = weight_refs[0].shape

    wanted = list(range(chunks - len(rest), chunks))
    block = column_block(model_width)
    first_copies = []
    for index in range(model_width // block):
        cols = slice(index * block, (index + 1) * block)
        first_copies.append(
            pltpu.make_async_copy(
                latents_hbm.at[:, :, cols], latents_ref.at[:, :, cols], first_sems.at[0, index]
            )
        )
        if chunks > 1:
            first_copies.append(
                pltpu.make_async_copy(
                    begun_hbm.at[:, cols], begun_ref.at[:, cols], first_sems.at[1, index]
                )
            )
    for copy in first_copies[: len(first_copies) // (model_width // block)]:
        copy.start()
    out_weights = ProjectionWeights(out_weight_ref, out_vmem, out_sems, chunks, wanted, width)
    for copy in first_copies[len(first_copies) // (model_width // block) :]:
        copy.start()
    copies = []
    for index in range(parts):
        for shard in range(shards):
            start = pl.multiple_of((seq ^ offsets[shard]) * depth, depth)
            copy = pltpu.make_async_copy(
                weight_refs[index].at[shard],
                weight_vmem.at[index, pl.ds(start, depth)],
                sems.at[index],
            )
            copy.start()
            copies.append(copy)

    gather_rows(rest, rows_ref, particles)
    for index in range(model_width // out_weights.block):
        cols = out_weights.wait(index)
        each = len(first_copies) // (model_width // block)
        for copy in first_copies[index * each : (index + 1) * each]:
            copy.wait()
        flat = latents_ref[:, :, cols].reshape(rows, out_weights.block).astype(jnp.float32)
        begun = begun_ref[:, cols] if chunks > 1 else flat
        velocity = begun + jnp.dot(
            rows_ref[...], out_vmem[:, cols], preferred_element_type=jnp.float32
        )
        clean_ref[:, cols] = (flat - sigma * velocity).astype(jnp.bfloat16)
        stepped_ref[:, :, cols] = (
            (flat - velocity * (1.0 / STEPS))
            .astype(jnp.bfloat16)
            .reshape(particles, tokens, out_weights.block)
        )

    for index in range(parts):
        for copy in copies[index * shards : (index + 1) * shards]:
            copy.wait()
        doms = parts // depth_parts
        dom_of = (dom + doms - index // depth_parts) % doms
        group_of = (group + depth_parts - index % depth_parts) % depth_parts
        embedded_ref[dom_of * depth_parts + group_of] = jnp.dot(
            clean_ref[...], weight_vmem[index], preferred_element_type=jnp.float32
        )
    count = parts * columns
    blocks = [embedded_ref[index] for index in range(parts)]
    centre = sum(jnp.sum(piece, axis=1, keepdims=True) for piece in blocks) * (1.0 / count)
    blocks = [piece - centre for piece in blocks]
    variance = sum(jnp.sum(piece * piece, axis=1, keepdims=True) for piece in blocks) * (
        1.0 / count
    )
    inverse = lax.rsqrt(variance + norm_eps)
    share = features_ref.shape[2]
    for index, piece in enumerate(blocks):
        cols = slice(index * columns, (index + 1) * columns)
        feature = jax.nn.gelu(piece * inverse * gain_ref[:, cols]).astype(jnp.bfloat16)
        start = index * columns % share
        features_ref[index * columns // share, :, start : start + columns] = feature


def project_embed(
    ids,
    offsets,
    latents,
    begun,
    attended,
    chunks,
    width,
    out_weight,
    weights,
    gain,
    depth_parts,
    after,
):
    particles, tokens, model_width = latents.shape
    rows = particles * tokens
    parts = len(weights)
    columns = weights[0].shape[2]
    count = parts * columns
    out_depth = model_width * len(attended) // chunks
    pieces = ([] if begun is None else [begun]) + attended
    vmem = pl.BlockSpec(memory_space=pltpu.VMEM)
    smem = pl.BlockSpec(memory_space=pltpu.SMEM)
    hbm = pl.BlockSpec(memory_space=pltpu.HBM)
    inputs = 4 + len(pieces) + parts + len(after)
    groups = model_width // column_block(model_width)

    def kernel(*refs):
        project_kernel(
            chunks,
            width,
            len(pieces),
            parts,
            offsets,
            depth_parts,
            refs[:inputs],
            refs[inputs:],
        )

    return pl.pallas_call(
        kernel,
        in_specs=[smem, hbm, vmem, hbm]
        + ([] if begun is None else [hbm])
        + [vmem] * len(attended)
        + [hbm] * parts
        + [pl.BlockSpec(memory_space=pl.ANY)] * len(after),
        out_specs=[vmem, vmem],
        out_shape=[
            jax.ShapeDtypeStruct(latents.shape, jnp.bfloat16),
            jax.ShapeDtypeStruct((depth_parts, rows, count // depth_parts), jnp.bfloat16),
        ],
        scratch_shapes=[
            pltpu.VMEM((out_depth, model_width), jnp.bfloat16),
            pltpu.VMEM((parts, model_width, columns), jnp.bfloat16),
            pltpu.VMEM((rows, out_depth), jnp.bfloat16),
            pltpu.VMEM((rows, model_width), jnp.bfloat16),
            pltpu.VMEM((parts, rows, columns), jnp.float32),
            pltpu.VMEM(latents.shape, latents.dtype),
            pltpu.VMEM((rows, model_width), jnp.float32),
            pltpu.SemaphoreType.DMA((groups, model_width // width * len(attended))),
            pltpu.SemaphoreType.DMA((parts,)),
            pltpu.SemaphoreType.DMA((2, groups)),
        ],
        compiler_params=pltpu.CompilerParams(vmem_limit_bytes=60 * MIB),
        cost_estimate=pl.CostEstimate(
            flops=2 * rows * model_width * (out_depth + count),
            bytes_accessed=2 * model_width * (out_depth + count) + 12 * rows * model_width,
            transcendentals=rows * count,
        ),
        name="project_embed",
    )(ids, latents, gain.reshape(1, count), out_weight, *pieces, *weights, *after)


def reward_kernel(particles, scale, parts, doms, offsets, joined, *refs):
    ids_ref, prev_ref, head_ref = refs[:3]
    features_refs, weight_refs = refs[3 : 3 + doms], refs[3 + doms : -4]
    out_ref, weight_vmem, rows_ref, sems = refs[-4:]
    dom, group, seq = ids_ref[0], ids_ref[1], ids_ref[2]
    _, depth, columns = weight_refs[0].shape
    rows = features_refs[0].shape[1]
    places = [
        (pair, shard)
        for pair in range(len(weight_refs) // parts)
        for shard in range(weight_refs[pair * parts].shape[0])
    ]
    count = len(places)

    copies = []
    for place, (pair, shard) in enumerate(places):
        lane = place % joined * columns
        for index in range(parts):
            copy = pltpu.make_async_copy(
                weight_refs[pair * parts + index].at[shard],
                weight_vmem.at[
                    place // joined,
                    index * depth : (index + 1) * depth,
                    lane : lane + columns,
                ],
                sems.at[place, index],
            )
            copy.start()
            copies.append(copy)
    for step, features_ref in enumerate(features_refs):
        for index in range(parts):
            rows_ref[step * rows : (step + 1) * rows, index * depth : (index + 1) * depth] = (
                features_ref[(group + parts - index) % parts]
            )
    totals = jnp.zeros((doms * particles, joined * columns), jnp.float32)
    for step in range(count // joined):
        for copy in copies[step * joined * parts : (step + 1) * joined * parts]:
            copy.wait()
        hidden = jnp.dot(rows_ref[...], weight_vmem[step], preferred_element_type=jnp.float32)
        head = jnp.concatenate(
            [
                head_ref[(seq ^ offset) * doms + dom]
                for offset in offsets[step * joined : (step + 1) * joined]
            ],
            axis=1,
        )
        scored = jax.nn.gelu(hidden) * head
        totals += jnp.sum(scored.reshape(doms * particles, rows // particles, -1), axis=1)

    sums = jnp.sum(totals, axis=1, keepdims=True) * scale
    shape = out_ref.shape[1:]
    out_rows = lax.broadcasted_iota(jnp.int32, shape, 0)
    lanes = lax.broadcasted_iota(jnp.int32, shape, 1)
    logits = jnp.zeros(shape, jnp.float32)
    for index in range(doms * particles):
        step, particle = divmod(index, particles)
        value = sums[index : index + 1]
        if step == 0:
            value = value + jnp.where(seq == 0, prev_ref[particle], 0.0)
        here = jnp.logical_and(out_rows == (dom + doms - step) % doms, lanes == particle)
        logits += jnp.where(here, value, 0.0)
    out_ref[...] = jnp.broadcast_to(logits[None], out_ref.shape)


def reward(ids, prev_logw, features, weights, parts, offsets, head, particles, scale, copies):
    _, depth, columns = weights[0].shape
    rows, doms = features[0].shape[1], len(features)
    count = len(offsets)
    joined = 2 if columns % LANES == 0 and count % 2 == 0 else 1
    smem = pl.BlockSpec(memory_space=pltpu.SMEM)
    vmem = pl.BlockSpec(memory_space=pltpu.VMEM)
    return pl.pallas_call(
        functools.partial(reward_kernel, particles, scale, parts, doms, offsets, joined),
        in_specs=[smem, smem, vmem]
        + [vmem] * doms
        + [pl.BlockSpec(memory_space=pltpu.HBM)] * len(weights),
        out_specs=vmem,
        out_shape=jax.ShapeDtypeStruct((copies, 8, LANES), jnp.float32),
        scratch_shapes=[
            pltpu.VMEM((count // joined, parts * depth, joined * columns), jnp.bfloat16),
            pltpu.VMEM((doms * rows, parts * depth), jnp.bfloat16),
            pltpu.SemaphoreType.DMA((count, parts)),
        ],
        compiler_params=pltpu.CompilerParams(vmem_limit_bytes=60 * MIB),
        cost_estimate=pl.CostEstimate(
            flops=2 * doms * rows * parts * depth * count * columns,
            bytes_accessed=2 * parts * depth * count * columns,
            transcendentals=doms * rows * count * columns,
        ),
        name="reward",
    )(ids, prev_logw, head, *features, *weights)


def finish_kernel(particles, doms, ids_ref, resampled_ref, parts_ref, out_ref, same_ref):
    logits = jnp.sum(parts_ref[...], axis=0)
    rows = lax.broadcasted_iota(jnp.int32, logits.shape, 0)
    lanes = lax.broadcasted_iota(jnp.int32, logits.shape, 1)
    valid = jnp.logical_and(rows < doms, lanes < particles)
    highest = jnp.max(jnp.where(valid, logits, -jnp.inf))
    total = jnp.sum(jnp.where(valid, jnp.exp(logits - highest), 0.0), axis=1, keepdims=True)
    log_total = highest + jnp.log(jnp.sum(total, axis=0, keepdims=True))
    own = jnp.sum(jnp.where(rows == ids_ref[0], logits, 0.0), axis=0, keepdims=True)
    out_ref[...] = (own - log_total)[:, :particles]


def finish(ids, parts, resampled, particles, doms):
    vmem = pl.BlockSpec(memory_space=pltpu.VMEM)
    anywhere = pl.BlockSpec(memory_space=pl.ANY)
    log_weights, resampled = pl.pallas_call(
        functools.partial(finish_kernel, particles, doms),
        in_specs=[pl.BlockSpec(memory_space=pltpu.SMEM), anywhere, vmem],
        out_specs=[vmem, anywhere],
        out_shape=[
            jax.ShapeDtypeStruct((1, particles), jnp.float32),
            jax.ShapeDtypeStruct(resampled.shape, resampled.dtype),
        ],
        input_output_aliases={1: 1},
        compiler_params=pltpu.CompilerParams(vmem_limit_bytes=2 * MIB),
        name="log_weights",
    )(ids, resampled, parts)
    return resampled, log_weights.reshape(particles)


def resample_kernel(ids_ref, ancestors_ref, own_ref, other_ref, out_ref):
    index = pl.program_id(0)
    own = ancestors_ref[index] // pl.num_programs(0) == ids_ref[0]

    @pl.when(own)
    def _():
        out_ref[...] = own_ref[...]

    @pl.when(jnp.logical_not(own))
    def _():
        out_ref[...] = other_ref[...]


def resample(ids, ancestors, own, other):
    particles, tokens, columns = own.shape
    block = (1, tokens, columns)
    parent = pl.BlockSpec(block, lambda i, ids, ancestors: (ancestors[i] % particles, 0, 0))
    return pl.pallas_call(
        resample_kernel,
        grid_spec=pltpu.PrefetchScalarGridSpec(
            num_scalar_prefetch=2,
            grid=(particles,),
            in_specs=[parent, parent],
            out_specs=pl.BlockSpec(block, lambda i, ids, ancestors: (i, 0, 0)),
        ),
        out_shape=jax.ShapeDtypeStruct(own.shape, own.dtype),
        compiler_params=pltpu.CompilerParams(vmem_limit_bytes=4 * MIB),
        name="resample",
    )(ids, ancestors, own, other)


def shifted(array, axis, step):
    count = lax.axis_size(axis)
    return lax.ppermute(array, axis, [(i, (i + step) % count) for i in range(count)])


def swapped(array, axis, bit):
    return lax.ppermute(array, axis, [(i, i ^ bit) for i in range(lax.axis_size(axis))])


def exchange(array):
    return lax.all_to_all(array, "seq", 0, 0, tiled=True)


def on_device(
    latents,
    queries,
    keys,
    values,
    out_weight,
    step_index,
    embed_weight,
    norm_gain,
    up_weight,
    head_weight,
    prev_logw,
    ancestors,
):
    seq_count = lax.axis_size("seq")
    group_count = lax.axis_size("groups")
    dom_count = lax.axis_size("dom")
    holders = group_count * dom_count
    dom = lax.axis_index("dom")
    group = lax.axis_index("groups")
    seq = lax.axis_index("seq")
    particles, tokens, model_width = latents.shape
    head_width = model_width // HEADS
    width = particles * model_width // seq_count
    chunks = 2 if width % (2 * LANES) == 0 else 1

    ids = jnp.stack([dom, group, seq, step_index[0]]).astype(jnp.int32)

    embed_columns = embed_weight.shape[1] // holders
    embed_share = lax.dynamic_slice_in_dim(
        embed_weight, (dom * group_count + group) * embed_columns, embed_columns, 1
    )[None]
    up_depth = up_weight.shape[0] // group_count
    up_columns = up_weight.shape[1] // dom_count
    up_share = lax.dynamic_slice(
        up_weight, (group * up_depth, dom * up_columns), (up_depth, up_columns)
    )[None]
    bits = [1 << place for place in reversed(range(1, seq_count.bit_length() - 1))]
    near = [0]
    for bit in bits[:-2]:
        embed_share = jnp.concatenate([embed_share, swapped(embed_share, "seq", bit)])
        up_share = jnp.concatenate([up_share, swapped(up_share, "seq", bit)])
        near = near + [offset ^ bit for offset in near]
    high, low = bits[-2:]

    def over_groups(array):
        return [array] + [shifted(array, "groups", k) for k in range(1, group_count)]

    packed = pack(queries, keys, values, chunks, width)
    embed_share = jnp.concatenate([embed_share, swapped(embed_share, "seq", high)])
    packed[0] = gate(packed[0], [embed_share])

    arrived = [exchange(packed[0])]
    up_high, up_low = swapped(up_share, "seq", high), swapped(up_share, "seq", low)
    own_pair, own_groups = swapped(up_share, "seq", 1), over_groups(up_share)
    for bit in (low, 1):
        embed_share = jnp.concatenate([embed_share, swapped(embed_share, "seq", bit)])
    after = [embed_share, up_high, up_low, own_pair, *own_groups[1:]]
    packed[1:] = [gate(piece, after) for piece in packed[1:]]

    arrived += [exchange(piece) for piece in packed[1:]]
    up_both = swapped(up_high, "seq", low)
    up_next = jnp.concatenate([up_high, up_low])
    next_pair, next_groups = swapped(up_next, "seq", 1), over_groups(up_next)
    embed_near = over_groups(embed_share)
    attended = [attention(arrived[0], head_width)]
    after = [up_both, next_pair, *next_groups[1:], *embed_near[1:]]
    attended[0] = gate(attended[0], after)

    returned = [exchange(attended[0])]
    both_pair, both_groups = swapped(up_both, "seq", 1), over_groups(up_both)
    own_pairs = over_groups(own_pair)
    attended += [attention(piece, head_width) for piece in arrived[1:]]
    after = [both_pair, *both_groups[1:], *own_pairs[1:]]
    attended[1:] = [gate(piece, after) for piece in attended[1:]]

    returned += [exchange(piece) for piece in attended[1:]]
    embed_parts = embed_near + [
        shifted(piece, "dom", k) for k in range(1, dom_count) for piece in embed_near
    ]
    next_pairs = over_groups(next_pair)
    both_pairs = [both_pair] + [swapped(piece, "seq", 1) for piece in both_groups[1:]]
    up_parts = own_groups + own_pairs + next_groups + next_pairs + both_groups + both_pairs
    up_offsets = [
        offset ^ bit ^ pair
        for bits in ((0,), (high, low), (high ^ low,))
        for pair in (0, 1)
        for bit in bits
        for offset in near
    ]
    embed_offsets = near + [offset ^ high for offset in near]
    for bit in (low, 1):
        embed_offsets = embed_offsets + [offset ^ bit for offset in embed_offsets]

    begun = first_project(latents, out_weight, returned.pop(0), chunks, width) if chunks > 1 else None
    stepped, features = project_embed(
        ids,
        embed_offsets,
        latents,
        begun,
        returned,
        chunks,
        width,
        out_weight,
        embed_parts,
        norm_gain,
        group_count,
        [*next_pairs[1:], *both_pairs[1:]],
    )
    stepped_other = shifted(stepped, "dom", 1)
    features_other = shifted(features, "dom", 1)

    scale = potential_scale / math.sqrt(tokens * seq_count)
    head = head_weight.reshape(seq_count * dom_count, 1, up_columns)
    partial = reward(
        ids,
        prev_logw,
        [features, features_other],
        up_parts,
        group_count,
        up_offsets,
        head,
        particles,
        scale,
        dom_count * seq_count,
    )
    logits = lax.all_to_all(partial, ("dom", "seq"), 0, 0, tiled=True)
    resampled = resample(ids, ancestors.astype(jnp.int32), stepped, stepped_other)
    return finish(ids, logits, resampled, particles, dom_count)


def solution(mesh):
    in_specs = (
        P(("groups", "dom"), "seq", None),
        P(("groups", "dom"), "seq", None),
        P(("groups", "dom"), "seq", None),
        P(("groups", "dom"), "seq", None),
        P(),
        P("groups"),
        P("seq", None),
        P(),
        P(None, "seq"),
        P(),
        P(("groups", "dom")),
        P(("groups", "dom")),
    )
    out_specs = (P(("groups", "dom"), "seq", None), P(("groups", "dom")))
    return jax.shard_map(
        on_device, mesh=mesh, in_specs=in_specs, out_specs=out_specs, check_vma=False
    )
```

```python
import functools
import math

import jax
import jax.numpy as jnp
from jax import lax
from jax.experimental import pallas as pl
from jax.experimental.pallas import tpu as pltpu
from jax.sharding import PartitionSpec as P

HEADS = 24
STEPS = 28
LANES = 128

potential_scale = 4.0
norm_eps = 1e-05
MIB = 1024 * 1024


def pack_kernel(chunks, width, q_ref, k_ref, v_ref, *out_refs):
    particles, _, model_width = q_ref.shape
    blocks = model_width // width
    part = width // chunks
    for index, ref in enumerate((q_ref, k_ref, v_ref)):
        for particle in range(particles):
            for block in range(blocks):
                for chunk in range(chunks):
                    start = block * width + chunk * part
                    out_refs[chunk][particle * blocks + block, index] = ref[
                        particle, :, start : start + part
                    ]


def pack(queries, keys, values, chunks, width):
    particles, tokens, model_width = queries.shape
    count = particles * model_width // width
    vmem = pl.BlockSpec(memory_space=pltpu.VMEM)
    shape = jax.ShapeDtypeStruct((count, 3, tokens, width // chunks), queries.dtype)
    return list(
        pl.pallas_call(
            functools.partial(pack_kernel, chunks, width),
            in_specs=[vmem] * 3,
            out_specs=[vmem] * chunks,
            out_shape=[shape] * chunks,
            compiler_params=pltpu.CompilerParams(vmem_limit_bytes=60 * MIB),
            name="pack_heads",
        )(queries, keys, values)
    )


def gate_kernel(*refs):
    pass


def gate(array, after):
    hbm = pl.BlockSpec(memory_space=pltpu.HBM)
    return pl.pallas_call(
        gate_kernel,
        in_specs=[hbm] + [pl.BlockSpec(memory_space=pl.ANY)] * len(after),
        out_specs=hbm,
        out_shape=jax.ShapeDtypeStruct(array.shape, array.dtype),
        input_output_aliases={0: 0},
        compiler_params=pltpu.CompilerParams(vmem_limit_bytes=60 * MIB),
        name="gate",
    )(array, *after)


def attention_kernel(head_width, block_sources, qkv_ref, *refs):
    out_ref = refs[-1]
    sources, _, tokens, columns = qkv_ref.shape
    total = sources * tokens
    rows = block_sources * tokens
    factor = 1.0 / math.sqrt(head_width) / math.log(2.0)
    k_all = qkv_ref[:, 1].reshape(total, columns)
    v_all = qkv_ref[:, 2].reshape(total, columns)
    for block in range(0, sources, block_sources):
        span = slice(block, block + block_sources)
        q_all = qkv_ref[span, 0].reshape(rows, columns)
        pieces = []
        for head in range(columns // head_width):
            cols = slice(head * head_width, (head + 1) * head_width)
            scores = lax.dot_general(
                q_all[:, cols],
                k_all[:, cols],
                (((1,), (1,)), ((), ())),
                preferred_element_type=jnp.float32,
            )
            highest = jnp.max(scores, axis=1, keepdims=True)
            expanded = jnp.exp2((scores - highest) * factor)
            norm = 1.0 / jnp.sum(expanded, axis=1, keepdims=True)
            weights = (expanded * norm).astype(jnp.bfloat16)
            pieces.append(jnp.dot(weights, v_all[:, cols], preferred_element_type=jnp.float32))
        joined = jnp.concatenate(pieces, axis=1).astype(jnp.bfloat16)
        out_ref[span] = joined.reshape(block_sources, tokens, columns)


def attention(qkv, head_width, width, start, earlier, after):
    sources, _, tokens, columns = qkv.shape
    total = sources * tokens
    block_sources = max(1, min(sources, 512 // tokens))
    while sources % block_sources:
        block_sources -= 1
    step = LANES if columns % LANES == 0 and LANES % head_width == 0 else columns
    scores_bytes = 4 * block_sources * tokens * total
    first = start // step
    unread = earlier + after
    return pl.pallas_call(
        functools.partial(attention_kernel, head_width, block_sources),
        grid=(columns // step,),
        in_specs=[pl.BlockSpec((sources, 3, tokens, step), lambda i: (0, 0, 0, i))]
        + [pl.BlockSpec(memory_space=pl.ANY)] * len(unread),
        out_specs=pl.BlockSpec((sources, tokens, step), lambda i: (0, 0, first + i)),
        out_shape=jax.ShapeDtypeStruct((sources, tokens, width), jnp.bfloat16),
        input_output_aliases={1: 0} if earlier else {},
        compiler_params=pltpu.CompilerParams(vmem_limit_bytes=8 * MIB + 6 * scores_bytes),
        cost_estimate=pl.CostEstimate(
            flops=4 * total * total * columns,
            bytes_accessed=8 * total * columns,
            transcendentals=columns // head_width * total * total,
        ),
        name="attention",
    )(qkv, *unread)


def column_block(model_width):
    return 512 if model_width % 512 == 0 else model_width


def project_kernel(parts, offsets, depth_parts, refs_in, refs_out):
    ids_ref, latents_hbm, gain_ref, out_weight_ref, attended_ref = refs_in[:5]
    weight_refs = refs_in[5 : 5 + parts]
    stepped_ref, features_ref = refs_out[:2]
    out_vmem, weight_vmem, rows_ref, clean_ref, embedded_ref, latents_ref = refs_out[2:8]
    out_sems, sems = refs_out[8:]
    dom, group, seq = ids_ref[0], ids_ref[1], ids_ref[2]
    sigma = ids_ref[3].astype(jnp.float32) * (1.0 / STEPS)
    particles, tokens, model_width = latents_ref.shape
    rows = particles * tokens
    shards, depth, columns = weight_refs[0].shape

    block = column_block(model_width)
    first_copies = []
    for index in range(model_width // block):
        cols = slice(index * block, (index + 1) * block)
        first_copies += [
            pltpu.make_async_copy(
                out_weight_ref.at[:, cols], out_vmem.at[:, cols], out_sems.at[0, index]
            ),
            pltpu.make_async_copy(
                latents_hbm.at[:, :, cols], latents_ref.at[:, :, cols], out_sems.at[1, index]
            ),
        ]
    copies = []
    for index in range(parts):
        for shard in range(shards):
            start = pl.multiple_of((seq ^ offsets[shard]) * depth, depth)
            copies.append(
                pltpu.make_async_copy(
                    weight_refs[index].at[shard],
                    weight_vmem.at[index, pl.ds(start, depth)],
                    sems.at[index],
                )
            )
    for copy in first_copies + copies:
        copy.start()

    count, _, width = attended_ref.shape
    blocks = count // particles
    for piece in range(count):
        particle, place = divmod(piece, blocks)
        rows_ref[
            particle * tokens : (particle + 1) * tokens, place * width : (place + 1) * width
        ] = attended_ref[piece]
    for index in range(model_width // block):
        cols = slice(index * block, (index + 1) * block)
        for copy in first_copies[2 * index : 2 * index + 2]:
            copy.wait()
        flat = latents_ref[:, :, cols].reshape(rows, block).astype(jnp.float32)
        velocity = flat + jnp.dot(
            rows_ref[...], out_vmem[:, cols], preferred_element_type=jnp.float32
        )
        clean_ref[:, cols] = (flat - sigma * velocity).astype(jnp.bfloat16)
        stepped_ref[:, :, cols] = (
            (flat - velocity * (1.0 / STEPS)).astype(jnp.bfloat16).reshape(particles, tokens, block)
        )

    for index in range(parts):
        for copy in copies[index * shards : (index + 1) * shards]:
            copy.wait()
        doms = parts // depth_parts
        dom_of = (dom + doms - index // depth_parts) % doms
        group_of = (group + depth_parts - index % depth_parts) % depth_parts
        embedded_ref[dom_of * depth_parts + group_of] = jnp.dot(
            clean_ref[...], weight_vmem[index], preferred_element_type=jnp.float32
        )
    count = parts * columns
    blocks = [embedded_ref[index] for index in range(parts)]
    centre = sum(jnp.sum(piece, axis=1, keepdims=True) for piece in blocks) * (1.0 / count)
    blocks = [piece - centre for piece in blocks]
    variance = sum(jnp.sum(piece * piece, axis=1, keepdims=True) for piece in blocks) * (
        1.0 / count
    )
    inverse = lax.rsqrt(variance + norm_eps)
    share = features_ref.shape[2]
    for index, piece in enumerate(blocks):
        cols = slice(index * columns, (index + 1) * columns)
        feature = jax.nn.gelu(piece * inverse * gain_ref[:, cols]).astype(jnp.bfloat16)
        start = index * columns % share
        features_ref[index * columns // share, :, start : start + columns] = feature


def project_embed(
    ids, offsets, latents, attended, out_weight, weights, gain, depth_parts, after
):
    particles, tokens, model_width = latents.shape
    rows = particles * tokens
    parts = len(weights)
    columns = weights[0].shape[2]
    count = parts * columns
    groups = model_width // column_block(model_width)
    vmem = pl.BlockSpec(memory_space=pltpu.VMEM)
    hbm = pl.BlockSpec(memory_space=pltpu.HBM)
    inputs = 5 + parts + len(after)

    def kernel(*refs):
        project_kernel(parts, offsets, depth_parts, refs[:inputs], refs[inputs:])

    return pl.pallas_call(
        kernel,
        in_specs=[pl.BlockSpec(memory_space=pltpu.SMEM), hbm, vmem, hbm, vmem]
        + [hbm] * parts
        + [pl.BlockSpec(memory_space=pl.ANY)] * len(after),
        out_specs=[vmem, vmem],
        out_shape=[
            jax.ShapeDtypeStruct(latents.shape, jnp.bfloat16),
            jax.ShapeDtypeStruct((depth_parts, rows, count // depth_parts), jnp.bfloat16),
        ],
        scratch_shapes=[
            pltpu.VMEM((model_width, model_width), jnp.bfloat16),
            pltpu.VMEM((parts, model_width, columns), jnp.bfloat16),
            pltpu.VMEM((rows, model_width), jnp.bfloat16),
            pltpu.VMEM((rows, model_width), jnp.bfloat16),
            pltpu.VMEM((parts, rows, columns), jnp.float32),
            pltpu.VMEM(latents.shape, latents.dtype),
            pltpu.SemaphoreType.DMA((2, groups)),
            pltpu.SemaphoreType.DMA((parts,)),
        ],
        compiler_params=pltpu.CompilerParams(vmem_limit_bytes=60 * MIB),
        cost_estimate=pl.CostEstimate(
            flops=2 * rows * model_width * (model_width + count),
            bytes_accessed=2 * model_width * (model_width + count) + 8 * rows * model_width,
            transcendentals=rows * count,
        ),
        name="project_embed",
    )(ids, latents, gain.reshape(1, count), out_weight, attended, *weights, *after)


def reward_kernel(particles, scale, parts, doms, offsets, joined, *refs):
    ids_ref, prev_ref, head_ref = refs[:3]
    features_refs, weight_refs = refs[3 : 3 + doms], refs[3 + doms : -4]
    out_ref, weight_vmem, rows_ref, sems = refs[-4:]
    dom, group, seq = ids_ref[0], ids_ref[1], ids_ref[2]
    _, depth, columns = weight_refs[0].shape
    rows = features_refs[0].shape[1]
    places = [
        (pair, shard)
        for pair in range(len(weight_refs) // parts)
        for shard in range(weight_refs[pair * parts].shape[0])
    ]
    count = len(places)

    copies = []
    for place, (pair, shard) in enumerate(places):
        lane = place % joined * columns
        for index in range(parts):
            copy = pltpu.make_async_copy(
                weight_refs[pair * parts + index].at[shard],
                weight_vmem.at[
                    place // joined,
                    index * depth : (index + 1) * depth,
                    lane : lane + columns,
                ],
                sems.at[place, index],
            )
            copy.start()
            copies.append(copy)
    for step, features_ref in enumerate(features_refs):
        for index in range(parts):
            rows_ref[step * rows : (step + 1) * rows, index * depth : (index + 1) * depth] = (
                features_ref[(group + parts - index) % parts]
            )
    totals = jnp.zeros((doms * particles, joined * columns), jnp.float32)
    for step in range(count // joined):
        for copy in copies[step * joined * parts : (step + 1) * joined * parts]:
            copy.wait()
        hidden = jnp.dot(rows_ref[...], weight_vmem[step], preferred_element_type=jnp.float32)
        head = jnp.concatenate(
            [
                head_ref[(seq ^ offset) * doms + dom]
                for offset in offsets[step * joined : (step + 1) * joined]
            ],
            axis=1,
        )
        scored = jax.nn.gelu(hidden) * head
        totals += jnp.sum(scored.reshape(doms * particles, rows // particles, -1), axis=1)

    sums = jnp.sum(totals, axis=1, keepdims=True) * scale
    shape = out_ref.shape[1:]
    out_rows = lax.broadcasted_iota(jnp.int32, shape, 0)
    lanes = lax.broadcasted_iota(jnp.int32, shape, 1)
    logits = jnp.zeros(shape, jnp.float32)
    for index in range(doms * particles):
        step, particle = divmod(index, particles)
        value = sums[index : index + 1]
        if step == 0:
            value = value + jnp.where(seq == 0, prev_ref[particle], 0.0)
        here = jnp.logical_and(out_rows == (dom + doms - step) % doms, lanes == particle)
        logits += jnp.where(here, value, 0.0)
    out_ref[...] = jnp.broadcast_to(logits[None], out_ref.shape)


def reward(ids, prev_logw, features, weights, parts, offsets, head, particles, scale, copies):
    _, depth, columns = weights[0].shape
    rows, doms = features[0].shape[1], len(features)
    count = len(offsets)
    joined = 2 if columns % LANES == 0 and count % 2 == 0 else 1
    smem = pl.BlockSpec(memory_space=pltpu.SMEM)
    vmem = pl.BlockSpec(memory_space=pltpu.VMEM)
    return pl.pallas_call(
        functools.partial(reward_kernel, particles, scale, parts, doms, offsets, joined),
        in_specs=[smem, smem, vmem]
        + [vmem] * doms
        + [pl.BlockSpec(memory_space=pltpu.HBM)] * len(weights),
        out_specs=vmem,
        out_shape=jax.ShapeDtypeStruct((copies, 8, LANES), jnp.float32),
        scratch_shapes=[
            pltpu.VMEM((count // joined, parts * depth, joined * columns), jnp.bfloat16),
            pltpu.VMEM((doms * rows, parts * depth), jnp.bfloat16),
            pltpu.SemaphoreType.DMA((count, parts)),
        ],
        compiler_params=pltpu.CompilerParams(vmem_limit_bytes=60 * MIB),
        cost_estimate=pl.CostEstimate(
            flops=2 * doms * rows * parts * depth * count * columns,
            bytes_accessed=2 * parts * depth * count * columns,
            transcendentals=doms * rows * count * columns,
        ),
        name="reward",
    )(ids, prev_logw, head, *features, *weights)


def finish_kernel(particles, doms, ids_ref, resampled_ref, parts_ref, out_ref, same_ref):
    logits = jnp.sum(parts_ref[...], axis=0)
    rows = lax.broadcasted_iota(jnp.int32, logits.shape, 0)
    lanes = lax.broadcasted_iota(jnp.int32, logits.shape, 1)
    valid = jnp.logical_and(rows < doms, lanes < particles)
    highest = jnp.max(jnp.where(valid, logits, -jnp.inf))
    total = jnp.sum(jnp.where(valid, jnp.exp(logits - highest), 0.0), axis=1, keepdims=True)
    log_total = highest + jnp.log(jnp.sum(total, axis=0, keepdims=True))
    own = jnp.sum(jnp.where(rows == ids_ref[0], logits, 0.0), axis=0, keepdims=True)
    out_ref[...] = (own - log_total)[:, :particles]


def finish(ids, parts, resampled, particles, doms):
    vmem = pl.BlockSpec(memory_space=pltpu.VMEM)
    anywhere = pl.BlockSpec(memory_space=pl.ANY)
    log_weights, resampled = pl.pallas_call(
        functools.partial(finish_kernel, particles, doms),
        in_specs=[pl.BlockSpec(memory_space=pltpu.SMEM), anywhere, vmem],
        out_specs=[vmem, anywhere],
        out_shape=[
            jax.ShapeDtypeStruct((1, particles), jnp.float32),
            jax.ShapeDtypeStruct(resampled.shape, resampled.dtype),
        ],
        input_output_aliases={1: 1},
        compiler_params=pltpu.CompilerParams(vmem_limit_bytes=2 * MIB),
        name="log_weights",
    )(ids, resampled, parts)
    return resampled, log_weights.reshape(particles)


def resample_kernel(ids_ref, ancestors_ref, own_ref, other_ref, out_ref):
    index = pl.program_id(0)
    own = ancestors_ref[index] // pl.num_programs(0) == ids_ref[0]

    @pl.when(own)
    def _():
        out_ref[...] = own_ref[...]

    @pl.when(jnp.logical_not(own))
    def _():
        out_ref[...] = other_ref[...]


def resample(ids, ancestors, own, other):
    particles, tokens, columns = own.shape
    block = (1, tokens, columns)
    parent = pl.BlockSpec(block, lambda i, ids, ancestors: (ancestors[i] % particles, 0, 0))
    return pl.pallas_call(
        resample_kernel,
        grid_spec=pltpu.PrefetchScalarGridSpec(
            num_scalar_prefetch=2,
            grid=(particles,),
            in_specs=[parent, parent],
            out_specs=pl.BlockSpec(block, lambda i, ids, ancestors: (i, 0, 0)),
        ),
        out_shape=jax.ShapeDtypeStruct(own.shape, own.dtype),
        compiler_params=pltpu.CompilerParams(vmem_limit_bytes=4 * MIB),
        name="resample",
    )(ids, ancestors, own, other)


def shifted(array, axis, step):
    count = lax.axis_size(axis)
    return lax.ppermute(array, axis, [(i, (i + step) % count) for i in range(count)])


def swapped(array, axis, bit):
    return lax.ppermute(array, axis, [(i, i ^ bit) for i in range(lax.axis_size(axis))])


def exchange(array):
    return lax.all_to_all(array, "seq", 0, 0, tiled=True)


def on_device(
    latents,
    queries,
    keys,
    values,
    out_weight,
    step_index,
    embed_weight,
    norm_gain,
    up_weight,
    head_weight,
    prev_logw,
    ancestors,
):
    seq_count = lax.axis_size("seq")
    group_count = lax.axis_size("groups")
    dom_count = lax.axis_size("dom")
    holders = group_count * dom_count
    dom = lax.axis_index("dom")
    group = lax.axis_index("groups")
    seq = lax.axis_index("seq")
    particles, tokens, model_width = latents.shape
    head_width = model_width // HEADS
    width = particles * model_width // seq_count
    chunks = 2 if width % (2 * LANES) == 0 else 1

    ids = jnp.stack([dom, group, seq, step_index[0]]).astype(jnp.int32)

    embed_columns = embed_weight.shape[1] // holders
    embed_share = lax.dynamic_slice_in_dim(
        embed_weight, (dom * group_count + group) * embed_columns, embed_columns, 1
    )[None]
    up_depth = up_weight.shape[0] // group_count
    up_columns = up_weight.shape[1] // dom_count
    up_share = lax.dynamic_slice(
        up_weight, (group * up_depth, dom * up_columns), (up_depth, up_columns)
    )[None]
    bits = [1 << place for place in reversed(range(1, seq_count.bit_length() - 1))]
    near = [0]
    for bit in bits[:-2]:
        embed_share = jnp.concatenate([embed_share, swapped(embed_share, "seq", bit)])
        up_share = jnp.concatenate([up_share, swapped(up_share, "seq", bit)])
        near = near + [offset ^ bit for offset in near]
    high, low = bits[-2:]

    def over_groups(array):
        return [array] + [shifted(array, "groups", k) for k in range(1, group_count)]

    packed = pack(queries, keys, values, chunks, width)
    embed_share = jnp.concatenate([embed_share, swapped(embed_share, "seq", high)])
    packed[0] = gate(packed[0], [embed_share])

    arrived = [exchange(packed[0])]
    up_high, up_low = swapped(up_share, "seq", high), swapped(up_share, "seq", low)
    own_pair, own_groups = swapped(up_share, "seq", 1), over_groups(up_share)
    for bit in (low, 1):
        embed_share = jnp.concatenate([embed_share, swapped(embed_share, "seq", bit)])
    after = [embed_share, up_high, up_low, own_pair, *own_groups[1:]]
    packed[1:] = [gate(piece, after) for piece in packed[1:]]

    arrived += [exchange(piece) for piece in packed[1:]]
    up_both = swapped(up_high, "seq", low)
    up_next = jnp.concatenate([up_high, up_low])
    next_pair, next_groups = swapped(up_next, "seq", 1), over_groups(up_next)
    embed_near = over_groups(embed_share)
    after = [up_both, next_pair, *next_groups[1:], *embed_near[1:]]
    attended = []
    for index, piece in enumerate(arrived):
        start = index * (width // chunks)
        attended = [
            attention(piece, head_width, width, start, attended, after if index else [])
        ]

    returned = exchange(attended[0])
    both_pair, both_groups = swapped(up_both, "seq", 1), over_groups(up_both)
    own_pairs = over_groups(own_pair)
    embed_parts = embed_near + [
        shifted(piece, "dom", k) for k in range(1, dom_count) for piece in embed_near
    ]
    next_pairs = over_groups(next_pair)
    both_pairs = [both_pair] + [swapped(piece, "seq", 1) for piece in both_groups[1:]]
    up_parts = own_groups + own_pairs + next_groups + next_pairs + both_groups + both_pairs
    up_offsets = [
        offset ^ bit ^ pair
        for bits in ((0,), (high, low), (high ^ low,))
        for pair in (0, 1)
        for bit in bits
        for offset in near
    ]
    embed_offsets = near + [offset ^ high for offset in near]
    for bit in (low, 1):
        embed_offsets = embed_offsets + [offset ^ bit for offset in embed_offsets]

    stepped, features = project_embed(
        ids,
        embed_offsets,
        latents,
        returned,
        out_weight,
        embed_parts,
        norm_gain,
        group_count,
        [*own_pairs[1:], *next_pairs[1:], *both_groups[1:], *both_pairs],
    )
    stepped_other = shifted(stepped, "dom", 1)
    features_other = shifted(features, "dom", 1)

    scale = potential_scale / math.sqrt(tokens * seq_count)
    head = head_weight.reshape(seq_count * dom_count, 1, up_columns)
    partial = reward(
        ids,
        prev_logw,
        [features, features_other],
        up_parts,
        group_count,
        up_offsets,
        head,
        particles,
        scale,
        dom_count * seq_count,
    )
    logits = lax.all_to_all(partial, ("dom", "seq"), 0, 0, tiled=True)
    resampled = resample(ids, ancestors.astype(jnp.int32), stepped, stepped_other)
    return finish(ids, logits, resampled, particles, dom_count)


def solution(mesh):
    in_specs = (
        P(("groups", "dom"), "seq", None),
        P(("groups", "dom"), "seq", None),
        P(("groups", "dom"), "seq", None),
        P(("groups", "dom"), "seq", None),
        P(),
        P("groups"),
        P("seq", None),
        P(),
        P(None, "seq"),
        P(),
        P(("groups", "dom")),
        P(("groups", "dom")),
    )
    out_specs = (P(("groups", "dom"), "seq", None), P(("groups", "dom")))
    return jax.shard_map(
        on_device, mesh=mesh, in_specs=in_specs, out_specs=out_specs, check_vma=False
    )
```

```python
import functools
import math

import jax
import jax.numpy as jnp
from jax import lax
from jax.experimental import pallas as pl
from jax.experimental.pallas import tpu as pltpu
from jax.sharding import PartitionSpec as P

HEADS = 24
STEPS = 28
LANES = 128

potential_scale = 4.0
norm_eps = 1e-05
MIB = 1024 * 1024


def pack_kernel(chunks, width, q_ref, k_ref, v_ref, *out_refs):
    particles, _, model_width = q_ref.shape
    blocks = model_width // width
    part = width // chunks
    for index, ref in enumerate((q_ref, k_ref, v_ref)):
        for particle in range(particles):
            for block in range(blocks):
                for chunk in range(chunks):
                    start = block * width + chunk * part
                    out_refs[chunk][particle * blocks + block, index] = ref[
                        particle, :, start : start + part
                    ]


def pack(queries, keys, values, chunks, width):
    particles, tokens, model_width = queries.shape
    count = particles * model_width // width
    vmem = pl.BlockSpec(memory_space=pltpu.VMEM)
    shape = jax.ShapeDtypeStruct((count, 3, tokens, width // chunks), queries.dtype)
    return list(
        pl.pallas_call(
            functools.partial(pack_kernel, chunks, width),
            in_specs=[vmem] * 3,
            out_specs=[vmem] * chunks,
            out_shape=[shape] * chunks,
            compiler_params=pltpu.CompilerParams(vmem_limit_bytes=60 * MIB),
            name="pack_heads",
        )(queries, keys, values)
    )


def gate_kernel(*refs):
    pass


def gate(array, after):
    hbm = pl.BlockSpec(memory_space=pltpu.HBM)
    return pl.pallas_call(
        gate_kernel,
        in_specs=[hbm] + [pl.BlockSpec(memory_space=pl.ANY)] * len(after),
        out_specs=hbm,
        out_shape=jax.ShapeDtypeStruct(array.shape, array.dtype),
        input_output_aliases={0: 0},
        compiler_params=pltpu.CompilerParams(vmem_limit_bytes=60 * MIB),
        name="gate",
    )(array, *after)


def attention_kernel(head_width, block_sources, qkv_ref, out_ref):
    sources, _, tokens, columns = qkv_ref.shape
    total = sources * tokens
    rows = block_sources * tokens
    factor = 1.0 / math.sqrt(head_width) / math.log(2.0)
    k_all = qkv_ref[:, 1].reshape(total, columns)
    v_all = qkv_ref[:, 2].reshape(total, columns)
    for block in range(0, sources, block_sources):
        span = slice(block, block + block_sources)
        q_all = qkv_ref[span, 0].reshape(rows, columns)
        pieces = []
        for head in range(columns // head_width):
            cols = slice(head * head_width, (head + 1) * head_width)
            scores = lax.dot_general(
                q_all[:, cols],
                k_all[:, cols],
                (((1,), (1,)), ((), ())),
                preferred_element_type=jnp.float32,
            )
            highest = jnp.max(scores, axis=1, keepdims=True)
            expanded = jnp.exp2((scores - highest) * factor)
            norm = 1.0 / jnp.sum(expanded, axis=1, keepdims=True)
            weights = (expanded * norm).astype(jnp.bfloat16)
            pieces.append(jnp.dot(weights, v_all[:, cols], preferred_element_type=jnp.float32))
        joined = jnp.concatenate(pieces, axis=1).astype(jnp.bfloat16)
        out_ref[span] = joined.reshape(block_sources, tokens, columns)


def attention(qkv, head_width):
    sources, _, tokens, columns = qkv.shape
    total = sources * tokens
    block_sources = max(1, min(sources, 512 // tokens))
    while sources % block_sources:
        block_sources -= 1
    step = LANES if columns % LANES == 0 and LANES % head_width == 0 else columns
    scores_bytes = 4 * block_sources * tokens * total
    return pl.pallas_call(
        functools.partial(attention_kernel, head_width, block_sources),
        grid=(columns // step,),
        in_specs=[pl.BlockSpec((sources, 3, tokens, step), lambda i: (0, 0, 0, i))],
        out_specs=pl.BlockSpec((sources, tokens, step), lambda i: (0, 0, i)),
        out_shape=jax.ShapeDtypeStruct((sources, tokens, columns), jnp.bfloat16),
        compiler_params=pltpu.CompilerParams(vmem_limit_bytes=8 * MIB + 6 * scores_bytes),
        cost_estimate=pl.CostEstimate(
            flops=4 * total * total * columns,
            bytes_accessed=8 * total * columns,
            transcendentals=columns // head_width * total * total,
        ),
        name="attention",
    )(qkv)


def column_block(model_width):
    return 512 if model_width % 512 == 0 else model_width


class ProjectionWeights:
    def __init__(self, weight_ref, vmem_ref, sems, chunks, wanted, width):
        depth, model_width = weight_ref.shape
        part = width // chunks
        blocks = depth // width
        self.block = column_block(model_width)
        self.copies = []
        for group in range(model_width // self.block):
            cols = slice(group * self.block, (group + 1) * self.block)
            for index in range(blocks * len(wanted)):
                start = index // len(wanted) * width + wanted[index % len(wanted)] * part
                self.copies.append(
                    pltpu.make_async_copy(
                        weight_ref.at[start : start + part, cols],
                        vmem_ref.at[index * part : (index + 1) * part, cols],
                        sems.at[group, index],
                    )
                )
        self.per_group = blocks * len(wanted)
        for copy in self.copies:
            copy.start()

    def wait(self, group):
        for copy in self.copies[group * self.per_group : (group + 1) * self.per_group]:
            copy.wait()
        return slice(group * self.block, (group + 1) * self.block)


def gather_rows(piece_refs, rows_ref, particles):
    count, tokens, part = piece_refs[0].shape
    blocks = count // particles
    for index in range(blocks * len(piece_refs)):
        ref = piece_refs[index % len(piece_refs)]
        place = index // len(piece_refs)
        for particle in range(particles):
            rows_ref[
                particle * tokens : (particle + 1) * tokens, index * part : (index + 1) * part
            ] = ref[particle * blocks + place]


def first_project_kernel(chunks, width, latents_ref, weight_ref, piece_ref, out_ref, *scratch):
    weight_vmem, rows_ref, sems = scratch
    particles, tokens, model_width = latents_ref.shape
    weights = ProjectionWeights(weight_ref, weight_vmem, sems, chunks, [0], width)
    gather_rows([piece_ref], rows_ref, particles)
    for group in range(model_width // weights.block):
        cols = weights.wait(group)
        flat = latents_ref[:, :, cols].reshape(particles * tokens, weights.block)
        out_ref[:, cols] = flat.astype(jnp.float32) + jnp.dot(
            rows_ref[...], weight_vmem[:, cols], preferred_element_type=jnp.float32
        )


def first_project(latents, out_weight, piece, chunks, width):
    particles, tokens, model_width = latents.shape
    rows, depth = particles * tokens, model_width // chunks
    vmem = pl.BlockSpec(memory_space=pltpu.VMEM)
    return pl.pallas_call(
        functools.partial(first_project_kernel, chunks, width),
        in_specs=[vmem, pl.BlockSpec(memory_space=pltpu.HBM), vmem],
        out_specs=vmem,
        out_shape=jax.ShapeDtypeStruct((rows, model_width), jnp.float32),
        scratch_shapes=[
            pltpu.VMEM((depth, model_width), jnp.bfloat16),
            pltpu.VMEM((rows, depth), jnp.bfloat16),
            pltpu.SemaphoreType.DMA(
                (model_width // column_block(model_width), model_width // width)
            ),
        ],
        compiler_params=pltpu.CompilerParams(vmem_limit_bytes=60 * MIB),
        cost_estimate=pl.CostEstimate(
            flops=2 * rows * depth * model_width,
            bytes_accessed=2 * depth * model_width + 8 * rows * model_width,
            transcendentals=0,
        ),
        name="first_project",
    )(latents, out_weight, piece)


def project_kernel(chunks, width, pieces, parts, offsets, depth_parts, refs_in, refs_out):
    ids_ref, latents_hbm, gain_ref, out_weight_ref = refs_in[:4]
    rest, weight_refs = list(refs_in[4 : 4 + pieces]), refs_in[4 + pieces : 4 + pieces + parts]
    begun_hbm = rest.pop(0) if chunks > 1 else None
    stepped_ref, features_ref = refs_out[:2]
    out_vmem, weight_vmem, rows_ref, clean_ref, embedded_ref = refs_out[2:7]
    latents_ref, begun_ref, out_sems, sems, first_sems = refs_out[7:]
    dom, group, seq = ids_ref[0], ids_ref[1], ids_ref[2]
    sigma = ids_ref[3].astype(jnp.float32) * (1.0 / STEPS)
    particles, tokens, model_width = latents_ref.shape
    rows = particles * tokens
    shards, depth, columns = weight_refs[0].shape

    wanted = list(range(chunks - len(rest), chunks))
    block = column_block(model_width)
    first_copies = []
    for index in range(model_width // block):
        cols = slice(index * block, (index + 1) * block)
        first_copies.append(
            pltpu.make_async_copy(
                latents_hbm.at[:, :, cols], latents_ref.at[:, :, cols], first_sems.at[0, index]
            )
        )
        if chunks > 1:
            first_copies.append(
                pltpu.make_async_copy(
                    begun_hbm.at[:, cols], begun_ref.at[:, cols], first_sems.at[1, index]
                )
            )
    for copy in first_copies[: len(first_copies) // (model_width // block)]:
        copy.start()
    out_weights = ProjectionWeights(out_weight_ref, out_vmem, out_sems, chunks, wanted, width)
    for copy in first_copies[len(first_copies) // (model_width // block) :]:
        copy.start()
    copies = []
    for index in range(parts):
        for shard in range(shards):
            start = pl.multiple_of((seq ^ offsets[shard]) * depth, depth)
            copy = pltpu.make_async_copy(
                weight_refs[index].at[shard],
                weight_vmem.at[index, pl.ds(start, depth)],
                sems.at[index],
            )
            copy.start()
            copies.append(copy)

    gather_rows(rest, rows_ref, particles)
    each = len(first_copies) // (model_width // block)

    def product(index):
        cols = out_weights.wait(index)
        for copy in first_copies[index * each : (index + 1) * each]:
            copy.wait()
        return jnp.dot(rows_ref[...], out_vmem[:, cols], preferred_element_type=jnp.float32)

    following = product(0)
    for index in range(model_width // block):
        cols, projected = slice(index * block, (index + 1) * block), following
        if index + 1 < model_width // block:
            following = product(index + 1)
        flat = latents_ref[:, :, cols].reshape(rows, block).astype(jnp.float32)
        velocity = (begun_ref[:, cols] if chunks > 1 else flat) + projected
        clean_ref[:, cols] = (flat - sigma * velocity).astype(jnp.bfloat16)
        stepped_ref[:, :, cols] = (
            (flat - velocity * (1.0 / STEPS)).astype(jnp.bfloat16).reshape(particles, tokens, block)
        )

    for index in range(parts):
        for copy in copies[index * shards : (index + 1) * shards]:
            copy.wait()
        doms = parts // depth_parts
        dom_of = (dom + doms - index // depth_parts) % doms
        group_of = (group + depth_parts - index % depth_parts) % depth_parts
        embedded_ref[dom_of * depth_parts + group_of] = jnp.dot(
            clean_ref[...], weight_vmem[index], preferred_element_type=jnp.float32
        )
    count = parts * columns
    blocks = [embedded_ref[index] for index in range(parts)]
    centre = sum(jnp.sum(piece, axis=1, keepdims=True) for piece in blocks) * (1.0 / count)
    blocks = [piece - centre for piece in blocks]
    variance = sum(jnp.sum(piece * piece, axis=1, keepdims=True) for piece in blocks) * (
        1.0 / count
    )
    inverse = lax.rsqrt(variance + norm_eps)
    share = features_ref.shape[2]
    for index, piece in enumerate(blocks):
        cols = slice(index * columns, (index + 1) * columns)
        feature = jax.nn.gelu(piece * inverse * gain_ref[:, cols]).astype(jnp.bfloat16)
        start = index * columns % share
        features_ref[index * columns // share, :, start : start + columns] = feature


def project_embed(
    ids,
    offsets,
    latents,
    begun,
    attended,
    chunks,
    width,
    out_weight,
    weights,
    gain,
    depth_parts,
    after,
):
    particles, tokens, model_width = latents.shape
    rows = particles * tokens
    parts = len(weights)
    columns = weights[0].shape[2]
    count = parts * columns
    out_depth = model_width * len(attended) // chunks
    pieces = ([] if begun is None else [begun]) + attended
    vmem = pl.BlockSpec(memory_space=pltpu.VMEM)
    smem = pl.BlockSpec(memory_space=pltpu.SMEM)
    hbm = pl.BlockSpec(memory_space=pltpu.HBM)
    inputs = 4 + len(pieces) + parts + len(after)
    groups = model_width // column_block(model_width)

    def kernel(*refs):
        project_kernel(
            chunks,
            width,
            len(pieces),
            parts,
            offsets,
            depth_parts,
            refs[:inputs],
            refs[inputs:],
        )

    return pl.pallas_call(
        kernel,
        in_specs=[smem, hbm, vmem, hbm]
        + ([] if begun is None else [hbm])
        + [vmem] * len(attended)
        + [hbm] * parts
        + [pl.BlockSpec(memory_space=pl.ANY)] * len(after),
        out_specs=[vmem, vmem],
        out_shape=[
            jax.ShapeDtypeStruct(latents.shape, jnp.bfloat16),
            jax.ShapeDtypeStruct((depth_parts, rows, count // depth_parts), jnp.bfloat16),
        ],
        scratch_shapes=[
            pltpu.VMEM((out_depth, model_width), jnp.bfloat16),
            pltpu.VMEM((parts, model_width, columns), jnp.bfloat16),
            pltpu.VMEM((rows, out_depth), jnp.bfloat16),
            pltpu.VMEM((rows, model_width), jnp.bfloat16),
            pltpu.VMEM((parts, rows, columns), jnp.float32),
            pltpu.VMEM(latents.shape, latents.dtype),
            pltpu.VMEM((rows, model_width), jnp.float32),
            pltpu.SemaphoreType.DMA((groups, model_width // width * len(attended))),
            pltpu.SemaphoreType.DMA((parts,)),
            pltpu.SemaphoreType.DMA((2, groups)),
        ],
        compiler_params=pltpu.CompilerParams(vmem_limit_bytes=60 * MIB),
        cost_estimate=pl.CostEstimate(
            flops=2 * rows * model_width * (out_depth + count),
            bytes_accessed=2 * model_width * (out_depth + count) + 12 * rows * model_width,
            transcendentals=rows * count,
        ),
        name="project_embed",
    )(ids, latents, gain.reshape(1, count), out_weight, *pieces, *weights, *after)


def reward_kernel(particles, scale, parts, doms, offsets, joined, *refs):
    ids_ref, prev_ref, head_ref = refs[:3]
    features_refs, weight_refs = refs[3 : 3 + doms], refs[3 + doms : -4]
    out_ref, weight_vmem, rows_ref, sems = refs[-4:]
    dom, group, seq = ids_ref[0], ids_ref[1], ids_ref[2]
    _, depth, columns = weight_refs[0].shape
    rows = features_refs[0].shape[1]
    places = [
        (pair, shard)
        for pair in range(len(weight_refs) // parts)
        for shard in range(weight_refs[pair * parts].shape[0])
    ]
    count = len(places)

    copies = []
    for place, (pair, shard) in enumerate(places):
        lane = place % joined * columns
        for index in range(parts):
            copy = pltpu.make_async_copy(
                weight_refs[pair * parts + index].at[shard],
                weight_vmem.at[
                    place // joined,
                    index * depth : (index + 1) * depth,
                    lane : lane + columns,
                ],
                sems.at[place, index],
            )
            copy.start()
            copies.append(copy)
    for step, features_ref in enumerate(features_refs):
        for index in range(parts):
            rows_ref[step * rows : (step + 1) * rows, index * depth : (index + 1) * depth] = (
                features_ref[(group + parts - index) % parts]
            )
    def product(step):
        for copy in copies[step * joined * parts : (step + 1) * joined * parts]:
            copy.wait()
        return jnp.dot(rows_ref[...], weight_vmem[step], preferred_element_type=jnp.float32)

    linear, cubic = math.sqrt(2.0 / math.pi), math.sqrt(2.0 / math.pi) * 0.044715
    totals = jnp.zeros((doms * particles, joined * columns), jnp.float32)
    following = product(0)
    for step in range(count // joined):
        hidden = following
        if step + 1 < count // joined:
            following = product(step + 1)
        half_head = 0.5 * jnp.concatenate(
            [
                head_ref[(seq ^ offset) * doms + dom]
                for offset in offsets[step * joined : (step + 1) * joined]
            ],
            axis=1,
        )
        bent = jnp.tanh(hidden * (linear + cubic * (hidden * hidden)))
        scored = (hidden + hidden * bent) * half_head
        totals += jnp.sum(scored.reshape(doms * particles, rows // particles, -1), axis=1)

    sums = jnp.sum(totals, axis=1, keepdims=True) * scale
    shape = out_ref.shape[1:]
    out_rows = lax.broadcasted_iota(jnp.int32, shape, 0)
    lanes = lax.broadcasted_iota(jnp.int32, shape, 1)
    logits = jnp.zeros(shape, jnp.float32)
    for index in range(doms * particles):
        step, particle = divmod(index, particles)
        value = sums[index : index + 1]
        if step == 0:
            value = value + jnp.where(seq == 0, prev_ref[particle], 0.0)
        here = jnp.logical_and(out_rows == (dom + doms - step) % doms, lanes == particle)
        logits += jnp.where(here, value, 0.0)
    out_ref[...] = jnp.broadcast_to(logits[None], out_ref.shape)


def reward(ids, prev_logw, features, weights, parts, offsets, head, particles, scale, copies):
    _, depth, columns = weights[0].shape
    rows, doms = features[0].shape[1], len(features)
    count = len(offsets)
    joined = 2 if columns % LANES == 0 and count % 2 == 0 else 1
    smem = pl.BlockSpec(memory_space=pltpu.SMEM)
    vmem = pl.BlockSpec(memory_space=pltpu.VMEM)
    return pl.pallas_call(
        functools.partial(reward_kernel, particles, scale, parts, doms, offsets, joined),
        in_specs=[smem, smem, vmem]
        + [vmem] * doms
        + [pl.BlockSpec(memory_space=pltpu.HBM)] * len(weights),
        out_specs=vmem,
        out_shape=jax.ShapeDtypeStruct((copies, 8, LANES), jnp.float32),
        scratch_shapes=[
            pltpu.VMEM((count // joined, parts * depth, joined * columns), jnp.bfloat16),
            pltpu.VMEM((doms * rows, parts * depth), jnp.bfloat16),
            pltpu.SemaphoreType.DMA((count, parts)),
        ],
        compiler_params=pltpu.CompilerParams(vmem_limit_bytes=60 * MIB),
        cost_estimate=pl.CostEstimate(
            flops=2 * doms * rows * parts * depth * count * columns,
            bytes_accessed=2 * parts * depth * count * columns,
            transcendentals=doms * rows * count * columns,
        ),
        name="reward",
    )(ids, prev_logw, head, *features, *weights)


def finish_kernel(particles, doms, ids_ref, resampled_ref, parts_ref, out_ref, same_ref):
    logits = jnp.sum(parts_ref[...], axis=0)
    rows = lax.broadcasted_iota(jnp.int32, logits.shape, 0)
    lanes = lax.broadcasted_iota(jnp.int32, logits.shape, 1)
    valid = jnp.logical_and(rows < doms, lanes < particles)
    highest = jnp.max(jnp.where(valid, logits, -jnp.inf))
    total = jnp.sum(jnp.where(valid, jnp.exp(logits - highest), 0.0), axis=1, keepdims=True)
    log_total = highest + jnp.log(jnp.sum(total, axis=0, keepdims=True))
    own = jnp.sum(jnp.where(rows == ids_ref[0], logits, 0.0), axis=0, keepdims=True)
    out_ref[...] = (own - log_total)[:, :particles]


def finish(ids, parts, resampled, particles, doms):
    vmem = pl.BlockSpec(memory_space=pltpu.VMEM)
    anywhere = pl.BlockSpec(memory_space=pl.ANY)
    log_weights, resampled = pl.pallas_call(
        functools.partial(finish_kernel, particles, doms),
        in_specs=[pl.BlockSpec(memory_space=pltpu.SMEM), anywhere, vmem],
        out_specs=[vmem, anywhere],
        out_shape=[
            jax.ShapeDtypeStruct((1, particles), jnp.float32),
            jax.ShapeDtypeStruct(resampled.shape, resampled.dtype),
        ],
        input_output_aliases={1: 1},
        compiler_params=pltpu.CompilerParams(vmem_limit_bytes=2 * MIB),
        name="log_weights",
    )(ids, resampled, parts)
    return resampled, log_weights.reshape(particles)


def resample_kernel(ids_ref, ancestors_ref, own_ref, other_ref, out_ref):
    index = pl.program_id(0)
    own = ancestors_ref[index] // pl.num_programs(0) == ids_ref[0]

    @pl.when(own)
    def _():
        out_ref[...] = own_ref[...]

    @pl.when(jnp.logical_not(own))
    def _():
        out_ref[...] = other_ref[...]


def resample(ids, ancestors, own, other):
    particles, tokens, columns = own.shape
    block = (1, tokens, columns)
    parent = pl.BlockSpec(block, lambda i, ids, ancestors: (ancestors[i] % particles, 0, 0))
    return pl.pallas_call(
        resample_kernel,
        grid_spec=pltpu.PrefetchScalarGridSpec(
            num_scalar_prefetch=2,
            grid=(particles,),
            in_specs=[parent, parent],
            out_specs=pl.BlockSpec(block, lambda i, ids, ancestors: (i, 0, 0)),
        ),
        out_shape=jax.ShapeDtypeStruct(own.shape, own.dtype),
        compiler_params=pltpu.CompilerParams(vmem_limit_bytes=4 * MIB),
        name="resample",
    )(ids, ancestors, own, other)


def shifted(array, axis, step):
    count = lax.axis_size(axis)
    return lax.ppermute(array, axis, [(i, (i + step) % count) for i in range(count)])


def swapped(array, axis, bit):
    return lax.ppermute(array, axis, [(i, i ^ bit) for i in range(lax.axis_size(axis))])


def exchange(array):
    return lax.all_to_all(array, "seq", 0, 0, tiled=True)


def on_device(
    latents,
    queries,
    keys,
    values,
    out_weight,
    step_index,
    embed_weight,
    norm_gain,
    up_weight,
    head_weight,
    prev_logw,
    ancestors,
):
    seq_count = lax.axis_size("seq")
    group_count = lax.axis_size("groups")
    dom_count = lax.axis_size("dom")
    holders = group_count * dom_count
    dom = lax.axis_index("dom")
    group = lax.axis_index("groups")
    seq = lax.axis_index("seq")
    particles, tokens, model_width = latents.shape
    head_width = model_width // HEADS
    width = particles * model_width // seq_count
    chunks = 2 if width % (2 * LANES) == 0 else 1

    ids = jnp.stack([dom, group, seq, step_index[0]]).astype(jnp.int32)

    embed_columns = embed_weight.shape[1] // holders
    embed_share = lax.dynamic_slice_in_dim(
        embed_weight, (dom * group_count + group) * embed_columns, embed_columns, 1
    )[None]
    up_depth = up_weight.shape[0] // group_count
    up_columns = up_weight.shape[1] // dom_count
    up_share = lax.dynamic_slice(
        up_weight, (group * up_depth, dom * up_columns), (up_depth, up_columns)
    )[None]
    bits = [1 << place for place in reversed(range(1, seq_count.bit_length() - 1))]
    near = [0]
    for bit in bits[:-2]:
        embed_share = jnp.concatenate([embed_share, swapped(embed_share, "seq", bit)])
        up_share = jnp.concatenate([up_share, swapped(up_share, "seq", bit)])
        near = near + [offset ^ bit for offset in near]
    high, low = bits[-2:]

    def over_groups(array):
        return [array] + [shifted(array, "groups", k) for k in range(1, group_count)]

    packed = pack(queries, keys, values, chunks, width)
    embed_share = jnp.concatenate([embed_share, swapped(embed_share, "seq", high)])
    packed[0] = gate(packed[0], [embed_share])

    arrived = [exchange(packed[0])]
    up_high, up_low = swapped(up_share, "seq", high), swapped(up_share, "seq", low)
    own_pair, own_groups = swapped(up_share, "seq", 1), over_groups(up_share)
    for bit in (low, 1):
        embed_share = jnp.concatenate([embed_share, swapped(embed_share, "seq", bit)])
    after = [embed_share, up_high, up_low, own_pair, *own_groups[1:]]
    packed[1:] = [gate(piece, after) for piece in packed[1:]]

    arrived += [exchange(piece) for piece in packed[1:]]
    up_both = swapped(up_high, "seq", low)
    up_next = jnp.concatenate([up_high, up_low])
    next_pair, next_groups = swapped(up_next, "seq", 1), over_groups(up_next)
    embed_near = over_groups(embed_share)
    attended = [attention(arrived[0], head_width)]
    after = [up_both, next_pair, *next_groups[1:], *embed_near[1:]]
    attended[0] = gate(attended[0], after)

    returned = [exchange(attended[0])]
    both_pair, both_groups = swapped(up_both, "seq", 1), over_groups(up_both)
    own_pairs = over_groups(own_pair)
    attended += [attention(piece, head_width) for piece in arrived[1:]]
    after = [both_pair, *both_groups[1:], *own_pairs[1:]]
    attended[1:] = [gate(piece, after) for piece in attended[1:]]

    returned += [exchange(piece) for piece in attended[1:]]
    embed_parts = embed_near + [
        shifted(piece, "dom", k) for k in range(1, dom_count) for piece in embed_near
    ]
    next_pairs = over_groups(next_pair)
    both_pairs = [both_pair] + [swapped(piece, "seq", 1) for piece in both_groups[1:]]
    up_parts = own_groups + own_pairs + next_groups + next_pairs + both_groups + both_pairs
    up_offsets = [
        offset ^ bit ^ pair
        for bits in ((0,), (high, low), (high ^ low,))
        for pair in (0, 1)
        for bit in bits
        for offset in near
    ]
    embed_offsets = near + [offset ^ high for offset in near]
    for bit in (low, 1):
        embed_offsets = embed_offsets + [offset ^ bit for offset in embed_offsets]

    begun = first_project(latents, out_weight, returned.pop(0), chunks, width) if chunks > 1 else None
    stepped, features = project_embed(
        ids,
        embed_offsets,
        latents,
        begun,
        returned,
        chunks,
        width,
        out_weight,
        embed_parts,
        norm_gain,
        group_count,
        [*next_pairs[1:], *both_pairs[1:]],
    )
    stepped_other = shifted(stepped, "dom", 1)
    features_other = shifted(features, "dom", 1)

    scale = potential_scale / math.sqrt(tokens * seq_count)
    head = head_weight.reshape(seq_count * dom_count, 1, up_columns)
    partial = reward(
        ids,
        prev_logw,
        [features, features_other],
        up_parts,
        group_count,
        up_offsets,
        head,
        particles,
        scale,
        dom_count * seq_count,
    )
    logits = lax.all_to_all(partial, ("dom", "seq"), 0, 0, tiled=True)
    resampled = resample(ids, ancestors.astype(jnp.int32), stepped, stepped_other)
    return finish(ids, logits, resampled, particles, dom_count)


def solution(mesh):
    in_specs = (
        P(("groups", "dom"), "seq", None),
        P(("groups", "dom"), "seq", None),
        P(("groups", "dom"), "seq", None),
        P(("groups", "dom"), "seq", None),
        P(),
        P("groups"),
        P("seq", None),
        P(),
        P(None, "seq"),
        P(),
        P(("groups", "dom")),
        P(("groups", "dom")),
    )
    out_specs = (P(("groups", "dom"), "seq", None), P(("groups", "dom")))
    return jax.shard_map(
        on_device, mesh=mesh, in_specs=in_specs, out_specs=out_specs, check_vma=False
    )
```

```python
import functools
import math

import jax
import jax.numpy as jnp
from jax import lax
from jax.experimental import pallas as pl
from jax.experimental.pallas import tpu as pltpu
from jax.sharding import PartitionSpec as P

HEADS = 24
STEPS = 28
LANES = 128

potential_scale = 4.0
norm_eps = 1e-05
MIB = 1024 * 1024


def pack_kernel(chunks, width, q_ref, k_ref, v_ref, *out_refs):
    particles, _, model_width = q_ref.shape
    blocks = model_width // width
    part = width // chunks
    for index, ref in enumerate((q_ref, k_ref, v_ref)):
        for particle in range(particles):
            for block in range(blocks):
                for chunk in range(chunks):
                    start = block * width + chunk * part
                    out_refs[chunk][particle * blocks + block, index] = ref[
                        particle, :, start : start + part
                    ]


def pack(queries, keys, values, chunks, width):
    particles, tokens, model_width = queries.shape
    count = particles * model_width // width
    vmem = pl.BlockSpec(memory_space=pltpu.VMEM)
    shape = jax.ShapeDtypeStruct((count, 3, tokens, width // chunks), queries.dtype)
    return list(
        pl.pallas_call(
            functools.partial(pack_kernel, chunks, width),
            in_specs=[vmem] * 3,
            out_specs=[vmem] * chunks,
            out_shape=[shape] * chunks,
            compiler_params=pltpu.CompilerParams(vmem_limit_bytes=60 * MIB),
            name="pack_heads",
        )(queries, keys, values)
    )


def gate_kernel(*refs):
    pass


def gate(array, after):
    hbm = pl.BlockSpec(memory_space=pltpu.HBM)
    return pl.pallas_call(
        gate_kernel,
        in_specs=[hbm] + [pl.BlockSpec(memory_space=pl.ANY)] * len(after),
        out_specs=hbm,
        out_shape=jax.ShapeDtypeStruct(array.shape, array.dtype),
        input_output_aliases={0: 0},
        compiler_params=pltpu.CompilerParams(vmem_limit_bytes=60 * MIB),
        name="gate",
    )(array, *after)


def attention_kernel(head_width, block_sources, qkv_ref, out_ref):
    sources, _, tokens, columns = qkv_ref.shape
    total = sources * tokens
    rows = block_sources * tokens
    factor = 1.0 / math.sqrt(head_width) / math.log(2.0)
    k_all = qkv_ref[:, 1].reshape(total, columns)
    v_all = qkv_ref[:, 2].reshape(total, columns)
    for block in range(0, sources, block_sources):
        span = slice(block, block + block_sources)
        q_all = qkv_ref[span, 0].reshape(rows, columns)
        pieces = []
        for head in range(columns // head_width):
            cols = slice(head * head_width, (head + 1) * head_width)
            scores = lax.dot_general(
                q_all[:, cols],
                k_all[:, cols],
                (((1,), (1,)), ((), ())),
                preferred_element_type=jnp.float32,
            )
            highest = jnp.max(scores, axis=1, keepdims=True)
            expanded = jnp.exp2((scores - highest) * factor)
            norm = 1.0 / jnp.sum(expanded, axis=1, keepdims=True)
            weights = (expanded * norm).astype(jnp.bfloat16)
            pieces.append(jnp.dot(weights, v_all[:, cols], preferred_element_type=jnp.float32))
        joined = jnp.concatenate(pieces, axis=1).astype(jnp.bfloat16)
        out_ref[span] = joined.reshape(block_sources, tokens, columns)


def attention(qkv, head_width):
    sources, _, tokens, columns = qkv.shape
    total = sources * tokens
    block_sources = max(1, min(sources, 512 // tokens))
    while sources % block_sources:
        block_sources -= 1
    step = LANES if columns % LANES == 0 and LANES % head_width == 0 else columns
    scores_bytes = 4 * block_sources * tokens * total
    return pl.pallas_call(
        functools.partial(attention_kernel, head_width, block_sources),
        grid=(columns // step,),
        in_specs=[pl.BlockSpec((sources, 3, tokens, step), lambda i: (0, 0, 0, i))],
        out_specs=pl.BlockSpec((sources, tokens, step), lambda i: (0, 0, i)),
        out_shape=jax.ShapeDtypeStruct((sources, tokens, columns), jnp.bfloat16),
        compiler_params=pltpu.CompilerParams(vmem_limit_bytes=8 * MIB + 6 * scores_bytes),
        cost_estimate=pl.CostEstimate(
            flops=4 * total * total * columns,
            bytes_accessed=8 * total * columns,
            transcendentals=columns // head_width * total * total,
        ),
        name="attention",
    )(qkv)


def column_block(model_width):
    return 512 if model_width % 512 == 0 else model_width


class ProjectionWeights:
    def __init__(self, weight_ref, vmem_ref, sems, chunks, wanted, width):
        depth, model_width = weight_ref.shape
        part = width // chunks
        blocks = depth // width
        self.block = column_block(model_width)
        self.copies = []
        for group in range(model_width // self.block):
            cols = slice(group * self.block, (group + 1) * self.block)
            for index in range(blocks * len(wanted)):
                start = index // len(wanted) * width + wanted[index % len(wanted)] * part
                self.copies.append(
                    pltpu.make_async_copy(
                        weight_ref.at[start : start + part, cols],
                        vmem_ref.at[index * part : (index + 1) * part, cols],
                        sems.at[group, index],
                    )
                )
        self.per_group = blocks * len(wanted)
        for copy in self.copies:
            copy.start()

    def wait(self, group):
        for copy in self.copies[group * self.per_group : (group + 1) * self.per_group]:
            copy.wait()
        return slice(group * self.block, (group + 1) * self.block)


def gather_rows(piece_refs, rows_ref, particles):
    count, tokens, part = piece_refs[0].shape
    blocks = count // particles
    for index in range(blocks * len(piece_refs)):
        ref = piece_refs[index % len(piece_refs)]
        place = index // len(piece_refs)
        for particle in range(particles):
            rows_ref[
                particle * tokens : (particle + 1) * tokens, index * part : (index + 1) * part
            ] = ref[particle * blocks + place]


def first_project_kernel(chunks, width, latents_ref, weight_ref, piece_ref, out_ref, *scratch):
    weight_vmem, rows_ref, sems = scratch
    particles, tokens, model_width = latents_ref.shape
    weights = ProjectionWeights(weight_ref, weight_vmem, sems, chunks, [0], width)
    gather_rows([piece_ref], rows_ref, particles)
    for group in range(model_width // weights.block):
        cols = weights.wait(group)
        flat = latents_ref[:, :, cols].reshape(particles * tokens, weights.block)
        out_ref[:, cols] = flat.astype(jnp.float32) + jnp.dot(
            rows_ref[...], weight_vmem[:, cols], preferred_element_type=jnp.float32
        )


def first_project(latents, out_weight, piece, chunks, width):
    particles, tokens, model_width = latents.shape
    rows, depth = particles * tokens, model_width // chunks
    vmem = pl.BlockSpec(memory_space=pltpu.VMEM)
    return pl.pallas_call(
        functools.partial(first_project_kernel, chunks, width),
        in_specs=[vmem, pl.BlockSpec(memory_space=pltpu.HBM), vmem],
        out_specs=vmem,
        out_shape=jax.ShapeDtypeStruct((rows, model_width), jnp.float32),
        scratch_shapes=[
            pltpu.VMEM((depth, model_width), jnp.bfloat16),
            pltpu.VMEM((rows, depth), jnp.bfloat16),
            pltpu.SemaphoreType.DMA(
                (model_width // column_block(model_width), model_width // width)
            ),
        ],
        compiler_params=pltpu.CompilerParams(vmem_limit_bytes=60 * MIB),
        cost_estimate=pl.CostEstimate(
            flops=2 * rows * depth * model_width,
            bytes_accessed=2 * depth * model_width + 8 * rows * model_width,
            transcendentals=0,
        ),
        name="first_project",
    )(latents, out_weight, piece)


def project_kernel(chunks, width, pieces, parts, offsets, depth_parts, refs_in, refs_out):
    ids_ref, latents_hbm, gain_ref, out_weight_ref = refs_in[:4]
    rest, weight_refs = list(refs_in[4 : 4 + pieces]), refs_in[4 + pieces : 4 + pieces + parts]
    begun_hbm = rest.pop(0) if chunks > 1 else None
    stepped_ref, features_ref = refs_out[:2]
    out_vmem, weight_vmem, rows_ref, clean_ref, embedded_ref = refs_out[2:7]
    latents_ref, begun_ref, out_sems, sems, first_sems = refs_out[7:]
    dom, group, seq = ids_ref[0], ids_ref[1], ids_ref[2]
    sigma = ids_ref[3].astype(jnp.float32) * (1.0 / STEPS)
    particles, tokens, model_width = latents_ref.shape
    rows = particles * tokens
    shards, depth, columns = weight_refs[0].shape

    wanted = list(range(chunks - len(rest), chunks))
    block = column_block(model_width)
    first_copies = []
    for index in range(model_width // block):
        cols = slice(index * block, (index + 1) * block)
        first_copies.append(
            pltpu.make_async_copy(
                latents_hbm.at[:, :, cols], latents_ref.at[:, :, cols], first_sems.at[0, index]
            )
        )
        if chunks > 1:
            first_copies.append(
                pltpu.make_async_copy(
                    begun_hbm.at[:, cols], begun_ref.at[:, cols], first_sems.at[1, index]
                )
            )
    for copy in first_copies[: len(first_copies) // (model_width // block)]:
        copy.start()
    out_weights = ProjectionWeights(out_weight_ref, out_vmem, out_sems, chunks, wanted, width)
    for copy in first_copies[len(first_copies) // (model_width // block) :]:
        copy.start()
    copies = []
    for index in range(parts):
        for shard in range(shards):
            start = pl.multiple_of((seq ^ offsets[shard]) * depth, depth)
            copy = pltpu.make_async_copy(
                weight_refs[index].at[shard],
                weight_vmem.at[index, pl.ds(start, depth)],
                sems.at[index],
            )
            copy.start()
            copies.append(copy)

    gather_rows(rest, rows_ref, particles)
    for index in range(model_width // out_weights.block):
        cols = out_weights.wait(index)
        each = len(first_copies) // (model_width // block)
        for copy in first_copies[index * each : (index + 1) * each]:
            copy.wait()
        flat = latents_ref[:, :, cols].reshape(rows, out_weights.block).astype(jnp.float32)
        begun = begun_ref[:, cols] if chunks > 1 else flat
        velocity = begun + jnp.dot(
            rows_ref[...], out_vmem[:, cols], preferred_element_type=jnp.float32
        )
        clean_ref[:, cols] = (flat - sigma * velocity).astype(jnp.bfloat16)
        stepped_ref[:, :, cols] = (
            (flat - velocity * (1.0 / STEPS))
            .astype(jnp.bfloat16)
            .reshape(particles, tokens, out_weights.block)
        )

    for index in range(parts):
        for copy in copies[index * shards : (index + 1) * shards]:
            copy.wait()
        doms = parts // depth_parts
        dom_of = (dom + doms - index // depth_parts) % doms
        group_of = (group + depth_parts - index % depth_parts) % depth_parts
        embedded_ref[dom_of * depth_parts + group_of] = jnp.dot(
            clean_ref[...], weight_vmem[index], preferred_element_type=jnp.float32
        )
    count = parts * columns
    blocks = [embedded_ref[index] for index in range(parts)]
    centre = sum(jnp.sum(piece, axis=1, keepdims=True) for piece in blocks) * (1.0 / count)
    blocks = [piece - centre for piece in blocks]
    variance = sum(jnp.sum(piece * piece, axis=1, keepdims=True) for piece in blocks) * (
        1.0 / count
    )
    inverse = lax.rsqrt(variance + norm_eps)
    share = features_ref.shape[2]
    for index, piece in enumerate(blocks):
        cols = slice(index * columns, (index + 1) * columns)
        feature = jax.nn.gelu(piece * inverse * gain_ref[:, cols]).astype(jnp.bfloat16)
        start = index * columns % share
        features_ref[index * columns // share, :, start : start + columns] = feature


def project_embed(
    ids,
    offsets,
    latents,
    begun,
    attended,
    chunks,
    width,
    out_weight,
    weights,
    gain,
    depth_parts,
    after,
):
    particles, tokens, model_width = latents.shape
    rows = particles * tokens
    parts = len(weights)
    columns = weights[0].shape[2]
    count = parts * columns
    out_depth = model_width * len(attended) // chunks
    pieces = ([] if begun is None else [begun]) + attended
    vmem = pl.BlockSpec(memory_space=pltpu.VMEM)
    smem = pl.BlockSpec(memory_space=pltpu.SMEM)
    hbm = pl.BlockSpec(memory_space=pltpu.HBM)
    inputs = 4 + len(pieces) + parts + len(after)
    groups = model_width // column_block(model_width)

    def kernel(*refs):
        project_kernel(
            chunks,
            width,
            len(pieces),
            parts,
            offsets,
            depth_parts,
            refs[:inputs],
            refs[inputs:],
        )

    return pl.pallas_call(
        kernel,
        in_specs=[smem, hbm, vmem, hbm]
        + ([] if begun is None else [hbm])
        + [vmem] * len(attended)
        + [hbm] * parts
        + [pl.BlockSpec(memory_space=pl.ANY)] * len(after),
        out_specs=[vmem, vmem],
        out_shape=[
            jax.ShapeDtypeStruct(latents.shape, jnp.bfloat16),
            jax.ShapeDtypeStruct((depth_parts, rows, count // depth_parts), jnp.bfloat16),
        ],
        scratch_shapes=[
            pltpu.VMEM((out_depth, model_width), jnp.bfloat16),
            pltpu.VMEM((parts, model_width, columns), jnp.bfloat16),
            pltpu.VMEM((rows, out_depth), jnp.bfloat16),
            pltpu.VMEM((rows, model_width), jnp.bfloat16),
            pltpu.VMEM((parts, rows, columns), jnp.float32),
            pltpu.VMEM(latents.shape, latents.dtype),
            pltpu.VMEM((rows, model_width), jnp.float32),
            pltpu.SemaphoreType.DMA((groups, model_width // width * len(attended))),
            pltpu.SemaphoreType.DMA((parts,)),
            pltpu.SemaphoreType.DMA((2, groups)),
        ],
        compiler_params=pltpu.CompilerParams(vmem_limit_bytes=60 * MIB),
        cost_estimate=pl.CostEstimate(
            flops=2 * rows * model_width * (out_depth + count),
            bytes_accessed=2 * model_width * (out_depth + count) + 12 * rows * model_width,
            transcendentals=rows * count,
        ),
        name="project_embed",
    )(ids, latents, gain.reshape(1, count), out_weight, *pieces, *weights, *after)


def reward_kernel(particles, scale, parts, doms, offsets, joined, *refs):
    ids_ref, prev_ref, head_ref = refs[:3]
    features_refs, weight_refs = refs[3 : 3 + doms], refs[3 + doms : -4]
    out_ref, weight_vmem, rows_ref, sems = refs[-4:]
    dom, group, seq = ids_ref[0], ids_ref[1], ids_ref[2]
    _, depth, columns = weight_refs[0].shape
    rows = features_refs[0].shape[1]
    places = [
        (pair, shard)
        for pair in range(len(weight_refs) // parts)
        for shard in range(weight_refs[pair * parts].shape[0])
    ]
    count = len(places)

    copies = []
    for place, (pair, shard) in enumerate(places):
        lane = place % joined * columns
        for index in range(parts):
            copy = pltpu.make_async_copy(
                weight_refs[pair * parts + index].at[shard],
                weight_vmem.at[
                    place // joined,
                    index * depth : (index + 1) * depth,
                    lane : lane + columns,
                ],
                sems.at[place, index],
            )
            copy.start()
            copies.append(copy)
    for step, features_ref in enumerate(features_refs):
        for index in range(parts):
            rows_ref[step * rows : (step + 1) * rows, index * depth : (index + 1) * depth] = (
                features_ref[(group + parts - index) % parts]
            )
    totals = jnp.zeros((doms * particles, joined * columns), jnp.float32)
    for step in range(count // joined):
        for copy in copies[step * joined * parts : (step + 1) * joined * parts]:
            copy.wait()
        hidden = jnp.dot(rows_ref[...], weight_vmem[step], preferred_element_type=jnp.float32)
        head = jnp.concatenate(
            [
                head_ref[(seq ^ offset) * doms + dom]
                for offset in offsets[step * joined : (step + 1) * joined]
            ],
            axis=1,
        )
        scored = jax.nn.gelu(hidden) * head
        totals += jnp.sum(scored.reshape(doms * particles, rows // particles, -1), axis=1)

    sums = jnp.sum(totals, axis=1, keepdims=True) * scale
    shape = out_ref.shape[1:]
    out_rows = lax.broadcasted_iota(jnp.int32, shape, 0)
    lanes = lax.broadcasted_iota(jnp.int32, shape, 1)
    logits = jnp.zeros(shape, jnp.float32)
    for index in range(doms * particles):
        step, particle = divmod(index, particles)
        value = sums[index : index + 1]
        if step == 0:
            value = value + jnp.where(seq == 0, prev_ref[particle], 0.0)
        here = jnp.logical_and(out_rows == (dom + doms - step) % doms, lanes == particle)
        logits += jnp.where(here, value, 0.0)
    out_ref[...] = jnp.broadcast_to(logits[None], out_ref.shape)


def reward(ids, prev_logw, features, weights, parts, offsets, head, particles, scale, copies):
    _, depth, columns = weights[0].shape
    rows, doms = features[0].shape[1], len(features)
    count = len(offsets)
    joined = 1
    smem = pl.BlockSpec(memory_space=pltpu.SMEM)
    vmem = pl.BlockSpec(memory_space=pltpu.VMEM)
    return pl.pallas_call(
        functools.partial(reward_kernel, particles, scale, parts, doms, offsets, joined),
        in_specs=[smem, smem, vmem]
        + [vmem] * doms
        + [pl.BlockSpec(memory_space=pltpu.HBM)] * len(weights),
        out_specs=vmem,
        out_shape=jax.ShapeDtypeStruct((copies, 8, LANES), jnp.float32),
        scratch_shapes=[
            pltpu.VMEM((count // joined, parts * depth, joined * columns), jnp.bfloat16),
            pltpu.VMEM((doms * rows, parts * depth), jnp.bfloat16),
            pltpu.SemaphoreType.DMA((count, parts)),
        ],
        compiler_params=pltpu.CompilerParams(vmem_limit_bytes=60 * MIB),
        cost_estimate=pl.CostEstimate(
            flops=2 * doms * rows * parts * depth * count * columns,
            bytes_accessed=2 * parts * depth * count * columns,
            transcendentals=doms * rows * count * columns,
        ),
        name="reward",
    )(ids, prev_logw, head, *features, *weights)


def finish_kernel(particles, doms, ids_ref, resampled_ref, parts_ref, out_ref, same_ref):
    logits = jnp.sum(parts_ref[...], axis=0)
    rows = lax.broadcasted_iota(jnp.int32, logits.shape, 0)
    lanes = lax.broadcasted_iota(jnp.int32, logits.shape, 1)
    valid = jnp.logical_and(rows < doms, lanes < particles)
    highest = jnp.max(jnp.where(valid, logits, -jnp.inf))
    total = jnp.sum(jnp.where(valid, jnp.exp(logits - highest), 0.0), axis=1, keepdims=True)
    log_total = highest + jnp.log(jnp.sum(total, axis=0, keepdims=True))
    own = jnp.sum(jnp.where(rows == ids_ref[0], logits, 0.0), axis=0, keepdims=True)
    out_ref[...] = (own - log_total)[:, :particles]


def finish(ids, parts, resampled, particles, doms):
    vmem = pl.BlockSpec(memory_space=pltpu.VMEM)
    anywhere = pl.BlockSpec(memory_space=pl.ANY)
    log_weights, resampled = pl.pallas_call(
        functools.partial(finish_kernel, particles, doms),
        in_specs=[pl.BlockSpec(memory_space=pltpu.SMEM), anywhere, vmem],
        out_specs=[vmem, anywhere],
        out_shape=[
            jax.ShapeDtypeStruct((1, particles), jnp.float32),
            jax.ShapeDtypeStruct(resampled.shape, resampled.dtype),
        ],
        input_output_aliases={1: 1},
        compiler_params=pltpu.CompilerParams(vmem_limit_bytes=2 * MIB),
        name="log_weights",
    )(ids, resampled, parts)
    return resampled, log_weights.reshape(particles)


def resample_kernel(ids_ref, ancestors_ref, own_ref, other_ref, out_ref):
    index = pl.program_id(0)
    own = ancestors_ref[index] // pl.num_programs(0) == ids_ref[0]

    @pl.when(own)
    def _():
        out_ref[...] = own_ref[...]

    @pl.when(jnp.logical_not(own))
    def _():
        out_ref[...] = other_ref[...]


def resample(ids, ancestors, own, other):
    particles, tokens, columns = own.shape
    block = (1, tokens, columns)
    parent = pl.BlockSpec(block, lambda i, ids, ancestors: (ancestors[i] % particles, 0, 0))
    return pl.pallas_call(
        resample_kernel,
        grid_spec=pltpu.PrefetchScalarGridSpec(
            num_scalar_prefetch=2,
            grid=(particles,),
            in_specs=[parent, parent],
            out_specs=pl.BlockSpec(block, lambda i, ids, ancestors: (i, 0, 0)),
        ),
        out_shape=jax.ShapeDtypeStruct(own.shape, own.dtype),
        compiler_params=pltpu.CompilerParams(vmem_limit_bytes=4 * MIB),
        name="resample",
    )(ids, ancestors, own, other)


def shifted(array, axis, step):
    count = lax.axis_size(axis)
    return lax.ppermute(array, axis, [(i, (i + step) % count) for i in range(count)])


def swapped(array, axis, bit):
    return lax.ppermute(array, axis, [(i, i ^ bit) for i in range(lax.axis_size(axis))])


def exchange(array):
    return lax.all_to_all(array, "seq", 0, 0, tiled=True)


def on_device(
    latents,
    queries,
    keys,
    values,
    out_weight,
    step_index,
    embed_weight,
    norm_gain,
    up_weight,
    head_weight,
    prev_logw,
    ancestors,
):
    seq_count = lax.axis_size("seq")
    group_count = lax.axis_size("groups")
    dom_count = lax.axis_size("dom")
    holders = group_count * dom_count
    dom = lax.axis_index("dom")
    group = lax.axis_index("groups")
    seq = lax.axis_index("seq")
    particles, tokens, model_width = latents.shape
    head_width = model_width // HEADS
    width = particles * model_width // seq_count
    chunks = 2 if width % (2 * LANES) == 0 else 1

    ids = jnp.stack([dom, group, seq, step_index[0]]).astype(jnp.int32)

    embed_columns = embed_weight.shape[1] // holders
    embed_share = lax.dynamic_slice_in_dim(
        embed_weight, (dom * group_count + group) * embed_columns, embed_columns, 1
    )[None]
    up_depth = up_weight.shape[0] // group_count
    up_columns = up_weight.shape[1] // dom_count
    up_share = lax.dynamic_slice(
        up_weight, (group * up_depth, dom * up_columns), (up_depth, up_columns)
    )[None]
    bits = [1 << place for place in reversed(range(1, seq_count.bit_length() - 1))]
    near = [0]
    for bit in bits[:-2]:
        embed_share = jnp.concatenate([embed_share, swapped(embed_share, "seq", bit)])
        up_share = jnp.concatenate([up_share, swapped(up_share, "seq", bit)])
        near = near + [offset ^ bit for offset in near]
    high, low = bits[-2:]

    def over_groups(array):
        return [array] + [shifted(array, "groups", k) for k in range(1, group_count)]

    packed = pack(queries, keys, values, chunks, width)
    embed_share = jnp.concatenate([embed_share, swapped(embed_share, "seq", high)])
    packed[0] = gate(packed[0], [embed_share])

    arrived = [exchange(packed[0])]
    up_high, up_low = swapped(up_share, "seq", high), swapped(up_share, "seq", low)
    own_pair, own_groups = swapped(up_share, "seq", 1), over_groups(up_share)
    for bit in (low, 1):
        embed_share = jnp.concatenate([embed_share, swapped(embed_share, "seq", bit)])
    after = [embed_share, up_high, up_low, own_pair, *own_groups[1:]]
    packed[1:] = [gate(piece, after) for piece in packed[1:]]

    arrived += [exchange(piece) for piece in packed[1:]]
    up_both = swapped(up_high, "seq", low)
    up_next = jnp.concatenate([up_high, up_low])
    next_pair, next_groups = swapped(up_next, "seq", 1), over_groups(up_next)
    embed_near = over_groups(embed_share)
    attended = [attention(arrived[0], head_width)]
    after = [up_both, next_pair, *next_groups[1:], *embed_near[1:]]
    attended[0] = gate(attended[0], after)

    returned = [exchange(attended[0])]
    both_pair, both_groups = swapped(up_both, "seq", 1), over_groups(up_both)
    own_pairs = over_groups(own_pair)
    attended += [attention(piece, head_width) for piece in arrived[1:]]
    after = [both_pair, *both_groups[1:], *own_pairs[1:]]
    attended[1:] = [gate(piece, after) for piece in attended[1:]]

    returned += [exchange(piece) for piece in attended[1:]]
    embed_parts = embed_near + [
        shifted(piece, "dom", k) for k in range(1, dom_count) for piece in embed_near
    ]
    next_pairs = over_groups(next_pair)
    both_pairs = [both_pair] + [swapped(piece, "seq", 1) for piece in both_groups[1:]]
    up_parts = own_groups + own_pairs + next_groups + next_pairs + both_groups + both_pairs
    up_offsets = [
        offset ^ bit ^ pair
        for bits in ((0,), (high, low), (high ^ low,))
        for pair in (0, 1)
        for bit in bits
        for offset in near
    ]
    embed_offsets = near + [offset ^ high for offset in near]
    for bit in (low, 1):
        embed_offsets = embed_offsets + [offset ^ bit for offset in embed_offsets]

    begun = first_project(latents, out_weight, returned.pop(0), chunks, width) if chunks > 1 else None
    stepped, features = project_embed(
        ids,
        embed_offsets,
        latents,
        begun,
        returned,
        chunks,
        width,
        out_weight,
        embed_parts,
        norm_gain,
        group_count,
        [*next_pairs[1:], *both_pairs[1:]],
    )
    stepped_other = shifted(stepped, "dom", 1)
    features_other = shifted(features, "dom", 1)

    scale = potential_scale / math.sqrt(tokens * seq_count)
    head = head_weight.reshape(seq_count * dom_count, 1, up_columns)
    partial = reward(
        ids,
        prev_logw,
        [features, features_other],
        up_parts,
        group_count,
        up_offsets,
        head,
        particles,
        scale,
        dom_count * seq_count,
    )
    logits = lax.all_to_all(partial, ("dom", "seq"), 0, 0, tiled=True)
    resampled = resample(ids, ancestors.astype(jnp.int32), stepped, stepped_other)
    return finish(ids, logits, resampled, particles, dom_count)


def solution(mesh):
    in_specs = (
        P(("groups", "dom"), "seq", None),
        P(("groups", "dom"), "seq", None),
        P(("groups", "dom"), "seq", None),
        P(("groups", "dom"), "seq", None),
        P(),
        P("groups"),
        P("seq", None),
        P(),
        P(None, "seq"),
        P(),
        P(("groups", "dom")),
        P(("groups", "dom")),
    )
    out_specs = (P(("groups", "dom"), "seq", None), P(("groups", "dom")))
    return jax.shard_map(
        on_device, mesh=mesh, in_specs=in_specs, out_specs=out_specs, check_vma=False
    )
```

```python
import functools
import math

import jax
import jax.numpy as jnp
from jax import lax
from jax.experimental import pallas as pl
from jax.experimental.pallas import tpu as pltpu
from jax.sharding import PartitionSpec as P

HEADS = 24
STEPS = 28
LANES = 128

potential_scale = 4.0
norm_eps = 1e-05
MIB = 1024 * 1024


def pack_kernel(chunks, width, q_ref, k_ref, v_ref, *out_refs):
    particles, _, model_width = q_ref.shape
    blocks = model_width // width
    part = width // chunks
    for index, ref in enumerate((q_ref, k_ref, v_ref)):
        for particle in range(particles):
            for block in range(blocks):
                for chunk in range(chunks):
                    start = block * width + chunk * part
                    out_refs[chunk][particle * blocks + block, index] = ref[
                        particle, :, start : start + part
                    ]


def pack(queries, keys, values, chunks, width):
    particles, tokens, model_width = queries.shape
    count = particles * model_width // width
    vmem = pl.BlockSpec(memory_space=pltpu.VMEM)
    shape = jax.ShapeDtypeStruct((count, 3, tokens, width // chunks), queries.dtype)
    return list(
        pl.pallas_call(
            functools.partial(pack_kernel, chunks, width),
            in_specs=[vmem] * 3,
            out_specs=[vmem] * chunks,
            out_shape=[shape] * chunks,
            compiler_params=pltpu.CompilerParams(vmem_limit_bytes=60 * MIB),
            name="pack_heads",
        )(queries, keys, values)
    )


def gate_kernel(*refs):
    pass


def gate(array, after):
    hbm = pl.BlockSpec(memory_space=pltpu.HBM)
    return pl.pallas_call(
        gate_kernel,
        in_specs=[hbm] + [pl.BlockSpec(memory_space=pl.ANY)] * len(after),
        out_specs=hbm,
        out_shape=jax.ShapeDtypeStruct(array.shape, array.dtype),
        input_output_aliases={0: 0},
        compiler_params=pltpu.CompilerParams(vmem_limit_bytes=60 * MIB),
        name="gate",
    )(array, *after)


def attention_kernel(head_width, block_sources, qkv_ref, out_ref):
    sources, _, tokens, columns = qkv_ref.shape
    total = sources * tokens
    rows = block_sources * tokens
    factor = 1.0 / math.sqrt(head_width) / math.log(2.0)
    k_all = qkv_ref[:, 1].reshape(total, columns)
    v_all = qkv_ref[:, 2].reshape(total, columns)
    for block in range(0, sources, block_sources):
        span = slice(block, block + block_sources)
        q_all = qkv_ref[span, 0].reshape(rows, columns)
        pieces = []
        for head in range(columns // head_width):
            cols = slice(head * head_width, (head + 1) * head_width)
            scores = lax.dot_general(
                q_all[:, cols],
                k_all[:, cols],
                (((1,), (1,)), ((), ())),
                preferred_element_type=jnp.float32,
            )
            highest = jnp.max(scores, axis=1, keepdims=True)
            expanded = jnp.exp2((scores - highest) * factor)
            norm = 1.0 / jnp.sum(expanded, axis=1, keepdims=True)
            weights = (expanded * norm).astype(jnp.bfloat16)
            pieces.append(jnp.dot(weights, v_all[:, cols], preferred_element_type=jnp.float32))
        joined = jnp.concatenate(pieces, axis=1).astype(jnp.bfloat16)
        out_ref[span] = joined.reshape(block_sources, tokens, columns)


def attention(qkv, head_width):
    sources, _, tokens, columns = qkv.shape
    total = sources * tokens
    block_sources = max(1, min(sources, 512 // tokens))
    while sources % block_sources:
        block_sources -= 1
    step = LANES if columns % LANES == 0 and LANES % head_width == 0 else columns
    scores_bytes = 4 * block_sources * tokens * total
    return pl.pallas_call(
        functools.partial(attention_kernel, head_width, block_sources),
        grid=(columns // step,),
        in_specs=[pl.BlockSpec((sources, 3, tokens, step), lambda i: (0, 0, 0, i))],
        out_specs=pl.BlockSpec((sources, tokens, step), lambda i: (0, 0, i)),
        out_shape=jax.ShapeDtypeStruct((sources, tokens, columns), jnp.bfloat16),
        compiler_params=pltpu.CompilerParams(vmem_limit_bytes=8 * MIB + 6 * scores_bytes),
        cost_estimate=pl.CostEstimate(
            flops=4 * total * total * columns,
            bytes_accessed=8 * total * columns,
            transcendentals=columns // head_width * total * total,
        ),
        name="attention",
    )(qkv)


def column_block(model_width):
    return 512 if model_width % 512 == 0 else model_width


class ProjectionWeights:
    def __init__(self, weight_ref, vmem_ref, sems, chunks, wanted, width):
        depth, model_width = weight_ref.shape
        part = width // chunks
        blocks = depth // width
        self.block = column_block(model_width)
        self.copies = []
        for group in range(model_width // self.block):
            cols = slice(group * self.block, (group + 1) * self.block)
            for index in range(blocks * len(wanted)):
                start = index // len(wanted) * width + wanted[index % len(wanted)] * part
                self.copies.append(
                    pltpu.make_async_copy(
                        weight_ref.at[start : start + part, cols],
                        vmem_ref.at[index * part : (index + 1) * part, cols],
                        sems.at[group, index],
                    )
                )
        self.per_group = blocks * len(wanted)
        for copy in self.copies:
            copy.start()

    def wait(self, group):
        for copy in self.copies[group * self.per_group : (group + 1) * self.per_group]:
            copy.wait()
        return slice(group * self.block, (group + 1) * self.block)


def gather_rows(piece_refs, rows_ref, particles):
    count, tokens, part = piece_refs[0].shape
    blocks = count // particles
    for index in range(blocks * len(piece_refs)):
        ref = piece_refs[index % len(piece_refs)]
        place = index // len(piece_refs)
        for particle in range(particles):
            rows_ref[
                particle * tokens : (particle + 1) * tokens, index * part : (index + 1) * part
            ] = ref[particle * blocks + place]


def first_project_kernel(chunks, width, latents_ref, weight_ref, piece_ref, out_ref, *scratch):
    weight_vmem, rows_ref, sems = scratch
    particles, tokens, model_width = latents_ref.shape
    weights = ProjectionWeights(weight_ref, weight_vmem, sems, chunks, [0], width)
    gather_rows([piece_ref], rows_ref, particles)
    for group in range(model_width // weights.block):
        cols = weights.wait(group)
        flat = latents_ref[:, :, cols].reshape(particles * tokens, weights.block)
        out_ref[:, cols] = flat.astype(jnp.float32) + jnp.dot(
            rows_ref[...], weight_vmem[:, cols], preferred_element_type=jnp.float32
        )


def first_project(latents, out_weight, piece, chunks, width):
    particles, tokens, model_width = latents.shape
    rows, depth = particles * tokens, model_width // chunks
    vmem = pl.BlockSpec(memory_space=pltpu.VMEM)
    return pl.pallas_call(
        functools.partial(first_project_kernel, chunks, width),
        in_specs=[vmem, pl.BlockSpec(memory_space=pltpu.HBM), vmem],
        out_specs=vmem,
        out_shape=jax.ShapeDtypeStruct((rows, model_width), jnp.float32),
        scratch_shapes=[
            pltpu.VMEM((depth, model_width), jnp.bfloat16),
            pltpu.VMEM((rows, depth), jnp.bfloat16),
            pltpu.SemaphoreType.DMA(
                (model_width // column_block(model_width), model_width // width)
            ),
        ],
        compiler_params=pltpu.CompilerParams(vmem_limit_bytes=60 * MIB),
        cost_estimate=pl.CostEstimate(
            flops=2 * rows * depth * model_width,
            bytes_accessed=2 * depth * model_width + 8 * rows * model_width,
            transcendentals=0,
        ),
        name="first_project",
    )(latents, out_weight, piece)


def project_kernel(chunks, width, pieces, parts, offsets, depth_parts, refs_in, refs_out):
    ids_ref, latents_hbm, gain_ref, out_weight_ref = refs_in[:4]
    rest, weight_refs = list(refs_in[4 : 4 + pieces]), refs_in[4 + pieces : 4 + pieces + parts]
    begun_hbm = rest.pop(0) if chunks > 1 else None
    stepped_ref, features_ref = refs_out[:2]
    out_vmem, weight_vmem, rows_ref, clean_ref, embedded_ref = refs_out[2:7]
    latents_ref, begun_ref, out_sems, sems, first_sems = refs_out[7:]
    dom, group, seq = ids_ref[0], ids_ref[1], ids_ref[2]
    sigma = ids_ref[3].astype(jnp.float32) * (1.0 / STEPS)
    particles, tokens, model_width = latents_ref.shape
    rows = particles * tokens
    shards, depth, columns = weight_refs[0].shape
    joined = parts // weight_vmem.shape[0]

    wanted = list(range(chunks - len(rest), chunks))
    block = column_block(model_width)
    first_copies = []
    for index in range(model_width // block):
        cols = slice(index * block, (index + 1) * block)
        first_copies.append(
            pltpu.make_async_copy(
                latents_hbm.at[:, :, cols], latents_ref.at[:, :, cols], first_sems.at[0, index]
            )
        )
        if chunks > 1:
            first_copies.append(
                pltpu.make_async_copy(
                    begun_hbm.at[:, cols], begun_ref.at[:, cols], first_sems.at[1, index]
                )
            )
    for copy in first_copies[: len(first_copies) // (model_width // block)]:
        copy.start()
    out_weights = ProjectionWeights(out_weight_ref, out_vmem, out_sems, chunks, wanted, width)
    for copy in first_copies[len(first_copies) // (model_width // block) :]:
        copy.start()
    copies = []
    for index in range(parts):
        for shard in range(shards):
            start = pl.multiple_of((seq ^ offsets[shard]) * depth, depth)
            copy = pltpu.make_async_copy(
                weight_refs[index].at[shard],
                weight_vmem.at[
                    index // joined,
                    pl.ds(start, depth),
                    index % joined * columns : (index % joined + 1) * columns,
                ],
                sems.at[index],
            )
            copy.start()
            copies.append(copy)

    gather_rows(rest, rows_ref, particles)
    for index in range(model_width // out_weights.block):
        cols = out_weights.wait(index)
        each = len(first_copies) // (model_width // block)
        for copy in first_copies[index * each : (index + 1) * each]:
            copy.wait()
        flat = latents_ref[:, :, cols].reshape(rows, out_weights.block).astype(jnp.float32)
        begun = begun_ref[:, cols] if chunks > 1 else flat
        velocity = begun + jnp.dot(
            rows_ref[...], out_vmem[:, cols], preferred_element_type=jnp.float32
        )
        clean_ref[:, cols] = (flat - sigma * velocity).astype(jnp.bfloat16)
        stepped_ref[:, :, cols] = (
            (flat - velocity * (1.0 / STEPS))
            .astype(jnp.bfloat16)
            .reshape(particles, tokens, out_weights.block)
        )

    doms = parts // depth_parts
    for step in range(parts // joined):
        for copy in copies[step * joined * shards : (step + 1) * joined * shards]:
            copy.wait()
        product = jnp.dot(clean_ref[...], weight_vmem[step], preferred_element_type=jnp.float32)
        for lane in range(joined):
            index = step * joined + lane
            dom_of = (dom + doms - index // depth_parts) % doms
            group_of = (group + depth_parts - index % depth_parts) % depth_parts
            embedded_ref[dom_of * depth_parts + group_of] = product[
                :, lane * columns : (lane + 1) * columns
            ]
    count = parts * columns
    blocks = [embedded_ref[index] for index in range(parts)]
    centre = sum(jnp.sum(piece, axis=1, keepdims=True) for piece in blocks) * (1.0 / count)
    blocks = [piece - centre for piece in blocks]
    variance = sum(jnp.sum(piece * piece, axis=1, keepdims=True) for piece in blocks) * (
        1.0 / count
    )
    inverse = lax.rsqrt(variance + norm_eps)
    share = features_ref.shape[2]
    for index, piece in enumerate(blocks):
        cols = slice(index * columns, (index + 1) * columns)
        feature = jax.nn.gelu(piece * inverse * gain_ref[:, cols]).astype(jnp.bfloat16)
        start = index * columns % share
        features_ref[index * columns // share, :, start : start + columns] = feature


def project_embed(
    ids,
    offsets,
    latents,
    begun,
    attended,
    chunks,
    width,
    out_weight,
    weights,
    gain,
    depth_parts,
    after,
):
    particles, tokens, model_width = latents.shape
    rows = particles * tokens
    parts = len(weights)
    columns = weights[0].shape[2]
    count = parts * columns
    out_depth = model_width * len(attended) // chunks
    pieces = ([] if begun is None else [begun]) + attended
    joined = 2 if columns % LANES == 0 and parts % 2 == 0 else 1
    vmem = pl.BlockSpec(memory_space=pltpu.VMEM)
    smem = pl.BlockSpec(memory_space=pltpu.SMEM)
    hbm = pl.BlockSpec(memory_space=pltpu.HBM)
    inputs = 4 + len(pieces) + parts + len(after)
    groups = model_width // column_block(model_width)

    def kernel(*refs):
        project_kernel(
            chunks,
            width,
            len(pieces),
            parts,
            offsets,
            depth_parts,
            refs[:inputs],
            refs[inputs:],
        )

    return pl.pallas_call(
        kernel,
        in_specs=[smem, hbm, vmem, hbm]
        + ([] if begun is None else [hbm])
        + [vmem] * len(attended)
        + [hbm] * parts
        + [pl.BlockSpec(memory_space=pl.ANY)] * len(after),
        out_specs=[vmem, vmem],
        out_shape=[
            jax.ShapeDtypeStruct(latents.shape, jnp.bfloat16),
            jax.ShapeDtypeStruct((depth_parts, rows, count // depth_parts), jnp.bfloat16),
        ],
        scratch_shapes=[
            pltpu.VMEM((out_depth, model_width), jnp.bfloat16),
            pltpu.VMEM((parts // joined, model_width, joined * columns), jnp.bfloat16),
            pltpu.VMEM((rows, out_depth), jnp.bfloat16),
            pltpu.VMEM((rows, model_width), jnp.bfloat16),
            pltpu.VMEM((parts, rows, columns), jnp.float32),
            pltpu.VMEM(latents.shape, latents.dtype),
            pltpu.VMEM((rows, model_width), jnp.float32),
            pltpu.SemaphoreType.DMA((groups, model_width // width * len(attended))),
            pltpu.SemaphoreType.DMA((parts,)),
            pltpu.SemaphoreType.DMA((2, groups)),
        ],
        compiler_params=pltpu.CompilerParams(vmem_limit_bytes=60 * MIB),
        cost_estimate=pl.CostEstimate(
            flops=2 * rows * model_width * (out_depth + count),
            bytes_accessed=2 * model_width * (out_depth + count) + 12 * rows * model_width,
            transcendentals=rows * count,
        ),
        name="project_embed",
    )(ids, latents, gain.reshape(1, count), out_weight, *pieces, *weights, *after)


def reward_kernel(particles, scale, parts, doms, offsets, joined, *refs):
    ids_ref, prev_ref, head_ref = refs[:3]
    features_refs, weight_refs = refs[3 : 3 + doms], refs[3 + doms : -4]
    out_ref, weight_vmem, rows_ref, sems = refs[-4:]
    dom, group, seq = ids_ref[0], ids_ref[1], ids_ref[2]
    _, depth, columns = weight_refs[0].shape
    rows = features_refs[0].shape[1]
    places = [
        (pair, shard)
        for pair in range(len(weight_refs) // parts)
        for shard in range(weight_refs[pair * parts].shape[0])
    ]
    count = len(places)

    copies = []
    for place, (pair, shard) in enumerate(places):
        lane = place % joined * columns
        for index in range(parts):
            copy = pltpu.make_async_copy(
                weight_refs[pair * parts + index].at[shard],
                weight_vmem.at[
                    place // joined,
                    index * depth : (index + 1) * depth,
                    lane : lane + columns,
                ],
                sems.at[place, index],
            )
            copy.start()
            copies.append(copy)
    for step, features_ref in enumerate(features_refs):
        for index in range(parts):
            rows_ref[step * rows : (step + 1) * rows, index * depth : (index + 1) * depth] = (
                features_ref[(group + parts - index) % parts]
            )
    totals = jnp.zeros((doms * particles, joined * columns), jnp.float32)
    for step in range(count // joined):
        for copy in copies[step * joined * parts : (step + 1) * joined * parts]:
            copy.wait()
        hidden = jnp.dot(rows_ref[...], weight_vmem[step], preferred_element_type=jnp.float32)
        head = jnp.concatenate(
            [
                head_ref[(seq ^ offset) * doms + dom]
                for offset in offsets[step * joined : (step + 1) * joined]
            ],
            axis=1,
        )
        scored = jax.nn.gelu(hidden) * head
        totals += jnp.sum(scored.reshape(doms * particles, rows // particles, -1), axis=1)

    sums = jnp.sum(totals, axis=1, keepdims=True) * scale
    shape = out_ref.shape[1:]
    out_rows = lax.broadcasted_iota(jnp.int32, shape, 0)
    lanes = lax.broadcasted_iota(jnp.int32, shape, 1)
    logits = jnp.zeros(shape, jnp.float32)
    for index in range(doms * particles):
        step, particle = divmod(index, particles)
        value = sums[index : index + 1]
        if step == 0:
            value = value + jnp.where(seq == 0, prev_ref[particle], 0.0)
        here = jnp.logical_and(out_rows == (dom + doms - step) % doms, lanes == particle)
        logits += jnp.where(here, value, 0.0)
    out_ref[...] = jnp.broadcast_to(logits[None], out_ref.shape)


def reward(ids, prev_logw, features, weights, parts, offsets, head, particles, scale, copies):
    _, depth, columns = weights[0].shape
    rows, doms = features[0].shape[1], len(features)
    count = len(offsets)
    joined = next(n for n in (4, 2, 1) if n == 1 or columns % LANES == 0 == count % n)
    smem = pl.BlockSpec(memory_space=pltpu.SMEM)
    vmem = pl.BlockSpec(memory_space=pltpu.VMEM)
    return pl.pallas_call(
        functools.partial(reward_kernel, particles, scale, parts, doms, offsets, joined),
        in_specs=[smem, smem, vmem]
        + [vmem] * doms
        + [pl.BlockSpec(memory_space=pltpu.HBM)] * len(weights),
        out_specs=vmem,
        out_shape=jax.ShapeDtypeStruct((copies, 8, LANES), jnp.float32),
        scratch_shapes=[
            pltpu.VMEM((count // joined, parts * depth, joined * columns), jnp.bfloat16),
            pltpu.VMEM((doms * rows, parts * depth), jnp.bfloat16),
            pltpu.SemaphoreType.DMA((count, parts)),
        ],
        compiler_params=pltpu.CompilerParams(vmem_limit_bytes=60 * MIB),
        cost_estimate=pl.CostEstimate(
            flops=2 * doms * rows * parts * depth * count * columns,
            bytes_accessed=2 * parts * depth * count * columns,
            transcendentals=doms * rows * count * columns,
        ),
        name="reward",
    )(ids, prev_logw, head, *features, *weights)


def finish_kernel(particles, doms, ids_ref, resampled_ref, parts_ref, out_ref, same_ref):
    logits = jnp.sum(parts_ref[...], axis=0)
    rows = lax.broadcasted_iota(jnp.int32, logits.shape, 0)
    lanes = lax.broadcasted_iota(jnp.int32, logits.shape, 1)
    valid = jnp.logical_and(rows < doms, lanes < particles)
    highest = jnp.max(jnp.where(valid, logits, -jnp.inf))
    total = jnp.sum(jnp.where(valid, jnp.exp(logits - highest), 0.0), axis=1, keepdims=True)
    log_total = highest + jnp.log(jnp.sum(total, axis=0, keepdims=True))
    own = jnp.sum(jnp.where(rows == ids_ref[0], logits, 0.0), axis=0, keepdims=True)
    out_ref[...] = (own - log_total)[:, :particles]


def finish(ids, parts, resampled, particles, doms):
    vmem = pl.BlockSpec(memory_space=pltpu.VMEM)
    anywhere = pl.BlockSpec(memory_space=pl.ANY)
    log_weights, resampled = pl.pallas_call(
        functools.partial(finish_kernel, particles, doms),
        in_specs=[pl.BlockSpec(memory_space=pltpu.SMEM), anywhere, vmem],
        out_specs=[vmem, anywhere],
        out_shape=[
            jax.ShapeDtypeStruct((1, particles), jnp.float32),
            jax.ShapeDtypeStruct(resampled.shape, resampled.dtype),
        ],
        input_output_aliases={1: 1},
        compiler_params=pltpu.CompilerParams(vmem_limit_bytes=2 * MIB),
        name="log_weights",
    )(ids, resampled, parts)
    return resampled, log_weights.reshape(particles)


def resample_kernel(ids_ref, ancestors_ref, own_ref, other_ref, out_ref):
    index = pl.program_id(0)
    own = ancestors_ref[index] // pl.num_programs(0) == ids_ref[0]

    @pl.when(own)
    def _():
        out_ref[...] = own_ref[...]

    @pl.when(jnp.logical_not(own))
    def _():
        out_ref[...] = other_ref[...]


def resample(ids, ancestors, own, other):
    particles, tokens, columns = own.shape
    block = (1, tokens, columns)
    parent = pl.BlockSpec(block, lambda i, ids, ancestors: (ancestors[i] % particles, 0, 0))
    return pl.pallas_call(
        resample_kernel,
        grid_spec=pltpu.PrefetchScalarGridSpec(
            num_scalar_prefetch=2,
            grid=(particles,),
            in_specs=[parent, parent],
            out_specs=pl.BlockSpec(block, lambda i, ids, ancestors: (i, 0, 0)),
        ),
        out_shape=jax.ShapeDtypeStruct(own.shape, own.dtype),
        compiler_params=pltpu.CompilerParams(vmem_limit_bytes=4 * MIB),
        name="resample",
    )(ids, ancestors, own, other)


def shifted(array, axis, step):
    count = lax.axis_size(axis)
    return lax.ppermute(array, axis, [(i, (i + step) % count) for i in range(count)])


def swapped(array, axis, bit):
    return lax.ppermute(array, axis, [(i, i ^ bit) for i in range(lax.axis_size(axis))])


def exchange(array):
    return lax.all_to_all(array, "seq", 0, 0, tiled=True)


def on_device(
    latents,
    queries,
    keys,
    values,
    out_weight,
    step_index,
    embed_weight,
    norm_gain,
    up_weight,
    head_weight,
    prev_logw,
    ancestors,
):
    seq_count = lax.axis_size("seq")
    group_count = lax.axis_size("groups")
    dom_count = lax.axis_size("dom")
    holders = group_count * dom_count
    dom = lax.axis_index("dom")
    group = lax.axis_index("groups")
    seq = lax.axis_index("seq")
    particles, tokens, model_width = latents.shape
    head_width = model_width // HEADS
    width = particles * model_width // seq_count
    chunks = 2 if width % (2 * LANES) == 0 else 1

    ids = jnp.stack([dom, group, seq, step_index[0]]).astype(jnp.int32)

    embed_columns = embed_weight.shape[1] // holders
    embed_share = lax.dynamic_slice_in_dim(
        embed_weight, (dom * group_count + group) * embed_columns, embed_columns, 1
    )[None]
    up_depth = up_weight.shape[0] // group_count
    up_columns = up_weight.shape[1] // dom_count
    up_share = lax.dynamic_slice(
        up_weight, (group * up_depth, dom * up_columns), (up_depth, up_columns)
    )[None]
    bits = [1 << place for place in reversed(range(1, seq_count.bit_length() - 1))]
    near = [0]
    for bit in bits[:-2]:
        embed_share = jnp.concatenate([embed_share, swapped(embed_share, "seq", bit)])
        up_share = jnp.concatenate([up_share, swapped(up_share, "seq", bit)])
        near = near + [offset ^ bit for offset in near]
    high, low = bits[-2:]

    def over_groups(array):
        return [array] + [shifted(array, "groups", k) for k in range(1, group_count)]

    packed = pack(queries, keys, values, chunks, width)
    embed_share = jnp.concatenate([embed_share, swapped(embed_share, "seq", high)])
    packed[0] = gate(packed[0], [embed_share])

    arrived = [exchange(packed[0])]
    up_high, up_low = swapped(up_share, "seq", high), swapped(up_share, "seq", low)
    own_pair, own_groups = swapped(up_share, "seq", 1), over_groups(up_share)
    for bit in (low, 1):
        embed_share = jnp.concatenate([embed_share, swapped(embed_share, "seq", bit)])
    after = [embed_share, up_high, up_low, own_pair, *own_groups[1:]]
    packed[1:] = [gate(piece, after) for piece in packed[1:]]

    arrived += [exchange(piece) for piece in packed[1:]]
    up_both = swapped(up_high, "seq", low)
    up_next = jnp.concatenate([up_high, up_low])
    next_pair, next_groups = swapped(up_next, "seq", 1), over_groups(up_next)
    embed_near = over_groups(embed_share)
    attended = [attention(arrived[0], head_width)]
    after = [up_both, next_pair, *next_groups[1:], *embed_near[1:]]
    attended[0] = gate(attended[0], after)

    returned = [exchange(attended[0])]
    both_pair, both_groups = swapped(up_both, "seq", 1), over_groups(up_both)
    own_pairs = over_groups(own_pair)
    attended += [attention(piece, head_width) for piece in arrived[1:]]
    after = [both_pair, *both_groups[1:], *own_pairs[1:]]
    attended[1:] = [gate(piece, after) for piece in attended[1:]]

    returned += [exchange(piece) for piece in attended[1:]]
    embed_parts = embed_near + [
        shifted(piece, "dom", k) for k in range(1, dom_count) for piece in embed_near
    ]
    next_pairs = over_groups(next_pair)
    both_pairs = [both_pair] + [swapped(piece, "seq", 1) for piece in both_groups[1:]]
    up_parts = own_groups + own_pairs + next_groups + next_pairs + both_groups + both_pairs
    up_offsets = [
        offset ^ bit ^ pair
        for bits in ((0,), (high, low), (high ^ low,))
        for pair in (0, 1)
        for bit in bits
        for offset in near
    ]
    embed_offsets = near + [offset ^ high for offset in near]
    for bit in (low, 1):
        embed_offsets = embed_offsets + [offset ^ bit for offset in embed_offsets]

    begun = first_project(latents, out_weight, returned.pop(0), chunks, width) if chunks > 1 else None
    stepped, features = project_embed(
        ids,
        embed_offsets,
        latents,
        begun,
        returned,
        chunks,
        width,
        out_weight,
        embed_parts,
        norm_gain,
        group_count,
        [*next_pairs[1:], *both_pairs[1:]],
    )
    stepped_other = shifted(stepped, "dom", 1)
    features_other = shifted(features, "dom", 1)

    scale = potential_scale / math.sqrt(tokens * seq_count)
    head = head_weight.reshape(seq_count * dom_count, 1, up_columns)
    partial = reward(
        ids,
        prev_logw,
        [features, features_other],
        up_parts,
        group_count,
        up_offsets,
        head,
        particles,
        scale,
        dom_count * seq_count,
    )
    logits = lax.all_to_all(partial, ("dom", "seq"), 0, 0, tiled=True)
    resampled = resample(ids, ancestors.astype(jnp.int32), stepped, stepped_other)
    return finish(ids, logits, resampled, particles, dom_count)


def solution(mesh):
    in_specs = (
        P(("groups", "dom"), "seq", None),
        P(("groups", "dom"), "seq", None),
        P(("groups", "dom"), "seq", None),
        P(("groups", "dom"), "seq", None),
        P(),
        P("groups"),
        P("seq", None),
        P(),
        P(None, "seq"),
        P(),
        P(("groups", "dom")),
        P(("groups", "dom")),
    )
    out_specs = (P(("groups", "dom"), "seq", None), P(("groups", "dom")))
    return jax.shard_map(
        on_device, mesh=mesh, in_specs=in_specs, out_specs=out_specs, check_vma=False
    )
```

```python
import functools
import math

import jax
import jax.numpy as jnp
from jax import lax
from jax.experimental import pallas as pl
from jax.experimental.pallas import tpu as pltpu
from jax.sharding import PartitionSpec as P

HEADS = 24
STEPS = 28
LANES = 128

potential_scale = 4.0
norm_eps = 1e-05
MIB = 1024 * 1024


def pack_kernel(chunks, width, q_ref, k_ref, v_ref, *out_refs):
    particles, _, model_width = q_ref.shape
    blocks = model_width // width
    part = width // chunks
    for index, ref in enumerate((q_ref, k_ref, v_ref)):
        for particle in range(particles):
            for block in range(blocks):
                for chunk in range(chunks):
                    start = block * width + chunk * part
                    out_refs[chunk][particle * blocks + block, index] = ref[
                        particle, :, start : start + part
                    ]


def pack(queries, keys, values, chunks, width):
    particles, tokens, model_width = queries.shape
    count = particles * model_width // width
    vmem = pl.BlockSpec(memory_space=pltpu.VMEM)
    shape = jax.ShapeDtypeStruct((count, 3, tokens, width // chunks), queries.dtype)
    return list(
        pl.pallas_call(
            functools.partial(pack_kernel, chunks, width),
            in_specs=[vmem] * 3,
            out_specs=[vmem] * chunks,
            out_shape=[shape] * chunks,
            compiler_params=pltpu.CompilerParams(vmem_limit_bytes=60 * MIB),
            name="pack_heads",
        )(queries, keys, values)
    )


def gate_kernel(*refs):
    pass


def gate(array, after):
    hbm = pl.BlockSpec(memory_space=pltpu.HBM)
    return pl.pallas_call(
        gate_kernel,
        in_specs=[hbm] + [pl.BlockSpec(memory_space=pl.ANY)] * len(after),
        out_specs=hbm,
        out_shape=jax.ShapeDtypeStruct(array.shape, array.dtype),
        input_output_aliases={0: 0},
        compiler_params=pltpu.CompilerParams(vmem_limit_bytes=60 * MIB),
        name="gate",
    )(array, *after)


def attention_kernel(head_width, block_sources, qkv_ref, out_ref):
    sources, _, tokens, columns = qkv_ref.shape
    total = sources * tokens
    rows = block_sources * tokens
    factor = 1.0 / math.sqrt(head_width) / math.log(2.0)
    k_all = qkv_ref[:, 1].reshape(total, columns)
    v_all = qkv_ref[:, 2].reshape(total, columns)
    for block in range(0, sources, block_sources):
        span = slice(block, block + block_sources)
        q_all = qkv_ref[span, 0].reshape(rows, columns)
        pieces = []
        for head in range(columns // head_width):
            cols = slice(head * head_width, (head + 1) * head_width)
            scores = lax.dot_general(
                q_all[:, cols],
                k_all[:, cols],
                (((1,), (1,)), ((), ())),
                preferred_element_type=jnp.float32,
            )
            highest = jnp.max(scores, axis=1, keepdims=True)
            expanded = jnp.exp2((scores - highest) * factor)
            norm = 1.0 / jnp.sum(expanded, axis=1, keepdims=True)
            weights = (expanded * norm).astype(jnp.bfloat16)
            pieces.append(jnp.dot(weights, v_all[:, cols], preferred_element_type=jnp.float32))
        joined = jnp.concatenate(pieces, axis=1).astype(jnp.bfloat16)
        out_ref[span] = joined.reshape(block_sources, tokens, columns)


def attention(qkv, head_width):
    sources, _, tokens, columns = qkv.shape
    total = sources * tokens
    block_sources = max(1, min(sources, 512 // tokens))
    while sources % block_sources:
        block_sources -= 1
    step = LANES if columns % LANES == 0 and LANES % head_width == 0 else columns
    scores_bytes = 4 * block_sources * tokens * total
    return pl.pallas_call(
        functools.partial(attention_kernel, head_width, block_sources),
        grid=(columns // step,),
        in_specs=[pl.BlockSpec((sources, 3, tokens, step), lambda i: (0, 0, 0, i))],
        out_specs=pl.BlockSpec((sources, tokens, step), lambda i: (0, 0, i)),
        out_shape=jax.ShapeDtypeStruct((sources, tokens, columns), jnp.bfloat16),
        compiler_params=pltpu.CompilerParams(vmem_limit_bytes=8 * MIB + 6 * scores_bytes),
        cost_estimate=pl.CostEstimate(
            flops=4 * total * total * columns,
            bytes_accessed=8 * total * columns,
            transcendentals=columns // head_width * total * total,
        ),
        name="attention",
    )(qkv)


def column_block(model_width):
    return 512 if model_width % 512 == 0 else model_width


class ProjectionWeights:
    def __init__(self, weight_ref, vmem_ref, sems, chunks, wanted, width):
        depth, model_width = weight_ref.shape
        part = width // chunks
        blocks = depth // width
        self.block = column_block(model_width)
        self.copies = []
        for group in range(model_width // self.block):
            cols = slice(group * self.block, (group + 1) * self.block)
            for index in range(blocks * len(wanted)):
                start = index // len(wanted) * width + wanted[index % len(wanted)] * part
                self.copies.append(
                    pltpu.make_async_copy(
                        weight_ref.at[start : start + part, cols],
                        vmem_ref.at[index * part : (index + 1) * part, cols],
                        sems.at[group, index],
                    )
                )
        self.per_group = blocks * len(wanted)
        for copy in self.copies:
            copy.start()

    def wait(self, group):
        for copy in self.copies[group * self.per_group : (group + 1) * self.per_group]:
            copy.wait()
        return slice(group * self.block, (group + 1) * self.block)


def gather_rows(piece_refs, rows_ref, particles):
    count, tokens, part = piece_refs[0].shape
    blocks = count // particles
    for index in range(blocks * len(piece_refs)):
        ref = piece_refs[index % len(piece_refs)]
        place = index // len(piece_refs)
        for particle in range(particles):
            rows_ref[
                particle * tokens : (particle + 1) * tokens, index * part : (index + 1) * part
            ] = ref[particle * blocks + place]


def first_project_kernel(chunks, width, latents_ref, weight_ref, piece_ref, out_ref, *scratch):
    weight_vmem, rows_ref, sems = scratch
    particles, tokens, model_width = latents_ref.shape
    weights = ProjectionWeights(weight_ref, weight_vmem, sems, chunks, [0], width)
    gather_rows([piece_ref], rows_ref, particles)
    for group in range(model_width // weights.block):
        cols = weights.wait(group)
        flat = latents_ref[:, :, cols].reshape(particles * tokens, weights.block)
        out_ref[:, cols] = flat.astype(jnp.float32) + jnp.dot(
            rows_ref[...], weight_vmem[:, cols], preferred_element_type=jnp.float32
        )


def first_project(latents, out_weight, piece, chunks, width):
    particles, tokens, model_width = latents.shape
    rows, depth = particles * tokens, model_width // chunks
    vmem = pl.BlockSpec(memory_space=pltpu.VMEM)
    return pl.pallas_call(
        functools.partial(first_project_kernel, chunks, width),
        in_specs=[vmem, pl.BlockSpec(memory_space=pltpu.HBM), vmem],
        out_specs=vmem,
        out_shape=jax.ShapeDtypeStruct((rows, model_width), jnp.float32),
        scratch_shapes=[
            pltpu.VMEM((depth, model_width), jnp.bfloat16),
            pltpu.VMEM((rows, depth), jnp.bfloat16),
            pltpu.SemaphoreType.DMA(
                (model_width // column_block(model_width), model_width // width)
            ),
        ],
        compiler_params=pltpu.CompilerParams(vmem_limit_bytes=60 * MIB),
        cost_estimate=pl.CostEstimate(
            flops=2 * rows * depth * model_width,
            bytes_accessed=2 * depth * model_width + 8 * rows * model_width,
            transcendentals=0,
        ),
        name="first_project",
    )(latents, out_weight, piece)


def project_kernel(chunks, width, pieces, parts, offsets, depth_parts, refs_in, refs_out):
    ids_ref, latents_hbm, gain_ref, out_weight_ref = refs_in[:4]
    rest, weight_refs = list(refs_in[4 : 4 + pieces]), refs_in[4 + pieces : 4 + pieces + parts]
    begun_hbm = rest.pop(0) if chunks > 1 else None
    stepped_ref, features_ref = refs_out[:2]
    out_vmem, weight_vmem, rows_ref, clean_ref, embedded_ref = refs_out[2:7]
    latents_ref, begun_ref, out_sems, sems, first_sems = refs_out[7:]
    dom, group, seq = ids_ref[0], ids_ref[1], ids_ref[2]
    sigma = ids_ref[3].astype(jnp.float32) * (1.0 / STEPS)
    particles, tokens, model_width = latents_ref.shape
    rows = particles * tokens
    shards, depth, columns = weight_refs[0].shape
    joined = parts // weight_vmem.shape[0]

    wanted = list(range(chunks - len(rest), chunks))
    block = column_block(model_width)
    first_copies = []
    for index in range(model_width // block):
        cols = slice(index * block, (index + 1) * block)
        first_copies.append(
            pltpu.make_async_copy(
                latents_hbm.at[:, :, cols], latents_ref.at[:, :, cols], first_sems.at[0, index]
            )
        )
        if chunks > 1:
            first_copies.append(
                pltpu.make_async_copy(
                    begun_hbm.at[:, cols], begun_ref.at[:, cols], first_sems.at[1, index]
                )
            )
    for copy in first_copies[: len(first_copies) // (model_width // block)]:
        copy.start()
    out_weights = ProjectionWeights(out_weight_ref, out_vmem, out_sems, chunks, wanted, width)
    for copy in first_copies[len(first_copies) // (model_width // block) :]:
        copy.start()
    copies = []
    for index in range(parts):
        for shard in range(shards):
            start = pl.multiple_of((seq ^ offsets[shard]) * depth, depth)
            copy = pltpu.make_async_copy(
                weight_refs[index].at[shard],
                weight_vmem.at[
                    index // joined,
                    pl.ds(start, depth),
                    index % joined * columns : (index % joined + 1) * columns,
                ],
                sems.at[index],
            )
            copy.start()
            copies.append(copy)

    gather_rows(rest, rows_ref, particles)
    for index in range(model_width // out_weights.block):
        cols = out_weights.wait(index)
        each = len(first_copies) // (model_width // block)
        for copy in first_copies[index * each : (index + 1) * each]:
            copy.wait()
        flat = latents_ref[:, :, cols].reshape(rows, out_weights.block).astype(jnp.float32)
        begun = begun_ref[:, cols] if chunks > 1 else flat
        velocity = begun + jnp.dot(
            rows_ref[...], out_vmem[:, cols], preferred_element_type=jnp.float32
        )
        clean_ref[:, cols] = (flat - sigma * velocity).astype(jnp.bfloat16)
        stepped_ref[:, :, cols] = (
            (flat - velocity * (1.0 / STEPS))
            .astype(jnp.bfloat16)
            .reshape(particles, tokens, out_weights.block)
        )

    doms = parts // depth_parts
    for step in range(parts // joined):
        for copy in copies[step * joined * shards : (step + 1) * joined * shards]:
            copy.wait()
        product = jnp.dot(clean_ref[...], weight_vmem[step], preferred_element_type=jnp.float32)
        for lane in range(joined):
            index = step * joined + lane
            dom_of = (dom + doms - index // depth_parts) % doms
            group_of = (group + depth_parts - index % depth_parts) % depth_parts
            embedded_ref[dom_of * depth_parts + group_of] = product[
                :, lane * columns : (lane + 1) * columns
            ]
    count = parts * columns
    blocks = [embedded_ref[index] for index in range(parts)]
    centre = sum(jnp.sum(piece, axis=1, keepdims=True) for piece in blocks) * (1.0 / count)
    blocks = [piece - centre for piece in blocks]
    variance = sum(jnp.sum(piece * piece, axis=1, keepdims=True) for piece in blocks) * (
        1.0 / count
    )
    inverse = lax.rsqrt(variance + norm_eps)
    share = features_ref.shape[2]
    for index, piece in enumerate(blocks):
        cols = slice(index * columns, (index + 1) * columns)
        feature = jax.nn.gelu(piece * inverse * gain_ref[:, cols]).astype(jnp.bfloat16)
        start = index * columns % share
        features_ref[index * columns // share, :, start : start + columns] = feature


def project_embed(
    ids,
    offsets,
    latents,
    begun,
    attended,
    chunks,
    width,
    out_weight,
    weights,
    gain,
    depth_parts,
    after,
):
    particles, tokens, model_width = latents.shape
    rows = particles * tokens
    parts = len(weights)
    columns = weights[0].shape[2]
    count = parts * columns
    out_depth = model_width * len(attended) // chunks
    pieces = ([] if begun is None else [begun]) + attended
    joined = next(n for n in (4, 2, 1) if n == 1 or columns % LANES == 0 == parts % n)
    vmem = pl.BlockSpec(memory_space=pltpu.VMEM)
    smem = pl.BlockSpec(memory_space=pltpu.SMEM)
    hbm = pl.BlockSpec(memory_space=pltpu.HBM)
    inputs = 4 + len(pieces) + parts + len(after)
    groups = model_width // column_block(model_width)

    def kernel(*refs):
        project_kernel(
            chunks,
            width,
            len(pieces),
            parts,
            offsets,
            depth_parts,
            refs[:inputs],
            refs[inputs:],
        )

    return pl.pallas_call(
        kernel,
        in_specs=[smem, hbm, vmem, hbm]
        + ([] if begun is None else [hbm])
        + [vmem] * len(attended)
        + [hbm] * parts
        + [pl.BlockSpec(memory_space=pl.ANY)] * len(after),
        out_specs=[vmem, vmem],
        out_shape=[
            jax.ShapeDtypeStruct(latents.shape, jnp.bfloat16),
            jax.ShapeDtypeStruct((depth_parts, rows, count // depth_parts), jnp.bfloat16),
        ],
        scratch_shapes=[
            pltpu.VMEM((out_depth, model_width), jnp.bfloat16),
            pltpu.VMEM((parts // joined, model_width, joined * columns), jnp.bfloat16),
            pltpu.VMEM((rows, out_depth), jnp.bfloat16),
            pltpu.VMEM((rows, model_width), jnp.bfloat16),
            pltpu.VMEM((parts, rows, columns), jnp.float32),
            pltpu.VMEM(latents.shape, latents.dtype),
            pltpu.VMEM((rows, model_width), jnp.float32),
            pltpu.SemaphoreType.DMA((groups, model_width // width * len(attended))),
            pltpu.SemaphoreType.DMA((parts,)),
            pltpu.SemaphoreType.DMA((2, groups)),
        ],
        compiler_params=pltpu.CompilerParams(vmem_limit_bytes=60 * MIB),
        cost_estimate=pl.CostEstimate(
            flops=2 * rows * model_width * (out_depth + count),
            bytes_accessed=2 * model_width * (out_depth + count) + 12 * rows * model_width,
            transcendentals=rows * count,
        ),
        name="project_embed",
    )(ids, latents, gain.reshape(1, count), out_weight, *pieces, *weights, *after)


def reward_kernel(particles, scale, parts, doms, offsets, joined, *refs):
    ids_ref, prev_ref, head_ref = refs[:3]
    features_refs, weight_refs = refs[3 : 3 + doms], refs[3 + doms : -4]
    out_ref, weight_vmem, rows_ref, sems = refs[-4:]
    dom, group, seq = ids_ref[0], ids_ref[1], ids_ref[2]
    _, depth, columns = weight_refs[0].shape
    rows = features_refs[0].shape[1]
    places = [
        (pair, shard)
        for pair in range(len(weight_refs) // parts)
        for shard in range(weight_refs[pair * parts].shape[0])
    ]
    count = len(places)

    copies = []
    for place, (pair, shard) in enumerate(places):
        lane = place % joined * columns
        for index in range(parts):
            copy = pltpu.make_async_copy(
                weight_refs[pair * parts + index].at[shard],
                weight_vmem.at[
                    place // joined,
                    index * depth : (index + 1) * depth,
                    lane : lane + columns,
                ],
                sems.at[place, index],
            )
            copy.start()
            copies.append(copy)
    for step, features_ref in enumerate(features_refs):
        for index in range(parts):
            rows_ref[step * rows : (step + 1) * rows, index * depth : (index + 1) * depth] = (
                features_ref[(group + parts - index) % parts]
            )
    totals = jnp.zeros((doms * particles, joined * columns), jnp.float32)
    for step in range(count // joined):
        for copy in copies[step * joined * parts : (step + 1) * joined * parts]:
            copy.wait()
        hidden = jnp.dot(rows_ref[...], weight_vmem[step], preferred_element_type=jnp.float32)
        head = jnp.concatenate(
            [
                head_ref[(seq ^ offset) * doms + dom]
                for offset in offsets[step * joined : (step + 1) * joined]
            ],
            axis=1,
        )
        scored = jax.nn.gelu(hidden) * head
        totals += jnp.sum(scored.reshape(doms * particles, rows // particles, -1), axis=1)

    sums = jnp.sum(totals, axis=1, keepdims=True) * scale
    shape = out_ref.shape[1:]
    out_rows = lax.broadcasted_iota(jnp.int32, shape, 0)
    lanes = lax.broadcasted_iota(jnp.int32, shape, 1)
    logits = jnp.zeros(shape, jnp.float32)
    for index in range(doms * particles):
        step, particle = divmod(index, particles)
        value = sums[index : index + 1]
        if step == 0:
            value = value + jnp.where(seq == 0, prev_ref[particle], 0.0)
        here = jnp.logical_and(out_rows == (dom + doms - step) % doms, lanes == particle)
        logits += jnp.where(here, value, 0.0)
    out_ref[...] = jnp.broadcast_to(logits[None], out_ref.shape)


def reward(ids, prev_logw, features, weights, parts, offsets, head, particles, scale, copies):
    _, depth, columns = weights[0].shape
    rows, doms = features[0].shape[1], len(features)
    count = len(offsets)
    joined = next(n for n in (4, 2, 1) if n == 1 or columns % LANES == 0 == count % n)
    smem = pl.BlockSpec(memory_space=pltpu.SMEM)
    vmem = pl.BlockSpec(memory_space=pltpu.VMEM)
    return pl.pallas_call(
        functools.partial(reward_kernel, particles, scale, parts, doms, offsets, joined),
        in_specs=[smem, smem, vmem]
        + [vmem] * doms
        + [pl.BlockSpec(memory_space=pltpu.HBM)] * len(weights),
        out_specs=vmem,
        out_shape=jax.ShapeDtypeStruct((copies, 8, LANES), jnp.float32),
        scratch_shapes=[
            pltpu.VMEM((count // joined, parts * depth, joined * columns), jnp.bfloat16),
            pltpu.VMEM((doms * rows, parts * depth), jnp.bfloat16),
            pltpu.SemaphoreType.DMA((count, parts)),
        ],
        compiler_params=pltpu.CompilerParams(vmem_limit_bytes=60 * MIB),
        cost_estimate=pl.CostEstimate(
            flops=2 * doms * rows * parts * depth * count * columns,
            bytes_accessed=2 * parts * depth * count * columns,
            transcendentals=doms * rows * count * columns,
        ),
        name="reward",
    )(ids, prev_logw, head, *features, *weights)


def finish_kernel(particles, doms, ids_ref, resampled_ref, parts_ref, out_ref, same_ref):
    logits = jnp.sum(parts_ref[...], axis=0)
    rows = lax.broadcasted_iota(jnp.int32, logits.shape, 0)
    lanes = lax.broadcasted_iota(jnp.int32, logits.shape, 1)
    valid = jnp.logical_and(rows < doms, lanes < particles)
    highest = jnp.max(jnp.where(valid, logits, -jnp.inf))
    total = jnp.sum(jnp.where(valid, jnp.exp(logits - highest), 0.0), axis=1, keepdims=True)
    log_total = highest + jnp.log(jnp.sum(total, axis=0, keepdims=True))
    own = jnp.sum(jnp.where(rows == ids_ref[0], logits, 0.0), axis=0, keepdims=True)
    out_ref[...] = (own - log_total)[:, :particles]


def finish(ids, parts, resampled, particles, doms):
    vmem = pl.BlockSpec(memory_space=pltpu.VMEM)
    anywhere = pl.BlockSpec(memory_space=pl.ANY)
    log_weights, resampled = pl.pallas_call(
        functools.partial(finish_kernel, particles, doms),
        in_specs=[pl.BlockSpec(memory_space=pltpu.SMEM), anywhere, vmem],
        out_specs=[vmem, anywhere],
        out_shape=[
            jax.ShapeDtypeStruct((1, particles), jnp.float32),
            jax.ShapeDtypeStruct(resampled.shape, resampled.dtype),
        ],
        input_output_aliases={1: 1},
        compiler_params=pltpu.CompilerParams(vmem_limit_bytes=2 * MIB),
        name="log_weights",
    )(ids, resampled, parts)
    return resampled, log_weights.reshape(particles)


def resample_kernel(ids_ref, ancestors_ref, own_ref, other_ref, out_ref):
    index = pl.program_id(0)
    own = ancestors_ref[index] // pl.num_programs(0) == ids_ref[0]

    @pl.when(own)
    def _():
        out_ref[...] = own_ref[...]

    @pl.when(jnp.logical_not(own))
    def _():
        out_ref[...] = other_ref[...]


def resample(ids, ancestors, own, other):
    particles, tokens, columns = own.shape
    block = (1, tokens, columns)
    parent = pl.BlockSpec(block, lambda i, ids, ancestors: (ancestors[i] % particles, 0, 0))
    return pl.pallas_call(
        resample_kernel,
        grid_spec=pltpu.PrefetchScalarGridSpec(
            num_scalar_prefetch=2,
            grid=(particles,),
            in_specs=[parent, parent],
            out_specs=pl.BlockSpec(block, lambda i, ids, ancestors: (i, 0, 0)),
        ),
        out_shape=jax.ShapeDtypeStruct(own.shape, own.dtype),
        compiler_params=pltpu.CompilerParams(vmem_limit_bytes=4 * MIB),
        name="resample",
    )(ids, ancestors, own, other)


def shifted(array, axis, step):
    count = lax.axis_size(axis)
    return lax.ppermute(array, axis, [(i, (i + step) % count) for i in range(count)])


def swapped(array, axis, bit):
    return lax.ppermute(array, axis, [(i, i ^ bit) for i in range(lax.axis_size(axis))])


def exchange(array):
    return lax.all_to_all(array, "seq", 0, 0, tiled=True)


def on_device(
    latents,
    queries,
    keys,
    values,
    out_weight,
    step_index,
    embed_weight,
    norm_gain,
    up_weight,
    head_weight,
    prev_logw,
    ancestors,
):
    seq_count = lax.axis_size("seq")
    group_count = lax.axis_size("groups")
    dom_count = lax.axis_size("dom")
    holders = group_count * dom_count
    dom = lax.axis_index("dom")
    group = lax.axis_index("groups")
    seq = lax.axis_index("seq")
    particles, tokens, model_width = latents.shape
    head_width = model_width // HEADS
    width = particles * model_width // seq_count
    chunks = 2 if width % (2 * LANES) == 0 else 1

    ids = jnp.stack([dom, group, seq, step_index[0]]).astype(jnp.int32)

    embed_columns = embed_weight.shape[1] // holders
    embed_share = lax.dynamic_slice_in_dim(
        embed_weight, (dom * group_count + group) * embed_columns, embed_columns, 1
    )[None]
    up_depth = up_weight.shape[0] // group_count
    up_columns = up_weight.shape[1] // dom_count
    up_share = lax.dynamic_slice(
        up_weight, (group * up_depth, dom * up_columns), (up_depth, up_columns)
    )[None]
    bits = [1 << place for place in reversed(range(1, seq_count.bit_length() - 1))]
    near = [0]
    for bit in bits[:-2]:
        embed_share = jnp.concatenate([embed_share, swapped(embed_share, "seq", bit)])
        up_share = jnp.concatenate([up_share, swapped(up_share, "seq", bit)])
        near = near + [offset ^ bit for offset in near]
    high, low = bits[-2:]

    def over_groups(array):
        return [array] + [shifted(array, "groups", k) for k in range(1, group_count)]

    packed = pack(queries, keys, values, chunks, width)
    embed_share = jnp.concatenate([embed_share, swapped(embed_share, "seq", high)])
    packed[0] = gate(packed[0], [embed_share])

    arrived = [exchange(packed[0])]
    up_high, up_low = swapped(up_share, "seq", high), swapped(up_share, "seq", low)
    own_pair, own_groups = swapped(up_share, "seq", 1), over_groups(up_share)
    for bit in (low, 1):
        embed_share = jnp.concatenate([embed_share, swapped(embed_share, "seq", bit)])
    after = [embed_share, up_high, up_low, own_pair, *own_groups[1:]]
    packed[1:] = [gate(piece, after) for piece in packed[1:]]

    arrived += [exchange(piece) for piece in packed[1:]]
    up_both = swapped(up_high, "seq", low)
    up_next = jnp.concatenate([up_high, up_low])
    next_pair, next_groups = swapped(up_next, "seq", 1), over_groups(up_next)
    embed_near = over_groups(embed_share)
    attended = [attention(arrived[0], head_width)]
    after = [up_both, next_pair, *next_groups[1:], *embed_near[1:]]
    attended[0] = gate(attended[0], after)

    returned = [exchange(attended[0])]
    both_pair, both_groups = swapped(up_both, "seq", 1), over_groups(up_both)
    own_pairs = over_groups(own_pair)
    attended += [attention(piece, head_width) for piece in arrived[1:]]
    after = [both_pair, *both_groups[1:], *own_pairs[1:]]
    attended[1:] = [gate(piece, after) for piece in attended[1:]]

    returned += [exchange(piece) for piece in attended[1:]]
    embed_parts = embed_near + [
        shifted(piece, "dom", k) for k in range(1, dom_count) for piece in embed_near
    ]
    next_pairs = over_groups(next_pair)
    both_pairs = [both_pair] + [swapped(piece, "seq", 1) for piece in both_groups[1:]]
    up_parts = own_groups + own_pairs + next_groups + next_pairs + both_groups + both_pairs
    up_offsets = [
        offset ^ bit ^ pair
        for bits in ((0,), (high, low), (high ^ low,))
        for pair in (0, 1)
        for bit in bits
        for offset in near
    ]
    embed_offsets = near + [offset ^ high for offset in near]
    for bit in (low, 1):
        embed_offsets = embed_offsets + [offset ^ bit for offset in embed_offsets]

    begun = first_project(latents, out_weight, returned.pop(0), chunks, width) if chunks > 1 else None
    stepped, features = project_embed(
        ids,
        embed_offsets,
        latents,
        begun,
        returned,
        chunks,
        width,
        out_weight,
        embed_parts,
        norm_gain,
        group_count,
        [*next_pairs[1:], *both_pairs[1:]],
    )
    stepped_other = shifted(stepped, "dom", 1)
    features_other = shifted(features, "dom", 1)

    scale = potential_scale / math.sqrt(tokens * seq_count)
    head = head_weight.reshape(seq_count * dom_count, 1, up_columns)
    partial = reward(
        ids,
        prev_logw,
        [features, features_other],
        up_parts,
        group_count,
        up_offsets,
        head,
        particles,
        scale,
        dom_count * seq_count,
    )
    logits = lax.all_to_all(partial, ("dom", "seq"), 0, 0, tiled=True)
    resampled = resample(ids, ancestors.astype(jnp.int32), stepped, stepped_other)
    return finish(ids, logits, resampled, particles, dom_count)


def solution(mesh):
    in_specs = (
        P(("groups", "dom"), "seq", None),
        P(("groups", "dom"), "seq", None),
        P(("groups", "dom"), "seq", None),
        P(("groups", "dom"), "seq", None),
        P(),
        P("groups"),
        P("seq", None),
        P(),
        P(None, "seq"),
        P(),
        P(("groups", "dom")),
        P(("groups", "dom")),
    )
    out_specs = (P(("groups", "dom"), "seq", None), P(("groups", "dom")))
    return jax.shard_map(
        on_device, mesh=mesh, in_specs=in_specs, out_specs=out_specs, check_vma=False
    )
```
